128 devices in a mesh: seq: 64 (over y, x_lo, z, core), ffn: 2 (over x_hi).
Axes of the slice: x: 4 (x_hi: 2, x_lo: 2; x = x_hi * 2 + x_lo), y: 4, z: 4, core: 2. Of those that a mesh axis runs over, the one named last changes fastest.
Arguments:
- tokens: bfloat16 [16384, 2048], P(('seq', 'ffn')), may hold values from -6 to 6
- caption_len: int32 [64], P('seq'), may hold values from 128 to 192, as said below
- norm1_gain: float32 [2048], replicated, may hold values from 0.5 to 1.5
- norm1_bias: float32 [2048], replicated, may hold values from -4 to 4
- w_query: float32 [2048, 2048], P('seq', 'ffn'), may hold values from -0.125 to 0.125
- w_key: float32 [2048, 2048], P('seq', 'ffn'), may hold values from -0.125 to 0.125
- w_value: float32 [2048, 2048], P('seq', 'ffn'), may hold values from -0.125 to 0.125
- inner_gain: float32 [2048], P('ffn'), may hold values from 0.5 to 1.5
- inner_bias: float32 [2048], P('ffn'), may hold values from -4 to 4
- w_proj: float32 [2048, 2048], P('ffn', 'seq'), may hold values from -0.125 to 0.125
- norm2_gain: float32 [2048], replicated, may hold values from 0.5 to 1.5
- norm2_bias: float32 [2048], replicated, may hold values from -4 to 4
- w_up: float32 [2048, 8192], P('seq', 'ffn'), may hold values from -0.125 to 0.125
- ffn_norm_gain: float32 [8192], P('ffn'), may hold values from 0.5 to 1.5
- ffn_norm_bias: float32 [8192], P('ffn'), may hold values from -4 to 4
- w_down: float32 [8192, 2048], P('ffn', 'seq'), may hold values from -0.0625 to 0.0625
- cotangent: bfloat16 [16384, 2048], P(('seq', 'ffn')), may hold values from -24 to 24
Outputs:
- layer_out: bfloat16 [16384, 2048], P(('seq', 'ffn'))
- grad_input: bfloat16 [16384, 2048], P(('seq', 'ffn'))
- grad_norm1_gain: float32 [2048], replicated
- grad_norm1_bias: float32 [2048], replicated
- grad_query: float32 [2048, 2048], P('seq', 'ffn')
- grad_key: float32 [2048, 2048], P('seq', 'ffn')
- grad_value: float32 [2048, 2048], P('seq', 'ffn')
- grad_inner_gain: float32 [2048], P('ffn')
- grad_inner_bias: float32 [2048], P('ffn')
- grad_proj: float32 [2048, 2048], P('ffn', 'seq')
- grad_norm2_gain: float32 [2048], replicated
- grad_norm2_bias: float32 [2048], replicated
- grad_up: float32 [2048, 8192], P('seq', 'ffn')
- grad_ffn_gain: float32 [8192], P('ffn')
- grad_ffn_bias: float32 [8192], P('ffn')
- grad_down: float32 [8192, 2048], P('ffn', 'seq')
The draws below stay inside these ranges and needn't reach their ends.
Inputs may be any that keep to these rules, and one draw needn't show every extreme that they name: A sequence's valid slots are its first 64 + caption_len; some sequence has exactly 192 caption tokens and some other exactly 128.
All inputs are finite; a program needn't handle non-finite values.
Results may differ from the reference program's by a relative error of at most 0.014.
Values may be sent and summed in bfloat16 or wider, within the bound.
A program may use at most 256 MiB of HBM per device.

```python
import math
import jax
import jax.numpy as jnp
from jax import lax

D = 2048
HEADS = 32
HEAD_DIM = 64
FF = 8192
SLOTS = 256
IMAGE = 64
SEQS = 64
TOKENS = 16384


def draw_caption_len(key, part):
    key = jax.random.fold_in(key, 11)
    key_len, key_pick = jax.random.split(key)
    short_len = (SLOTS - IMAGE) * 2 // 3
    long_len = SLOTS - IMAGE
    lengths = jax.random.randint(key_len, (SEQS,), short_len, long_len + 1)
    picked = jax.random.permutation(key_pick, SEQS)
    lengths = lengths.at[picked[0]].set(long_len).at[picked[1]].set(short_len)
    return lengths.astype(jnp.int32)


def with_spikes(entries, key, source, target, parts, factor):
    owner, partner = [(jnp.arange(entries.shape[dim]) // (entries.shape[dim] // parts)).reshape([-1 if axis == dim else 1 for axis in range(entries.ndim)]) for dim in (source, target)]
    chosen = jax.random.permutation(key, parts)[partner]
    strong = (owner == chosen) | (owner == (partner + parts // 2) % parts)
    return jnp.where(strong, factor * entries, entries)


def shard_levels(key, dims, cuts, smallest, largest):
    def one(dim, shards_of):
        steps = jax.random.uniform(jax.random.fold_in(jax.random.fold_in(key, 6), dim), (shards_of,), jnp.float32, smallest / len(cuts), largest / len(cuts))
        return jnp.repeat(jnp.exp(steps), dims[dim] // shards_of).reshape((-1,) + (1,) * (len(dims) - dim - 1))

    factor_of = one(*cuts[0])
    for cut in cuts[1:]:
        factor_of = factor_of * one(*cut)
    return factor_of


def normal_values(rng, dims, width, bound, shards=(), kind=jnp.bfloat16):
    entries = jax.random.normal(rng, dims, jnp.float32) * width
    if len(shards) > 0:
        entries = shard_levels(rng, dims, shards, -0.22, 0.18) * entries
    return jnp.clip(entries, min=-bound, max=bound).astype(kind)


def noise_with(stream_key, shape, scale, bound, cuts, heavy, dtype=jnp.bfloat16):
    array = scale * jax.random.normal(stream_key, shape, jnp.float32)
    if cuts:
        array = array * shard_levels(stream_key, shape, cuts, -0.22, 0.18)
    return jnp.clip(with_spikes(array, jax.random.fold_in(stream_key, 3), *heavy), -bound, bound).astype(dtype)


def setup_inputs(seed: int = 0) -> dict:
    seeds = jax.random.split(jax.random.key(seed), 18)
    return {
        "tokens": normal_values(seeds[0], (TOKENS, D), 1.0, 6.0, ((0, 128),)),
        "caption_len": draw_caption_len(jax.random.fold_in(seeds[17], 71), 0),
        "norm1_gain": jnp.clip(1.0 + 0.1 * jax.random.normal(seeds[2], (D,), jnp.float32), 0.5, 1.5),
        "norm1_bias": normal_values(seeds[3], (D,), 0.3, 4.0, (), jnp.float32),
        "w_query": normal_values(seeds[4], (D, D), D ** -0.5, 0.125, ((0, 64), (1, 2)), jnp.float32),
        "w_key": normal_values(seeds[5], (D, D), D ** -0.5, 0.125, ((0, 64), (1, 2)), jnp.float32),
        "w_value": normal_values(seeds[6], (D, D), D ** -0.5, 0.125, ((0, 64), (1, 2)), jnp.float32),
        "inner_gain": jnp.clip(1.0 + 0.1 * jax.random.normal(seeds[7], (D,), jnp.float32), 0.5, 1.5),
        "inner_bias": normal_values(seeds[8], (D,), 0.3, 4.0, ((0, 2),), jnp.float32),
        "w_proj": normal_values(seeds[9], (D, D), D ** -0.5, 0.125, ((0, 2), (1, 64)), jnp.float32),
        "norm2_gain": jnp.clip(1.0 + 0.1 * jax.random.normal(seeds[10], (D,), jnp.float32), 0.5, 1.5),
        "norm2_bias": normal_values(seeds[11], (D,), 0.3, 4.0, (), jnp.float32),
        "w_up": normal_values(seeds[12], (D, FF), D ** -0.5, 0.125, ((0, 64), (1, 2)), jnp.float32),
        "ffn_norm_gain": jnp.clip(1.0 + 0.1 * jax.random.normal(seeds[13], (FF,), jnp.float32), 0.5, 1.5),
        "ffn_norm_bias": normal_values(seeds[14], (FF,), 0.3, 4.0, ((0, 2),), jnp.float32),
        "w_down": normal_values(seeds[15], (FF, D), FF ** -0.5, 0.0625, ((0, 2), (1, 64)), jnp.float32),
        "cotangent": noise_with(seeds[16], (TOKENS, D), 1.0, 24.0, ((0, 128),), (0, 1, 128, 5.5)),
    }


norm_eps = 1e-05
highest = lax.Precision.HIGHEST

@jax.custom_vjp
def low(v):
    return lax.optimization_barrier(v.astype(jnp.bfloat16)).astype(jnp.float32)

@jax.custom_vjp
def low_back(v):
    return v

def low_keep(v):
    return (low(v), None)

def low_pass(kept, grad):
    return (grad,)

def back_keep(v):
    return (v, None)

def back_low(kept, grad):
    return (low(grad),)
low.defvjp(low_keep, low_pass)
low_back.defvjp(back_keep, back_low)

def matmul(left_side, right_side):
    return jnp.dot(left_side, right_side, precision=highest, preferred_element_type=jnp.float32)

def norm_rows(values, norm_gain, norm_bias):
    center = lax.optimization_barrier(jnp.mean(values, -1, keepdims=True))
    spread = lax.optimization_barrier(jnp.mean(values * values, -1, keepdims=True)) - center * center
    return (values - center) * lax.rsqrt(spread + norm_eps) * norm_gain + norm_bias

def xpos_tables(direction):
    half_dim = HEAD_DIM // 2
    pair_index = jnp.arange(half_dim).astype(jnp.float32)
    frequency = jnp.power(10000.0, -pair_index / half_dim)
    xpos_zeta = (pair_index / half_dim + 0.4) / 1.4
    position = jnp.arange(SLOTS).astype(jnp.float32)[:, None]
    phase_angle = position * frequency
    xpos_decay = jnp.exp(direction * position / 512.0 * jnp.log(xpos_zeta))
    cosine_table = jnp.concatenate([jnp.cos(phase_angle) * xpos_decay] * 2, -1)[:, None, :]
    sine_table = jnp.concatenate([jnp.sin(phase_angle) * xpos_decay] * 2, -1)[:, None, :]
    return (cosine_table, sine_table)

def rotated(values):
    half_dim = values.shape[-1] // 2
    return jnp.concatenate([-values[..., half_dim:], values[..., :half_dim]], -1)

def apply_xpos(values, cosine_table, sine_table):
    return values * cosine_table + rotated(values) * sine_table

def attend(block_parts):
    queries, keys_rot, values_in, valid_len = block_parts
    scores = low_back(HEAD_DIM ** (-0.5) * jnp.einsum('bqhd,bkhd->bhqk', queries, keys_rot, precision=highest))
    position = jnp.arange(SLOTS)
    allowed = (position[None, :] <= position[:, None])[None] & (position[None, None, :] < valid_len[:, None, None])
    scores = jnp.where(allowed[:, None], scores, -1e+30)
    row_peak = lax.optimization_barrier(jnp.max(scores, -1, keepdims=True))
    row_exps = jnp.exp(scores - row_peak)
    attn_probs = low(row_exps / lax.optimization_barrier(jnp.sum(row_exps, -1, keepdims=True)))
    return jnp.einsum('bhqk,bkhd->bqhd', attn_probs, values_in, precision=highest)

def reference(tokens, caption_len, norm1_gain, norm1_bias, w_query, w_key, w_value, inner_gain, inner_bias, w_proj, norm2_gain, norm2_bias, w_up, ffn_norm_gain, ffn_norm_bias, w_down, cotangent):
    seq_group = math.gcd(SEQS, 16)
    row_group = math.gcd(TOKENS, 4096)
    valid_all = (IMAGE + caption_len).astype(jnp.int32).reshape(SEQS // seq_group, seq_group)
    cos_up, sin_up = xpos_tables(1.0)
    cos_down, sin_down = xpos_tables(-1.0)
    head_shape = (SEQS, SLOTS, HEADS, HEAD_DIM)
    group_shape = (SEQS // seq_group, seq_group, SLOTS, HEADS, HEAD_DIM)

    def forward(tokens_f, gain_one, bias_one, query_m, key_m, value_m, gain_inner, bias_inner, proj_m, gain_two, bias_two, up_m, gain_ffn, bias_ffn, down_m):
        first_rows = low(norm_rows(tokens_f, gain_one, bias_one))
        queries = low_back(matmul(first_rows, low(query_m)))
        keys_raw = low_back(matmul(first_rows, low(key_m)))
        values_in = low(low_back(matmul(first_rows, low(value_m))))
        query_rot = low(apply_xpos(queries.reshape(head_shape), cos_up, sin_up)).reshape(group_shape)
        key_rot = low(apply_xpos(keys_raw.reshape(head_shape), cos_down, sin_down)).reshape(group_shape)
        mixed_heads = lax.map(jax.checkpoint(attend), (query_rot, key_rot, values_in.reshape(group_shape), valid_all))
        mixed_heads = low_back(mixed_heads.reshape(TOKENS, D))
        context = low(norm_rows(mixed_heads, gain_inner, bias_inner))
        attended = tokens_f + low_back(matmul(context, low(proj_m)))
        up_low = low(up_m)
        down_low = low(down_m)

        def feed_block(row_block):
            second_rows = low(norm_rows(row_block, gain_two, bias_two))
            up_proj = low_back(matmul(second_rows, up_low))
            activated = jax.nn.gelu(up_proj, approximate=False)
            ffn_normed = low(norm_rows(activated, gain_ffn, bias_ffn))
            return low_back(matmul(ffn_normed, down_low))
        ffn_out = lax.map(jax.checkpoint(feed_block), attended.reshape(TOKENS // row_group, row_group, D))
        return attended + ffn_out.reshape(TOKENS, D)
    primals = (tokens.astype(jnp.float32), norm1_gain, norm1_bias, w_query, w_key, w_value, inner_gain, inner_bias, w_proj, norm2_gain, norm2_bias, w_up, ffn_norm_gain, ffn_norm_bias, w_down)
    layer_out, pullback = jax.vjp(forward, *primals)
    gradients = pullback(cotangent.astype(jnp.float32))
    return (layer_out.astype(jnp.bfloat16), gradients[0].astype(jnp.bfloat16), gradients[1], gradients[2], gradients[3], gradients[4], gradients[5], gradients[6], gradients[7], gradients[8], gradients[9], gradients[10], gradients[11], gradients[12], gradients[13], gradients[14])
```

```python
import functools

import jax
import jax.numpy as jnp
import numpy as np
from jax import lax
from jax.experimental import pallas as pl
from jax.experimental.pallas import tpu as pltpu
from jax.sharding import PartitionSpec as P

D = 2048
HEAD_DIM = 64
FF = 8192
SLOTS = 256
IMAGE = 64
EPS = 1e-05
F32 = jnp.float32
BF16 = jnp.bfloat16
MESH = pl.DeviceIdType.MESH
VMEM = pltpu.VMEM
N_SEM = 192


def device_at(y, x, z, c):
    return (((y * 2 + x % 2) * 4 + z) * 2 + c, x // 2)


def line_slot(x, c):
    return ((x % 2) * 2 + c) * 2 + x // 2


class Net:
    def __init__(self, send, recv, local):
        seq, ffn = lax.axis_index("seq"), lax.axis_index("ffn")
        self.y, self.z, self.c = seq // 16, (seq // 2) % 4, seq % 2
        self.x = ffn * 2 + (seq // 8) % 2
        self.send, self.recv, self.local = send, recv, local
        self.used, self.used_local = 0, 0
        self.out = []

    def along_x(self, dx, dc=0):
        return device_at(self.y, (self.x + dx) % 4, self.z, (self.c + dc) % 2)

    def along_y(self, dy):
        return device_at((self.y + dy) % 4, self.x, self.z, self.c)

    def along_z(self, dz):
        return device_at(self.y, self.x, (self.z + dz) % 4, self.c)

    def pair(self, dx, dc):
        x = (self.x // 2) * 2 + (self.x + dx) % 2
        return device_at(self.y, x, self.z, (self.c + dc) % 2)

    def greet(self, partners):
        barrier = pltpu.get_barrier_semaphore()
        for partner in partners:
            pl.semaphore_signal(barrier, inc=1, device_id=partner, device_id_type=MESH)
        pl.semaphore_wait(barrier, len(partners))

    def push(self, src, dst, device):
        k = self.used
        self.used += 1
        copy = pltpu.make_async_remote_copy(
            src_ref=src,
            dst_ref=dst,
            send_sem=self.send.at[k],
            recv_sem=self.recv.at[k],
            device_id=device,
            device_id_type=MESH,
        )
        copy.start()
        self.out.append(copy)
        return k

    def arrived(self, k, landed):
        pltpu.make_async_remote_copy(
            src_ref=landed,
            dst_ref=landed,
            send_sem=self.send.at[k],
            recv_sem=self.recv.at[k],
            device_id=self.along_x(0, 1),
            device_id_type=MESH,
        ).wait_recv()

    def keep(self, src, dst):
        copy = pltpu.make_async_copy(src, dst, self.local.at[self.used_local])
        self.used_local += 1
        copy.start()
        return copy

    def drain(self):
        for copy in self.out:
            copy.wait_send()
        self.out = []


def add_into(dst, *terms):
    def step(i, carry):
        rows = pl.ds(pl.multiple_of(i * 16, 16), 16)
        total = terms[0][rows, :].astype(F32)
        for term in terms[1:]:
            total = total + term[rows, :].astype(F32)
        dst[rows, :] = total.astype(dst.dtype)
        return carry

    lax.fori_loop(0, dst.shape[0] // 16, step, 0)


class LineGather:
    def __init__(self, net, own, full):
        self.net, self.own, self.full = net, own, full

    def block(self, dx, dc=0, half=None):
        net = self.net
        slot = line_slot((net.x + dx) % 4, (net.c + dc) % 2)
        if half is None:
            return self.full.at[slot]
        return self.full.at[slot, pl.ds(64 * half, 64)]

    def start(self):
        net, mine = self.net, self.block(0)
        self.a = net.push(self.own, mine, net.along_x(1))
        self.b = net.push(self.own, mine, net.along_x(-1))
        self.s0 = net.push(self.own, mine, net.along_x(0, 1))
        self.kept = net.keep(self.own, mine)

    def forward(self):
        net = self.net
        net.arrived(self.a, self.block(-1))
        self.fa = net.push(self.block(-1, 0, 0), self.block(-1, 0, 0), net.along_x(1))
        self.sa = net.push(self.block(-1), self.block(-1), net.along_x(0, 1))
        net.arrived(self.b, self.block(1))
        self.fb = net.push(self.block(1, 0, 1), self.block(1, 0, 1), net.along_x(-1))
        self.sb = net.push(self.block(1), self.block(1), net.along_x(0, 1))

    def share(self):
        net = self.net
        net.arrived(self.fa, self.block(2, 0, 0))
        self.sfa = net.push(self.block(2, 0, 0), self.block(2, 0, 0), net.along_x(0, 1))
        net.arrived(self.fb, self.block(2, 0, 1))
        self.sfb = net.push(self.block(2, 0, 1), self.block(2, 0, 1), net.along_x(0, 1))

    def finish(self):
        net = self.net
        net.arrived(self.s0, self.block(0, 1))
        net.arrived(self.sa, self.block(-1, 1))
        net.arrived(self.sb, self.block(1, 1))
        net.arrived(self.sfa, self.block(2, 1, 0))
        net.arrived(self.sfb, self.block(2, 1, 1))
        self.kept.wait()


class RingSum:
    def __init__(self, net, mine, landing, ahead, behind):
        self.net, self.mine, self.landing = net, mine, landing
        self.ahead, self.behind = ahead, behind

    def start_far(self):
        net, land = self.net, self.landing
        self.f0 = net.push(self.mine(2, 0), land.at[0], self.ahead)
        self.f1 = net.push(self.mine(2, 1), land.at[1], self.behind)

    def start_near(self, d):
        net, land = self.net, self.landing
        if d == 1:
            self.r1 = net.push(self.mine(1, 1), land.at[3], self.ahead)
        else:
            self.r0 = net.push(self.mine(-1, 0), land.at[4], self.behind)

    def pass_on(self):
        net, land = self.net, self.landing
        net.arrived(self.f0, land.at[0])
        add_into(land.at[0], land.at[0], self.mine(1, 0))
        self.s0 = net.push(land.at[0], land.at[2], self.ahead)
        net.arrived(self.f1, land.at[1])
        add_into(land.at[1], land.at[1], self.mine(-1, 1))
        self.s1 = net.push(land.at[1], land.at[5], self.behind)

    def finish(self, out=None):
        net, land = self.net, self.landing
        net.arrived(self.s0, land.at[2])
        net.arrived(self.r0, land.at[4])
        add_into(land.at[2] if out is None else out(0), self.mine(0, 0), land.at[2], land.at[4])
        net.arrived(self.r1, land.at[3])
        net.arrived(self.s1, land.at[5])
        add_into(land.at[3] if out is None else out(1), self.mine(0, 1), land.at[3], land.at[5])


class LineSum:
    def __init__(self, net, part, other, landing):
        self.net, self.part, self.other = net, part, other
        self.ring = RingSum(net, self.mine, landing, net.along_x(1), net.along_x(-1))

    def block(self, dx, dc):
        net = self.net
        return self.part.at[line_slot((net.x + dx) % 4, (net.c + dc) % 2)]

    def mine(self, d, half):
        return self.other.at[d % 4, pl.ds(64 * half, 64)]

    def start(self):
        net = self.net
        self.k = {
            d: net.push(self.block(d, 1), self.other.at[d % 4], net.along_x(0, 1))
            for d in (2, 1, -1, 0)
        }

    def chip(self):
        for d in (2, 1, -1, 0):
            self.net.arrived(self.k[d], self.other.at[d % 4])
            add_into(self.other.at[d % 4], self.other.at[d % 4], self.block(d, 0))
            if d == 2:
                self.ring.start_far()
            elif d:
                self.ring.start_near(d)

    def pass_on(self):
        self.ring.pass_on()

    def finish(self, out):
        self.ring.finish(lambda half: out.at[pl.ds(64 * half, 64)])


class GridGather:
    def __init__(self, net, pieces, full):
        self.net, self.pieces, self.full = net, pieces, full

    def spot(self, dx, dc):
        net = self.net
        return self.full.at[net.y, (net.x + dx) % 2, net.z, pl.ds(32 * ((net.c + dc) % 2), 32)]

    def exchange(self):
        net = self.net
        self.k = {}
        for dx, dc in ((1, 0), (1, 1), (0, 1)):
            to = ((net.x + dx) % 2) * 2 + (net.c + dc) % 2
            self.k[dx, dc] = net.push(self.pieces.at[to], self.spot(0, 0), net.pair(dx, dc))
        me = (net.x % 2) * 2 + net.c
        self.kept = net.keep(self.pieces.at[me], self.spot(0, 0))

    def slab(self, t, dp, dq, half=None):
        net = self.net
        dy, dz = (dq, dp) if t == 0 else (dp, dq)
        at = ((net.y + dy) % 4, t, (net.z + dz) % 4)
        return self.full.at[at] if half is None else self.full.at[(*at, pl.ds(32 * half, 32))]

    def to_p(self, t, d):
        return self.net.along_z(d) if t == 0 else self.net.along_y(d)

    def to_q(self, t, d):
        return self.net.along_y(d) if t == 0 else self.net.along_z(d)

    def same(self, ref, device):
        return self.net.push(ref, ref, device)

    def second(self, t, dp):
        self.q[t, dp] = (
            self.same(self.slab(t, dp, 0), self.to_q(t, 1)),
            self.same(self.slab(t, dp, 0), self.to_q(t, -1)),
        )

    def start(self):
        for dx, dc in ((0, 1), (1, 0), (1, 1)):
            self.net.arrived(self.k[dx, dc], self.spot(dx, dc))
        self.kept.wait()
        self.p, self.q, self.f = {}, {}, {}
        for t in (0, 1):
            self.p[t] = (
                self.same(self.slab(t, 0, 0), self.to_p(t, 1)),
                self.same(self.slab(t, 0, 0), self.to_p(t, -1)),
            )
        for t in (0, 1):
            self.second(t, 0)

    def near(self):
        net = self.net
        for t in (0, 1):
            a, b = self.p[t]
            net.arrived(a, self.slab(t, -1, 0))
            fa = self.same(self.slab(t, -1, 0, 0), self.to_p(t, 1))
            net.arrived(b, self.slab(t, 1, 0))
            fb = self.same(self.slab(t, 1, 0, 1), self.to_p(t, -1))
            self.f[t] = (fa, fb)
        for t in (0, 1):
            self.second(t, -1)
            self.second(t, 1)

    def far(self):
        for t in (0, 1):
            self.net.arrived(self.f[t][0], self.slab(t, 2, 0, 0))
            self.net.arrived(self.f[t][1], self.slab(t, 2, 0, 1))
            self.second(t, 2)

    def pass_on(self, dp):
        net = self.net
        for t in (0, 1):
            a, b = self.q[t, dp]
            net.arrived(a, self.slab(t, dp, -1))
            fa = self.same(self.slab(t, dp, -1, 0), self.to_q(t, 1))
            net.arrived(b, self.slab(t, dp, 1))
            fb = self.same(self.slab(t, dp, 1, 1), self.to_q(t, -1))
            self.f[t, dp] = (fa, fb)

    def finish(self):
        for dp in (0, -1, 1, 2):
            for t in (0, 1):
                self.net.arrived(self.f[t, dp][0], self.slab(t, dp, 2, 0))
                self.net.arrived(self.f[t, dp][1], self.slab(t, dp, 2, 1))


class GridSum:
    def __init__(self, net, part, landing, done, out):
        self.net, self.part, self.landing, self.done, self.out = net, part, landing, done, out
        self.rings = {}
        for t in (0, 1):
            for dp in (2, 1, -1, 0):
                self.rings[t, dp] = RingSum(
                    net,
                    functools.partial(self.term, t, dp),
                    landing.at[t, dp % 4],
                    self.to_q(t, 1),
                    self.to_q(t, -1),
                )
            self.rings[t] = RingSum(
                net,
                functools.partial(self.column, t),
                landing.at[t, 4],
                self.to_p(t, 1),
                self.to_p(t, -1),
            )

    def to_p(self, t, d):
        return self.net.along_z(d) if t == 0 else self.net.along_y(d)

    def to_q(self, t, d):
        return self.net.along_y(d) if t == 0 else self.net.along_z(d)

    def term(self, t, dp, dq, half):
        net = self.net
        dy, dz = (dq, dp) if t == 0 else (dp, dq)
        return self.part.at[(net.y + dy) % 4, t, (net.z + dz) % 4, pl.ds(32 * half, 32)]

    def column(self, t, dp, half):
        return self.landing.at[t, dp % 4, 2 + half]

    def start(self, dp):
        for t in (0, 1):
            self.rings[t, dp].start_far()
        for t in (0, 1):
            self.rings[t, dp].start_near(1)
            self.rings[t, dp].start_near(-1)

    def pass_on(self, dp):
        for t in (0, 1):
            self.rings[t, dp].pass_on()

    def finish(self, dp):
        for t in (0, 1):
            self.rings[t, dp].finish()
            if dp == 2:
                self.rings[t].start_far()
            elif dp:
                self.rings[t].start_near(dp)

    def pass_on_last(self):
        for t in (0, 1):
            self.rings[t].pass_on()

    def finish_last(self):
        net = self.net
        for t in (0, 1):
            self.rings[t].finish(lambda half: self.done.at[t, half])
        me = (net.x % 2) * 2 + net.c
        self.k = {}
        for dx, dc in ((1, 0), (1, 1), (0, 1)):
            src = self.done.at[(net.x + dx) % 2, (net.c + dc) % 2]
            self.k[dx, dc] = net.push(src, self.out.at[me], net.pair(dx, dc))
        self.kept = net.keep(self.done.at[net.x % 2, net.c], self.out.at[me])

    def collect(self):
        net = self.net
        for dx, dc in ((1, 0), (1, 1), (0, 1)):
            at = ((net.x + dx) % 2) * 2 + (net.c + dc) % 2
            net.arrived(self.k[dx, dc], self.out.at[at])
        self.kept.wait()


class SmallSum:
    def __init__(self, net, own, slots, me, partners):
        self.net, self.own, self.slots, self.me, self.partners = net, own, slots, me, partners

    def start(self):
        net = self.net
        self.k = [(net.push(self.own, self.slots.at[self.me], to), at) for to, at in self.partners]
        self.slots[self.me] = self.own[...]

    def finish(self, out):
        for k, at in self.k:
            self.net.arrived(k, self.slots.at[at])
        total = self.slots[0]
        for i in range(1, self.slots.shape[0]):
            total = total + self.slots[i]
        out[...] = total


def line_partners(net):
    return [
        (net.along_x(dx, dc), ((net.x - dx) % 4) * 2 + (net.c + dc) % 2)
        for dx in range(4)
        for dc in range(2)
        if dx or dc
    ]


def sem_scratch():
    return [
        pltpu.SemaphoreType.DMA((N_SEM,)),
        pltpu.SemaphoreType.DMA((N_SEM,)),
        pltpu.SemaphoreType.DMA((16,)),
    ]


def spec(space):
    return pl.BlockSpec(memory_space=space)


def shape(dims, dtype):
    return jax.ShapeDtypeStruct(dims, dtype)


def comm_call(body, name, collective_id, ins, in_spaces, outs, out_spaces, scratch, mib):
    return pl.pallas_call(
        body,
        out_shape=outs,
        in_specs=[spec(s) for s in in_spaces],
        out_specs=[spec(s) for s in out_spaces],
        scratch_shapes=scratch + sem_scratch(),
        compiler_params=pltpu.CompilerParams(
            collective_id=collective_id, has_side_effects=True, vmem_limit_bytes=mib << 20
        ),
        name=name,
    )(*ins)


def x_neighbours(net):
    return [net.along_x(1), net.along_x(-1), net.along_x(0, 1)]


def grid_neighbours(net):
    return [net.along_y(1), net.along_y(-1), net.along_z(1), net.along_z(-1)]


def pair_neighbours(net):
    return [net.pair(1, 0), net.pair(1, 1), net.pair(0, 1)]


def first_kernel(rows, cap, pieces, full_rows, caps, full_weights, cap_slots, send, recv, local):
    net = Net(send, recv, local)
    net.greet(x_neighbours(net) + grid_neighbours(net) + pair_neighbours(net))
    weights = GridGather(net, pieces, full_weights)
    weights.exchange()
    me = (net.x % 2) * 2 + net.c
    cap_k = {}
    for dx, dc in ((1, 0), (1, 1), (0, 1)):
        cap_k[dx, dc] = net.push(cap, cap_slots.at[me], net.pair(dx, dc))
    cap_slots[me] = cap[...]
    line = LineGather(net, rows, full_rows)
    line.start()
    weights.start()
    weights.near()
    line.forward()
    weights.far()
    weights.pass_on(0)
    line.share()
    weights.pass_on(-1)
    weights.pass_on(1)
    weights.pass_on(2)
    for dx, dc in ((1, 0), (1, 1), (0, 1)):
        net.arrived(cap_k[dx, dc], cap_slots.at[((net.x + dx) % 2) * 2 + (net.c + dc) % 2])
    caps[...] = cap_slots[...]
    line.finish()
    weights.finish()
    net.drain()


def first_call(rows, cap, pieces):
    width = pieces.shape[2]
    return comm_call(
        first_kernel,
        "gather_first",
        1,
        (rows, cap, pieces),
        (pl.ANY, VMEM, pl.ANY),
        (
            shape((8, 128, D), BF16),
            shape((4, 8, 128), jnp.int32),
            shape((4, 2, 4, 64, width), BF16),
        ),
        (pl.ANY, VMEM, pl.ANY),
        [VMEM((4, 8, 128), jnp.int32)],
        16,
    )


def stats_kernel(own, out, slots, send, recv, local):
    net = Net(send, recv, local)
    partners = line_partners(net)
    net.greet([to for to, _ in partners])
    total = SmallSum(net, own, slots, net.x * 2 + net.c, partners)
    total.start()
    total.finish(out)
    net.drain()


def stats_call(own, collective_id):
    return pl.pallas_call(
        stats_kernel,
        out_shape=shape(own.shape, F32),
        in_specs=[spec(VMEM)],
        out_specs=spec(VMEM),
        scratch_shapes=[VMEM((8, *own.shape), F32)] + sem_scratch(),
        compiler_params=pltpu.CompilerParams(
            collective_id=collective_id, has_side_effects=True, vmem_limit_bytes=8 << 20
        ),
        name="token_sums",
    )(own)


def norm_parts(values):
    center = jnp.mean(values, -1, keepdims=True)
    spread = jnp.mean(values * values, -1, keepdims=True) - center * center
    inv_std = lax.rsqrt(spread + EPS)
    return (values - center) * inv_std, inv_std


def by_rows(rows, step):
    def body(i, carry):
        step(pl.ds(pl.multiple_of(i * 16, 16), 16))
        return carry

    lax.fori_loop(0, rows // 16, body, 0)


def second_kernel(
    part, tokens, gain, bias, pieces, cot, attended, full_rows, full_weights, full_cot,
    other, landing, rows, send, recv, local,
):
    net = Net(send, recv, local)
    net.greet(x_neighbours(net) + grid_neighbours(net) + pair_neighbours(net))
    total = LineSum(net, part, other, landing)
    weights = GridGather(net, pieces, full_weights)
    cots = LineGather(net, cot, full_cot)
    line = LineGather(net, rows, full_rows)
    total.start()
    weights.exchange()
    total.chip()
    weights.start()
    total.pass_on()
    weights.near()
    total.finish(attended)

    def norm(at):
        values = tokens[at, :].astype(F32) + attended[at, :]
        attended[at, :] = values
        hat, _ = norm_parts(values)
        rows[at, :] = (hat * gain[...] + bias[...]).astype(BF16)

    by_rows(128, norm)
    line.start()
    weights.far()
    weights.pass_on(0)
    line.forward()
    cots.start()
    line.share()
    weights.pass_on(-1)
    cots.forward()
    weights.pass_on(1)
    weights.pass_on(2)
    cots.share()
    line.finish()
    cots.finish()
    weights.finish()
    net.drain()


def second_call(part, tokens, gain, bias, pieces, cot):
    width = pieces.shape[2]
    return comm_call(
        second_kernel,
        "sum_norm_gather",
        2,
        (part, tokens, gain, bias, pieces, cot),
        (VMEM, VMEM, VMEM, VMEM, pl.ANY, pl.ANY),
        (
            shape((128, D), F32),
            shape((8, 128, D), BF16),
            shape((4, 2, 4, 64, width), BF16),
            shape((8, 128, D), BF16),
        ),
        (VMEM, pl.ANY, pl.ANY, pl.ANY),
        [VMEM((4, 128, D), BF16), VMEM((6, 64, D), BF16), VMEM((128, D), BF16)],
        24,
    )


def norm_back(grad, gain, hat, inv_std):
    scaled = grad * gain
    return inv_std * (
        scaled
        - jnp.mean(scaled, -1, keepdims=True)
        - hat * jnp.mean(scaled * hat, -1, keepdims=True)
    )


def fold8(values):
    return values[:8] + values[8:]


def third_kernel(
    part, attended, cot, gain, grads, grad_attended, full_rows, sums, shard,
    other, landing, rows, grid_landing, done, send, recv, local,
):
    net = Net(send, recv, local)
    net.greet(x_neighbours(net) + grid_neighbours(net) + pair_neighbours(net))
    total = LineSum(net, part, other, landing)
    weights = GridSum(net, grads, grid_landing, done, shard)
    line = LineGather(net, rows, full_rows)
    total.start()
    weights.start(2)
    total.chip()
    weights.start(1)
    weights.start(-1)
    weights.start(0)
    weights.pass_on(2)
    total.pass_on()
    weights.finish(2)
    weights.pass_on(1)
    total.finish(grad_attended)
    sums[...] = jnp.zeros_like(sums)

    def back(at):
        grad = grad_attended[at, :]
        hat, inv_std = norm_parts(attended[at, :])
        sums[0] += fold8(grad * hat)
        sums[1] += fold8(grad)
        value = cot[at, :].astype(F32) + norm_back(grad, gain[...], hat, inv_std)
        grad_attended[at, :] = value
        rows[at, :] = value.astype(BF16)

    by_rows(128, back)
    line.start()
    weights.pass_on(-1)
    weights.finish(1)
    weights.finish(-1)
    line.forward()
    weights.pass_on(0)
    weights.finish(0)
    line.share()
    weights.pass_on_last()
    weights.finish_last()
    line.finish()
    weights.collect()
    net.drain()


def third_call(part, attended, cot, gain, grads):
    width = grads.shape[-1]
    return comm_call(
        third_kernel,
        "sum_back_gather",
        3,
        (part, attended, cot, gain, grads),
        (VMEM,) * 5,
        (
            shape((128, D), F32),
            shape((8, 128, D), BF16),
            shape((2, 8, D), F32),
            shape((4, 32, width), BF16),
        ),
        (VMEM, pl.ANY, VMEM, pl.ANY),
        [
            VMEM((4, 128, D), BF16),
            VMEM((6, 64, D), BF16),
            VMEM((128, D), BF16),
            VMEM((2, 5, 6, 32, width), BF16),
            VMEM((2, 2, 32, width), BF16),
        ],
        44,
    )


def fourth_kernel(
    part, part_out, attended, grad_attended, tokens, gain, grads, outer_sums, inner,
    layer_out, grad_input, shard, outer_out, inner_out,
    other, other_out, landing, landing_out, work, grid_landing, done,
    sums, outer, line_slots, y_slots, z_slots, inner_y, inner_z, half_sum, inner_half,
    send, recv, local,
):
    net = Net(send, recv, local)
    others = line_partners(net)
    y_all = [(net.along_y(d), (net.y - d) % 4) for d in (1, 2, 3)]
    z_all = [(net.along_z(d), (net.z - d) % 4) for d in (1, 2, 3)]
    net.greet([to for to, _ in others + y_all + z_all] + pair_neighbours(net))
    total = LineSum(net, part, other, landing)
    total_out = LineSum(net, part_out, other_out, landing_out)
    weights = GridSum(net, grads, grid_landing, done, shard)
    total.start()
    inner_first = SmallSum(net, inner, inner_y, net.y, y_all)
    inner_first.start()
    weights.start(2)
    total.chip()
    weights.start(1)
    weights.start(-1)
    weights.start(0)
    total_out.start()
    weights.pass_on(2)
    total.pass_on()
    total_out.chip()
    weights.finish(2)
    weights.pass_on(1)
    weights.pass_on(-1)
    total.finish(work)
    sums[...] = jnp.zeros_like(sums)

    def back(at):
        grad = work[at, :]
        hat, inv_std = norm_parts(tokens[at, :].astype(F32))
        sums[0] += fold8(grad * hat)
        sums[1] += fold8(grad)
        value = grad_attended[at, :] + norm_back(grad, gain[...], hat, inv_std)
        grad_input[at, :] = value.astype(BF16)

    by_rows(128, back)
    for i in range(4):
        row = jnp.sum(sums[i] if i < 2 else outer_sums[i - 2], 0, keepdims=True)
        outer[2 * i : 2 * i + 1, :] = row[:, :1024]
        outer[2 * i + 1 : 2 * i + 2, :] = row[:, 1024:]
    outer_x = SmallSum(net, outer, line_slots, net.x * 2 + net.c, others)
    outer_x.start()
    inner_first.finish(inner_half.at[0])
    inner_last = SmallSum(net, inner_half.at[0], inner_z, net.z, z_all)
    inner_last.start()
    weights.finish(1)
    weights.finish(-1)
    weights.pass_on(0)
    total_out.pass_on()
    outer_x.finish(half_sum.at[0])
    outer_y = SmallSum(net, half_sum.at[0], y_slots, net.y, y_all)
    outer_y.start()
    weights.finish(0)
    weights.pass_on_last()
    total_out.finish(work)

    def out(at):
        layer_out[at, :] = (attended[at, :] + work[at, :]).astype(BF16)

    by_rows(128, out)
    outer_y.finish(half_sum.at[1])
    outer_z = SmallSum(net, half_sum.at[1], z_slots, net.z, z_all)
    outer_z.start()
    inner_last.finish(inner_half.at[1])
    me = (net.x % 2) * 2 + net.c
    inner_k = {}
    for dx, dc in ((1, 0), (1, 1), (0, 1)):
        inner_k[dx, dc] = net.push(inner_half.at[1], inner_out.at[me], net.pair(dx, dc))
    inner_out[me] = inner_half[1]
    weights.finish_last()
    outer_z.finish(outer_out)
    for dx, dc in ((1, 0), (1, 1), (0, 1)):
        net.arrived(inner_k[dx, dc], inner_out.at[((net.x + dx) % 2) * 2 + (net.c + dc) % 2])
    weights.collect()
    net.drain()


def fourth_call(part, part_out, attended, grad_attended, tokens, gain, grads, outer_sums, inner):
    width = grads.shape[-1]
    n = inner.shape[0]
    return comm_call(
        fourth_kernel,
        "sum_last",
        4,
        (part, part_out, attended, grad_attended, tokens, gain, grads, outer_sums, inner),
        (VMEM,) * 9,
        (
            shape((128, D), BF16),
            shape((128, D), BF16),
            shape((4, 32, width), BF16),
            shape((8, 1024), F32),
            shape((4, n, 128), F32),
        ),
        (VMEM, VMEM, pl.ANY, VMEM, VMEM),
        [
            VMEM((4, 128, D), BF16),
            VMEM((4, 128, D), BF16),
            VMEM((6, 64, D), BF16),
            VMEM((6, 64, D), BF16),
            VMEM((128, D), F32),
            VMEM((2, 5, 6, 32, width), BF16),
            VMEM((2, 2, 32, width), BF16),
            VMEM((2, 8, D), F32),
            VMEM((8, 1024), F32),
            VMEM((8, 8, 1024), F32),
            VMEM((4, 8, 1024), F32),
            VMEM((4, 8, 1024), F32),
            VMEM((4, n, 128), F32),
            VMEM((4, n, 128), F32),
            VMEM((2, 8, 1024), F32),
            VMEM((2, n, 128), F32),
        ],
        48,
    )


def xpos_tables(direction):
    half = HEAD_DIM // 2
    pair = np.arange(half, dtype=np.float32)
    frequency = np.power(np.float32(10000.0), -pair / half).astype(np.float32)
    zeta = ((pair / half + 0.4) / 1.4).astype(np.float32)
    position = np.arange(SLOTS, dtype=np.float32)[:, None]
    angle = (position * frequency).astype(np.float32).astype(np.float64)
    decay = np.exp(direction * position / 512.0 * np.log(zeta.astype(np.float64)))
    cosine, sine = np.cos(angle) * decay, np.sin(angle) * decay
    cosine = np.concatenate([cosine] * 2, -1)
    sine = np.concatenate([-sine, sine], -1)
    return np.tile(cosine, (1, 4)).astype(np.float32), np.tile(sine, (1, 4)).astype(np.float32)


def tables():
    return np.stack([*xpos_tables(1.0), *xpos_tables(-1.0)])


def swapped(values):
    lane = lax.broadcasted_iota(jnp.int32, values.shape, 1)
    return jnp.where(lane % 64 < 32, pltpu.roll(values, 224, 1), pltpu.roll(values, 32, 1))


def dot_nn(a, b):
    return lax.dot_general(a, b, (((1,), (0,)), ((), ())), preferred_element_type=F32)


def dot_nt(a, b):
    return lax.dot_general(a, b, (((1,), (1,)), ((), ())), preferred_element_type=F32)


def dot_tn(a, b):
    return lax.dot_general(a, b, (((0,), (0,)), ((), ())), preferred_element_type=F32)


def head_of(values, head):
    lane = lax.broadcasted_iota(jnp.int32, values.shape, 1)
    return jnp.where(lane // 64 == head, values, jnp.zeros_like(values))


def head_probs(query, key, head, allowed):
    scores = dot_nt(head_of(query, head), key) * HEAD_DIM**-0.5
    scores = jnp.where(allowed, scores, -1e30)
    exps = jnp.exp(scores - jnp.max(scores, -1, keepdims=True))
    return exps / jnp.sum(exps, -1, keepdims=True)


def allowed_slots(cap):
    query = lax.broadcasted_iota(jnp.int32, (SLOTS, SLOTS), 0)
    key = lax.broadcasted_iota(jnp.int32, (SLOTS, SLOTS), 1)
    return (key <= query) & (key < IMAGE + cap[0, 0:1, 0:1])


def attend_kernel(rows, weights, cap, table, query_out, key_out, value_out, mixed_out):
    qkv = dot_nn(rows[...], weights[...])
    query, key, value = qkv[:, :256], qkv[:, 256:512], qkv[:, 512:].astype(BF16)
    query = (query * table[0] + swapped(query) * table[1]).astype(BF16)
    key = (key * table[2] + swapped(key) * table[3]).astype(BF16)
    query_out[...], key_out[...], value_out[...] = query, key, value
    allowed = allowed_slots(cap)
    mixed = jnp.zeros((SLOTS, 256), F32)
    for head in range(4):
        probs = head_probs(query, key, head, allowed).astype(BF16)
        mixed = mixed + dot_nn(probs, head_of(value, head))
    mixed_out[...] = mixed


def attend(rows, weights, caps, table):
    block = pl.BlockSpec((SLOTS, 256), lambda b: (b, 0))
    return pl.pallas_call(
        attend_kernel,
        grid=(4,),
        out_shape=[shape((1024, 256), BF16)] * 3 + [shape((1024, 256), F32)],
        in_specs=[
            pl.BlockSpec((SLOTS, D), lambda b: (b, 0)),
            pl.BlockSpec((D, 768), lambda b: (0, 0)),
            pl.BlockSpec((1, 8, 128), lambda b: (b, 0, 0)),
            pl.BlockSpec((4, SLOTS, 256), lambda b: (0, 0, 0)),
        ],
        out_specs=[block] * 4,
        compiler_params=pltpu.CompilerParams(vmem_limit_bytes=32 << 20),
        name="attend",
    )(rows, weights, caps, table)


def attend_back_kernel(query_in, key_in, value_in, grad_in, cap, table, grads_out):
    query, key, value, grad = query_in[...], key_in[...], value_in[...], grad_in[...]
    allowed = allowed_slots(cap)
    grad_query = jnp.zeros((SLOTS, 256), F32)
    grad_key = jnp.zeros((SLOTS, 256), F32)
    grad_value = jnp.zeros((SLOTS, 256), F32)
    for head in range(4):
        probs = head_probs(query, key, head, allowed)
        grad_head = head_of(grad, head)
        grad_probs = dot_nt(grad_head, value)
        grad_value = grad_value + dot_tn(probs.astype(BF16), grad_head)
        delta = jnp.sum(probs * grad_probs, -1, keepdims=True)
        grad_scores = (probs * (grad_probs - delta)).astype(BF16)
        grad_query = grad_query + dot_nn(grad_scores, head_of(key, head))
        grad_key = grad_key + dot_tn(grad_scores, head_of(query, head))
    grad_query = grad_query * HEAD_DIM**-0.5
    grad_key = grad_key * HEAD_DIM**-0.5
    grads_out[:, :256] = (grad_query * table[0] + swapped(grad_query * table[1])).astype(BF16)
    grads_out[:, 256:512] = (grad_key * table[2] + swapped(grad_key * table[3])).astype(BF16)
    grads_out[:, 512:] = grad_value.astype(BF16)


def attend_back(query, key, value, grad, caps, table):
    block = pl.BlockSpec((SLOTS, 256), lambda b: (b, 0))
    return pl.pallas_call(
        attend_back_kernel,
        grid=(4,),
        out_shape=shape((1024, 768), BF16),
        in_specs=[block] * 4
        + [
            pl.BlockSpec((1, 8, 128), lambda b: (b, 0, 0)),
            pl.BlockSpec((4, SLOTS, 256), lambda b: (0, 0, 0)),
        ],
        out_specs=pl.BlockSpec((SLOTS, 768), lambda b: (b, 0)),
        compiler_params=pltpu.CompilerParams(vmem_limit_bytes=32 << 20),
        name="attend_back",
    )(query, key, value, grad, caps, table)


def quarters(shard):
    return shard.astype(BF16).reshape(32, 4, -1).transpose(1, 0, 2)


def from_quarters(pieces):
    return pieces.transpose(1, 0, 2).reshape(32, -1).astype(F32)


def token_sums(terms, collective_id):
    sums = jnp.concatenate([jnp.sum(t, -1).reshape(8, 128) for t in terms], 0)
    sums = stats_call(sums, collective_id)
    return [sums[8 * i : 8 * i + 8].reshape(1024, 1) for i in range(len(terms))]


def per_device(
    tokens, caption_len, norm1_gain, norm1_bias, w_query, w_key, w_value, inner_gain, inner_bias,
    w_proj, norm2_gain, norm2_bias, w_up, ffn_norm_gain, ffn_norm_bias, w_down, cotangent,
):
    seq = lax.axis_index("seq")
    place = ((seq // 8) % 2) * 2 + seq % 2
    table = jnp.asarray(tables())
    pieces1 = jnp.concatenate([quarters(w) for w in (w_query, w_key, w_value, w_proj.T)], -1)
    pieces2 = jnp.concatenate([quarters(w) for w in (w_up, w_down.T)], -1)
    my_gain = lax.dynamic_slice(inner_gain, (place * 256,), (256,))
    my_bias = lax.dynamic_slice(inner_bias, (place * 256,), (256,))
    my_ffn_gain = lax.dynamic_slice(ffn_norm_gain, (place * 1024,), (1024,))
    my_ffn_bias = lax.dynamic_slice(ffn_norm_bias, (place * 1024,), (1024,))
    cap = jnp.broadcast_to(caption_len.reshape(1, 1), (8, 128))

    first_hat, _ = norm_parts(tokens.astype(F32))
    first_rows = (first_hat * norm1_gain + norm1_bias).astype(BF16)
    rows1, caps, weights1 = first_call(first_rows, cap, pieces1)
    rows1, weights1 = rows1.reshape(1024, D), weights1.reshape(D, 1024)

    query, key, value, mixed = attend(rows1, weights1, caps, table)
    s0, s1 = token_sums((mixed, mixed * mixed), 5)
    center = s0 / D
    inner_inv = lax.rsqrt(s1 / D - center * center + EPS)
    context_hat = (mixed - center) * inner_inv
    context = (context_hat * my_gain + my_bias).astype(BF16)
    proj_t = weights1[:, 768:]
    attn_part = dot_nt(context, proj_t).astype(BF16).reshape(8, 128, D)

    attended, rows2, weights2, cots = second_call(
        attn_part, tokens, norm2_gain.reshape(1, D), norm2_bias.reshape(1, D), pieces2, cotangent
    )
    rows2, weights2, cots = rows2.reshape(1024, D), weights2.reshape(D, 2048), cots.reshape(1024, D)
    up, down_t = weights2[:, :1024], weights2[:, 1024:]

    up_proj = dot_nn(rows2, up)
    cdf = 0.5 * (1.0 + lax.erf(up_proj * np.float32(0.5**0.5)))
    activated = up_proj * cdf
    slope = cdf + up_proj * jnp.exp(-0.5 * up_proj * up_proj) * np.float32((2 * np.pi) ** -0.5)
    grad_ffn = dot_nn(cots, down_t)
    scaled = grad_ffn * my_ffn_gain
    s0, s1, t0, t1 = token_sums((activated, activated * activated, scaled, scaled * activated), 6)
    center = s0 / FF
    ffn_inv = lax.rsqrt(s1 / FF - center * center + EPS)
    ffn_hat = (activated - center) * ffn_inv
    ffn_b = (ffn_hat * my_ffn_gain + my_ffn_bias).astype(BF16)
    out_part = dot_nt(ffn_b, down_t).astype(BF16).reshape(8, 128, D)
    ffn_gain_part = jnp.sum(grad_ffn * ffn_hat, 0)
    ffn_bias_part = jnp.sum(grad_ffn, 0)
    hat_mean = (t1 - center * t0) * ffn_inv / FF
    grad_activated = ffn_inv * (scaled - t0 / FF - ffn_hat * hat_mean)
    grad_up_b = (grad_activated * slope).astype(BF16)
    second_part = dot_nt(grad_up_b, up).astype(BF16).reshape(8, 128, D)
    grads2 = jnp.concatenate(
        [dot_tn(rows2, grad_up_b).astype(BF16), dot_tn(cots, ffn_b).astype(BF16)], -1
    ).reshape(4, 2, 4, 64, 2048)

    grad_attended, grad_rows, outer_sums, shard2 = third_call(
        second_part, attended, cotangent, norm2_gain.reshape(1, D), grads2
    )
    grad_rows = grad_rows.reshape(1024, D)

    grad_context = dot_nn(grad_rows, proj_t)
    scaled = grad_context * my_gain
    t0, t1 = token_sums((scaled, scaled * context_hat), 7)
    inner_gain_part = jnp.sum(grad_context * context_hat, 0)
    inner_bias_part = jnp.sum(grad_context, 0)
    grad_mixed = (inner_inv * (scaled - t0 / D - context_hat * (t1 / D))).astype(BF16)
    grads_qkv = attend_back(query, key, value, grad_mixed, caps, table)
    first_part = dot_nt(grads_qkv, weights1[:, :768]).astype(BF16).reshape(8, 128, D)
    grads1 = jnp.concatenate(
        [dot_tn(rows1, grads_qkv).astype(BF16), dot_tn(grad_rows, context).astype(BF16)], -1
    ).reshape(4, 2, 4, 64, 1024)
    inner = jnp.concatenate([inner_gain_part, inner_bias_part, ffn_gain_part, ffn_bias_part])
    inner = jnp.pad(inner.reshape(20, 128), ((0, 4), (0, 0)))

    layer_out, grad_input, shard1, outer, inner = fourth_call(
        first_part, out_part, attended, grad_attended, tokens, norm1_gain.reshape(1, D), grads1,
        outer_sums, inner,
    )
    outer = outer.reshape(4, D)
    inner = inner.reshape(4, 24 * 128)
    return (
        layer_out,
        grad_input,
        outer[0],
        outer[1],
        from_quarters(shard1[:, :, :256]),
        from_quarters(shard1[:, :, 256:512]),
        from_quarters(shard1[:, :, 512:768]),
        inner[:, :256].reshape(-1),
        inner[:, 256:512].reshape(-1),
        from_quarters(shard1[:, :, 768:]).T,
        outer[2],
        outer[3],
        from_quarters(shard2[:, :, :1024]),
        inner[:, 512:1536].reshape(-1),
        inner[:, 1536:2560].reshape(-1),
        from_quarters(shard2[:, :, 1024:]).T,
    )


def solution(mesh):
    rows = P(("seq", "ffn"), None)
    by_rows_, by_columns, half = P("seq", "ffn"), P("ffn", "seq"), P("ffn")
    return jax.shard_map(
        per_device,
        mesh=mesh,
        in_specs=(
            rows, P("seq"), P(), P(), by_rows_, by_rows_, by_rows_, half, half, by_columns,
            P(), P(), by_rows_, half, half, by_columns, rows,
        ),
        out_specs=(
            rows, rows, P(), P(), by_rows_, by_rows_, by_rows_, half, half, by_columns,
            P(), P(), by_rows_, half, half, by_columns,
        ),
        check_vma=False,
    )
```

```python
import functools

import jax
import jax.numpy as jnp
import numpy as np
from jax import lax
from jax.experimental import pallas as pl
from jax.experimental.pallas import tpu as pltpu
from jax.sharding import PartitionSpec as P

D = 2048
HEAD_DIM = 64
FF = 8192
SLOTS = 256
IMAGE = 64
EPS = 1e-05
F32 = jnp.float32
BF16 = jnp.bfloat16
MESH = pl.DeviceIdType.MESH
VMEM = pltpu.VMEM


def device_at(y, x, z, c):
    return (((y * 2 + x % 2) * 4 + z) * 2 + c, x // 2)


def line_slot(x, c):
    return ((x % 2) * 2 + c) * 2 + x // 2


class Net:
    def __init__(self, send, recv, local):
        seq, ffn = lax.axis_index("seq"), lax.axis_index("ffn")
        self.y, self.z, self.c = seq // 16, (seq // 2) % 4, seq % 2
        self.x = ffn * 2 + (seq // 8) % 2
        self.send, self.recv, self.local = send, recv, local
        self.used, self.used_local = 0, 0
        self.out = []

    def along_x(self, dx, dc=0):
        return device_at(self.y, (self.x + dx) % 4, self.z, (self.c + dc) % 2)

    def along_y(self, dy):
        return device_at((self.y + dy) % 4, self.x, self.z, self.c)

    def along_z(self, dz):
        return device_at(self.y, self.x, (self.z + dz) % 4, self.c)

    def pair(self, dx, dc):
        x = (self.x // 2) * 2 + (self.x + dx) % 2
        return device_at(self.y, x, self.z, (self.c + dc) % 2)

    def greet(self, partners):
        barrier = pltpu.get_barrier_semaphore()
        for partner in partners:
            pl.semaphore_signal(barrier, inc=1, device_id=partner, device_id_type=MESH)
        pl.semaphore_wait(barrier, len(partners))

    def push(self, src, dst, device):
        k = self.used
        self.used += 1
        copy = pltpu.make_async_remote_copy(
            src_ref=src,
            dst_ref=dst,
            send_sem=self.send.at[k],
            recv_sem=self.recv.at[k],
            device_id=device,
            device_id_type=MESH,
        )
        copy.start()
        self.out.append(copy)
        return k

    def arrived(self, k, landed):
        pltpu.make_async_remote_copy(
            src_ref=landed,
            dst_ref=landed,
            send_sem=self.send.at[k],
            recv_sem=self.recv.at[k],
            device_id=self.along_x(0, 1),
            device_id_type=MESH,
        ).wait_recv()

    def keep(self, src, dst):
        copy = pltpu.make_async_copy(src, dst, self.local.at[self.used_local])
        self.used_local += 1
        copy.start()
        return copy

    def drain(self):
        for copy in self.out:
            copy.wait_send()
        assert (self.used, max(self.used_local, 1)) == (self.send.shape[0], self.local.shape[0])


def add_into(dst, *terms):
    def step(i, carry):
        rows = pl.ds(pl.multiple_of(i * 16, 16), 16)
        total = terms[0][rows, :].astype(F32)
        for term in terms[1:]:
            total = total + term[rows, :].astype(F32)
        dst[rows, :] = total.astype(dst.dtype)
        return carry

    lax.fori_loop(0, dst.shape[0] // 16, step, 0)


def line_rows(ref, slot, half=None):
    if half is None:
        return ref.at[pl.ds(pl.multiple_of(slot * 128, 128), 128)]
    return ref.at[pl.ds(pl.multiple_of(slot * 128 + 64 * half, 64), 64)]


class LineGather:
    def __init__(self, net, own, full):
        self.net, self.own, self.full = net, own, full

    def block(self, dx, dc=0, half=None):
        net = self.net
        return line_rows(self.full, line_slot((net.x + dx) % 4, (net.c + dc) % 2), half)

    def start(self):
        net, mine = self.net, self.block(0)
        self.a = net.push(self.own, mine, net.along_x(1))
        self.b = net.push(self.own, mine, net.along_x(-1))
        self.s0 = net.push(self.own, mine, net.along_x(0, 1))
        self.kept = net.keep(self.own, mine)

    def forward(self):
        net = self.net
        net.arrived(self.a, self.block(-1))
        self.fa = net.push(self.block(-1, 0, 0), self.block(-1, 0, 0), net.along_x(1))
        self.sa = net.push(self.block(-1), self.block(-1), net.along_x(0, 1))
        net.arrived(self.b, self.block(1))
        self.fb = net.push(self.block(1, 0, 1), self.block(1, 0, 1), net.along_x(-1))
        self.sb = net.push(self.block(1), self.block(1), net.along_x(0, 1))

    def share(self):
        net = self.net
        net.arrived(self.fa, self.block(2, 0, 0))
        self.sfa = net.push(self.block(2, 0, 0), self.block(2, 0, 0), net.along_x(0, 1))
        net.arrived(self.fb, self.block(2, 0, 1))
        self.sfb = net.push(self.block(2, 0, 1), self.block(2, 0, 1), net.along_x(0, 1))

    def finish(self):
        net = self.net
        net.arrived(self.s0, self.block(0, 1))
        net.arrived(self.sa, self.block(-1, 1))
        net.arrived(self.sb, self.block(1, 1))
        net.arrived(self.sfa, self.block(2, 1, 0))
        net.arrived(self.sfb, self.block(2, 1, 1))
        self.kept.wait()


class RingSum:
    def __init__(self, net, mine, landing, ahead, behind):
        self.net, self.mine, self.landing = net, mine, landing
        self.ahead, self.behind = ahead, behind

    def start_far(self):
        net, land = self.net, self.landing
        self.f0 = net.push(self.mine(2, 0), land.at[0], self.ahead)
        self.f1 = net.push(self.mine(2, 1), land.at[1], self.behind)

    def start_near(self, d):
        net, land = self.net, self.landing
        if d == 1:
            self.r1 = net.push(self.mine(1, 1), land.at[3], self.ahead)
        else:
            self.r0 = net.push(self.mine(-1, 0), land.at[4], self.behind)

    def pass_on(self):
        net, land = self.net, self.landing
        net.arrived(self.f0, land.at[0])
        add_into(land.at[0], land.at[0], self.mine(1, 0))
        self.s0 = net.push(land.at[0], land.at[2], self.ahead)
        net.arrived(self.f1, land.at[1])
        add_into(land.at[1], land.at[1], self.mine(-1, 1))
        self.s1 = net.push(land.at[1], land.at[5], self.behind)

    def finish(self, out=None):
        net, land = self.net, self.landing
        net.arrived(self.s0, land.at[2])
        net.arrived(self.r0, land.at[4])
        add_into(land.at[2] if out is None else out(0), self.mine(0, 0), land.at[2], land.at[4])
        net.arrived(self.r1, land.at[3])
        net.arrived(self.s1, land.at[5])
        add_into(land.at[3] if out is None else out(1), self.mine(0, 1), land.at[3], land.at[5])


class LineSum:
    def __init__(self, net, part, other, landing):
        self.net, self.part, self.other = net, part, other
        self.ring = RingSum(net, self.mine, landing, net.along_x(1), net.along_x(-1))
        self.k = {}

    def block(self, dx, dc):
        net = self.net
        return line_rows(self.part, line_slot((net.x + dx) % 4, (net.c + dc) % 2))

    def mine(self, d, half):
        return self.other.at[d % 4, pl.ds(64 * half, 64)]

    def start(self, *steps):
        net = self.net
        for d in steps:
            self.k[d] = net.push(self.block(d, 1), self.other.at[d % 4], net.along_x(0, 1))

    def chip(self, *steps):
        for d in steps:
            self.net.arrived(self.k[d], self.other.at[d % 4])
            add_into(self.other.at[d % 4], self.other.at[d % 4], self.block(d, 0))
            if d == 2:
                self.ring.start_far()
            elif d:
                self.ring.start_near(d)

    def pass_on(self):
        self.ring.pass_on()

    def finish(self, out):
        self.ring.finish(lambda half: out.at[pl.ds(64 * half, 64)])


def shard_rows(ref, y, x_lo, z, c=None):
    if c is None:
        return ref.at[pl.ds(pl.multiple_of(((y * 2 + x_lo) * 4 + z) * 64, 64), 64)]
    return ref.at[pl.ds(pl.multiple_of((((y * 2 + x_lo) * 4 + z) * 2 + c) * 32, 32), 32)]


class GridGather:
    def __init__(self, net, pieces, full):
        self.net, self.pieces, self.full = net, pieces, full

    def spot(self, dx, dc):
        net = self.net
        return shard_rows(self.full, net.y, (net.x + dx) % 2, net.z, (net.c + dc) % 2)

    def exchange(self):
        net = self.net
        self.k = {}
        for dx, dc in ((1, 0), (1, 1), (0, 1)):
            to = ((net.x + dx) % 2) * 2 + (net.c + dc) % 2
            self.k[dx, dc] = net.push(self.pieces.at[to], self.spot(0, 0), net.pair(dx, dc))
        me = (net.x % 2) * 2 + net.c
        self.kept = net.keep(self.pieces.at[me], self.spot(0, 0))

    def slab(self, t, dp, dq, half=None):
        net = self.net
        dy, dz = (dq, dp) if t == 0 else (dp, dq)
        return shard_rows(self.full, (net.y + dy) % 4, t, (net.z + dz) % 4, half)

    def to_p(self, t, d):
        return self.net.along_z(d) if t == 0 else self.net.along_y(d)

    def to_q(self, t, d):
        return self.net.along_y(d) if t == 0 else self.net.along_z(d)

    def same(self, ref, device):
        return self.net.push(ref, ref, device)

    def second(self, t, dp):
        self.q[t, dp] = (
            self.same(self.slab(t, dp, 0), self.to_q(t, 1)),
            self.same(self.slab(t, dp, 0), self.to_q(t, -1)),
        )

    def start(self):
        for dx, dc in ((0, 1), (1, 0), (1, 1)):
            self.net.arrived(self.k[dx, dc], self.spot(dx, dc))
        self.kept.wait()
        self.p, self.q, self.f = {}, {}, {}
        for t in (0, 1):
            self.p[t] = (
                self.same(self.slab(t, 0, 0), self.to_p(t, 1)),
                self.same(self.slab(t, 0, 0), self.to_p(t, -1)),
            )
        for t in (0, 1):
            self.second(t, 0)

    def near(self):
        net = self.net
        for t in (0, 1):
            a, b = self.p[t]
            net.arrived(a, self.slab(t, -1, 0))
            fa = self.same(self.slab(t, -1, 0, 0), self.to_p(t, 1))
            net.arrived(b, self.slab(t, 1, 0))
            fb = self.same(self.slab(t, 1, 0, 1), self.to_p(t, -1))
            self.f[t] = (fa, fb)
        for t in (0, 1):
            self.second(t, -1)
            self.second(t, 1)

    def far(self):
        for t in (0, 1):
            self.net.arrived(self.f[t][0], self.slab(t, 2, 0, 0))
            self.net.arrived(self.f[t][1], self.slab(t, 2, 0, 1))
            self.second(t, 2)

    def pass_on(self, dp):
        net = self.net
        for t in (0, 1):
            a, b = self.q[t, dp]
            net.arrived(a, self.slab(t, dp, -1))
            fa = self.same(self.slab(t, dp, -1, 0), self.to_q(t, 1))
            net.arrived(b, self.slab(t, dp, 1))
            fb = self.same(self.slab(t, dp, 1, 1), self.to_q(t, -1))
            self.f[t, dp] = (fa, fb)

    def finish(self):
        for dp in (0, -1, 1, 2):
            for t in (0, 1):
                self.net.arrived(self.f[t, dp][0], self.slab(t, dp, 2, 0))
                self.net.arrived(self.f[t, dp][1], self.slab(t, dp, 2, 1))


class GridSum:
    def __init__(self, net, part, landing, done, out):
        self.net, self.part, self.landing, self.done, self.out = net, part, landing, done, out
        self.rings = {}
        for t in (0, 1):
            for dp in (2, 1, -1, 0):
                self.rings[t, dp] = RingSum(
                    net,
                    functools.partial(self.term, t, dp),
                    landing.at[t, dp % 4],
                    self.to_q(t, 1),
                    self.to_q(t, -1),
                )
            self.rings[t] = RingSum(
                net,
                functools.partial(self.column, t),
                landing.at[t, 4],
                self.to_p(t, 1),
                self.to_p(t, -1),
            )

    def to_p(self, t, d):
        return self.net.along_z(d) if t == 0 else self.net.along_y(d)

    def to_q(self, t, d):
        return self.net.along_y(d) if t == 0 else self.net.along_z(d)

    def term(self, t, dp, dq, half):
        net = self.net
        dy, dz = (dq, dp) if t == 0 else (dp, dq)
        return shard_rows(self.part, (net.y + dy) % 4, t, (net.z + dz) % 4, half)

    def column(self, t, dp, half):
        return self.landing.at[t, dp % 4, 2 + half]

    def start(self, dy):
        for dp in (2, 1, -1, 0):
            if dy == 2:
                self.rings[0, dp].start_far()
            elif dy:
                self.rings[0, dp].start_near(dy)
        self.rings[1, dy].start_far()
        self.rings[1, dy].start_near(1)
        self.rings[1, dy].start_near(-1)

    def pass_on(self, dp):
        for t in (0, 1):
            self.rings[t, dp].pass_on()

    def finish(self, dp):
        for t in (0, 1):
            self.rings[t, dp].finish()
            if dp == 2:
                self.rings[t].start_far()
            elif dp:
                self.rings[t].start_near(dp)

    def pass_on_last(self):
        for t in (0, 1):
            self.rings[t].pass_on()

    def finish_last(self):
        net = self.net
        for t in (0, 1):
            self.rings[t].finish(lambda half: self.done.at[t, half])
        me = (net.x % 2) * 2 + net.c
        self.k = {}
        for dx, dc in ((1, 0), (1, 1), (0, 1)):
            src = self.done.at[(net.x + dx) % 2, (net.c + dc) % 2]
            self.k[dx, dc] = net.push(src, self.out.at[me], net.pair(dx, dc))
        self.kept = net.keep(self.done.at[net.x % 2, net.c], self.out.at[me])

    def collect(self):
        net = self.net
        for dx, dc in ((1, 0), (1, 1), (0, 1)):
            at = ((net.x + dx) % 2) * 2 + (net.c + dc) % 2
            net.arrived(self.k[dx, dc], self.out.at[at])
        self.kept.wait()


class SmallSum:
    def __init__(self, net, own, slots, me, partners):
        self.net, self.own, self.slots, self.me, self.partners = net, own, slots, me, partners

    def start(self):
        net = self.net
        self.k = [(net.push(self.own, self.slots.at[self.me], to), at) for to, at in self.partners]
        self.slots[self.me] = self.own[...]

    def total(self):
        for k, at in self.k:
            self.net.arrived(k, self.slots.at[at])
        total = self.slots[0]
        for i in range(1, self.slots.shape[0]):
            total = total + self.slots[i]
        return total

    def finish(self, out):
        out[...] = self.total()


def line_partners(net):
    return [
        (net.along_x(dx, dc), ((net.x - dx) % 4) * 2 + (net.c + dc) % 2)
        for dx in range(4)
        for dc in range(2)
        if dx or dc
    ]


def sem_scratch(pushes, keeps):
    return [
        pltpu.SemaphoreType.DMA((pushes,)),
        pltpu.SemaphoreType.DMA((pushes,)),
        pltpu.SemaphoreType.DMA((keeps,)),
    ]


def spec(space):
    return pl.BlockSpec(memory_space=space)


def shape(dims, dtype):
    return jax.ShapeDtypeStruct(dims, dtype)


def comm_call(body, name, collective_id, ins, in_spaces, outs, out_spaces, scratch, mib, sems):
    return pl.pallas_call(
        body,
        out_shape=outs,
        in_specs=[spec(s) for s in in_spaces],
        out_specs=[spec(s) for s in out_spaces],
        scratch_shapes=scratch + sem_scratch(*sems),
        compiler_params=pltpu.CompilerParams(
            collective_id=collective_id, has_side_effects=True, vmem_limit_bytes=mib << 20
        ),
        name=name,
    )(*ins)


def x_neighbours(net):
    return [net.along_x(1), net.along_x(-1), net.along_x(0, 1)]


def grid_neighbours(net):
    return [net.along_y(1), net.along_y(-1), net.along_z(1), net.along_z(-1)]


def pair_neighbours(net):
    return [net.pair(1, 0), net.pair(1, 1), net.pair(0, 1)]


def first_kernel(rows, cap, pieces, full_rows, caps, full_weights, cap_slots, send, recv, local):
    net = Net(send, recv, local)
    net.greet(x_neighbours(net) + grid_neighbours(net) + pair_neighbours(net))
    weights = GridGather(net, pieces, full_weights)
    weights.exchange()
    me = (net.x % 2) * 2 + net.c
    cap_k = {}
    for dx, dc in ((1, 0), (1, 1), (0, 1)):
        cap_k[dx, dc] = net.push(cap, cap_slots.at[me], net.pair(dx, dc))
    cap_slots[me] = cap[...]
    line = LineGather(net, rows, full_rows)
    line.start()
    weights.start()
    weights.near()
    line.forward()
    weights.far()
    weights.pass_on(0)
    line.share()
    weights.pass_on(-1)
    weights.pass_on(1)
    weights.pass_on(2)
    for dx, dc in ((1, 0), (1, 1), (0, 1)):
        net.arrived(cap_k[dx, dc], cap_slots.at[((net.x + dx) % 2) * 2 + (net.c + dc) % 2])
    caps[...] = cap_slots[...]
    line.finish()
    weights.finish()
    net.drain()


def first_call(rows, cap, pieces):
    width = pieces.shape[2]
    return comm_call(
        first_kernel,
        "gather_first",
        1,
        (rows, cap, pieces),
        (pl.ANY, VMEM, pl.ANY),
        (
            shape((1024, D), BF16),
            shape((4, 8, 128), jnp.int32),
            shape((D, width), BF16),
        ),
        (pl.ANY, VMEM, pl.ANY),
        [VMEM((4, 8, 128), jnp.int32)],
        16,
        (55, 2),
    )


def stats_kernel(own, out, slots, send, recv, local):
    net = Net(send, recv, local)
    partners = line_partners(net)
    net.greet([to for to, _ in partners])
    total = SmallSum(net, own, slots, net.x * 2 + net.c, partners)
    total.start()
    total.finish(out)
    net.drain()


def stats_call(own, collective_id):
    return pl.pallas_call(
        stats_kernel,
        out_shape=shape(own.shape, F32),
        in_specs=[spec(VMEM)],
        out_specs=spec(VMEM),
        scratch_shapes=[VMEM((8, *own.shape), F32)] + sem_scratch(7, 1),
        compiler_params=pltpu.CompilerParams(
            collective_id=collective_id, has_side_effects=True, vmem_limit_bytes=8 << 20
        ),
        name="token_sums",
    )(own)


def norm_parts(values):
    center = jnp.mean(values, -1, keepdims=True)
    spread = jnp.mean(values * values, -1, keepdims=True) - center * center
    inv_std = lax.rsqrt(spread + EPS)
    return (values - center) * inv_std, inv_std


def by_rows(rows, step):
    def body(i, carry):
        step(pl.ds(pl.multiple_of(i * 16, 16), 16))
        return carry

    lax.fori_loop(0, rows // 16, body, 0)


def second_kernel(
    part, tokens, gain, bias, pieces, cot, attended, full_rows, full_weights, full_cot,
    other, landing, rows, send, recv, local,
):
    net = Net(send, recv, local)
    net.greet(x_neighbours(net) + grid_neighbours(net) + pair_neighbours(net))
    total = LineSum(net, part, other, landing)
    weights = GridGather(net, pieces, full_weights)
    cots = LineGather(net, cot, full_cot)
    line = LineGather(net, rows, full_rows)
    total.start(2, 1, -1, 0)
    weights.exchange()
    total.chip(2, 1, -1, 0)
    weights.start()
    total.pass_on()
    weights.near()
    total.finish(attended)

    def norm(at):
        values = tokens[at, :].astype(F32) + attended[at, :]
        attended[at, :] = values
        hat, _ = norm_parts(values)
        rows[at, :] = (hat * gain[...] + bias[...]).astype(BF16)

    by_rows(128, norm)
    line.start()
    weights.far()
    weights.pass_on(0)
    line.forward()
    cots.start()
    line.share()
    weights.pass_on(-1)
    cots.forward()
    weights.pass_on(1)
    weights.pass_on(2)
    cots.share()
    line.finish()
    cots.finish()
    weights.finish()
    net.drain()


def second_call(part, tokens, gain, bias, pieces, cot):
    width = pieces.shape[2]
    return comm_call(
        second_kernel,
        "sum_norm_gather",
        2,
        (part, tokens, gain, bias, pieces, cot),
        (VMEM, VMEM, VMEM, VMEM, pl.ANY, pl.ANY),
        (
            shape((128, D), F32),
            shape((1024, D), BF16),
            shape((D, width), BF16),
            shape((1024, D), BF16),
        ),
        (VMEM, pl.ANY, pl.ANY, pl.ANY),
        [VMEM((4, 128, D), BF16), VMEM((6, 64, D), BF16), VMEM((128, D), BF16)],
        24,
        (71, 3),
    )


def norm_back(grad, gain, hat, inv_std):
    scaled = grad * gain
    return inv_std * (
        scaled
        - jnp.mean(scaled, -1, keepdims=True)
        - hat * jnp.mean(scaled * hat, -1, keepdims=True)
    )


def fold8(values):
    return values[:8] + values[8:]


def block_rows(base, step):
    def body(i, carry):
        step(
            pl.ds(pl.multiple_of(i * 16, 16), 16),
            pl.ds(pl.multiple_of(base + i * 16, 16), 16),
        )
        return carry

    lax.fori_loop(0, 16, body, 0)


def lane_sums(values):
    total = values[:, :128]
    for k in range(1, values.shape[1] // 128):
        total = total + values[:, 128 * k : 128 * k + 128]
    return total


def row_of(partial):
    return jnp.sum(partial.T, 0, keepdims=True)


def columns_of(*rows):
    n = rows[0].shape[1]
    return jnp.concatenate([*rows, jnp.zeros((128 - len(rows), n), F32)], 0).T


def third_kernel(
    rows_in, weights_in, cots_in, gain, bias, attended, cot, norm_gain,
    out_part, grad_attended, grad_rows, sums, unit_sums, shard, grads_up,
    rows, up, down, cots, act, slope, gffn, ffn_b, grad_up, work, partial, cols,
    own_s, slots_s, own_t, slots_t, part, other, landing, own_rows, grads, grid_landing, done,
    send, recv, local,
):
    net = Net(send, recv, local)
    load_up = net.keep(weights_in.at[:, pl.ds(0, 1024)], up)
    load_rows = [net.keep(rows_in.at[pl.ds(256 * b, 256)], rows.at[pl.ds(256 * b, 256)]) for b in range(4)]
    load_down = net.keep(weights_in.at[:, pl.ds(1024, 1024)], down)
    load_cots = [net.keep(cots_in.at[pl.ds(256 * b, 256)], cots.at[pl.ds(256 * b, 256)]) for b in range(4)]
    others = line_partners(net)
    net.greet([to for to, _ in others] + grid_neighbours(net) + pair_neighbours(net))
    me = net.x * 2 + net.c
    total = LineSum(net, part, other, landing)
    weights = GridSum(net, grads, grid_landing, done, shard)
    line = LineGather(net, own_rows, grad_rows)
    sum_s = SmallSum(net, own_s, slots_s, me, others)
    sum_t = SmallSum(net, own_t, slots_t, me, others)
    unit_sums[...] = jnp.zeros_like(unit_sums)

    load_up.wait()
    for b in range(4):
        load_rows[b].wait()
        work[...] = dot_nn(rows[256 * b : 256 * b + 256, :], up[...])

        def gelu(at, to):
            value = work[at, :]
            cdf = 0.5 * (1.0 + lax.erf(value * np.float32(0.5**0.5)))
            density = jnp.exp(-0.5 * value * value) * np.float32((2 * np.pi) ** -0.5)
            slope[to, :] = (cdf + value * density).astype(BF16)
            value = value * cdf
            act[to, :] = value
            partial[0, at, :] = lane_sums(value)
            partial[1, at, :] = lane_sums(value * value)

        block_rows(256 * b, gelu)
        for i in range(2):
            own_s[i : i + 1, 256 * b : 256 * b + 256] = row_of(partial[i])
    sum_s.start()

    load_down.wait()
    for b in range(4):
        load_cots[b].wait()
        gffn[256 * b : 256 * b + 256, :] = dot_nn(cots[256 * b : 256 * b + 256, :], down[...])

        def scale(at, to):
            grad = gffn[to, :]
            unit_sums[1] += fold8(grad)
            grad = grad * gain[...]
            partial[0, at, :] = lane_sums(grad)
            partial[1, at, :] = lane_sums(grad * act[to, :])

        block_rows(256 * b, scale)
        for i in range(2):
            own_t[i : i + 1, 256 * b : 256 * b + 256] = row_of(partial[i])
    sum_t.start()

    both = sum_s.total()
    center = both[0:1] * (1.0 / FF)
    inv_std = lax.rsqrt(both[1:2] * (1.0 / FF) - center * center + EPS)
    cols[...] = columns_of(center, inv_std)

    def normed(at):
        hat = (act[at, :] - cols[at, 0:1]) * cols[at, 1:2]
        act[at, :] = hat
        ffn_b[at, :] = (hat * gain[...] + bias[...]).astype(BF16)
        unit_sums[0] += fold8(gffn[at, :] * hat)

    by_rows(1024, normed)
    both = sum_t.total()
    cols[...] = columns_of(
        inv_std,
        both[0:1] * (1.0 / FF),
        (both[1:2] - center * both[0:1]) * inv_std * (1.0 / FF),
    )
    for q in range(4):
        seq_of = ((net.x + q // 2) % 2) * 2 + (net.c + 1 + q) % 2
        base = pl.multiple_of(seq_of * 256, 256)

        def back(at, to):
            grad = gffn[to, :] * gain[...] - cols[to, 1:2] - act[to, :] * cols[to, 2:3]
            grad_up[to, :] = (grad * cols[to, 0:1] * slope[to, :].astype(F32)).astype(BF16)

        block_rows(base, back)
        mine = grad_up[pl.ds(base, 256), :]
        for h in range(2):
            part[pl.ds(base, 256), 1024 * h : 1024 * h + 1024] = dot_nt(
                mine, up[1024 * h : 1024 * h + 1024, :]
            ).astype(BF16)
        if q == 0:
            total.start(2)
        if q == 1:
            total.start(0)
            total.chip(2)
        if q == 2:
            total.start(1, -1)
    total.chip(1, -1, 0)

    def down_rows(dy):
        at = pl.ds(pl.multiple_of(((net.y + dy) % 4) * 512, 512), 512)
        grads[at, :] = dot_tn(cots[:, at], ffn_b[...]).astype(BF16)
        weights.start(dy)

    down_rows(2)
    total.pass_on()
    down_rows(1)
    down_rows(-1)
    down_rows(0)
    weights.pass_on(2)
    total.finish(grad_attended)
    sums[...] = jnp.zeros_like(sums)

    def norm_grad(at):
        grad = grad_attended[at, :]
        hat, inv = norm_parts(attended[at, :])
        sums[0] += fold8(grad * hat)
        sums[1] += fold8(grad)
        value = cot[at, :].astype(F32) + norm_back(grad, norm_gain[...], hat, inv)
        grad_attended[at, :] = value
        own_rows[at, :] = value.astype(BF16)

    by_rows(128, norm_grad)
    line.start()
    weights.pass_on(1)
    weights.pass_on(-1)
    weights.finish(2)
    weights.pass_on(0)
    weights.finish(1)
    for b in range(4):
        for h in range(2):
            cots[256 * b : 256 * b + 256, 1024 * h : 1024 * h + 1024] = dot_nt(
                ffn_b[256 * b : 256 * b + 256, :], down[1024 * h : 1024 * h + 1024, :]
            ).astype(BF16)
        if b == 1:
            weights.finish(-1)
    save_out = net.keep(cots, out_part)
    line.forward()
    weights.finish(0)
    weights.pass_on_last()
    for h in range(4):
        up[512 * h : 512 * h + 512, :] = dot_tn(
            rows[:, 512 * h : 512 * h + 512], grad_up[...]
        ).astype(BF16)
        if h == 1:
            line.share()
            weights.finish_last()
    save_grads = net.keep(up, grads_up)
    line.finish()
    weights.collect()
    save_out.wait()
    save_grads.wait()
    net.drain()


def third_call(rows, weights, cots, gain, bias, attended, cot, norm_gain):
    big, half = VMEM((1024, D), BF16), VMEM((D, 1024), BF16)
    return comm_call(
        third_kernel,
        "feed_forward",
        3,
        (rows, weights, cots, gain, bias, attended, cot, norm_gain),
        (pl.ANY, pl.ANY, pl.ANY, VMEM, VMEM, VMEM, VMEM, VMEM),
        (
            shape((1024, D), BF16),
            shape((128, D), F32),
            shape((1024, D), BF16),
            shape((2, 8, D), F32),
            shape((2, 8, 1024), F32),
            shape((4, 32, 1024), BF16),
            shape((D, 1024), BF16),
        ),
        (pl.ANY, VMEM, pl.ANY, VMEM, VMEM, pl.ANY, pl.ANY),
        [
            big,
            half,
            half,
            big,
            VMEM((1024, 1024), F32),
            VMEM((1024, 1024), BF16),
            VMEM((1024, 1024), F32),
            VMEM((1024, 1024), BF16),
            VMEM((1024, 1024), BF16),
            VMEM((256, 1024), F32),
            VMEM((2, 256, 128), F32),
            VMEM((1024, 128), F32),
            VMEM((2, 1024), F32),
            VMEM((8, 2, 1024), F32),
            VMEM((2, 1024), F32),
            VMEM((8, 2, 1024), F32),
            big,
            VMEM((4, 128, D), BF16),
            VMEM((6, 64, D), BF16),
            VMEM((128, D), BF16),
            half,
            VMEM((2, 5, 6, 32, 1024), BF16),
            VMEM((2, 2, 32, 1024), BF16),
        ],
        62,
        (96, 14),
    )


def fourth_kernel(
    part, part_out, attended, grad_attended, tokens, gain, grads, grads_up, outer_sums, inner,
    layer_out, grad_input, shard, shard_up, outer_out, inner_out,
    other, other_out, landing, landing_out, work, grid_landing, done, grid_landing_up, done_up,
    sums, outer, line_slots, y_slots, z_slots, inner_y, inner_z, half_sum, inner_half,
    send, recv, local,
):
    net = Net(send, recv, local)
    others = line_partners(net)
    y_all = [(net.along_y(d), (net.y - d) % 4) for d in (1, 2, 3)]
    z_all = [(net.along_z(d), (net.z - d) % 4) for d in (1, 2, 3)]
    net.greet([to for to, _ in others + y_all + z_all] + pair_neighbours(net))
    total = LineSum(net, part, other, landing)
    total_out = LineSum(net, part_out, other_out, landing_out)
    weights = GridSum(net, grads, grid_landing, done, shard)
    weights_up = GridSum(net, grads_up, grid_landing_up, done_up, shard_up)
    total.start(2, 1, -1, 0)
    inner_first = SmallSum(net, inner, inner_y, net.y, y_all)
    inner_first.start()
    for dy in (2, 1, -1, 0):
        weights_up.start(dy)
    total.chip(2, 1, -1, 0)
    for dy in (2, 1, -1, 0):
        weights.start(dy)
    total_out.start(2, 1, -1, 0)
    weights_up.pass_on(2)
    weights_up.pass_on(1)
    weights_up.pass_on(-1)
    weights_up.pass_on(0)
    weights.pass_on(2)
    total.pass_on()
    total_out.chip(2, 1, -1, 0)
    weights.finish(2)
    weights.pass_on(1)
    weights.pass_on(-1)
    total.finish(work)
    sums[...] = jnp.zeros_like(sums)

    def back(at):
        grad = work[at, :]
        hat, inv_std = norm_parts(tokens[at, :].astype(F32))
        sums[0] += fold8(grad * hat)
        sums[1] += fold8(grad)
        value = grad_attended[at, :] + norm_back(grad, gain[...], hat, inv_std)
        grad_input[at, :] = value.astype(BF16)

    by_rows(128, back)
    for i in range(4):
        row = jnp.sum(sums[i] if i < 2 else outer_sums[i - 2], 0, keepdims=True)
        outer[2 * i : 2 * i + 1, :] = row[:, :1024]
        outer[2 * i + 1 : 2 * i + 2, :] = row[:, 1024:]
    outer_x = SmallSum(net, outer, line_slots, net.x * 2 + net.c, others)
    outer_x.start()
    inner_first.finish(inner_half.at[0])
    inner_last = SmallSum(net, inner_half.at[0], inner_z, net.z, z_all)
    inner_last.start()
    for dp in (2, 1, -1, 0):
        weights_up.finish(dp)
    weights.finish(1)
    weights.finish(-1)
    weights_up.pass_on_last()
    weights.pass_on(0)
    total_out.pass_on()
    outer_x.finish(half_sum.at[0])
    outer_y = SmallSum(net, half_sum.at[0], y_slots, net.y, y_all)
    outer_y.start()
    weights.finish(0)
    weights.pass_on_last()
    total_out.finish(work)

    def out(at):
        layer_out[at, :] = (attended[at, :] + work[at, :]).astype(BF16)

    by_rows(128, out)
    outer_y.finish(half_sum.at[1])
    outer_z = SmallSum(net, half_sum.at[1], z_slots, net.z, z_all)
    outer_z.start()
    inner_last.finish(inner_half.at[1])
    me = (net.x % 2) * 2 + net.c
    inner_k = {}
    for dx, dc in ((1, 0), (1, 1), (0, 1)):
        inner_k[dx, dc] = net.push(inner_half.at[1], inner_out.at[me], net.pair(dx, dc))
    inner_out[me] = inner_half[1]
    weights_up.finish_last()
    weights.finish_last()
    outer_z.finish(outer_out)
    for dx, dc in ((1, 0), (1, 1), (0, 1)):
        net.arrived(inner_k[dx, dc], inner_out.at[((net.x + dx) % 2) * 2 + (net.c + dc) % 2])
    weights.collect()
    weights_up.collect()
    net.drain()


def fourth_call(part, part_out, attended, grad_attended, tokens, gain, grads, grads_up, outer_sums, inner):
    width = grads.shape[-1]
    n = inner.shape[0]
    return comm_call(
        fourth_kernel,
        "sum_last",
        4,
        (part, part_out, attended, grad_attended, tokens, gain, grads, grads_up, outer_sums, inner),
        (VMEM,) * 10,
        (
            shape((128, D), BF16),
            shape((128, D), BF16),
            shape((4, 32, width), BF16),
            shape((4, 32, width), BF16),
            shape((8, 1024), F32),
            shape((4, n, 128), F32),
        ),
        (VMEM, VMEM, pl.ANY, pl.ANY, VMEM, VMEM),
        [
            VMEM((4, 128, D), BF16),
            VMEM((4, 128, D), BF16),
            VMEM((6, 64, D), BF16),
            VMEM((6, 64, D), BF16),
            VMEM((128, D), F32),
            VMEM((2, 5, 6, 32, width), BF16),
            VMEM((2, 2, 32, width), BF16),
            VMEM((2, 5, 6, 32, width), BF16),
            VMEM((2, 2, 32, width), BF16),
            VMEM((2, 8, D), F32),
            VMEM((8, 1024), F32),
            VMEM((8, 8, 1024), F32),
            VMEM((4, 8, 1024), F32),
            VMEM((4, 8, 1024), F32),
            VMEM((4, n, 128), F32),
            VMEM((4, n, 128), F32),
            VMEM((2, 8, 1024), F32),
            VMEM((2, n, 128), F32),
        ],
        56,
        (168, 2),
    )


def xpos_tables(direction):
    half = HEAD_DIM // 2
    pair = np.arange(half, dtype=np.float32)
    frequency = np.power(np.float32(10000.0), -pair / half).astype(np.float32)
    zeta = ((pair / half + 0.4) / 1.4).astype(np.float32)
    position = np.arange(SLOTS, dtype=np.float32)[:, None]
    angle = (position * frequency).astype(np.float32).astype(np.float64)
    decay = np.exp(direction * position / 512.0 * np.log(zeta.astype(np.float64)))
    cosine, sine = np.cos(angle) * decay, np.sin(angle) * decay
    cosine = np.concatenate([cosine] * 2, -1)
    sine = np.concatenate([-sine, sine], -1)
    return np.tile(cosine, (1, 4)).astype(np.float32), np.tile(sine, (1, 4)).astype(np.float32)


def tables():
    return np.stack([*xpos_tables(1.0), *xpos_tables(-1.0)])


def swapped(values):
    lane = lax.broadcasted_iota(jnp.int32, values.shape, 1)
    return jnp.where(lane % 64 < 32, pltpu.roll(values, 224, 1), pltpu.roll(values, 32, 1))


def dot_nn(a, b):
    return lax.dot_general(a, b, (((1,), (0,)), ((), ())), preferred_element_type=F32)


def dot_nt(a, b):
    return lax.dot_general(a, b, (((1,), (1,)), ((), ())), preferred_element_type=F32)


def dot_tn(a, b):
    return lax.dot_general(a, b, (((0,), (0,)), ((), ())), preferred_element_type=F32)


def head_of(values, head):
    lane = lax.broadcasted_iota(jnp.int32, values.shape, 1)
    return jnp.where(lane // 64 == head, values, jnp.zeros_like(values))


def head_probs(query, key, head, allowed):
    scores = dot_nt(head_of(query, head), key) * HEAD_DIM**-0.5
    scores = jnp.where(allowed, scores, -1e30)
    exps = jnp.exp(scores - jnp.max(scores, -1, keepdims=True))
    return exps / jnp.sum(exps, -1, keepdims=True)


def allowed_slots(cap):
    query = lax.broadcasted_iota(jnp.int32, (SLOTS, SLOTS), 0)
    key = lax.broadcasted_iota(jnp.int32, (SLOTS, SLOTS), 1)
    return (key <= query) & (key < IMAGE + cap[0, 0:1, 0:1])


def attend_kernel(rows, weights, cap, table, query_out, key_out, value_out, mixed_out):
    qkv = dot_nn(rows[...], weights[...])
    query, key, value = qkv[:, :256], qkv[:, 256:512], qkv[:, 512:].astype(BF16)
    query = (query * table[0] + swapped(query) * table[1]).astype(BF16)
    key = (key * table[2] + swapped(key) * table[3]).astype(BF16)
    query_out[...], key_out[...], value_out[...] = query, key, value
    allowed = allowed_slots(cap)
    mixed = jnp.zeros((SLOTS, 256), F32)
    for head in range(4):
        probs = head_probs(query, key, head, allowed).astype(BF16)
        mixed = mixed + dot_nn(probs, head_of(value, head))
    mixed_out[...] = mixed


def attend(rows, weights, caps, table):
    block = pl.BlockSpec((SLOTS, 256), lambda b: (b, 0))
    return pl.pallas_call(
        attend_kernel,
        grid=(4,),
        out_shape=[shape((1024, 256), BF16)] * 3 + [shape((1024, 256), F32)],
        in_specs=[
            pl.BlockSpec((SLOTS, D), lambda b: (b, 0)),
            pl.BlockSpec((D, 768), lambda b: (0, 0)),
            pl.BlockSpec((1, 8, 128), lambda b: (b, 0, 0)),
            pl.BlockSpec((4, SLOTS, 256), lambda b: (0, 0, 0)),
        ],
        out_specs=[block] * 4,
        compiler_params=pltpu.CompilerParams(vmem_limit_bytes=32 << 20),
        name="attend",
    )(rows, weights, caps, table)


def attend_back_kernel(query_in, key_in, value_in, grad_in, cap, table, grads_out):
    query, key, value, grad = query_in[...], key_in[...], value_in[...], grad_in[...]
    allowed = allowed_slots(cap)
    grad_query = jnp.zeros((SLOTS, 256), F32)
    grad_key = jnp.zeros((SLOTS, 256), F32)
    grad_value = jnp.zeros((SLOTS, 256), F32)
    for head in range(4):
        probs = head_probs(query, key, head, allowed)
        grad_head = head_of(grad, head)
        grad_probs = dot_nt(grad_head, value)
        grad_value = grad_value + dot_tn(probs.astype(BF16), grad_head)
        delta = jnp.sum(probs * grad_probs, -1, keepdims=True)
        grad_scores = (probs * (grad_probs - delta)).astype(BF16)
        grad_query = grad_query + dot_nn(grad_scores, head_of(key, head))
        grad_key = grad_key + dot_tn(grad_scores, head_of(query, head))
    grad_query = grad_query * HEAD_DIM**-0.5
    grad_key = grad_key * HEAD_DIM**-0.5
    grads_out[:, :256] = (grad_query * table[0] + swapped(grad_query * table[1])).astype(BF16)
    grads_out[:, 256:512] = (grad_key * table[2] + swapped(grad_key * table[3])).astype(BF16)
    grads_out[:, 512:] = grad_value.astype(BF16)


def attend_back(query, key, value, grad, caps, table):
    block = pl.BlockSpec((SLOTS, 256), lambda b: (b, 0))
    return pl.pallas_call(
        attend_back_kernel,
        grid=(4,),
        out_shape=shape((1024, 768), BF16),
        in_specs=[block] * 4
        + [
            pl.BlockSpec((1, 8, 128), lambda b: (b, 0, 0)),
            pl.BlockSpec((4, SLOTS, 256), lambda b: (0, 0, 0)),
        ],
        out_specs=pl.BlockSpec((SLOTS, 768), lambda b: (b, 0)),
        compiler_params=pltpu.CompilerParams(vmem_limit_bytes=32 << 20),
        name="attend_back",
    )(query, key, value, grad, caps, table)


def quarters(shard):
    return shard.astype(BF16).reshape(32, 4, -1).transpose(1, 0, 2)


def from_quarters(pieces):
    return pieces.transpose(1, 0, 2).reshape(32, -1).astype(F32)


def token_sums(terms, collective_id):
    sums = jnp.concatenate([jnp.sum(t, -1).reshape(8, 128) for t in terms], 0)
    sums = stats_call(sums, collective_id)
    return [sums[8 * i : 8 * i + 8].reshape(1024, 1) for i in range(len(terms))]


def per_device(
    tokens, caption_len, norm1_gain, norm1_bias, w_query, w_key, w_value, inner_gain, inner_bias,
    w_proj, norm2_gain, norm2_bias, w_up, ffn_norm_gain, ffn_norm_bias, w_down, cotangent,
):
    seq = lax.axis_index("seq")
    place = ((seq // 8) % 2) * 2 + seq % 2
    table = jnp.asarray(tables())
    pieces1 = jnp.concatenate([quarters(w) for w in (w_query, w_key, w_value, w_proj.T)], -1)
    pieces2 = jnp.concatenate([quarters(w) for w in (w_up, w_down.T)], -1)
    my_gain = lax.dynamic_slice(inner_gain, (place * 256,), (256,))
    my_bias = lax.dynamic_slice(inner_bias, (place * 256,), (256,))
    my_ffn_gain = lax.dynamic_slice(ffn_norm_gain, (place * 1024,), (1024,))
    my_ffn_bias = lax.dynamic_slice(ffn_norm_bias, (place * 1024,), (1024,))
    cap = jnp.broadcast_to(caption_len.reshape(1, 1), (8, 128))

    first_hat, _ = norm_parts(tokens.astype(F32))
    first_rows = (first_hat * norm1_gain + norm1_bias).astype(BF16)
    rows1, caps, weights1 = first_call(first_rows, cap, pieces1)

    query, key, value, mixed = attend(rows1, weights1, caps, table)
    s0, s1 = token_sums((mixed, mixed * mixed), 5)
    center = s0 / D
    inner_inv = lax.rsqrt(s1 / D - center * center + EPS)
    context_hat = (mixed - center) * inner_inv
    context = (context_hat * my_gain + my_bias).astype(BF16)
    proj_t = weights1[:, 768:]
    attn_part = dot_nt(context, proj_t).astype(BF16)

    attended, rows2, weights2, cots = second_call(
        attn_part, tokens, norm2_gain.reshape(1, D), norm2_bias.reshape(1, D), pieces2, cotangent
    )
    out_part, grad_attended, grad_rows, outer_sums, unit_sums, shard_down, grads_up = third_call(
        rows2, weights2, cots, my_ffn_gain.reshape(1, 1024), my_ffn_bias.reshape(1, 1024),
        attended, cotangent, norm2_gain.reshape(1, D),
    )

    grad_context = dot_nn(grad_rows, proj_t)
    scaled = grad_context * my_gain
    t0, t1 = token_sums((scaled, scaled * context_hat), 7)
    inner_gain_part = jnp.sum(grad_context * context_hat, 0)
    inner_bias_part = jnp.sum(grad_context, 0)
    grad_mixed = (inner_inv * (scaled - t0 / D - context_hat * (t1 / D))).astype(BF16)
    grads_qkv = attend_back(query, key, value, grad_mixed, caps, table)
    first_part = dot_nt(grads_qkv, weights1[:, :768]).astype(BF16)
    grads1 = jnp.concatenate(
        [dot_tn(rows1, grads_qkv).astype(BF16), dot_tn(grad_rows, context).astype(BF16)], -1
    )
    inner = jnp.concatenate([inner_gain_part, inner_bias_part, jnp.sum(unit_sums, 1).reshape(2048)])
    inner = jnp.pad(inner.reshape(20, 128), ((0, 4), (0, 0)))

    layer_out, grad_input, shard1, shard_up, outer, inner = fourth_call(
        first_part, out_part, attended, grad_attended, tokens, norm1_gain.reshape(1, D), grads1,
        grads_up, outer_sums, inner,
    )
    outer = outer.reshape(4, D)
    inner = inner.reshape(4, 24 * 128)
    return (
        layer_out,
        grad_input,
        outer[0],
        outer[1],
        from_quarters(shard1[:, :, :256]),
        from_quarters(shard1[:, :, 256:512]),
        from_quarters(shard1[:, :, 512:768]),
        inner[:, :256].reshape(-1),
        inner[:, 256:512].reshape(-1),
        from_quarters(shard1[:, :, 768:]).T,
        outer[2],
        outer[3],
        from_quarters(shard_up),
        inner[:, 512:1536].reshape(-1),
        inner[:, 1536:2560].reshape(-1),
        from_quarters(shard_down).T,
    )


def solution(mesh):
    rows = P(("seq", "ffn"), None)
    by_rows_, by_columns, half = P("seq", "ffn"), P("ffn", "seq"), P("ffn")
    return jax.shard_map(
        per_device,
        mesh=mesh,
        in_specs=(
            rows, P("seq"), P(), P(), by_rows_, by_rows_, by_rows_, half, half, by_columns,
            P(), P(), by_rows_, half, half, by_columns, rows,
        ),
        out_specs=(
            rows, rows, P(), P(), by_rows_, by_rows_, by_rows_, half, half, by_columns,
            P(), P(), by_rows_, half, half, by_columns,
        ),
        check_vma=False,
    )
```

```python
import functools

import jax
import jax.numpy as jnp
import numpy as np
from jax import lax
from jax.experimental import pallas as pl
from jax.experimental.pallas import tpu as pltpu
from jax.sharding import PartitionSpec as P

D = 2048
HEAD_DIM = 64
FF = 8192
SLOTS = 256
IMAGE = 64
EPS = 1e-05
F32 = jnp.float32
BF16 = jnp.bfloat16
MESH = pl.DeviceIdType.MESH
VMEM = pltpu.VMEM
HBM = pltpu.HBM


def device_at(y, x, z, c):
    return (((y * 2 + x % 2) * 4 + z) * 2 + c, x // 2)


def line_slot(x, c):
    return ((x % 2) * 2 + c) * 2 + x // 2


class Net:
    def __init__(self, send, recv, local):
        seq, ffn = lax.axis_index("seq"), lax.axis_index("ffn")
        self.y, self.z, self.c = seq // 16, (seq // 2) % 4, seq % 2
        self.x = ffn * 2 + (seq // 8) % 2
        self.send, self.recv, self.local = send, recv, local
        self.used, self.used_local = 0, 0
        self.out = []

    def along_x(self, dx, dc=0):
        return device_at(self.y, (self.x + dx) % 4, self.z, (self.c + dc) % 2)

    def along_y(self, dy):
        return device_at((self.y + dy) % 4, self.x, self.z, self.c)

    def along_z(self, dz):
        return device_at(self.y, self.x, (self.z + dz) % 4, self.c)

    def pair(self, dx, dc):
        x = (self.x // 2) * 2 + (self.x + dx) % 2
        return device_at(self.y, x, self.z, (self.c + dc) % 2)

    def greet(self, partners):
        barrier = pltpu.get_barrier_semaphore()
        for partner in partners:
            pl.semaphore_signal(barrier, inc=1, device_id=partner, device_id_type=MESH)
        pl.semaphore_wait(barrier, len(partners))

    def push(self, src, dst, device):
        k = self.used
        self.used += 1
        copy = pltpu.make_async_remote_copy(
            src_ref=src,
            dst_ref=dst,
            send_sem=self.send.at[k],
            recv_sem=self.recv.at[k],
            device_id=device,
            device_id_type=MESH,
        )
        copy.start()
        self.out.append(copy)
        return k

    def arrived(self, k, landed):
        pltpu.make_async_remote_copy(
            src_ref=landed,
            dst_ref=landed,
            send_sem=self.send.at[k],
            recv_sem=self.recv.at[k],
            device_id=self.along_x(0, 1),
            device_id_type=MESH,
        ).wait_recv()

    def keep(self, src, dst):
        copy = pltpu.make_async_copy(src, dst, self.local.at[self.used_local])
        self.used_local += 1
        copy.start()
        return copy

    def drain(self):
        for copy in self.out:
            copy.wait_send()
        assert (self.used, self.used_local) == (self.send.shape[0], self.local.shape[0])


def add_into(dst, *terms):
    def step(i, carry):
        rows = pl.ds(pl.multiple_of(i * 16, 16), 16)
        total = terms[0][rows, :].astype(F32)
        for term in terms[1:]:
            total = total + term[rows, :].astype(F32)
        dst[rows, :] = total.astype(dst.dtype)
        return carry

    lax.fori_loop(0, dst.shape[0] // 16, step, 0)


def line_rows(ref, slot, half=None):
    if half is None:
        return ref.at[pl.ds(pl.multiple_of(slot * 128, 128), 128)]
    return ref.at[pl.ds(pl.multiple_of(slot * 128 + 64 * half, 64), 64)]


class LineGather:
    def __init__(self, net, own, full):
        self.net, self.own, self.full = net, own, full

    def block(self, dx, dc=0, half=None):
        net = self.net
        return line_rows(self.full, line_slot((net.x + dx) % 4, (net.c + dc) % 2), half)

    def start(self):
        net, mine = self.net, self.block(0)
        self.a = net.push(self.own, mine, net.along_x(1))
        self.b = net.push(self.own, mine, net.along_x(-1))
        self.s0 = net.push(self.own, mine, net.along_x(0, 1))
        self.kept = net.keep(self.own, mine)
        self.sends = net.out[-3:]

    def sent(self):
        for copy in self.sends:
            copy.wait_send()
        self.net.out = [copy for copy in self.net.out if all(copy is not s for s in self.sends)]

    def forward(self):
        net = self.net
        net.arrived(self.a, self.block(-1))
        self.fa = net.push(self.block(-1, 0, 0), self.block(-1, 0, 0), net.along_x(1))
        self.sa = net.push(self.block(-1), self.block(-1), net.along_x(0, 1))
        net.arrived(self.b, self.block(1))
        self.fb = net.push(self.block(1, 0, 1), self.block(1, 0, 1), net.along_x(-1))
        self.sb = net.push(self.block(1), self.block(1), net.along_x(0, 1))

    def share(self):
        net = self.net
        net.arrived(self.fa, self.block(2, 0, 0))
        self.sfa = net.push(self.block(2, 0, 0), self.block(2, 0, 0), net.along_x(0, 1))
        net.arrived(self.fb, self.block(2, 0, 1))
        self.sfb = net.push(self.block(2, 0, 1), self.block(2, 0, 1), net.along_x(0, 1))

    def finish(self):
        net = self.net
        net.arrived(self.s0, self.block(0, 1))
        net.arrived(self.sa, self.block(-1, 1))
        net.arrived(self.sb, self.block(1, 1))
        net.arrived(self.sfa, self.block(2, 1, 0))
        net.arrived(self.sfb, self.block(2, 1, 1))
        self.kept.wait()


class RingSum:
    def __init__(self, net, mine, landing, ahead, behind):
        self.net, self.mine, self.landing = net, mine, landing
        self.ahead, self.behind = ahead, behind

    def start_far(self):
        net, land = self.net, self.landing
        self.f0 = net.push(self.mine(2, 0), land.at[0], self.ahead)
        self.f1 = net.push(self.mine(2, 1), land.at[1], self.behind)

    def start_near(self, d):
        net, land = self.net, self.landing
        if d == 1:
            self.r1 = net.push(self.mine(1, 1), land.at[3], self.ahead)
        else:
            self.r0 = net.push(self.mine(-1, 0), land.at[4], self.behind)

    def pass_on(self):
        net, land = self.net, self.landing
        net.arrived(self.f0, land.at[0])
        add_into(land.at[0], land.at[0], self.mine(1, 0))
        self.s0 = net.push(land.at[0], land.at[2], self.ahead)
        net.arrived(self.f1, land.at[1])
        add_into(land.at[1], land.at[1], self.mine(-1, 1))
        self.s1 = net.push(land.at[1], land.at[5], self.behind)

    def finish(self, out=None):
        net, land = self.net, self.landing
        net.arrived(self.s0, land.at[2])
        net.arrived(self.r0, land.at[4])
        add_into(land.at[2] if out is None else out(0), self.mine(0, 0), land.at[2], land.at[4])
        net.arrived(self.r1, land.at[3])
        net.arrived(self.s1, land.at[5])
        add_into(land.at[3] if out is None else out(1), self.mine(0, 1), land.at[3], land.at[5])


class LineSum:
    def __init__(self, net, part, other, landing):
        self.net, self.part, self.other = net, part, other
        self.ring = RingSum(net, self.mine, landing, net.along_x(1), net.along_x(-1))
        self.k = {}

    def block(self, dx, dc):
        net = self.net
        return line_rows(self.part, line_slot((net.x + dx) % 4, (net.c + dc) % 2))

    def mine(self, d, half):
        return self.other.at[d % 4, pl.ds(64 * half, 64)]

    def start(self, *steps):
        net = self.net
        for d in steps:
            self.k[d] = net.push(self.block(d, 1), self.other.at[d % 4], net.along_x(0, 1))

    def chip(self, *steps):
        for d in steps:
            self.net.arrived(self.k[d], self.other.at[d % 4])
            add_into(self.other.at[d % 4], self.other.at[d % 4], self.block(d, 0))
            if d == 2:
                self.ring.start_far()
            elif d:
                self.ring.start_near(d)

    def pass_on(self):
        self.ring.pass_on()

    def finish(self, out):
        self.ring.finish(lambda half: out.at[pl.ds(64 * half, 64)])


def shard_rows(ref, y, x_lo, z, c=None):
    if c is None:
        return ref.at[pl.ds(pl.multiple_of(((y * 2 + x_lo) * 4 + z) * 64, 64), 64)]
    return ref.at[pl.ds(pl.multiple_of((((y * 2 + x_lo) * 4 + z) * 2 + c) * 32, 32), 32)]


class GridGather:
    def __init__(self, net, pieces, full):
        self.net, self.pieces, self.full = net, pieces, full

    def spot(self, dx, dc):
        net = self.net
        return shard_rows(self.full, net.y, (net.x + dx) % 2, net.z, (net.c + dc) % 2)

    def exchange(self):
        net = self.net
        self.k = {}
        for dx, dc in ((1, 0), (1, 1), (0, 1)):
            to = ((net.x + dx) % 2) * 2 + (net.c + dc) % 2
            self.k[dx, dc] = net.push(self.pieces.at[to], self.spot(0, 0), net.pair(dx, dc))
        me = (net.x % 2) * 2 + net.c
        self.kept = net.keep(self.pieces.at[me], self.spot(0, 0))

    def slab(self, t, dp, dq, half=None):
        net = self.net
        dy, dz = (dq, dp) if t == 0 else (dp, dq)
        return shard_rows(self.full, (net.y + dy) % 4, t, (net.z + dz) % 4, half)

    def to_p(self, t, d):
        return self.net.along_z(d) if t == 0 else self.net.along_y(d)

    def to_q(self, t, d):
        return self.net.along_y(d) if t == 0 else self.net.along_z(d)

    def same(self, ref, device):
        return self.net.push(ref, ref, device)

    def second(self, t, dp):
        self.q[t, dp] = (
            self.same(self.slab(t, dp, 0), self.to_q(t, 1)),
            self.same(self.slab(t, dp, 0), self.to_q(t, -1)),
        )

    def start(self):
        for dx, dc in ((0, 1), (1, 0), (1, 1)):
            self.net.arrived(self.k[dx, dc], self.spot(dx, dc))
        self.kept.wait()
        self.p, self.q, self.f = {}, {}, {}
        for t in (0, 1):
            self.p[t] = (
                self.same(self.slab(t, 0, 0), self.to_p(t, 1)),
                self.same(self.slab(t, 0, 0), self.to_p(t, -1)),
            )
        for t in (0, 1):
            self.second(t, 0)

    def near(self):
        net = self.net
        for t in (0, 1):
            a, b = self.p[t]
            net.arrived(a, self.slab(t, -1, 0))
            fa = self.same(self.slab(t, -1, 0, 0), self.to_p(t, 1))
            net.arrived(b, self.slab(t, 1, 0))
            fb = self.same(self.slab(t, 1, 0, 1), self.to_p(t, -1))
            self.f[t] = (fa, fb)
        for t in (0, 1):
            self.second(t, -1)
            self.second(t, 1)

    def far(self):
        for t in (0, 1):
            self.net.arrived(self.f[t][0], self.slab(t, 2, 0, 0))
            self.net.arrived(self.f[t][1], self.slab(t, 2, 0, 1))
            self.second(t, 2)

    def pass_on(self, dp):
        net = self.net
        for t in (0, 1):
            a, b = self.q[t, dp]
            net.arrived(a, self.slab(t, dp, -1))
            fa = self.same(self.slab(t, dp, -1, 0), self.to_q(t, 1))
            net.arrived(b, self.slab(t, dp, 1))
            fb = self.same(self.slab(t, dp, 1, 1), self.to_q(t, -1))
            self.f[t, dp] = (fa, fb)

    def finish(self):
        for dp in (0, -1, 1, 2):
            for t in (0, 1):
                self.net.arrived(self.f[t, dp][0], self.slab(t, dp, 2, 0))
                self.net.arrived(self.f[t, dp][1], self.slab(t, dp, 2, 1))


class GridSum:
    def __init__(self, net, part, landing, done, out):
        self.net, self.part, self.landing, self.done, self.out = net, part, landing, done, out
        self.rings = {}
        for t in (0, 1):
            for dp in (2, 1, -1, 0):
                self.rings[t, dp] = RingSum(
                    net,
                    functools.partial(self.term, t, dp),
                    landing.at[t, dp % 4],
                    self.to_q(t, 1),
                    self.to_q(t, -1),
                )
            self.rings[t] = RingSum(
                net,
                functools.partial(self.column, t),
                landing.at[t, 4],
                self.to_p(t, 1),
                self.to_p(t, -1),
            )

    def to_p(self, t, d):
        return self.net.along_z(d) if t == 0 else self.net.along_y(d)

    def to_q(self, t, d):
        return self.net.along_y(d) if t == 0 else self.net.along_z(d)

    def term(self, t, dp, dq, half):
        net = self.net
        dy, dz = (dq, dp) if t == 0 else (dp, dq)
        return shard_rows(self.part, (net.y + dy) % 4, t, (net.z + dz) % 4, half)

    def column(self, t, dp, half):
        return self.landing.at[t, dp % 4, 2 + half]

    def start(self, dy):
        for dp in (2, 1, -1, 0):
            if dy == 2:
                self.rings[0, dp].start_far()
            elif dy:
                self.rings[0, dp].start_near(dy)
        self.rings[1, dy].start_far()
        self.rings[1, dy].start_near(1)
        self.rings[1, dy].start_near(-1)

    def pass_on(self, dp):
        for t in (0, 1):
            self.rings[t, dp].pass_on()

    def finish(self, dp):
        for t in (0, 1):
            self.rings[t, dp].finish()
            if dp == 2:
                self.rings[t].start_far()
            elif dp:
                self.rings[t].start_near(dp)

    def pass_on_last(self):
        for t in (0, 1):
            self.rings[t].pass_on()

    def finish_last(self):
        net = self.net
        for t in (0, 1):
            self.rings[t].finish(lambda half: self.done.at[t, half])
        me = (net.x % 2) * 2 + net.c
        self.k = {}
        for dx, dc in ((1, 0), (1, 1), (0, 1)):
            src = self.done.at[(net.x + dx) % 2, (net.c + dc) % 2]
            self.k[dx, dc] = net.push(src, self.out.at[me], net.pair(dx, dc))
        self.kept = net.keep(self.done.at[net.x % 2, net.c], self.out.at[me])

    def collect(self):
        net = self.net
        for dx, dc in ((1, 0), (1, 1), (0, 1)):
            at = ((net.x + dx) % 2) * 2 + (net.c + dc) % 2
            net.arrived(self.k[dx, dc], self.out.at[at])
        self.kept.wait()


class SmallSum:
    def __init__(self, net, own, slots, me, partners):
        self.net, self.own, self.slots, self.me, self.partners = net, own, slots, me, partners

    def start(self):
        net = self.net
        self.k = [(net.push(self.own, self.slots.at[self.me], to), at) for to, at in self.partners]
        self.slots[self.me] = self.own[...]

    def total(self):
        for k, at in self.k:
            self.net.arrived(k, self.slots.at[at])
        total = self.slots[0]
        for i in range(1, self.slots.shape[0]):
            total = total + self.slots[i]
        return total

    def finish(self, out):
        out[...] = self.total()


def line_partners(net):
    return [
        (net.along_x(dx, dc), ((net.x - dx) % 4) * 2 + (net.c + dc) % 2)
        for dx in range(4)
        for dc in range(2)
        if dx or dc
    ]


def sem_scratch(pushes, keeps):
    return [
        pltpu.SemaphoreType.DMA((pushes,)),
        pltpu.SemaphoreType.DMA((pushes,)),
        pltpu.SemaphoreType.DMA((keeps,)),
    ]


def spec(space):
    return pl.BlockSpec(memory_space=space)


def shape(dims, dtype):
    return jax.ShapeDtypeStruct(dims, dtype)


class Staged:
    def __init__(self, loads, stores):
        self.loads, self.stores, self.started = loads, stores, []
        for copy, _ in loads:
            copy.start()

    def wait(self, *refs):
        for copy, ref in list(self.loads):
            if not refs or any(ref is r for r in refs):
                copy.wait()
                self.loads = [pair for pair in self.loads if pair[1] is not ref]

    def put(self, *refs):
        for copy, ref in list(self.stores):
            if not refs or any(ref is r for r in refs):
                copy.start()
                self.started.append(copy)
                self.stores = [pair for pair in self.stores if pair[1] is not ref]

    def finish(self):
        self.wait()
        self.put()
        for copy in self.started:
            copy.wait()


def comm_call(body, name, collective_id, ins, in_spaces, outs, out_spaces, scratch, mib, sems):
    n_in, n_out = len(ins), len(outs)
    buffers = [space(v.shape, v.dtype) for v, space in zip(ins, in_spaces) if space is not HBM]
    buffers += [space(v.shape, v.dtype) for v, space in zip(outs, out_spaces) if space is not HBM]
    n = len(buffers)

    def kernel(*refs):
        sem = refs[-1]
        rest = list(refs[n_in + n_out : n_in + n_out + n])
        loads, stores, args = [], [], []
        for i, (ref, space) in enumerate(zip(refs, (*in_spaces, *out_spaces))):
            if space is HBM:
                args.append(ref)
                continue
            buffer = rest.pop(0)
            args.append(buffer)
            at = sem.at[len(loads) + len(stores)]
            if i < n_in:
                loads.append((pltpu.make_async_copy(ref, buffer, at), buffer))
            else:
                stores.append((pltpu.make_async_copy(buffer, ref, at), buffer))
        io = Staged(loads, stores)
        body(io, *args, *refs[n_in + n_out + n : -1])
        io.finish()

    return pl.pallas_call(
        kernel,
        out_shape=outs,
        in_specs=[spec(HBM)] * n_in,
        out_specs=[spec(HBM)] * n_out,
        scratch_shapes=buffers + scratch + sem_scratch(*sems) + [pltpu.SemaphoreType.DMA((n,))],
        compiler_params=pltpu.CompilerParams(
            collective_id=collective_id, has_side_effects=True, vmem_limit_bytes=mib << 20
        ),
        name=name,
    )(*ins)


def x_neighbours(net):
    return [net.along_x(1), net.along_x(-1), net.along_x(0, 1)]


def grid_neighbours(net):
    return [net.along_y(1), net.along_y(-1), net.along_z(1), net.along_z(-1)]


def pair_neighbours(net):
    return [net.pair(1, 0), net.pair(1, 1), net.pair(0, 1)]


def norm_parts(values):
    center = jnp.mean(values, -1, keepdims=True)
    spread = jnp.mean(values * values, -1, keepdims=True) - center * center
    inv_std = lax.rsqrt(spread + EPS)
    return (values - center) * inv_std, inv_std


def by_rows(rows, step):
    def body(i, carry):
        step(pl.ds(pl.multiple_of(i * 16, 16), 16))
        return carry

    lax.fori_loop(0, rows // 16, body, 0)


def norm_back(grad, gain, hat, inv_std):
    scaled = grad * gain
    return inv_std * (
        scaled
        - jnp.mean(scaled, -1, keepdims=True)
        - hat * jnp.mean(scaled * hat, -1, keepdims=True)
    )


def fold8(values):
    return values[:8] + values[8:]


def block_rows(base, step):
    def body(i, carry):
        step(
            pl.ds(pl.multiple_of(i * 16, 16), 16),
            pl.ds(pl.multiple_of(base + i * 16, 16), 16),
        )
        return carry

    lax.fori_loop(0, 16, body, 0)


def lane_sums(values):
    total = values[:, :128]
    for k in range(1, values.shape[1] // 128):
        total = total + values[:, 128 * k : 128 * k + 128]
    return total


def row_of(partial):
    return jnp.sum(partial.T, 0, keepdims=True)


def columns_of(*rows):
    n = rows[0].shape[1]
    return jnp.concatenate([*rows, jnp.zeros((128 - len(rows), n), F32)], 0).T


def xpos_tables(direction):
    half = HEAD_DIM // 2
    pair = np.arange(half, dtype=np.float32)
    frequency = np.power(np.float32(10000.0), -pair / half).astype(np.float32)
    zeta = ((pair / half + 0.4) / 1.4).astype(np.float32)
    position = np.arange(SLOTS, dtype=np.float32)[:, None]
    angle = (position * frequency).astype(np.float32).astype(np.float64)
    decay = np.exp(direction * position / 512.0 * np.log(zeta.astype(np.float64)))
    cosine, sine = np.cos(angle) * decay, np.sin(angle) * decay
    cosine = np.concatenate([cosine] * 2, -1)
    sine = np.concatenate([-sine, sine], -1)
    return np.tile(cosine, (1, 4)).astype(np.float32), np.tile(sine, (1, 4)).astype(np.float32)


def tables():
    return np.stack([*xpos_tables(1.0), *xpos_tables(-1.0)])


def swapped(values):
    lane = lax.broadcasted_iota(jnp.int32, values.shape, 1)
    return jnp.where(lane % 64 < 32, pltpu.roll(values, 224, 1), pltpu.roll(values, 32, 1))


def dot_nn(a, b):
    return lax.dot_general(a, b, (((1,), (0,)), ((), ())), preferred_element_type=F32)


def dot_nt(a, b):
    return lax.dot_general(a, b, (((1,), (1,)), ((), ())), preferred_element_type=F32)


def dot_tn(a, b):
    return lax.dot_general(a, b, (((0,), (0,)), ((), ())), preferred_element_type=F32)


def head_of(values, head):
    lane = lax.broadcasted_iota(jnp.int32, values.shape, 1)
    return jnp.where(lane // 64 == head, values, jnp.zeros_like(values))


def head_probs(query, key, head, allowed):
    scores = dot_nt(head_of(query, head), key) * HEAD_DIM**-0.5
    scores = jnp.where(allowed, scores, -1e30)
    exps = jnp.exp(scores - jnp.max(scores, -1, keepdims=True))
    return exps / jnp.sum(exps, -1, keepdims=True)


def allowed_slots(cap):
    query = lax.broadcasted_iota(jnp.int32, (SLOTS, SLOTS), 0)
    key = lax.broadcasted_iota(jnp.int32, (SLOTS, SLOTS), 1)
    return (key <= query) & (key < IMAGE + cap[0:1, 0:1])


def attend(rows, weights, cap, table, at, query_out, key_out, value_out, mixed_out):
    qkv = dot_nn(rows, weights[:, :768])
    query, key, value = qkv[:, :256], qkv[:, 256:512], qkv[:, 512:].astype(BF16)
    query = (query * table[0] + swapped(query) * table[1]).astype(BF16)
    key = (key * table[2] + swapped(key) * table[3]).astype(BF16)
    query_out[at, :], key_out[at, :], value_out[at, :] = query, key, value
    allowed = allowed_slots(cap)
    mixed = jnp.zeros((SLOTS, 256), F32)
    for head in range(4):
        probs = head_probs(query, key, head, allowed).astype(BF16)
        mixed = mixed + dot_nn(probs, head_of(value, head))
    mixed_out[at, :] = mixed


def attend_back(query, key, value, grad, cap, table):
    allowed = allowed_slots(cap)
    grad_query = jnp.zeros((SLOTS, 256), F32)
    grad_key = jnp.zeros((SLOTS, 256), F32)
    grad_value = jnp.zeros((SLOTS, 256), F32)
    for head in range(4):
        probs = head_probs(query, key, head, allowed)
        grad_head = head_of(grad, head)
        grad_probs = dot_nt(grad_head, value)
        grad_value = grad_value + dot_tn(probs.astype(BF16), grad_head)
        delta = jnp.sum(probs * grad_probs, -1, keepdims=True)
        grad_scores = (probs * (grad_probs - delta)).astype(BF16)
        grad_query = grad_query + dot_nn(grad_scores, head_of(key, head))
        grad_key = grad_key + dot_tn(grad_scores, head_of(query, head))
    grad_query = grad_query * HEAD_DIM**-0.5
    grad_key = grad_key * HEAD_DIM**-0.5
    return (
        (grad_query * table[0] + swapped(grad_query * table[1])).astype(BF16),
        (grad_key * table[2] + swapped(grad_key * table[3])).astype(BF16),
        grad_value.astype(BF16),
    )


def place_of(net):
    return (net.x % 2) * 2 + net.c


def my_lanes(ref, net, n):
    return ref[:, pl.ds(pl.multiple_of(place_of(net) * n, n), n)]


def sequence_at(net, q):
    seq_of = ((net.x + q // 2) % 2) * 2 + (net.c + 1 + q) % 2
    return pl.multiple_of(seq_of * SLOTS, SLOTS)


def split_shard(shard, pieces, lane):
    n = shard.shape[1] // 4
    for d in range(4):
        pieces[d, :, lane : lane + n] = shard[:, n * d : n * d + n].astype(BF16)


def first_kernel(
    io, tokens, cap, gain, bias, w_query, w_key, w_value, w_proj, inner_gain, inner_bias,
    gain2, bias2, w_up, w_down, cot, table,
    rows1_out, weights1_out, rows2, weights2, cots, query, key, value, hat, context, inner_inv,
    caps, attended,
    rows, rows1, weights1, pieces1, pieces2, caps_in, cap_slots, mixed, partial, cols,
    own_s, slots_s, part, other, landing, send, recv, local,
):
    net = Net(send, recv, local)
    for i, shard in enumerate((w_query, w_key, w_value, w_proj)):
        io.wait(shard)
        split_shard(shard, pieces1, 256 * i)
    io.wait(tokens, cap, gain, bias)

    def norm(at):
        one, _ = norm_parts(tokens[at, :].astype(F32))
        rows[at, :] = (one * gain[...] + bias[...]).astype(BF16)

    by_rows(128, norm)
    caps_in[...] = jnp.full((8, 128), cap[0], jnp.int32)
    others = line_partners(net)
    net.greet([to for to, _ in others] + grid_neighbours(net) + pair_neighbours(net))
    gather1 = GridGather(net, pieces1, weights1)
    gather2 = GridGather(net, pieces2, weights2)
    line1 = LineGather(net, rows, rows1)
    line2 = LineGather(net, rows, rows2)
    line_cot = LineGather(net, cot, cots)
    total = LineSum(net, part, other, landing)
    sum_s = SmallSum(net, own_s, slots_s, net.x * 2 + net.c, others)

    gather1.exchange()
    cap_k = {}
    for dx, dc in ((1, 0), (1, 1), (0, 1)):
        cap_k[dx, dc] = net.push(caps_in, cap_slots.at[place_of(net)], net.pair(dx, dc))
    cap_slots[place_of(net)] = caps_in[...]
    line1.start()
    for i, shard in enumerate((w_up, w_down)):
        io.wait(shard)
        split_shard(shard, pieces2, 1024 * i)
    io.wait()
    gather1.start()
    gather2.exchange()
    gather1.near()
    line1.forward()
    gather1.far()
    gather1.pass_on(0)
    line1.share()
    gather1.pass_on(-1)
    gather1.pass_on(1)
    line_cot.start()
    gather1.pass_on(2)
    gather2.start()
    for dx, dc in ((1, 0), (1, 1), (0, 1)):
        at = ((net.x + dx) % 2) * 2 + (net.c + dc) % 2
        net.arrived(cap_k[dx, dc], cap_slots.at[at])
    caps[...] = cap_slots[...]
    line1.finish()
    gather1.finish()
    io.put(caps)
    save = [net.keep(rows1, rows1_out), net.keep(weights1, weights1_out)]

    for b in range(4):
        at = slice(256 * b, 256 * b + 256)
        attend(rows1[at, :], weights1, caps.at[b], table, at, query, key, value, mixed)
        both = mixed[at, :]
        partial[0] = lane_sums(both)
        partial[1] = lane_sums(both * both)
        for i in range(2):
            own_s[i : i + 1, at] = row_of(partial[i])
        if b == 0:
            gather2.near()
        if b == 1:
            line_cot.forward()
        if b == 2:
            gather2.far()
    sum_s.start()
    gather2.pass_on(0)
    line_cot.share()
    both = sum_s.total()
    center = both[0:1] * (1.0 / D)
    inv_std = lax.rsqrt(both[1:2] * (1.0 / D) - center * center + EPS)
    inner_inv[...] = inv_std
    cols[...] = columns_of(center, inv_std)
    my_gain, my_bias = my_lanes(inner_gain, net, 256), my_lanes(inner_bias, net, 256)

    def inner(at):
        one = (mixed[at, :] - cols[at, 0:1]) * cols[at, 1:2]
        hat[at, :] = one
        context[at, :] = (one * my_gain + my_bias).astype(BF16)

    by_rows(1024, inner)
    io.put(query, key, value, hat, context, inner_inv)
    for q in range(4):
        at = pl.ds(sequence_at(net, q), SLOTS)
        mine = context[at, :]
        for h in range(2):
            part[at, 1024 * h : 1024 * h + 1024] = dot_nt(
                mine, weights1[1024 * h : 1024 * h + 1024, 768:]
            ).astype(BF16)
        if q == 0:
            total.start(2)
        if q == 1:
            total.start(0)
            total.chip(2)
    total.start(1, -1)
    total.chip(1, -1, 0)
    gather2.pass_on(-1)
    total.pass_on()
    gather2.pass_on(1)
    total.finish(attended)

    def norm2(at):
        values = tokens[at, :].astype(F32) + attended[at, :]
        attended[at, :] = values
        one, _ = norm_parts(values)
        rows[at, :] = (one * gain2[...] + bias2[...]).astype(BF16)

    line1.sent()
    by_rows(128, norm2)
    line2.start()
    io.put(attended)
    gather2.pass_on(2)
    line_cot.finish()
    line2.forward()
    gather2.finish()
    line2.share()
    line2.finish()
    for copy in save:
        copy.wait()
    net.drain()


def first_call(ins):
    return comm_call(
        first_kernel,
        "attention",
        1,
        ins,
        (VMEM, pltpu.SMEM) + (VMEM,) * 12 + (HBM, VMEM),
        (
            shape((1024, D), BF16),
            shape((D, 1024), BF16),
            shape((1024, D), BF16),
            shape((D, D), BF16),
            shape((1024, D), BF16),
            shape((1024, 256), BF16),
            shape((1024, 256), BF16),
            shape((1024, 256), BF16),
            shape((1024, 256), F32),
            shape((1024, 256), BF16),
            shape((1, 1024), F32),
            shape((4, 8, 128), jnp.int32),
            shape((128, D), F32),
        ),
        (HBM,) * 5 + (VMEM,) * 8,
        [
            VMEM((128, D), BF16),
            VMEM((1024, D), BF16),
            VMEM((D, 1024), BF16),
            VMEM((4, 32, 1024), BF16),
            VMEM((4, 32, 2048), BF16),
            VMEM((8, 128), jnp.int32),
            VMEM((4, 8, 128), jnp.int32),
            VMEM((1024, 256), F32),
            VMEM((2, 256, 128), F32),
            VMEM((1024, 128), F32),
            VMEM((2, 1024), F32),
            VMEM((8, 2, 1024), F32),
            VMEM((1024, D), BF16),
            VMEM((4, 128, D), BF16),
            VMEM((6, 64, D), BF16),
        ],
        63,
        (133, 7),
    )


def second_kernel(
    io, rows_in, weights_in, cots_in, gains, biases, attended, cot, norm_gain,
    out_part, grad_attended, grad_rows, sums, unit_sums, shard, grads_up,
    rows, up, down, cots, gain, bias, act, slope, gffn, ffn_b, grad_up, work, partial, cols,
    own_s, slots_s, own_t, slots_t, part, other, landing, own_rows, grads, grid_landing, done,
    send, recv, local,
):
    net = Net(send, recv, local)
    load_up = net.keep(weights_in.at[:, pl.ds(0, 1024)], up)
    load_rows = [net.keep(rows_in.at[pl.ds(256 * b, 256)], rows.at[pl.ds(256 * b, 256)]) for b in range(4)]
    load_down = net.keep(weights_in.at[:, pl.ds(1024, 1024)], down)
    load_cots = [net.keep(cots_in.at[pl.ds(256 * b, 256)], cots.at[pl.ds(256 * b, 256)]) for b in range(4)]
    others = line_partners(net)
    net.greet([to for to, _ in others] + grid_neighbours(net) + pair_neighbours(net))
    me = net.x * 2 + net.c
    total = LineSum(net, part, other, landing)
    weights = GridSum(net, grads, grid_landing, done, shard)
    line = LineGather(net, own_rows, grad_rows)
    sum_s = SmallSum(net, own_s, slots_s, me, others)
    sum_t = SmallSum(net, own_t, slots_t, me, others)
    unit_sums[...] = jnp.zeros_like(unit_sums)
    io.wait()
    gain[...], bias[...] = my_lanes(gains, net, 1024), my_lanes(biases, net, 1024)

    load_up.wait()
    for b in range(4):
        load_rows[b].wait()
        work[...] = dot_nn(rows[256 * b : 256 * b + 256, :], up[...])

        def gelu(at, to):
            value = work[at, :]
            cdf = 0.5 * (1.0 + lax.erf(value * np.float32(0.5**0.5)))
            density = jnp.exp(-0.5 * value * value) * np.float32((2 * np.pi) ** -0.5)
            slope[to, :] = (cdf + value * density).astype(BF16)
            value = value * cdf
            act[to, :] = value
            partial[0, at, :] = lane_sums(value)
            partial[1, at, :] = lane_sums(value * value)

        block_rows(256 * b, gelu)
        for i in range(2):
            own_s[i : i + 1, 256 * b : 256 * b + 256] = row_of(partial[i])
    sum_s.start()

    load_down.wait()
    for b in range(4):
        load_cots[b].wait()
        gffn[256 * b : 256 * b + 256, :] = dot_nn(cots[256 * b : 256 * b + 256, :], down[...])

        def scale(at, to):
            grad = gffn[to, :]
            unit_sums[1] += fold8(grad)
            grad = grad * gain[...]
            partial[0, at, :] = lane_sums(grad)
            partial[1, at, :] = lane_sums(grad * act[to, :])

        block_rows(256 * b, scale)
        for i in range(2):
            own_t[i : i + 1, 256 * b : 256 * b + 256] = row_of(partial[i])
    sum_t.start()

    both = sum_s.total()
    center = both[0:1] * (1.0 / FF)
    inv_std = lax.rsqrt(both[1:2] * (1.0 / FF) - center * center + EPS)
    cols[...] = columns_of(center, inv_std)

    def normed(at):
        hat = (act[at, :] - cols[at, 0:1]) * cols[at, 1:2]
        act[at, :] = hat
        ffn_b[at, :] = (hat * gain[...] + bias[...]).astype(BF16)
        unit_sums[0] += fold8(gffn[at, :] * hat)

    by_rows(1024, normed)
    both = sum_t.total()
    cols[...] = columns_of(
        inv_std,
        both[0:1] * (1.0 / FF),
        (both[1:2] - center * both[0:1]) * inv_std * (1.0 / FF),
    )
    for q in range(4):
        base = sequence_at(net, q)

        def back(at, to):
            grad = gffn[to, :] * gain[...] - cols[to, 1:2] - act[to, :] * cols[to, 2:3]
            grad_up[to, :] = (grad * cols[to, 0:1] * slope[to, :].astype(F32)).astype(BF16)

        block_rows(base, back)
        mine = grad_up[pl.ds(base, 256), :]
        for h in range(2):
            part[pl.ds(base, 256), 1024 * h : 1024 * h + 1024] = dot_nt(
                mine, up[1024 * h : 1024 * h + 1024, :]
            ).astype(BF16)
        if q == 0:
            total.start(2)
        if q == 1:
            total.start(0)
            total.chip(2)
        if q == 2:
            total.start(1, -1)
    total.chip(1, -1, 0)

    def down_rows(dy):
        at = pl.ds(pl.multiple_of(((net.y + dy) % 4) * 512, 512), 512)
        grads[at, :] = dot_tn(cots[:, at], ffn_b[...]).astype(BF16)
        weights.start(dy)

    down_rows(2)
    total.pass_on()
    down_rows(1)
    down_rows(-1)
    down_rows(0)
    weights.pass_on(2)
    total.finish(grad_attended)
    sums[...] = jnp.zeros_like(sums)

    def norm_grad(at):
        grad = grad_attended[at, :]
        hat, inv = norm_parts(attended[at, :])
        sums[0] += fold8(grad * hat)
        sums[1] += fold8(grad)
        value = cot[at, :].astype(F32) + norm_back(grad, norm_gain[...], hat, inv)
        grad_attended[at, :] = value
        own_rows[at, :] = value.astype(BF16)

    by_rows(128, norm_grad)
    line.start()
    io.put()
    weights.pass_on(1)
    weights.pass_on(-1)
    weights.finish(2)
    weights.pass_on(0)
    weights.finish(1)
    for b in range(4):
        for h in range(2):
            cots[256 * b : 256 * b + 256, 1024 * h : 1024 * h + 1024] = dot_nt(
                ffn_b[256 * b : 256 * b + 256, :], down[1024 * h : 1024 * h + 1024, :]
            ).astype(BF16)
        if b == 1:
            weights.finish(-1)
    save_out = net.keep(cots, out_part)
    line.forward()
    weights.finish(0)
    weights.pass_on_last()
    for h in range(4):
        up[512 * h : 512 * h + 512, :] = dot_tn(
            rows[:, 512 * h : 512 * h + 512], grad_up[...]
        ).astype(BF16)
        if h == 1:
            line.share()
            weights.finish_last()
    save_grads = net.keep(up, grads_up)
    line.finish()
    weights.collect()
    save_out.wait()
    save_grads.wait()
    net.drain()


def second_call(rows, weights, cots, gain, bias, attended, cot, norm_gain):
    big, half = VMEM((1024, D), BF16), VMEM((D, 1024), BF16)
    return comm_call(
        second_kernel,
        "feed_forward",
        2,
        (rows, weights, cots, gain, bias, attended, cot, norm_gain),
        (HBM, HBM, HBM, VMEM, VMEM, VMEM, VMEM, VMEM),
        (
            shape((1024, D), BF16),
            shape((128, D), F32),
            shape((1024, D), BF16),
            shape((2, 8, D), F32),
            shape((2, 8, 1024), F32),
            shape((4, 32, 1024), BF16),
            shape((D, 1024), BF16),
        ),
        (HBM, VMEM, HBM, VMEM, VMEM, HBM, HBM),
        [
            big,
            half,
            half,
            big,
            VMEM((1, 1024), F32),
            VMEM((1, 1024), F32),
            VMEM((1024, 1024), F32),
            VMEM((1024, 1024), BF16),
            VMEM((1024, 1024), F32),
            VMEM((1024, 1024), BF16),
            VMEM((1024, 1024), BF16),
            VMEM((256, 1024), F32),
            VMEM((2, 256, 128), F32),
            VMEM((1024, 128), F32),
            VMEM((2, 1024), F32),
            VMEM((8, 2, 1024), F32),
            VMEM((2, 1024), F32),
            VMEM((8, 2, 1024), F32),
            big,
            VMEM((4, 128, D), BF16),
            VMEM((6, 64, D), BF16),
            VMEM((128, D), BF16),
            half,
            VMEM((2, 5, 6, 32, 1024), BF16),
            VMEM((2, 2, 32, 1024), BF16),
        ],
        63,
        (96, 14),
    )


def third_kernel(
    io, grad_rows, grads_up, part_out, weights1, hat, inner_gain, context, inner_inv, query, key, value,
    caps, table, rows1, attended, grad_attended, tokens, gain, sums2, unit_sums,
    layer_out, grad_input, shard, shard_up, outer_out, inner_out,
    grad_all, gctx, grad_mixed, grads_qkv, my_gain, inner_sums, partial, cols, own_t, slots_t,
    other, landing, other_out, landing_out, work, grads, grid_landing, done,
    grid_landing_up, done_up, sums, outer, line_slots, y_slots, z_slots, half_sum,
    inner, inner_y, inner_z, inner_half, send, recv, local,
):
    net = Net(send, recv, local)
    load_all = [
        net.keep(grad_rows.at[pl.ds(256 * b, 256)], grad_all.at[pl.ds(256 * b, 256)]) for b in range(4)
    ]
    others = line_partners(net)
    y_all = [(net.along_y(d), (net.y - d) % 4) for d in (1, 2, 3)]
    z_all = [(net.along_z(d), (net.z - d) % 4) for d in (1, 2, 3)]
    net.greet([to for to, _ in others + y_all + z_all] + pair_neighbours(net))
    part = grad_all
    total = LineSum(net, part, other, landing)
    total_out = LineSum(net, part_out, other_out, landing_out)
    weights = GridSum(net, grads, grid_landing, done, shard)
    weights_up = GridSum(net, grads_up, grid_landing_up, done_up, shard_up)
    sum_t = SmallSum(net, own_t, slots_t, net.x * 2 + net.c, others)
    io.wait(inner_gain)
    my_gain[...] = my_lanes(inner_gain, net, 256)
    inner_sums[...] = jnp.zeros_like(inner_sums)
    sums[...] = jnp.zeros_like(sums)

    io.wait(grads_up)
    for dy in (2, 1, -1, 0):
        weights_up.start(dy)
    io.wait(part_out)
    total_out.start(2, 1, -1, 0)
    io.wait(weights1, hat)
    for b in range(4):
        load_all[b].wait()
        at = slice(256 * b, 256 * b + 256)
        gctx[at, :] = dot_nn(grad_all[at, :], weights1[:, 768:])

        def scale(at, to):
            grad, one = gctx[to, :], hat[to, :]
            inner_sums[0] += fold8(grad * one)
            inner_sums[1] += fold8(grad)
            grad = grad * my_gain[...]
            gctx[to, :] = grad
            partial[0, at, :] = lane_sums(grad)
            partial[1, at, :] = lane_sums(grad * one)

        block_rows(256 * b, scale)
        for i in range(2):
            own_t[i : i + 1, at] = row_of(partial[i])
    sum_t.start()
    io.wait()
    total_out.chip(2, 1, -1, 0)
    for h in range(4):
        at = slice(512 * h, 512 * h + 512)
        grads[at, 768:] = dot_tn(grad_all[:, at], context[...]).astype(BF16)
    weights_up.pass_on(2)
    both = sum_t.total() * (1.0 / D)
    cols[...] = columns_of(inner_inv[...], both[0:1], both[1:2])

    def mixed_grad(at):
        grad = gctx[at, :] - cols[at, 1:2] - hat[at, :] * cols[at, 2:3]
        grad_mixed[at, :] = (grad * cols[at, 0:1]).astype(BF16)

    by_rows(1024, mixed_grad)
    for q in range(4):
        base = sequence_at(net, q)
        at = pl.ds(base, SLOTS)
        cap = caps[base // SLOTS]
        found = attend_back(query[at, :], key[at, :], value[at, :], grad_mixed[at, :], cap, table)
        for i in range(3):
            grads_qkv[at, 256 * i : 256 * i + 256] = found[i]
        mine = grads_qkv[at, :]
        for h in range(2):
            part[at, 1024 * h : 1024 * h + 1024] = dot_nt(
                mine, weights1[1024 * h : 1024 * h + 1024, :768]
            ).astype(BF16)
        if q == 0:
            total.start(2)
            weights_up.pass_on(1)
            total_out.pass_on()
        if q == 1:
            total.start(0)
            total.chip(2)
            weights_up.pass_on(-1)
            weights_up.finish(2)
        if q == 2:
            weights_up.pass_on(0)
            weights_up.finish(1)
    total.start(1, -1)
    total.chip(1, -1, 0)

    def grad_rows_of(dy):
        at = pl.ds(pl.multiple_of(((net.y + dy) % 4) * 512, 512), 512)
        grads[at, :768] = dot_tn(rows1[:, at], grads_qkv[...]).astype(BF16)
        weights.start(dy)

    grad_rows_of(2)
    grad_rows_of(1)
    grad_rows_of(-1)
    grad_rows_of(0)
    weights_up.finish(-1)
    weights_up.finish(0)
    total.pass_on()
    weights.pass_on(2)
    weights_up.pass_on_last()
    total_out.finish(work)

    def out(at):
        layer_out[at, :] = (attended[at, :] + work[at, :]).astype(BF16)

    by_rows(128, out)
    io.put(layer_out)
    for k, (lane, n) in enumerate(((0, 256), (256, 256), (512, 1024), (1536, 1024))):
        terms = inner_sums[k] if k < 2 else unit_sums[k - 2]
        inner[0:1, lane : lane + n] = jnp.sum(terms, 0, keepdims=True)
    inner_first = SmallSum(net, inner, inner_y, net.y, y_all)
    inner_first.start()
    weights.pass_on(1)
    weights.finish(2)
    weights.pass_on(-1)
    weights.finish(1)
    weights.pass_on(0)
    total.finish(work)

    def back(at):
        grad = work[at, :]
        one, inv = norm_parts(tokens[at, :].astype(F32))
        sums[0] += fold8(grad * one)
        sums[1] += fold8(grad)
        value = grad_attended[at, :] + norm_back(grad, gain[...], one, inv)
        grad_input[at, :] = value.astype(BF16)

    by_rows(128, back)
    io.put(grad_input)
    for i in range(4):
        terms = sums[i] if i < 2 else sums2[i - 2]
        outer[i : i + 1, :] = jnp.sum(terms, 0, keepdims=True)
    outer_x = SmallSum(net, outer, line_slots, net.x * 2 + net.c, others)
    outer_x.start()
    weights.finish(-1)
    weights.finish(0)
    weights_up.finish_last()
    inner_first.finish(inner_half.at[0])
    inner_last = SmallSum(net, inner_half.at[0], inner_z, net.z, z_all)
    inner_last.start()
    outer_x.finish(half_sum.at[0])
    outer_y = SmallSum(net, half_sum.at[0], y_slots, net.y, y_all)
    outer_y.start()
    weights.pass_on_last()
    inner_last.finish(inner_half.at[1])
    inner_k = {}
    for dx, dc in ((1, 0), (1, 1), (0, 1)):
        inner_k[dx, dc] = net.push(inner_half.at[1], inner_out.at[place_of(net)], net.pair(dx, dc))
    inner_out[place_of(net)] = inner_half[1]
    outer_y.finish(half_sum.at[1])
    outer_z = SmallSum(net, half_sum.at[1], z_slots, net.z, z_all)
    outer_z.start()
    weights.finish_last()
    outer_z.finish(outer_out)
    for dx, dc in ((1, 0), (1, 1), (0, 1)):
        net.arrived(inner_k[dx, dc], inner_out.at[((net.x + dx) % 2) * 2 + (net.c + dc) % 2])
    weights_up.collect()
    weights.collect()
    net.drain()


def third_call(ins):
    big, half = VMEM((1024, D), BF16), VMEM((D, 1024), BF16)
    quarter, wide = VMEM((1024, 256), BF16), VMEM((1024, 256), F32)
    return comm_call(
        third_kernel,
        "attention_back",
        3,
        ins,
        (HBM,) + (VMEM,) * 19,
        (
            shape((128, D), BF16),
            shape((128, D), BF16),
            shape((4, 32, 1024), BF16),
            shape((4, 32, 1024), BF16),
            shape((4, D), F32),
            shape((4, 1, 2560), F32),
        ),
        (VMEM, VMEM, HBM, HBM, VMEM, VMEM),
        [
            big,
            wide,
            quarter,
            VMEM((1024, 768), BF16),
            VMEM((1, 256), F32),
            VMEM((2, 8, 256), F32),
            VMEM((2, 256, 128), F32),
            VMEM((1024, 128), F32),
            VMEM((2, 1024), F32),
            VMEM((8, 2, 1024), F32),
            VMEM((4, 128, D), BF16),
            VMEM((6, 64, D), BF16),
            VMEM((4, 128, D), BF16),
            VMEM((6, 64, D), BF16),
            VMEM((128, D), F32),
            half,
            VMEM((2, 5, 6, 32, 1024), BF16),
            VMEM((2, 2, 32, 1024), BF16),
            VMEM((2, 5, 6, 32, 1024), BF16),
            VMEM((2, 2, 32, 1024), BF16),
            VMEM((2, 8, D), F32),
            VMEM((4, D), F32),
            VMEM((8, 4, D), F32),
            VMEM((4, 4, D), F32),
            VMEM((4, 4, D), F32),
            VMEM((2, 4, D), F32),
            VMEM((1, 2560), F32),
            VMEM((4, 1, 2560), F32),
            VMEM((4, 1, 2560), F32),
            VMEM((2, 1, 2560), F32),
        ],
        63,
        (175, 6),
    )


def last_kernel(
    layer_in, input_in, shard, shard_up, shard_down, outer, inner,
    layer_out, grad_input, gain1, bias1, query, key, value, inner_gain, inner_bias, proj,
    gain2, bias2, up, ffn_gain, ffn_bias, down,
):
    layer_out[...] = layer_in[...]
    grad_input[...] = input_in[...]
    for i, ref in enumerate((gain1, bias1, gain2, bias2)):
        ref[...] = outer[i : i + 1, :]
    for d in range(4):
        for i, ref in enumerate((query, key, value, proj)):
            ref[:, 256 * d : 256 * d + 256] = shard[d, :, 256 * i : 256 * i + 256].astype(F32)
        up[:, 1024 * d : 1024 * d + 1024] = shard_up[d].astype(F32)
        down[:, 1024 * d : 1024 * d + 1024] = shard_down[d].astype(F32)
        for ref, lane, n in (
            (inner_gain, 0, 256), (inner_bias, 256, 256), (ffn_gain, 512, 1024), (ffn_bias, 1536, 1024),
        ):
            ref[:, n * d : n * d + n] = inner[d, :, lane : lane + n]


def whole(dims):
    return pl.BlockSpec(dims, lambda i: (0,) * len(dims))


def last_call(*ins):
    row, small, big = shape((1, D), F32), shape((32, 1024), F32), shape((32, 4096), F32)
    rows = shape((128, D), BF16)
    unit, wide = shape((1, 1024), F32), shape((1, 4096), F32)
    outs = (
        rows, rows, row, row, small, small, small, unit, unit, small, row, row, big, wide, wide, big,
    )
    return pl.pallas_call(
        last_kernel,
        out_shape=outs,
        grid=(1,),
        in_specs=[whole(v.shape) for v in ins],
        out_specs=[whole(v.shape) for v in outs],
        compiler_params=pltpu.CompilerParams(vmem_limit_bytes=63 << 20),
        name="results",
    )(*ins)


def per_device(
    tokens, caption_len, norm1_gain, norm1_bias, w_query, w_key, w_value, inner_gain, inner_bias,
    w_proj, norm2_gain, norm2_bias, w_up, ffn_norm_gain, ffn_norm_bias, w_down, cotangent,
):
    table = jnp.asarray(tables())
    line = lambda v: v.reshape(1, -1)
    (
        rows1, weights1, rows2, weights2, cots, query, key, value, hat, context, inner_inv, caps, attended,
    ) = first_call((
        tokens, caption_len, line(norm1_gain), line(norm1_bias), w_query, w_key, w_value, w_proj.T,
        line(inner_gain), line(inner_bias), line(norm2_gain), line(norm2_bias), w_up, w_down.T,
        cotangent, table,
    ))
    out_part, grad_attended, grad_rows, sums2, unit_sums, shard_down, grads_up = second_call(
        rows2, weights2, cots, line(ffn_norm_gain), line(ffn_norm_bias), attended, cotangent,
        line(norm2_gain),
    )
    layer_out, grad_input, shard, shard_up, outer, inner = third_call((
        grad_rows, grads_up, out_part, weights1, hat, line(inner_gain), context, inner_inv, query, key,
        value, caps, table, rows1, attended, grad_attended, tokens, line(norm1_gain), sums2, unit_sums,
    ))
    (
        layer_out, grad_input, gain1, bias1, query, key, value, gain_i, bias_i, proj, gain2, bias2,
        up, gain_f, bias_f, down,
    ) = last_call(layer_out, grad_input, shard, shard_up, shard_down, outer, inner)
    flat = lambda v: v.reshape(-1)
    return (
        layer_out, grad_input, flat(gain1), flat(bias1), query, key, value, flat(gain_i),
        flat(bias_i), proj.T, flat(gain2), flat(bias2), up, flat(gain_f), flat(bias_f), down.T,
    )


def solution(mesh):
    rows = P(("seq", "ffn"), None)
    by_rows_, by_columns, half = P("seq", "ffn"), P("ffn", "seq"), P("ffn")
    return jax.shard_map(
        per_device,
        mesh=mesh,
        in_specs=(
            rows, P("seq"), P(), P(), by_rows_, by_rows_, by_rows_, half, half, by_columns,
            P(), P(), by_rows_, half, half, by_columns, rows,
        ),
        out_specs=(
            rows, rows, P(), P(), by_rows_, by_rows_, by_rows_, half, half, by_columns,
            P(), P(), by_rows_, half, half, by_columns,
        ),
        check_vma=False,
    )
```

```python
import functools

import jax
import jax.numpy as jnp
import numpy as np
from jax import lax
from jax.experimental import pallas as pl
from jax.experimental.pallas import tpu as pltpu
from jax.sharding import PartitionSpec as P

D = 2048
HEAD_DIM = 64
FF = 8192
SLOTS = 256
IMAGE = 64
EPS = 1e-05
F32 = jnp.float32
BF16 = jnp.bfloat16
MESH = pl.DeviceIdType.MESH
VMEM = pltpu.VMEM
HBM = pltpu.HBM


def device_at(y, x, z, c):
    return (((y * 2 + x % 2) * 4 + z) * 2 + c, x // 2)


def line_slot(x, c):
    return ((x % 2) * 2 + c) * 2 + x // 2


class Net:
    def __init__(self, send, recv, local):
        seq, ffn = lax.axis_index("seq"), lax.axis_index("ffn")
        self.y, self.z, self.c = seq // 16, (seq // 2) % 4, seq % 2
        self.x = ffn * 2 + (seq // 8) % 2
        self.send, self.recv, self.local = send, recv, local
        self.used, self.used_local = 0, 0
        self.out = []

    def along_x(self, dx, dc=0):
        return device_at(self.y, (self.x + dx) % 4, self.z, (self.c + dc) % 2)

    def along_y(self, dy):
        return device_at((self.y + dy) % 4, self.x, self.z, self.c)

    def along_z(self, dz):
        return device_at(self.y, self.x, (self.z + dz) % 4, self.c)

    def pair(self, dx, dc):
        x = (self.x // 2) * 2 + (self.x + dx) % 2
        return device_at(self.y, x, self.z, (self.c + dc) % 2)

    def greet(self, partners):
        self.barrier, self.partners = pltpu.get_barrier_semaphore(), len(partners)
        for partner in partners:
            pl.semaphore_signal(self.barrier, inc=1, device_id=partner, device_id_type=MESH)

    def met(self):
        pl.semaphore_wait(self.barrier, self.partners)

    def push(self, src, dst, device):
        k = self.used
        self.used += 1
        copy = pltpu.make_async_remote_copy(
            src_ref=src,
            dst_ref=dst,
            send_sem=self.send.at[k],
            recv_sem=self.recv.at[k],
            device_id=device,
            device_id_type=MESH,
        )
        copy.start()
        self.out.append(copy)
        return k

    def arrived(self, k, landed):
        pltpu.make_async_remote_copy(
            src_ref=landed,
            dst_ref=landed,
            send_sem=self.send.at[k],
            recv_sem=self.recv.at[k],
            device_id=self.along_x(0, 1),
            device_id_type=MESH,
        ).wait_recv()

    def keep(self, src, dst):
        copy = pltpu.make_async_copy(src, dst, self.local.at[self.used_local])
        self.used_local += 1
        copy.start()
        return copy

    def drain(self):
        for copy in self.out:
            copy.wait_send()
        assert (self.used, self.used_local) == (self.send.shape[0], self.local.shape[0])


def add_into(dst, *terms):
    def step(i, carry):
        rows = pl.ds(pl.multiple_of(i * 16, 16), 16)
        total = terms[0][rows, :].astype(F32)
        for term in terms[1:]:
            total = total + term[rows, :].astype(F32)
        dst[rows, :] = total.astype(dst.dtype)
        return carry

    lax.fori_loop(0, dst.shape[0] // 16, step, 0)


class LineGather:
    def __init__(self, net, own, full, off=0, n=128):
        self.net, self.full, self.off, self.n = net, full, off, n
        self.own = own.at[pl.ds(off, n)]
        self.own_half = [own.at[pl.ds(off + n // 2 * h, n // 2)] for h in range(2)]

    def block(self, dx, dc=0, half=None):
        net, n = self.net, self.n
        base = line_slot((net.x + dx) % 4, (net.c + dc) % 2) * 128 + self.off
        if half is None:
            return self.full.at[pl.ds(pl.multiple_of(base, n), n)]
        return self.full.at[pl.ds(pl.multiple_of(base + n // 2 * half, n // 2), n // 2)]

    def start(self):
        net = self.net
        first = len(net.out)
        self.a, self.b = {}, {}
        for h in (0, 1):
            self.a[h] = net.push(self.own_half[h], self.block(0, 0, h), net.along_x(1))
            self.b[1 - h] = net.push(self.own_half[1 - h], self.block(0, 0, 1 - h), net.along_x(-1))
        self.s0 = net.push(self.own, self.block(0), net.along_x(0, 1))
        self.kept = net.keep(self.own, self.block(0))
        self.sends = net.out[first:]

    def sent(self):
        for copy in self.sends:
            copy.wait_send()
        self.net.out = [copy for copy in self.net.out if all(copy is not s for s in self.sends)]

    def forward(self):
        net = self.net
        net.arrived(self.a[0], self.block(-1, 0, 0))
        self.fa = net.push(self.block(-1, 0, 0), self.block(-1, 0, 0), net.along_x(1))
        net.arrived(self.b[1], self.block(1, 0, 1))
        self.fb = net.push(self.block(1, 0, 1), self.block(1, 0, 1), net.along_x(-1))
        net.arrived(self.a[1], self.block(-1, 0, 1))
        self.sa = net.push(self.block(-1), self.block(-1), net.along_x(0, 1))
        net.arrived(self.b[0], self.block(1, 0, 0))
        self.sb = net.push(self.block(1), self.block(1), net.along_x(0, 1))

    def share(self):
        net = self.net
        net.arrived(self.fa, self.block(2, 0, 0))
        self.sfa = net.push(self.block(2, 0, 0), self.block(2, 0, 0), net.along_x(0, 1))
        net.arrived(self.fb, self.block(2, 0, 1))
        self.sfb = net.push(self.block(2, 0, 1), self.block(2, 0, 1), net.along_x(0, 1))

    def finish(self):
        net = self.net
        net.arrived(self.s0, self.block(0, 1))
        net.arrived(self.sa, self.block(-1, 1))
        net.arrived(self.sb, self.block(1, 1))
        net.arrived(self.sfa, self.block(2, 1, 0))
        net.arrived(self.sfb, self.block(2, 1, 1))
        self.kept.wait()


class RingSum:
    def __init__(self, net, mine, landing, ahead, behind):
        self.net, self.mine, self.landing = net, mine, landing
        self.ahead, self.behind = ahead, behind

    def start_far(self):
        net, land = self.net, self.landing
        self.f0 = net.push(self.mine(2, 0), land.at[0], self.ahead)
        self.f1 = net.push(self.mine(2, 1), land.at[1], self.behind)

    def start_near(self, d):
        net, land = self.net, self.landing
        if d == 1:
            self.r1 = net.push(self.mine(1, 1), land.at[3], self.ahead)
        else:
            self.r0 = net.push(self.mine(-1, 0), land.at[4], self.behind)

    def pass_on(self):
        net, land = self.net, self.landing
        net.arrived(self.f0, land.at[0])
        add_into(land.at[0], land.at[0], self.mine(1, 0))
        self.s0 = net.push(land.at[0], land.at[2], self.ahead)
        net.arrived(self.f1, land.at[1])
        add_into(land.at[1], land.at[1], self.mine(-1, 1))
        self.s1 = net.push(land.at[1], land.at[5], self.behind)

    def finish(self, out=None):
        net, land = self.net, self.landing
        net.arrived(self.s0, land.at[2])
        net.arrived(self.r0, land.at[4])
        add_into(land.at[2] if out is None else out(0), self.mine(0, 0), land.at[2], land.at[4])
        net.arrived(self.r1, land.at[3])
        net.arrived(self.s1, land.at[5])
        add_into(land.at[3] if out is None else out(1), self.mine(0, 1), land.at[3], land.at[5])


class LineSum:
    def __init__(self, net, part, other, landing, off=0, n=128):
        self.net, self.part, self.other, self.off, self.n = net, part, other, off, n
        self.ring = RingSum(net, self.mine, landing, net.along_x(1), net.along_x(-1))
        self.k = {}

    def block(self, dx, dc):
        net = self.net
        base = line_slot((net.x + dx) % 4, (net.c + dc) % 2) * 128 + self.off
        return self.part.at[pl.ds(pl.multiple_of(base, self.n), self.n)]

    def mine(self, d, half):
        return self.other.at[d % 4, pl.ds(self.n // 2 * half, self.n // 2)]

    def start(self, *steps):
        net = self.net
        for d in steps:
            self.k[d] = net.push(self.block(d, 1), self.other.at[d % 4], net.along_x(0, 1))

    def chip(self, *steps):
        for d in steps:
            self.net.arrived(self.k[d], self.other.at[d % 4])
            add_into(self.other.at[d % 4], self.other.at[d % 4], self.block(d, 0))
            if d == 2:
                self.ring.start_far()
            elif d:
                self.ring.start_near(d)

    def pass_on(self):
        self.ring.pass_on()

    def finish(self, out):
        half = self.n // 2
        self.ring.finish(lambda h: out.at[pl.ds(self.off + half * h, half)])


def line_sums(net, part, other, landing):
    return [LineSum(net, part, other.at[k], landing.at[k], 64 * k, 64) for k in range(2)]


def line_gathers(net, own, full):
    return [LineGather(net, own, full, 64 * k, 64) for k in range(2)]


def shard_rows(ref, y, x_lo, z, c=None):
    if c is None:
        return ref.at[pl.ds(pl.multiple_of(((y * 2 + x_lo) * 4 + z) * 64, 64), 64)]
    return ref.at[pl.ds(pl.multiple_of((((y * 2 + x_lo) * 4 + z) * 2 + c) * 32, 32), 32)]


class GridGather:
    def __init__(self, net, pieces, full):
        self.net, self.pieces, self.full = net, pieces, full

    def spot(self, dx, dc):
        net = self.net
        return shard_rows(self.full, net.y, (net.x + dx) % 2, net.z, (net.c + dc) % 2)

    def exchange(self):
        net = self.net
        self.k = {}
        for dx, dc in ((1, 0), (1, 1), (0, 1)):
            to = ((net.x + dx) % 2) * 2 + (net.c + dc) % 2
            self.k[dx, dc] = net.push(self.pieces.at[to], self.spot(0, 0), net.pair(dx, dc))
        me = (net.x % 2) * 2 + net.c
        self.kept = net.keep(self.pieces.at[me], self.spot(0, 0))

    def slab(self, t, dp, dq, half=None):
        net = self.net
        dy, dz = (dq, dp) if t == 0 else (dp, dq)
        return shard_rows(self.full, (net.y + dy) % 4, t, (net.z + dz) % 4, half)

    def to_p(self, t, d):
        return self.net.along_z(d) if t == 0 else self.net.along_y(d)

    def to_q(self, t, d):
        return self.net.along_y(d) if t == 0 else self.net.along_z(d)

    def same(self, ref, device):
        return self.net.push(ref, ref, device)

    def second(self, t, dp):
        self.q[t, dp] = (
            self.same(self.slab(t, dp, 0), self.to_q(t, 1)),
            self.same(self.slab(t, dp, 0), self.to_q(t, -1)),
        )

    def start(self):
        for dx, dc in ((0, 1), (1, 0), (1, 1)):
            self.net.arrived(self.k[dx, dc], self.spot(dx, dc))
        self.kept.wait()
        self.p, self.q, self.f = {}, {}, {}
        for t in (0, 1):
            self.p[t] = (
                self.same(self.slab(t, 0, 0), self.to_p(t, 1)),
                self.same(self.slab(t, 0, 0), self.to_p(t, -1)),
            )
        for t in (0, 1):
            self.second(t, 0)

    def near(self):
        net = self.net
        for t in (0, 1):
            a, b = self.p[t]
            net.arrived(a, self.slab(t, -1, 0))
            fa = self.same(self.slab(t, -1, 0, 0), self.to_p(t, 1))
            net.arrived(b, self.slab(t, 1, 0))
            fb = self.same(self.slab(t, 1, 0, 1), self.to_p(t, -1))
            self.f[t] = (fa, fb)
        for t in (0, 1):
            self.second(t, -1)
            self.second(t, 1)

    def far(self):
        for t in (0, 1):
            self.net.arrived(self.f[t][0], self.slab(t, 2, 0, 0))
            self.net.arrived(self.f[t][1], self.slab(t, 2, 0, 1))
            self.second(t, 2)

    def pass_on(self, dp):
        net = self.net
        for t in (0, 1):
            a, b = self.q[t, dp]
            net.arrived(a, self.slab(t, dp, -1))
            fa = self.same(self.slab(t, dp, -1, 0), self.to_q(t, 1))
            net.arrived(b, self.slab(t, dp, 1))
            fb = self.same(self.slab(t, dp, 1, 1), self.to_q(t, -1))
            self.f[t, dp] = (fa, fb)

    def finish(self):
        for dp in (0, -1, 1, 2):
            for t in (0, 1):
                self.net.arrived(self.f[t, dp][0], self.slab(t, dp, 2, 0))
                self.net.arrived(self.f[t, dp][1], self.slab(t, dp, 2, 1))


class GridSum:
    def __init__(self, net, part, landing, done, out):
        self.net, self.part, self.landing, self.done, self.out = net, part, landing, done, out
        self.rings = {}
        for t in (0, 1):
            for dp in (2, 1, -1, 0):
                self.rings[t, dp] = RingSum(
                    net,
                    functools.partial(self.term, t, dp),
                    landing.at[t, dp % 4],
                    self.to_q(t, 1),
                    self.to_q(t, -1),
                )
            self.rings[t] = RingSum(
                net,
                functools.partial(self.column, t),
                landing.at[t, 4],
                self.to_p(t, 1),
                self.to_p(t, -1),
            )

    def to_p(self, t, d):
        return self.net.along_z(d) if t == 0 else self.net.along_y(d)

    def to_q(self, t, d):
        return self.net.along_y(d) if t == 0 else self.net.along_z(d)

    def term(self, t, dp, dq, half):
        net = self.net
        dy, dz = (dq, dp) if t == 0 else (dp, dq)
        return shard_rows(self.part, (net.y + dy) % 4, t, (net.z + dz) % 4, half)

    def column(self, t, dp, half):
        return self.landing.at[t, dp % 4, 2 + half]

    def start(self, dy):
        for dp in (2, 1, -1, 0):
            if dy == 2:
                self.rings[0, dp].start_far()
            elif dy:
                self.rings[0, dp].start_near(dy)
        self.rings[1, dy].start_far()
        self.rings[1, dy].start_near(1)
        self.rings[1, dy].start_near(-1)

    def pass_on(self, dp):
        for t in (0, 1):
            self.rings[t, dp].pass_on()

    def finish(self, dp):
        for t in (0, 1):
            self.rings[t, dp].finish()
            if dp == 2:
                self.rings[t].start_far()
            elif dp:
                self.rings[t].start_near(dp)

    def pass_on_last(self):
        for t in (0, 1):
            self.rings[t].pass_on()

    def finish_last(self):
        net = self.net
        for t in (0, 1):
            self.rings[t].finish(lambda half: self.done.at[t, half])
        me = (net.x % 2) * 2 + net.c
        self.k = {}
        for dx, dc in ((1, 0), (1, 1), (0, 1)):
            src = self.done.at[(net.x + dx) % 2, (net.c + dc) % 2]
            self.k[dx, dc] = net.push(src, self.out.at[me], net.pair(dx, dc))
        self.kept = net.keep(self.done.at[net.x % 2, net.c], self.out.at[me])

    def collect(self):
        net = self.net
        for dx, dc in ((1, 0), (1, 1), (0, 1)):
            at = ((net.x + dx) % 2) * 2 + (net.c + dc) % 2
            net.arrived(self.k[dx, dc], self.out.at[at])
        self.kept.wait()


class SmallSum:
    def __init__(self, net, own, slots, me, partners):
        self.net, self.own, self.slots, self.me, self.partners = net, own, slots, me, partners

    def start(self):
        net = self.net
        self.k = [(net.push(self.own, self.slots.at[self.me], to), at) for to, at in self.partners]
        self.slots[self.me] = self.own[...]

    def total(self):
        for k, at in self.k:
            self.net.arrived(k, self.slots.at[at])
        total = self.slots[0]
        for i in range(1, self.slots.shape[0]):
            total = total + self.slots[i]
        return total

    def finish(self, out):
        out[...] = self.total()


def line_partners(net):
    return [
        (net.along_x(dx, dc), ((net.x - dx) % 4) * 2 + (net.c + dc) % 2)
        for dx in range(4)
        for dc in range(2)
        if dx or dc
    ]


def grid_partners(net):
    return [
        (
            device_at((net.y + dy) % 4, net.x, (net.z + dz) % 4, net.c),
            ((net.y - dy) % 4) * 4 + (net.z - dz) % 4,
        )
        for dy in range(4)
        for dz in range(4)
        if dy or dz
    ]


def sem_scratch(pushes, keeps):
    return [
        pltpu.SemaphoreType.DMA((pushes,)),
        pltpu.SemaphoreType.DMA((pushes,)),
        pltpu.SemaphoreType.DMA((keeps,)),
    ]


def spec(space):
    return pl.BlockSpec(memory_space=space)


def shape(dims, dtype):
    return jax.ShapeDtypeStruct(dims, dtype)


class Staged:
    def __init__(self, loads, stores):
        self.loads, self.stores, self.started = loads, stores, []
        for copy, _ in loads:
            copy.start()

    def wait(self, *refs):
        for copy, ref in list(self.loads):
            if not refs or any(ref is r for r in refs):
                copy.wait()
                self.loads = [pair for pair in self.loads if pair[1] is not ref]

    def put(self, *refs):
        for copy, ref in list(self.stores):
            if not refs or any(ref is r for r in refs):
                copy.start()
                self.started.append(copy)
                self.stores = [pair for pair in self.stores if pair[1] is not ref]

    def finish(self):
        self.wait()
        self.put()
        for copy in self.started:
            copy.wait()


def comm_call(body, name, collective_id, ins, in_spaces, outs, out_spaces, scratch, mib, sems):
    n_in, n_out = len(ins), len(outs)
    buffers = [space(v.shape, v.dtype) for v, space in zip(ins, in_spaces) if space is not HBM]
    buffers += [space(v.shape, v.dtype) for v, space in zip(outs, out_spaces) if space is not HBM]
    n = len(buffers)

    def kernel(*refs):
        sem = refs[-1]
        rest = list(refs[n_in + n_out : n_in + n_out + n])
        loads, stores, args = [], [], []
        for i, (ref, space) in enumerate(zip(refs, (*in_spaces, *out_spaces))):
            if space is HBM:
                args.append(ref)
                continue
            buffer = rest.pop(0)
            args.append(buffer)
            at = sem.at[len(loads) + len(stores)]
            if i < n_in:
                loads.append((pltpu.make_async_copy(ref, buffer, at), buffer))
            else:
                stores.append((pltpu.make_async_copy(buffer, ref, at), buffer))
        io = Staged(loads, stores)
        body(io, *args, *refs[n_in + n_out + n : -1])
        io.finish()

    return pl.pallas_call(
        kernel,
        out_shape=outs,
        in_specs=[spec(HBM)] * n_in,
        out_specs=[spec(HBM)] * n_out,
        scratch_shapes=buffers + scratch + sem_scratch(*sems) + [pltpu.SemaphoreType.DMA((n,))],
        compiler_params=pltpu.CompilerParams(
            collective_id=collective_id, has_side_effects=True, vmem_limit_bytes=mib << 20
        ),
        name=name,
    )(*ins)


def x_neighbours(net):
    return [net.along_x(1), net.along_x(-1), net.along_x(0, 1)]


def grid_neighbours(net):
    return [net.along_y(1), net.along_y(-1), net.along_z(1), net.along_z(-1)]


def pair_neighbours(net):
    return [net.pair(1, 0), net.pair(1, 1), net.pair(0, 1)]


def norm_parts(values):
    center = jnp.mean(values, -1, keepdims=True)
    spread = jnp.mean(values * values, -1, keepdims=True) - center * center
    inv_std = lax.rsqrt(spread + EPS)
    return (values - center) * inv_std, inv_std


def by_rows(rows, step, chunk=16, off=0):
    def body(i, carry):
        step(pl.ds(pl.multiple_of(off + i * chunk, chunk), chunk))
        return carry

    lax.fori_loop(0, rows // chunk, body, 0)


def norm_back(grad, gain, hat, inv_std):
    scaled = grad * gain
    return inv_std * (
        scaled
        - jnp.mean(scaled, -1, keepdims=True)
        - hat * jnp.mean(scaled * hat, -1, keepdims=True)
    )


def fold8(values):
    return values[:8] + values[8:]


def block_rows(base, step):
    def body(i, carry):
        step(
            pl.ds(pl.multiple_of(i * 16, 16), 16),
            pl.ds(pl.multiple_of(base + i * 16, 16), 16),
        )
        return carry

    lax.fori_loop(0, 16, body, 0)


def lane_sums(values):
    total = values[:, :128]
    for k in range(1, values.shape[1] // 128):
        total = total + values[:, 128 * k : 128 * k + 128]
    return total


def row_of(partial):
    return jnp.sum(partial.T, 0, keepdims=True)


def spread(row):
    return jnp.broadcast_to(row, (128, row.shape[1])).T


def wide(values, lanes):
    return jnp.concatenate([values] * (lanes // 128), 1)


def xpos_tables(direction):
    half = HEAD_DIM // 2
    pair = np.arange(half, dtype=np.float32)
    frequency = np.power(np.float32(10000.0), -pair / half).astype(np.float32)
    zeta = ((pair / half + 0.4) / 1.4).astype(np.float32)
    position = np.arange(SLOTS, dtype=np.float32)[:, None]
    angle = (position * frequency).astype(np.float32).astype(np.float64)
    decay = np.exp(direction * position / 512.0 * np.log(zeta.astype(np.float64)))
    cosine, sine = np.cos(angle) * decay, np.sin(angle) * decay
    cosine = np.concatenate([cosine] * 2, -1)
    sine = np.concatenate([-sine, sine], -1)
    return np.tile(cosine, (1, 4)).astype(np.float32), np.tile(sine, (1, 4)).astype(np.float32)


def tables():
    return np.stack([*xpos_tables(1.0), *xpos_tables(-1.0)])


def swapped(values):
    lane = lax.broadcasted_iota(jnp.int32, values.shape, 1)
    return jnp.where(lane % 64 < 32, pltpu.roll(values, 224, 1), pltpu.roll(values, 32, 1))


def dot_nn(a, b):
    return lax.dot_general(a, b, (((1,), (0,)), ((), ())), preferred_element_type=F32)


def dot_nt(a, b):
    return lax.dot_general(a, b, (((1,), (1,)), ((), ())), preferred_element_type=F32)


def dot_tn(a, b):
    return lax.dot_general(a, b, (((0,), (0,)), ((), ())), preferred_element_type=F32)


def head_of(values, head):
    lane = lax.broadcasted_iota(jnp.int32, values.shape, 1)
    return jnp.where(lane // 64 == head, values, jnp.zeros_like(values))


def head_probs(query, key, head, allowed):
    scores = dot_nt(head_of(query, head), key) * HEAD_DIM**-0.5
    scores = jnp.where(allowed, scores, -1e30)
    exps = jnp.exp(scores - jnp.max(scores, -1, keepdims=True))
    return exps / jnp.sum(exps, -1, keepdims=True)


def allowed_slots(cap):
    query = lax.broadcasted_iota(jnp.int32, (SLOTS, SLOTS), 0)
    key = lax.broadcasted_iota(jnp.int32, (SLOTS, SLOTS), 1)
    return (key <= query) & (key < IMAGE + cap[0:1, 0:1])


def attend(rows, weights, cap, table, at, query_out, key_out, value_out, mixed_out):
    qkv = dot_nn(rows, weights[:, :768])
    query, key, value = qkv[:, :256], qkv[:, 256:512], qkv[:, 512:].astype(BF16)
    query = (query * table[0] + swapped(query) * table[1]).astype(BF16)
    key = (key * table[2] + swapped(key) * table[3]).astype(BF16)
    query_out[at, :], key_out[at, :], value_out[at, :] = query, key, value
    allowed = allowed_slots(cap)
    mixed = jnp.zeros((SLOTS, 256), F32)
    for head in range(4):
        probs = head_probs(query, key, head, allowed).astype(BF16)
        mixed = mixed + dot_nn(probs, head_of(value, head))
    mixed_out[at, :] = mixed


def attend_back(query, key, value, grad, cap, table):
    allowed = allowed_slots(cap)
    grad_query = jnp.zeros((SLOTS, 256), F32)
    grad_key = jnp.zeros((SLOTS, 256), F32)
    grad_value = jnp.zeros((SLOTS, 256), F32)
    for head in range(4):
        probs = head_probs(query, key, head, allowed)
        grad_head = head_of(grad, head)
        grad_probs = dot_nt(grad_head, value)
        grad_value = grad_value + dot_tn(probs.astype(BF16), grad_head)
        delta = jnp.sum(probs * grad_probs, -1, keepdims=True)
        grad_scores = (probs * (grad_probs - delta)).astype(BF16)
        grad_query = grad_query + dot_nn(grad_scores, head_of(key, head))
        grad_key = grad_key + dot_tn(grad_scores, head_of(query, head))
    grad_query = grad_query * HEAD_DIM**-0.5
    grad_key = grad_key * HEAD_DIM**-0.5
    return (
        (grad_query * table[0] + swapped(grad_query * table[1])).astype(BF16),
        (grad_key * table[2] + swapped(grad_key * table[3])).astype(BF16),
        grad_value.astype(BF16),
    )


def place_of(net):
    return (net.x % 2) * 2 + net.c


def my_lanes(ref, net, n):
    return ref[:, pl.ds(pl.multiple_of(place_of(net) * n, n), n)]


def sequence_at(net, q):
    seq_of = ((net.x + q // 2) % 2) * 2 + (net.c + 1 + q) % 2
    return pl.multiple_of(seq_of * SLOTS, SLOTS)


def split_shard(shard, pieces, lane):
    n = shard.shape[1] // 4
    for d in range(4):
        pieces[d, :, lane : lane + n] = shard[:, n * d : n * d + n].astype(BF16)


def first_kernel(
    io, tokens, cap, gain, bias, w_query, w_key, w_value, w_proj, inner_gain, inner_bias,
    gain2, bias2, w_up, w_down, cot, table,
    rows1_out, weights1_out, rows2, weights2, cots, query, key, value, hat, context, inner_inv,
    caps, attended,
    rows, rows1, weights1, pieces1, pieces2, caps_in, cap_slots, mixed, partial, cols,
    own_s, slots_s, part, other, landing, send, recv, local,
):
    net = Net(send, recv, local)
    others = line_partners(net)
    net.greet([to for to, _ in others] + grid_neighbours(net) + pair_neighbours(net))
    for i, shard in enumerate((w_query, w_key, w_value, w_proj)):
        io.wait(shard)
        split_shard(shard, pieces1, 256 * i)
    io.wait(tokens, cap, gain, bias)

    def norm(at):
        one, _ = norm_parts(tokens[at, :].astype(F32))
        rows[at, :] = (one * gain[...] + bias[...]).astype(BF16)

    by_rows(128, norm)
    caps_in[...] = jnp.full((8, 128), cap[0], jnp.int32)
    gather1 = GridGather(net, pieces1, weights1)
    gather2 = GridGather(net, pieces2, weights2)
    line1 = LineGather(net, rows, rows1)
    line_cot = LineGather(net, cot, cots)
    total = line_sums(net, part, other, landing)
    line2 = line_gathers(net, rows, rows2)
    sum_s = SmallSum(net, own_s, slots_s, net.x * 2 + net.c, others)

    net.met()
    gather1.exchange()
    line1.start()
    cap_k = {}
    for dx, dc in ((1, 0), (1, 1), (0, 1)):
        cap_k[dx, dc] = net.push(caps_in, cap_slots.at[place_of(net)], net.pair(dx, dc))
    cap_slots[place_of(net)] = caps_in[...]
    gather1.start()
    for i, shard in enumerate((w_up, w_down)):
        io.wait(shard)
        split_shard(shard, pieces2, 1024 * i)
    io.wait()
    gather1.near()
    gather1.pass_on(0)
    gather1.far()
    line1.forward()
    gather2.exchange()
    line_cot.start()
    gather1.pass_on(-1)
    gather1.pass_on(1)
    line1.share()
    gather1.pass_on(2)
    for dx, dc in ((1, 0), (1, 1), (0, 1)):
        at = ((net.x + dx) % 2) * 2 + (net.c + dc) % 2
        net.arrived(cap_k[dx, dc], cap_slots.at[at])
    caps[...] = cap_slots[...]
    line1.finish()
    gather1.finish()
    gather2.start()
    io.put(caps)
    save = [net.keep(rows1, rows1_out), net.keep(weights1, weights1_out)]

    for b in range(4):
        at = slice(256 * b, 256 * b + 256)
        attend(rows1[at, :], weights1, caps.at[b], table, at, query, key, value, mixed)
        both = mixed[at, :]
        partial[0] = lane_sums(both)
        partial[1] = lane_sums(both * both)
        for i in range(2):
            own_s[i : i + 1, at] = row_of(partial[i])
        if b == 2:
            line_cot.forward()
    sum_s.start()
    gather2.near()
    gather2.pass_on(0)
    both = sum_s.total()
    center = both[0:1] * (1.0 / D)
    inv_std = lax.rsqrt(both[1:2] * (1.0 / D) - center * center + EPS)
    inner_inv[...] = inv_std
    cols[0] = spread(center)
    cols[1] = spread(inv_std)
    my_gain, my_bias = my_lanes(inner_gain, net, 256), my_lanes(inner_bias, net, 256)

    def inner(at):
        one = (mixed[at, :] - wide(cols[0, at, :], 256)) * wide(cols[1, at, :], 256)
        hat[at, :] = one
        context[at, :] = (one * my_gain + my_bias).astype(BF16)

    by_rows(1024, inner, 64)
    io.put(query, key, value, hat, context, inner_inv)
    for q in range(4):
        at = pl.ds(sequence_at(net, q), SLOTS)
        mine = context[at, :]
        for h in range(2):
            part[at, 1024 * h : 1024 * h + 1024] = dot_nt(
                mine, weights1[1024 * h : 1024 * h + 1024, 768:]
            ).astype(BF16)
        for t in total:
            if q == 0:
                t.start(2)
            if q == 1:
                t.start(0)
                t.chip(2)
            if q == 2:
                t.start(1, -1)
    for t in total:
        t.chip(1, -1, 0)
    line_cot.share()
    gather2.far()
    line1.sent()

    def norm2(at):
        values = tokens[at, :].astype(F32) + attended[at, :]
        attended[at, :] = values
        one, _ = norm_parts(values)
        rows[at, :] = (one * gain2[...] + bias2[...]).astype(BF16)

    for t in total:
        t.pass_on()
    gather2.pass_on(-1)
    gather2.pass_on(1)
    for k in range(2):
        total[k].finish(attended)
        by_rows(64, norm2, 16, 64 * k)
        line2[k].start()
    io.put(attended)
    gather2.pass_on(2)
    line2[0].forward()
    line_cot.finish()
    line2[1].forward()
    line2[0].share()
    gather2.finish()
    line2[1].share()
    for line in line2:
        line.finish()
    for copy in save:
        copy.wait()
    net.drain()


def first_call(ins):
    return comm_call(
        first_kernel,
        "attention",
        1,
        ins,
        (VMEM, pltpu.SMEM) + (VMEM,) * 12 + (HBM, VMEM),
        (
            shape((1024, D), BF16),
            shape((D, 1024), BF16),
            shape((1024, D), BF16),
            shape((D, D), BF16),
            shape((1024, D), BF16),
            shape((1024, 256), BF16),
            shape((1024, 256), BF16),
            shape((1024, 256), BF16),
            shape((1024, 256), F32),
            shape((1024, 256), BF16),
            shape((1, 1024), F32),
            shape((4, 8, 128), jnp.int32),
            shape((128, D), F32),
        ),
        (HBM,) * 5 + (VMEM,) * 8,
        [
            VMEM((128, D), BF16),
            VMEM((1024, D), BF16),
            VMEM((D, 1024), BF16),
            VMEM((4, 32, 1024), BF16),
            VMEM((4, 32, 2048), BF16),
            VMEM((8, 128), jnp.int32),
            VMEM((4, 8, 128), jnp.int32),
            VMEM((1024, 256), F32),
            VMEM((2, 256, 128), F32),
            VMEM((2, 1024, 128), F32),
            VMEM((2, 1024), F32),
            VMEM((8, 2, 1024), F32),
            VMEM((1024, D), BF16),
            VMEM((2, 4, 64, D), BF16),
            VMEM((2, 6, 32, D), BF16),
        ],
        63,
        (160, 8),
    )


def second_kernel(
    io, rows_in, weights_in, cots_in, gains, biases, attended, cot, norm_gain,
    out_part, grad_attended, grad_rows, sums, unit_sums, shard, grads_up,
    rows, up, down, cots, gain, bias, act, slope, gffn, ffn_b, grad_up, work, partial, cols,
    own_s, slots_s, own_t, slots_t, part, other, landing, own_rows, grads, grid_landing, done,
    send, recv, local,
):
    net = Net(send, recv, local)
    others = line_partners(net)
    net.greet([to for to, _ in others] + grid_neighbours(net) + pair_neighbours(net))
    load_up = net.keep(weights_in.at[:, pl.ds(0, 1024)], up)
    load_rows = [net.keep(rows_in.at[pl.ds(256 * b, 256)], rows.at[pl.ds(256 * b, 256)]) for b in range(4)]
    load_down = net.keep(weights_in.at[:, pl.ds(1024, 1024)], down)
    load_cots = [net.keep(cots_in.at[pl.ds(256 * b, 256)], cots.at[pl.ds(256 * b, 256)]) for b in range(4)]
    me = net.x * 2 + net.c
    total = line_sums(net, part, other, landing)
    weights = GridSum(net, grads, grid_landing, done, shard)
    lines = line_gathers(net, own_rows, grad_rows)
    sum_s = SmallSum(net, own_s, slots_s, me, others)
    sum_t = SmallSum(net, own_t, slots_t, me, others)
    unit_sums[...] = jnp.zeros_like(unit_sums)
    io.wait(gains, biases)
    gain[...], bias[...] = my_lanes(gains, net, 1024), my_lanes(biases, net, 1024)

    load_up.wait()
    for b in range(4):
        load_rows[b].wait()
        work[...] = dot_nn(rows[256 * b : 256 * b + 256, :], up[...])

        def gelu(at, to):
            value = work[at, :]
            cdf = 0.5 * (1.0 + lax.erf(value * np.float32(0.5**0.5)))
            density = jnp.exp(-0.5 * value * value) * np.float32((2 * np.pi) ** -0.5)
            slope[to, :] = (cdf + value * density).astype(BF16)
            value = value * cdf
            act[to, :] = value
            partial[0, at, :] = lane_sums(value)
            partial[1, at, :] = lane_sums(value * value)

        block_rows(256 * b, gelu)
        for i in range(2):
            own_s[i : i + 1, 256 * b : 256 * b + 256] = row_of(partial[i])
    net.met()
    sum_s.start()

    load_down.wait()
    for b in range(4):
        load_cots[b].wait()
        gffn[256 * b : 256 * b + 256, :] = dot_nn(cots[256 * b : 256 * b + 256, :], down[...])

        def scale(at, to):
            grad = gffn[to, :]
            unit_sums[1] += fold8(grad)
            grad = grad * gain[...]
            partial[0, at, :] = lane_sums(grad)
            partial[1, at, :] = lane_sums(grad * act[to, :])

        block_rows(256 * b, scale)
        for i in range(2):
            own_t[i : i + 1, 256 * b : 256 * b + 256] = row_of(partial[i])
    sum_t.start()

    both = sum_s.total()
    center = both[0:1] * (1.0 / FF)
    inv_std = lax.rsqrt(both[1:2] * (1.0 / FF) - center * center + EPS)
    cols[0] = spread(center)
    cols[1] = spread(inv_std)

    def normed(at):
        hat = (act[at, :] - wide(cols[0, at, :], 1024)) * wide(cols[1, at, :], 1024)
        act[at, :] = hat
        ffn_b[at, :] = (hat * gain[...] + bias[...]).astype(BF16)
        unit_sums[0] += fold8(gffn[at, :] * hat)

    by_rows(1024, normed)
    both = sum_t.total()
    cols[0] = spread(both[0:1] * (1.0 / FF))
    cols[2] = spread((both[1:2] - center * both[0:1]) * inv_std * (1.0 / FF))
    for q in range(4):
        base = sequence_at(net, q)

        def back(at, to):
            grad = gffn[to, :] * gain[...] - wide(cols[0, to, :], 1024)
            grad = grad - act[to, :] * wide(cols[2, to, :], 1024)
            grad = grad * wide(cols[1, to, :], 1024)
            grad_up[to, :] = (grad * slope[to, :].astype(F32)).astype(BF16)

        block_rows(base, back)
        mine = grad_up[pl.ds(base, 256), :]
        for h in range(2):
            part[pl.ds(base, 256), 1024 * h : 1024 * h + 1024] = dot_nt(
                mine, up[1024 * h : 1024 * h + 1024, :]
            ).astype(BF16)
        for t in total:
            if q == 0:
                t.start(2)
            if q == 1:
                t.start(0)
                t.chip(2)
            if q == 2:
                t.start(1, -1)
    for t in total:
        t.chip(1, -1, 0)
    io.wait()
    sums[...] = jnp.zeros_like(sums)

    def down_rows(dy):
        at = pl.ds(pl.multiple_of(((net.y + dy) % 4) * 512, 512), 512)
        grads[at, :] = dot_tn(cots[:, at], ffn_b[...]).astype(BF16)
        weights.start(dy)

    def norm_grad(at):
        grad = grad_attended[at, :]
        hat, inv = norm_parts(attended[at, :])
        sums[0] += fold8(grad * hat)
        sums[1] += fold8(grad)
        value = cot[at, :].astype(F32) + norm_back(grad, norm_gain[...], hat, inv)
        grad_attended[at, :] = value
        own_rows[at, :] = value.astype(BF16)

    def out_rows(b):
        for h in range(2):
            cots[256 * b : 256 * b + 256, 1024 * h : 1024 * h + 1024] = dot_nt(
                ffn_b[256 * b : 256 * b + 256, :], down[1024 * h : 1024 * h + 1024, :]
            ).astype(BF16)

    def up_rows(h):
        up[512 * h : 512 * h + 512, :] = dot_tn(
            rows[:, 512 * h : 512 * h + 512], grad_up[...]
        ).astype(BF16)

    down_rows(2)
    for t in total:
        t.pass_on()
    down_rows(1)
    down_rows(-1)
    for k in range(2):
        total[k].finish(grad_attended)
        by_rows(64, norm_grad, 16, 64 * k)
        lines[k].start()
        if k == 0:
            down_rows(0)
    io.put()
    weights.pass_on(2)
    out_rows(0)
    lines[0].forward()
    weights.pass_on(1)
    weights.pass_on(-1)
    out_rows(1)
    weights.finish(2)
    weights.pass_on(0)
    out_rows(2)
    lines[1].forward()
    weights.finish(1)
    out_rows(3)
    save_out = net.keep(cots, out_part)
    lines[0].share()
    weights.finish(-1)
    up_rows(0)
    up_rows(1)
    weights.finish(0)
    weights.pass_on_last()
    up_rows(2)
    up_rows(3)
    save_grads = net.keep(up, grads_up)
    lines[1].share()
    weights.finish_last()
    for line in lines:
        line.finish()
    weights.collect()
    save_out.wait()
    save_grads.wait()
    net.drain()


def second_call(rows, weights, cots, gain, bias, attended, cot, norm_gain):
    big, half = VMEM((1024, D), BF16), VMEM((D, 1024), BF16)
    return comm_call(
        second_kernel,
        "feed_forward",
        2,
        (rows, weights, cots, gain, bias, attended, cot, norm_gain),
        (HBM, HBM, HBM, VMEM, VMEM, VMEM, VMEM, VMEM),
        (
            shape((1024, D), BF16),
            shape((128, D), F32),
            shape((1024, D), BF16),
            shape((2, 8, D), F32),
            shape((2, 8, 1024), F32),
            shape((4, 32, 1024), BF16),
            shape((D, 1024), BF16),
        ),
        (HBM, VMEM, HBM, VMEM, VMEM, HBM, HBM),
        [
            big,
            half,
            half,
            big,
            VMEM((1, 1024), F32),
            VMEM((1, 1024), F32),
            VMEM((1024, 1024), F32),
            VMEM((1024, 1024), BF16),
            VMEM((1024, 1024), F32),
            VMEM((1024, 1024), BF16),
            VMEM((1024, 1024), BF16),
            VMEM((256, 1024), F32),
            VMEM((2, 256, 128), F32),
            VMEM((3, 1024, 128), F32),
            VMEM((2, 1024), F32),
            VMEM((8, 2, 1024), F32),
            VMEM((2, 1024), F32),
            VMEM((8, 2, 1024), F32),
            big,
            VMEM((2, 4, 64, D), BF16),
            VMEM((2, 6, 32, D), BF16),
            VMEM((128, D), BF16),
            half,
            VMEM((2, 5, 6, 32, 1024), BF16),
            VMEM((2, 2, 32, 1024), BF16),
        ],
        63,
        (119, 15),
    )


def third_kernel(
    io, grad_rows, grads_up, part_out, weights1, hat, inner_gain, context, inner_inv, query, key, value,
    caps, table, rows1, attended, grad_attended, tokens, gain, sums2, unit_sums,
    layer_out, grad_input, shard, shard_up, outer_out, inner_out,
    grad_all, gctx, grad_mixed, grads_qkv, my_gain, inner_sums, partial, cols, own_t, slots_t,
    other, landing, other_out, landing_out, work, grads, grid_landing, done,
    grid_landing_up, done_up, sums, outer, line_slots, grid_slots, half_sum,
    inner, inner_slots, inner_whole, send, recv, local,
):
    net = Net(send, recv, local)
    others = line_partners(net)
    grid = grid_partners(net)
    me_x, me_grid = net.x * 2 + net.c, net.y * 4 + net.z
    net.greet([to for to, _ in others + grid] + pair_neighbours(net))
    load_all = [
        net.keep(grad_rows.at[pl.ds(256 * b, 256)], grad_all.at[pl.ds(256 * b, 256)]) for b in range(4)
    ]
    part = grad_all
    total = LineSum(net, part, other, landing)
    total_out = LineSum(net, part_out, other_out, landing_out)
    weights = GridSum(net, grads, grid_landing, done, shard)
    weights_up = GridSum(net, grads_up, grid_landing_up, done_up, shard_up)
    sum_t = SmallSum(net, own_t, slots_t, net.x * 2 + net.c, others)
    io.wait(inner_gain)
    my_gain[...] = my_lanes(inner_gain, net, 256)
    inner_sums[...] = jnp.zeros_like(inner_sums)
    sums[...] = jnp.zeros_like(sums)

    io.wait(grads_up)
    net.met()
    for dy in (2, 1, -1, 0):
        weights_up.start(dy)
    io.wait(part_out)
    total_out.start(2, 1, -1, 0)
    io.wait(weights1, hat)
    for b in range(4):
        load_all[b].wait()
        at = slice(256 * b, 256 * b + 256)
        gctx[at, :] = dot_nn(grad_all[at, :], weights1[:, 768:])

        def scale(at, to):
            grad, one = gctx[to, :], hat[to, :]
            inner_sums[0] += fold8(grad * one)
            inner_sums[1] += fold8(grad)
            grad = grad * my_gain[...]
            gctx[to, :] = grad
            partial[0, at, :] = lane_sums(grad)
            partial[1, at, :] = lane_sums(grad * one)

        block_rows(256 * b, scale)
        for i in range(2):
            own_t[i : i + 1, at] = row_of(partial[i])
    sum_t.start()
    io.wait()
    total_out.chip(2, 1, -1, 0)
    for h in range(4):
        at = slice(512 * h, 512 * h + 512)
        grads[at, 768:] = dot_tn(grad_all[:, at], context[...]).astype(BF16)
    weights_up.pass_on(2)
    both = sum_t.total() * (1.0 / D)
    for i, row in enumerate((inner_inv[...], both[0:1], both[1:2])):
        cols[i] = spread(row)

    def mixed_grad(at):
        inv, mean, slant = (wide(cols[i, at, :], 256) for i in range(3))
        grad_mixed[at, :] = ((gctx[at, :] - mean - hat[at, :] * slant) * inv).astype(BF16)

    by_rows(1024, mixed_grad, 64)
    for q in range(4):
        base = sequence_at(net, q)
        at = pl.ds(base, SLOTS)
        cap = caps[base // SLOTS]
        found = attend_back(query[at, :], key[at, :], value[at, :], grad_mixed[at, :], cap, table)
        for i in range(3):
            grads_qkv[at, 256 * i : 256 * i + 256] = found[i]
        mine = grads_qkv[at, :]
        for h in range(2):
            part[at, 1024 * h : 1024 * h + 1024] = dot_nt(
                mine, weights1[1024 * h : 1024 * h + 1024, :768]
            ).astype(BF16)
        if q == 0:
            total.start(2)
            weights_up.pass_on(1)
            total_out.pass_on()
        if q == 1:
            total.start(0)
            total.chip(2)
            weights_up.pass_on(-1)
            weights_up.finish(2)
        if q == 2:
            total.start(1, -1)
            weights_up.pass_on(0)
            weights_up.finish(1)
    total.chip(1, -1, 0)
    for k, (lane, n) in enumerate(((0, 256), (256, 256), (512, 1024), (1536, 1024))):
        terms = inner_sums[k] if k < 2 else unit_sums[k - 2]
        inner[0:1, lane : lane + n] = jnp.sum(terms, 0, keepdims=True)
    inner_grid = SmallSum(net, inner, inner_slots, me_grid, grid)
    inner_grid.start()

    def grad_rows_of(dy):
        at = pl.ds(pl.multiple_of(((net.y + dy) % 4) * 512, 512), 512)
        grads[at, :768] = dot_tn(rows1[:, at], grads_qkv[...]).astype(BF16)
        weights.start(dy)

    grad_rows_of(2)
    weights_up.finish(-1)
    total.pass_on()
    grad_rows_of(1)
    grad_rows_of(-1)
    grad_rows_of(0)
    weights_up.finish(0)
    weights.pass_on(2)
    weights_up.pass_on_last()
    total.finish(work)

    def back(at):
        grad = work[at, :]
        one, inv = norm_parts(tokens[at, :].astype(F32))
        sums[0] += fold8(grad * one)
        sums[1] += fold8(grad)
        value = grad_attended[at, :] + norm_back(grad, gain[...], one, inv)
        grad_input[at, :] = value.astype(BF16)

    by_rows(128, back)
    io.put(grad_input)
    for i in range(4):
        terms = sums[i] if i < 2 else sums2[i - 2]
        outer[i : i + 1, :] = jnp.sum(terms, 0, keepdims=True)
    outer_x = SmallSum(net, outer, line_slots, me_x, others)
    outer_x.start()
    weights.pass_on(1)
    weights.pass_on(-1)
    weights.finish(2)
    outer_x.finish(half_sum)
    outer_grid = SmallSum(net, half_sum, grid_slots, me_grid, grid)
    outer_grid.start()
    weights.pass_on(0)
    weights.finish(1)
    weights_up.finish_last()
    total_out.finish(work)

    def out(at):
        layer_out[at, :] = (attended[at, :] + work[at, :]).astype(BF16)

    by_rows(128, out)
    io.put(layer_out)
    weights.finish(-1)
    inner_grid.finish(inner_whole)
    inner_k = {}
    for dx, dc in ((1, 0), (1, 1), (0, 1)):
        inner_k[dx, dc] = net.push(inner_whole, inner_out.at[place_of(net)], net.pair(dx, dc))
    inner_out[place_of(net)] = inner_whole[...]
    weights.finish(0)
    weights.pass_on_last()
    outer_grid.finish(outer_out)
    for dx, dc in ((1, 0), (1, 1), (0, 1)):
        net.arrived(inner_k[dx, dc], inner_out.at[((net.x + dx) % 2) * 2 + (net.c + dc) % 2])
    io.put()
    weights.finish_last()
    weights_up.collect()
    weights.collect()
    net.drain()


def third_call(ins):
    big, half = VMEM((1024, D), BF16), VMEM((D, 1024), BF16)
    quarter, wide = VMEM((1024, 256), BF16), VMEM((1024, 256), F32)
    return comm_call(
        third_kernel,
        "attention_back",
        3,
        ins,
        (HBM,) + (VMEM,) * 19,
        (
            shape((128, D), BF16),
            shape((128, D), BF16),
            shape((4, 32, 1024), BF16),
            shape((4, 32, 1024), BF16),
            shape((4, D), F32),
            shape((4, 1, 2560), F32),
        ),
        (VMEM, VMEM, HBM, HBM, VMEM, VMEM),
        [
            big,
            wide,
            quarter,
            VMEM((1024, 768), BF16),
            VMEM((1, 256), F32),
            VMEM((2, 8, 256), F32),
            VMEM((2, 256, 128), F32),
            VMEM((3, 1024, 128), F32),
            VMEM((2, 1024), F32),
            VMEM((8, 2, 1024), F32),
            VMEM((4, 128, D), BF16),
            VMEM((6, 64, D), BF16),
            VMEM((4, 128, D), BF16),
            VMEM((6, 64, D), BF16),
            VMEM((128, D), F32),
            half,
            VMEM((2, 5, 6, 32, 1024), BF16),
            VMEM((2, 2, 32, 1024), BF16),
            VMEM((2, 5, 6, 32, 1024), BF16),
            VMEM((2, 2, 32, 1024), BF16),
            VMEM((2, 8, D), F32),
            VMEM((4, D), F32),
            VMEM((8, 4, D), F32),
            VMEM((16, 4, D), F32),
            VMEM((4, D), F32),
            VMEM((1, 2560), F32),
            VMEM((16, 1, 2560), F32),
            VMEM((1, 2560), F32),
        ],
        63,
        (193, 6),
    )


def last_kernel(
    layer_in, input_in, shard, shard_up, shard_down, outer, inner,
    layer_out, grad_input, gain1, bias1, query, key, value, inner_gain, inner_bias, proj,
    gain2, bias2, up, ffn_gain, ffn_bias, down,
):
    layer_out[...] = layer_in[...]
    grad_input[...] = input_in[...]
    for i, ref in enumerate((gain1, bias1, gain2, bias2)):
        ref[...] = outer[i : i + 1, :]
    for d in range(4):
        for i, ref in enumerate((query, key, value, proj)):
            ref[:, 256 * d : 256 * d + 256] = shard[d, :, 256 * i : 256 * i + 256].astype(F32)
        up[:, 1024 * d : 1024 * d + 1024] = shard_up[d].astype(F32)
        down[:, 1024 * d : 1024 * d + 1024] = shard_down[d].astype(F32)
        for ref, lane, n in (
            (inner_gain, 0, 256), (inner_bias, 256, 256), (ffn_gain, 512, 1024), (ffn_bias, 1536, 1024),
        ):
            ref[:, n * d : n * d + n] = inner[d, :, lane : lane + n]


def whole(dims):
    return pl.BlockSpec(dims, lambda i: (0,) * len(dims))


def last_call(*ins):
    row, small, big = shape((1, D), F32), shape((32, 1024), F32), shape((32, 4096), F32)
    rows = shape((128, D), BF16)
    unit, wide = shape((1, 1024), F32), shape((1, 4096), F32)
    outs = (
        rows, rows, row, row, small, small, small, unit, unit, small, row, row, big, wide, wide, big,
    )
    return pl.pallas_call(
        last_kernel,
        out_shape=outs,
        grid=(1,),
        in_specs=[whole(v.shape) for v in ins],
        out_specs=[whole(v.shape) for v in outs],
        compiler_params=pltpu.CompilerParams(vmem_limit_bytes=63 << 20),
        name="results",
    )(*ins)


def per_device(
    tokens, caption_len, norm1_gain, norm1_bias, w_query, w_key, w_value, inner_gain, inner_bias,
    w_proj, norm2_gain, norm2_bias, w_up, ffn_norm_gain, ffn_norm_bias, w_down, cotangent,
):
    table = jnp.asarray(tables())
    line = lambda v: v.reshape(1, -1)
    (
        rows1, weights1, rows2, weights2, cots, query, key, value, hat, context, inner_inv, caps, attended,
    ) = first_call((
        tokens, caption_len, line(norm1_gain), line(norm1_bias), w_query, w_key, w_value, w_proj.T,
        line(inner_gain), line(inner_bias), line(norm2_gain), line(norm2_bias), w_up, w_down.T,
        cotangent, table,
    ))
    out_part, grad_attended, grad_rows, sums2, unit_sums, shard_down, grads_up = second_call(
        rows2, weights2, cots, line(ffn_norm_gain), line(ffn_norm_bias), attended, cotangent,
        line(norm2_gain),
    )
    layer_out, grad_input, shard, shard_up, outer, inner = third_call((
        grad_rows, grads_up, out_part, weights1, hat, line(inner_gain), context, inner_inv, query, key,
        value, caps, table, rows1, attended, grad_attended, tokens, line(norm1_gain), sums2, unit_sums,
    ))
    (
        layer_out, grad_input, gain1, bias1, query, key, value, gain_i, bias_i, proj, gain2, bias2,
        up, gain_f, bias_f, down,
    ) = last_call(layer_out, grad_input, shard, shard_up, shard_down, outer, inner)
    flat = lambda v: v.reshape(-1)
    return (
        layer_out, grad_input, flat(gain1), flat(bias1), query, key, value, flat(gain_i),
        flat(bias_i), proj.T, flat(gain2), flat(bias2), up, flat(gain_f), flat(bias_f), down.T,
    )


def solution(mesh):
    rows = P(("seq", "ffn"), None)
    by_rows_, by_columns, half = P("seq", "ffn"), P("ffn", "seq"), P("ffn")
    return jax.shard_map(
        per_device,
        mesh=mesh,
        in_specs=(
            rows, P("seq"), P(), P(), by_rows_, by_rows_, by_rows_, half, half, by_columns,
            P(), P(), by_rows_, half, half, by_columns, rows,
        ),
        out_specs=(
            rows, rows, P(), P(), by_rows_, by_rows_, by_rows_, half, half, by_columns,
            P(), P(), by_rows_, half, half, by_columns,
        ),
        check_vma=False,
    )
```

```python
import functools

import jax
import jax.numpy as jnp
import numpy as np
from jax import lax
from jax.experimental import pallas as pl
from jax.experimental.pallas import tpu as pltpu
from jax.sharding import PartitionSpec as P

D = 2048
HEAD_DIM = 64
FF = 8192
SLOTS = 256
IMAGE = 64
EPS = 1e-05
F32 = jnp.float32
BF16 = jnp.bfloat16
MESH = pl.DeviceIdType.MESH
VMEM = pltpu.VMEM
HBM = pltpu.HBM


def device_at(y, x, z, c):
    return (((y * 2 + x % 2) * 4 + z) * 2 + c, x // 2)


def line_slot(x, c):
    return ((x % 2) * 2 + c) * 2 + x // 2


class Net:
    def __init__(self, send, recv, local):
        seq, ffn = lax.axis_index("seq"), lax.axis_index("ffn")
        self.y, self.z, self.c = seq // 16, (seq // 2) % 4, seq % 2
        self.x = ffn * 2 + (seq // 8) % 2
        self.send, self.recv, self.local = send, recv, local
        self.n_send, self.n_recv, self.n_local = 0, 0, 0

    def along_x(self, dx, dc=0):
        return device_at(self.y, (self.x + dx) % 4, self.z, (self.c + dc) % 2)

    def along_y(self, dy):
        return device_at((self.y + dy) % 4, self.x, self.z, self.c)

    def along_z(self, dz):
        return device_at(self.y, self.x, (self.z + dz) % 4, self.c)

    def pair(self, dx, dc):
        x = (self.x // 2) * 2 + (self.x + dx) % 2
        return device_at(self.y, x, self.z, (self.c + dc) % 2)

    def greet(self, partners):
        self.barrier, self.partners = pltpu.get_barrier_semaphore(), len(partners)
        for partner in partners:
            pl.semaphore_signal(self.barrier, inc=1, device_id=partner, device_id_type=MESH)

    def met(self):
        pl.semaphore_wait(self.barrier, self.partners)

    def out(self):
        self.n_send += 1
        return self.send.at[self.n_send - 1]

    def into(self):
        self.n_recv += 1
        return self.recv.at[self.n_recv - 1]

    def push(self, src, dst, device, out, into):
        pltpu.make_async_remote_copy(
            src_ref=src,
            dst_ref=dst,
            send_sem=out,
            recv_sem=into,
            device_id=device,
            device_id_type=MESH,
        ).start()

    def copies(self, semaphore, same_bytes):
        return pltpu.make_async_remote_copy(
            src_ref=same_bytes,
            dst_ref=same_bytes,
            send_sem=semaphore,
            recv_sem=semaphore,
            device_id=self.along_x(0, 1),
            device_id_type=MESH,
        )

    def arrived(self, into, same_bytes):
        self.copies(into, same_bytes).wait_recv()

    def left(self, out, same_bytes):
        self.copies(out, same_bytes).wait_send()

    def keep(self, src, dst):
        copy = pltpu.make_async_copy(src, dst, self.local.at[self.n_local])
        self.n_local += 1
        copy.start()
        return copy

    def close(self):
        found = self.n_send, self.n_recv, self.n_local
        assert found == tuple(s.shape[0] for s in (self.send, self.recv, self.local)), found


def add_into(dst, *terms):
    def step(i, carry):
        rows = pl.ds(pl.multiple_of(i * 16, 16), 16)
        total = terms[0][rows, :].astype(F32)
        for term in terms[1:]:
            total = total + term[rows, :].astype(F32)
        dst[rows, :] = total.astype(dst.dtype)
        return carry

    lax.fori_loop(0, dst.shape[0] // 16, step, 0)


def slot_row(slot, off, n, by_parts):
    return pl.multiple_of(off * 8 + slot * 64 if by_parts else slot * 128 + off, n)


class LineGather:
    def __init__(self, net, own, full, off=0, n=128, by_parts=False):
        self.net, self.full, self.off, self.n, self.by_parts = net, full, off, n, by_parts
        self.own = own.at[pl.ds(off, n)]
        self.own_half = [own.at[pl.ds(off + n // 2 * h, n // 2)] for h in range(2)]
        self.out = net.out()
        self.first, self.second, self.third, self.shared = (net.into() for _ in range(4))

    def block(self, dx, dc=0, half=None):
        net, n = self.net, self.n
        base = slot_row(line_slot((net.x + dx) % 4, (net.c + dc) % 2), self.off, n, self.by_parts)
        if half is None:
            return self.full.at[pl.ds(base, n)]
        return self.full.at[pl.ds(pl.multiple_of(base + n // 2 * half, n // 2), n // 2)]

    def push(self, src, dst, device, into):
        self.net.push(src, dst, device, self.out, into)

    def same(self, ref, device, into):
        self.net.push(ref, ref, device, self.out, into)

    def bytes_of(self, k):
        return self.full.at[pl.ds(0, k * self.n)]

    def start(self):
        net = self.net
        ahead, behind, other = net.along_x(1), net.along_x(-1), net.along_x(0, 1)
        self.push(self.own_half[0], self.block(0, 0, 0), ahead, self.first)
        self.push(self.own_half[1], self.block(0, 0, 1), behind, self.first)
        self.push(self.own_half[1], self.block(0, 0, 1), ahead, self.second)
        self.push(self.own_half[0], self.block(0, 0, 0), behind, self.second)
        self.push(self.own, self.block(0), other, self.shared)
        self.kept = net.keep(self.own, self.block(0))

    def forward(self):
        net = self.net
        net.arrived(self.first, self.bytes_of(1))
        self.same(self.block(-1, 0, 0), net.along_x(1), self.third)
        self.same(self.block(1, 0, 1), net.along_x(-1), self.third)
        net.arrived(self.second, self.bytes_of(1))
        self.same(self.block(-1), net.along_x(0, 1), self.shared)
        self.same(self.block(1), net.along_x(0, 1), self.shared)

    def share(self):
        net = self.net
        net.arrived(self.third, self.bytes_of(1))
        self.same(self.block(2, 0, 0), net.along_x(0, 1), self.shared)
        self.same(self.block(2, 0, 1), net.along_x(0, 1), self.shared)

    def finish(self):
        self.net.arrived(self.shared, self.bytes_of(4))
        self.kept.wait()

    def sent(self):
        self.net.left(self.out, self.bytes_of(7))


class RingSum:
    def __init__(self, net, mine, landing, ahead, behind, out):
        self.net, self.mine, self.landing = net, mine, landing
        self.ahead, self.behind, self.out = ahead, behind, out
        self.far, self.near = net.into(), net.into()

    def start_far(self):
        net, land = self.net, self.landing
        net.push(self.mine(2, 0), land.at[0], self.ahead, self.out, self.far)
        net.push(self.mine(2, 1), land.at[1], self.behind, self.out, self.far)

    def start_near(self, d):
        net, land = self.net, self.landing
        if d == 1:
            net.push(self.mine(1, 1), land.at[3], self.ahead, self.out, self.near)
        else:
            net.push(self.mine(-1, 0), land.at[4], self.behind, self.out, self.near)

    def pass_on(self):
        net, land = self.net, self.landing
        net.arrived(self.far, land.at[pl.ds(0, 2)])
        add_into(land.at[0], land.at[0], self.mine(1, 0))
        net.push(land.at[0], land.at[2], self.ahead, self.out, self.near)
        add_into(land.at[1], land.at[1], self.mine(-1, 1))
        net.push(land.at[1], land.at[5], self.behind, self.out, self.near)

    def finish(self, out=None):
        net, land = self.net, self.landing
        net.arrived(self.near, land.at[pl.ds(2, 4)])
        add_into(land.at[2] if out is None else out(0), self.mine(0, 0), land.at[2], land.at[4])
        add_into(land.at[3] if out is None else out(1), self.mine(0, 1), land.at[3], land.at[5])


class LineSum:
    def __init__(self, net, part, other, landing, off, by_parts):
        self.net, self.part, self.other, self.landing = net, part, other, landing
        self.off, self.by_parts = off, by_parts
        self.out, self.ring_out = net.out(), net.out()
        self.first, self.rest = net.into(), net.into()
        ends = net.along_x(1), net.along_x(-1)
        self.ring = RingSum(net, self.mine, landing, *ends, self.ring_out)

    def block(self, dx, dc):
        net = self.net
        slot = line_slot((net.x + dx) % 4, (net.c + dc) % 2)
        return self.part.at[pl.ds(slot_row(slot, self.off, 64, self.by_parts), 64)]

    def mine(self, d, half):
        return self.other.at[d % 4, pl.ds(32 * half, 32)]

    def start(self, *steps):
        for d in steps:
            into = self.first if d == 2 else self.rest
            place = self.other.at[d % 4]
            self.net.push(self.block(d, 1), place, self.net.along_x(0, 1), self.out, into)

    def add(self, d):
        add_into(self.other.at[d % 4], self.other.at[d % 4], self.block(d, 0))

    def chip_far(self):
        self.net.arrived(self.first, self.other.at[0])
        self.add(2)
        self.ring.start_far()

    def chip_near(self):
        self.net.arrived(self.rest, self.other.at[pl.ds(0, 3)])
        self.add(1)
        self.ring.start_near(1)
        self.add(-1)
        self.ring.start_near(-1)
        self.add(0)

    def part_sent(self):
        self.net.left(self.out, self.other)

    def pass_on(self):
        self.ring.pass_on()

    def finish(self, out):
        self.ring.finish(lambda h: out.at[pl.ds(self.off + 32 * h, 32)])

    def sent(self):
        self.net.left(self.ring_out, self.landing)


def line_sums(net, part, other, landing, by_parts):
    return [LineSum(net, part, other.at[k], landing.at[k], 64 * k, by_parts) for k in range(2)]


def line_gathers(net, own, full):
    return [LineGather(net, own, full, 64 * k, 64, True) for k in range(2)]


def shard_rows(ref, y, x_lo, z, c=None):
    if c is None:
        return ref.at[pl.ds(pl.multiple_of(((y * 2 + x_lo) * 4 + z) * 64, 64), 64)]
    return ref.at[pl.ds(pl.multiple_of((((y * 2 + x_lo) * 4 + z) * 2 + c) * 32, 32), 32)]


PAIR_STEPS = ((1, 0), (1, 1), (0, 1))


class GridGather:
    def __init__(self, net, pieces, full):
        self.net, self.pieces, self.full = net, pieces, full
        self.out, self.pair_out = net.out(), net.out()
        self.pair_into, self.last = net.into(), net.into()
        self.p, self.f = [net.into(), net.into()], [net.into(), net.into()]
        self.q = {(t, dp): net.into() for t in (0, 1) for dp in (0, -1, 1, 2)}

    def bytes_of(self, rows):
        return self.full.at[pl.ds(0, rows)]

    def exchange(self):
        net = self.net
        spot = shard_rows(self.full, net.y, net.x % 2, net.z, net.c)
        for dx, dc in PAIR_STEPS:
            to = ((net.x + dx) % 2) * 2 + (net.c + dc) % 2
            net.push(self.piece(to), spot, net.pair(dx, dc), self.pair_out, self.pair_into)
        self.kept = net.keep(self.piece((net.x % 2) * 2 + net.c), spot)

    def piece(self, d):
        return self.pieces.at[pl.ds(pl.multiple_of(32 * d, 32), 32)]

    def slab(self, t, dp, dq, half=None):
        net = self.net
        dy, dz = (dq, dp) if t == 0 else (dp, dq)
        return shard_rows(self.full, (net.y + dy) % 4, t, (net.z + dz) % 4, half)

    def to_p(self, t, d):
        return self.net.along_z(d) if t == 0 else self.net.along_y(d)

    def to_q(self, t, d):
        return self.net.along_y(d) if t == 0 else self.net.along_z(d)

    def same(self, ref, device, into):
        self.net.push(ref, ref, device, self.out, into)

    def second(self, t, dp):
        for d in (1, -1):
            self.same(self.slab(t, dp, 0), self.to_q(t, d), self.q[t, dp])

    def start(self):
        self.net.arrived(self.pair_into, self.bytes_of(96))
        self.kept.wait()
        for t in (0, 1):
            for d in (1, -1):
                self.same(self.slab(t, 0, 0), self.to_p(t, d), self.p[t])
        for t in (0, 1):
            self.second(t, 0)

    def near(self):
        for t in (0, 1):
            self.net.arrived(self.p[t], self.bytes_of(128))
            self.same(self.slab(t, -1, 0, 0), self.to_p(t, 1), self.f[t])
            self.same(self.slab(t, 1, 0, 1), self.to_p(t, -1), self.f[t])
        for t in (0, 1):
            self.second(t, -1)
            self.second(t, 1)

    def far(self):
        for t in (0, 1):
            self.net.arrived(self.f[t], self.bytes_of(64))
            self.second(t, 2)

    def pass_on(self, dp):
        for t in (0, 1):
            self.net.arrived(self.q[t, dp], self.bytes_of(128))
            self.same(self.slab(t, dp, -1, 0), self.to_q(t, 1), self.last)
            self.same(self.slab(t, dp, 1, 1), self.to_q(t, -1), self.last)

    def finish(self):
        self.net.arrived(self.last, self.bytes_of(512))

    def pair_sent(self):
        self.net.left(self.pair_out, self.bytes_of(96))

    def sent(self):
        self.net.left(self.out, self.bytes_of(1920))


class GridSum:
    def __init__(self, net, part, landing, done, shard):
        self.net, self.part, self.landing, self.done, self.shard = net, part, landing, done, shard
        self.out, self.pair_out, self.pair_into = net.out(), net.out(), net.into()
        self.rings = {}
        for t in (0, 1):
            for dp in (2, 1, -1, 0):
                self.rings[t, dp] = RingSum(
                    net,
                    functools.partial(self.term, t, dp),
                    landing.at[t, dp % 4],
                    self.to_q(t, 1),
                    self.to_q(t, -1),
                    self.out,
                )
            self.rings[t] = RingSum(
                net,
                functools.partial(self.column, t),
                landing.at[t, 4],
                self.to_p(t, 1),
                self.to_p(t, -1),
                self.out,
            )
        self.steps = [
            functools.partial(self.pass_on, 2),
            functools.partial(self.pass_on, 1),
            functools.partial(self.pass_on, -1),
            functools.partial(self.finish, 2),
            functools.partial(self.pass_on, 0),
            functools.partial(self.finish, 1),
            functools.partial(self.finish, -1),
            self.pass_on_last,
            functools.partial(self.finish, 0),
            self.finish_last,
            self.collect,
        ]

    def to_p(self, t, d):
        return self.net.along_z(d) if t == 0 else self.net.along_y(d)

    def to_q(self, t, d):
        return self.net.along_y(d) if t == 0 else self.net.along_z(d)

    def term(self, t, dp, dq, half):
        net = self.net
        dy, dz = (dq, dp) if t == 0 else (dp, dq)
        return shard_rows(self.part, (net.y + dy) % 4, t, (net.z + dz) % 4, half)

    def column(self, t, dp, half):
        return self.landing.at[t, dp % 4, 2 + half]

    def start(self, dy):
        for dp in (2, 1, -1, 0):
            if dy == 2:
                self.rings[0, dp].start_far()
            elif dy:
                self.rings[0, dp].start_near(dy)
        self.rings[1, dy].start_far()
        self.rings[1, dy].start_near(1)
        self.rings[1, dy].start_near(-1)

    def step(self, n=1):
        for _ in range(n):
            self.steps.pop(0)()

    def pass_on(self, dp):
        for t in (0, 1):
            self.rings[t, dp].pass_on()

    def finish(self, dp):
        for t in (0, 1):
            self.rings[t, dp].finish()
            if dp == 2:
                self.rings[t].start_far()
            elif dp:
                self.rings[t].start_near(dp)

    def pass_on_last(self):
        for t in (0, 1):
            self.rings[t].pass_on()

    def finish_last(self):
        net = self.net
        for t in (0, 1):
            self.rings[t].finish(lambda half: self.done.at[t, half])
        me = (net.x % 2) * 2 + net.c
        for dx, dc in PAIR_STEPS:
            src = self.done.at[(net.x + dx) % 2, (net.c + dc) % 2]
            net.push(src, self.shard.at[me], net.pair(dx, dc), self.pair_out, self.pair_into)
        self.kept = net.keep(self.done.at[net.x % 2, net.c], self.shard.at[me])

    def collect(self):
        self.net.arrived(self.pair_into, self.shard.at[pl.ds(0, 3)])
        self.kept.wait()

    def sent(self):
        self.net.left(self.out, self.part.at[pl.ds(0, 1920)])

    def pair_sent(self):
        self.net.left(self.pair_out, self.shard.at[pl.ds(0, 3)])


class SmallSum:
    def __init__(self, net, own, slots, me, partners):
        self.net, self.own, self.slots, self.me, self.partners = net, own, slots, me, partners
        self.out, self.into = net.out(), net.into()

    def start(self):
        for to, _ in self.partners:
            self.net.push(self.own, self.slots.at[self.me], to, self.out, self.into)
        self.slots[self.me] = self.own[...]

    def total(self):
        self.net.arrived(self.into, self.slots.at[pl.ds(0, len(self.partners))])
        total = self.slots[0]
        for i in range(1, self.slots.shape[0]):
            total = total + self.slots[i]
        return total

    def finish(self, out):
        out[...] = self.total()

    def sent(self):
        self.net.left(self.out, self.slots.at[pl.ds(0, len(self.partners))])


class PairShare:
    def __init__(self, net, own, slots):
        self.net, self.own, self.slots = net, own, slots
        self.out, self.into = net.out(), net.into()

    def start(self):
        net = self.net
        me = (net.x % 2) * 2 + net.c
        for dx, dc in PAIR_STEPS:
            net.push(self.own, self.slots.at[me], net.pair(dx, dc), self.out, self.into)
        self.slots[me] = self.own[...]

    def finish(self):
        self.net.arrived(self.into, self.slots.at[pl.ds(0, 3)])

    def sent(self):
        self.net.left(self.out, self.slots.at[pl.ds(0, 3)])


def line_partners(net):
    return [
        (net.along_x(dx, dc), ((net.x - dx) % 4) * 2 + (net.c + dc) % 2)
        for dx in range(4)
        for dc in range(2)
        if dx or dc
    ]


def grid_partners(net):
    return [
        (
            device_at((net.y + dy) % 4, net.x, (net.z + dz) % 4, net.c),
            ((net.y - dy) % 4) * 4 + (net.z - dz) % 4,
        )
        for dy in range(4)
        for dz in range(4)
        if dy or dz
    ]


def spec(space):
    return pl.BlockSpec(memory_space=space)


def shape(dims, dtype):
    return jax.ShapeDtypeStruct(dims, dtype)


class Staged:
    def __init__(self, loads, stores):
        self.loads, self.stores, self.started = loads, stores, []
        for copy, _ in loads:
            copy.start()

    def wait(self, *refs):
        for copy, ref in list(self.loads):
            if not refs or any(ref is r for r in refs):
                copy.wait()
                self.loads = [pair for pair in self.loads if pair[1] is not ref]

    def put(self, *refs):
        for copy, ref in list(self.stores):
            if not refs or any(ref is r for r in refs):
                copy.start()
                self.started.append(copy)
                self.stores = [pair for pair in self.stores if pair[1] is not ref]

    def finish(self):
        self.wait()
        self.put()
        for copy in self.started:
            copy.wait()


def comm_call(body, name, collective_id, ins, in_spaces, outs, out_spaces, scratch, mib, sems):
    n_in, n_out = len(ins), len(outs)
    buffers = [space(v.shape, v.dtype) for v, space in zip(ins, in_spaces) if space is not HBM]
    buffers += [space(v.shape, v.dtype) for v, space in zip(outs, out_spaces) if space is not HBM]
    n = len(buffers)

    def kernel(*refs):
        sem = refs[-1]
        rest = list(refs[n_in + n_out : n_in + n_out + n])
        loads, stores, args = [], [], []
        for i, (ref, space) in enumerate(zip(refs, (*in_spaces, *out_spaces))):
            if space is HBM:
                args.append(ref)
                continue
            buffer = rest.pop(0)
            args.append(buffer)
            at = sem.at[len(loads) + len(stores)]
            if i < n_in:
                loads.append((pltpu.make_async_copy(ref, buffer, at), buffer))
            else:
                stores.append((pltpu.make_async_copy(buffer, ref, at), buffer))
        io = Staged(loads, stores)
        body(io, *args, *refs[n_in + n_out + n : -1])
        io.finish()

    return pl.pallas_call(
        kernel,
        out_shape=outs,
        in_specs=[spec(HBM)] * n_in,
        out_specs=[spec(HBM)] * n_out,
        scratch_shapes=buffers
        + scratch
        + [pltpu.SemaphoreType.REGULAR((2,))]
        + [pltpu.SemaphoreType.DMA((k,)) for k in (*sems, n)],
        compiler_params=pltpu.CompilerParams(
            collective_id=collective_id, has_side_effects=True, vmem_limit_bytes=mib << 20
        ),
        name=name,
    )(*ins)


def norm_parts(values):
    center = jnp.mean(values, -1, keepdims=True)
    spread = jnp.mean(values * values, -1, keepdims=True) - center * center
    inv_std = lax.rsqrt(spread + EPS)
    return (values - center) * inv_std, inv_std


def by_rows(rows, step, chunk=16, off=0):
    def body(i, carry):
        step(pl.ds(pl.multiple_of(off + i * chunk, chunk), chunk))
        return carry

    lax.fori_loop(0, rows // chunk, body, 0)


def norm_back(grad, gain, hat, inv_std):
    scaled = grad * gain
    return inv_std * (
        scaled
        - jnp.mean(scaled, -1, keepdims=True)
        - hat * jnp.mean(scaled * hat, -1, keepdims=True)
    )


def fold8(values):
    return values[:8] + values[8:]


def block_rows(base, step):
    def body(i, carry):
        step(
            pl.ds(pl.multiple_of(i * 16, 16), 16),
            pl.ds(pl.multiple_of(base + i * 16, 16), 16),
        )
        return carry

    lax.fori_loop(0, 16, body, 0)


def lane_sums(values):
    total = values[:, :128]
    for k in range(1, values.shape[1] // 128):
        total = total + values[:, 128 * k : 128 * k + 128]
    return total


def row_of(partial):
    return jnp.sum(partial.T, 0, keepdims=True)


def spread(row):
    return jnp.broadcast_to(row, (128, row.shape[1])).T


def wide(values, lanes):
    return jnp.concatenate([values] * (lanes // 128), 1)


def xpos_tables(direction):
    half = HEAD_DIM // 2
    pair = np.arange(half, dtype=np.float32)
    frequency = np.power(np.float32(10000.0), -pair / half).astype(np.float32)
    zeta = ((pair / half + 0.4) / 1.4).astype(np.float32)
    position = np.arange(SLOTS, dtype=np.float32)[:, None]
    angle = (position * frequency).astype(np.float32).astype(np.float64)
    decay = np.exp(direction * position / 512.0 * np.log(zeta.astype(np.float64)))
    cosine, sine = np.cos(angle) * decay, np.sin(angle) * decay
    cosine = np.concatenate([cosine] * 2, -1)
    sine = np.concatenate([-sine, sine], -1)
    return np.tile(cosine, (1, 4)).astype(np.float32), np.tile(sine, (1, 4)).astype(np.float32)


def tables():
    return np.stack([*xpos_tables(1.0), *xpos_tables(-1.0)])


def swapped(values):
    lane = lax.broadcasted_iota(jnp.int32, values.shape, 1)
    return jnp.where(lane % 64 < 32, pltpu.roll(values, 224, 1), pltpu.roll(values, 32, 1))


def dot_nn(a, b):
    return lax.dot_general(a, b, (((1,), (0,)), ((), ())), preferred_element_type=F32)


def dot_nt(a, b):
    return lax.dot_general(a, b, (((1,), (1,)), ((), ())), preferred_element_type=F32)


def dot_tn(a, b):
    return lax.dot_general(a, b, (((0,), (0,)), ((), ())), preferred_element_type=F32)


def head_of(values, head):
    lane = lax.broadcasted_iota(jnp.int32, values.shape, 1)
    return jnp.where(lane // 64 == head, values, jnp.zeros_like(values))


def head_probs(query, key, head, allowed):
    scores = dot_nt(head_of(query, head), key) * HEAD_DIM**-0.5
    scores = jnp.where(allowed, scores, -1e30)
    exps = jnp.exp(scores - jnp.max(scores, -1, keepdims=True))
    return exps / jnp.sum(exps, -1, keepdims=True)


def allowed_slots(cap):
    query = lax.broadcasted_iota(jnp.int32, (SLOTS, SLOTS), 0)
    key = lax.broadcasted_iota(jnp.int32, (SLOTS, SLOTS), 1)
    return (key <= query) & (key < IMAGE + cap[0:1, 0:1])


def attend(rows, weights, cap, table, at, kept, mixed):
    qkv = dot_nn(rows, weights[:, :768])
    query, key, value = qkv[:, :256], qkv[:, 256:512], qkv[:, 512:].astype(BF16)
    query = (query * table(0) + swapped(query) * table(1)).astype(BF16)
    key = (key * table(2) + swapped(key) * table(3)).astype(BF16)
    for i, part in enumerate((query, key, value)):
        kept[at, 256 * i : 256 * i + 256] = part
    allowed = allowed_slots(cap)
    total = jnp.zeros((SLOTS, 256), F32)
    for head in range(4):
        probs = head_probs(query, key, head, allowed).astype(BF16)
        total = total + dot_nn(probs, head_of(value, head))
    mixed[at, :256] = total


def attend_back(query, key, value, grad, cap, table):
    allowed = allowed_slots(cap)
    grad_query = jnp.zeros((SLOTS, 256), F32)
    grad_key = jnp.zeros((SLOTS, 256), F32)
    grad_value = jnp.zeros((SLOTS, 256), F32)
    for head in range(4):
        probs = head_probs(query, key, head, allowed)
        grad_head = head_of(grad, head)
        grad_probs = dot_nt(grad_head, value)
        grad_value = grad_value + dot_tn(probs.astype(BF16), grad_head)
        delta = jnp.sum(probs * grad_probs, -1, keepdims=True)
        grad_scores = (probs * (grad_probs - delta)).astype(BF16)
        grad_query = grad_query + dot_nn(grad_scores, head_of(key, head))
        grad_key = grad_key + dot_tn(grad_scores, head_of(query, head))
    grad_query = grad_query * HEAD_DIM**-0.5
    grad_key = grad_key * HEAD_DIM**-0.5
    return (
        (grad_query * table(0) + swapped(grad_query * table(1))).astype(BF16),
        (grad_key * table(2) + swapped(grad_key * table(3))).astype(BF16),
        grad_value.astype(BF16),
    )


def place_of(net):
    return (net.x % 2) * 2 + net.c


def my_lanes(ref, net, n):
    return ref[:, pl.ds(pl.multiple_of(place_of(net) * n, n), n)]


def sequence_at(net, q):
    seq_of = ((net.x + q // 2) % 2) * 2 + (net.c + 1 + q) % 2
    return pl.multiple_of(seq_of * SLOTS, SLOTS)


def rows_along_y(net, dy):
    return pl.ds(pl.multiple_of(((net.y + dy) % 4) * 512, 512), 512)


def layer_kernel(
    io, tokens, cap, gain1, bias1, inner_gain, inner_bias, gain2, bias2, ffn_gains, ffn_biases, cot,
    w_query, w_key, w_value, w_proj, w_up, w_down, table_in,
    rows1_out, weights1_out, kept_out, hat_out, shard_down, shard_up, shard_proj, shard_qkv,
    layer_out, grad_input, outer_out, inner_out,
    own_rows, rows, cots, part, weights1, up, down, act, gffn, slope, kept, grad_up, partial, cols,
    caps_in, caps, ffn_gain, ffn_bias, my_gain, attended, grad_attended,
    work,     own_s, slots_s, own_u, slots_u, own_t, slots_t, other, landing, landing_down, landing_up,
    landing_proj, done, inner_inv, inner_sums, unit_sums, sums, outer, line_slots, grid_slots, half_sum,
    inner, inner_slots, inner_whole, credit, send, recv, local,
):
    net = Net(send, recv, local)
    others, grid = line_partners(net), grid_partners(net)
    net.greet([to for to, _ in others + grid])
    me, me_grid = net.x * 2 + net.c, net.y * 4 + net.z
    shards = [w_query, w_key, w_value, w_proj]
    load1 = [net.keep(w, act.at[pl.ds(32 * i, 32)]) for i, w in enumerate(shards)]
    load_table = net.keep(table_in, gffn.at[:, pl.ds(0, 256)])
    load2 = [
        net.keep(w.at[:, pl.ds(1024 * d, 1024)], act.at[pl.ds(128 + 128 * i + 32 * d, 32)])
        for i, w in enumerate((w_down, w_up))
        for d in range(4)
    ]
    gather1 = GridGather(net, slope.at[pl.ds(0, 128)], weights1)
    gather_down = GridGather(net, slope.at[pl.ds(128, 128)], down)
    gather_up = GridGather(net, slope.at[pl.ds(256, 128)], up)
    line1 = LineGather(net, own_rows, rows)
    line_cot = line_gathers(net, cot, cots)
    total = line_sums(net, part, other, landing, False)
    line2 = line_gathers(net, own_rows, rows)
    sum_s = SmallSum(net, own_s, slots_s, me, others)
    share_caps = PairShare(net, caps_in, caps)

    for i in range(4):
        load1[i].wait()
        for d in range(4):
            slope[32 * d : 32 * d + 32, 256 * i : 256 * i + 256] = act[
                32 * i : 32 * i + 32, 256 * d : 256 * d + 256
            ].astype(BF16)
    io.wait(tokens, cap, gain1, bias1)

    def norm1(at):
        one, _ = norm_parts(tokens[at, :].astype(F32))
        own_rows[at, :] = (one * gain1[...] + bias1[...]).astype(BF16)

    by_rows(128, norm1)
    caps_in[...] = jnp.full((8, 128), cap[0], jnp.int32)

    net.met()
    gather1.exchange()
    line1.start()
    share_caps.start()
    gather1.start()
    for copy in load2:
        copy.wait()
    slope[128:384, :] = act[128:384, :].astype(BF16)
    io.wait()
    for ref in (unit_sums, sums, inner_sums):
        ref[...] = jnp.zeros_like(ref)
    ffn_gain[...], ffn_bias[...] = my_lanes(ffn_gains, net, 1024), my_lanes(ffn_biases, net, 1024)
    my_gain[...] = my_lanes(inner_gain, net, 256)
    gather1.near()
    gather1.pass_on(0)
    gather1.far()
    line1.forward()
    gather_down.exchange()
    gather1.pass_on(-1)
    gather1.pass_on(1)
    line1.share()
    gather_up.exchange()
    for line in line_cot:
        line.start()
    gather1.pass_on(2)
    share_caps.finish()
    load_table.wait()
    line1.finish()
    gather1.finish()
    gather_down.start()
    save_rows, save_weights = net.keep(rows, rows1_out), net.keep(weights1, weights1_out)

    table = lambda i: gffn[256 * i : 256 * i + 256, :256]
    for b in range(4):
        at = slice(256 * b, 256 * b + 256)
        attend(rows[at, :], weights1, caps.at[b], table, at, kept, act)
        both = act[at, :256]
        partial[0] = lane_sums(both)
        partial[1] = lane_sums(both * both)
        for i in range(2):
            own_s[i : i + 1, at] = row_of(partial[i])
        if b == 2:
            gather_down.near()
            gather_down.pass_on(0)
    sum_s.start()
    for line in line_cot:
        line.forward()
    gather_down.far()
    gather_down.pass_on(-1)
    both = sum_s.total()
    center = both[0:1] * (1.0 / D)
    inv_std = lax.rsqrt(both[1:2] * (1.0 / D) - center * center + EPS)
    inner_inv[...] = inv_std
    cols[0] = spread(center)
    cols[1] = spread(inv_std)
    my_bias = my_lanes(inner_bias, net, 256)

    def inner_norm(at):
        one = (act[at, :256] - wide(cols[0, at, :], 256)) * wide(cols[1, at, :], 256)
        act[at, 256:512] = one
        kept[at, 768:] = (one * my_gain[...] + my_bias).astype(BF16)

    by_rows(1024, inner_norm, 64)
    save_hat = net.keep(act.at[:, pl.ds(256, 256)], hat_out)
    save_kept = net.keep(kept, kept_out)
    save_rows.wait()
    line1.sent()
    for q in range(4):
        at = pl.ds(sequence_at(net, q), SLOTS)
        mine = kept[at, 768:]
        for h in range(2):
            part[at, 1024 * h : 1024 * h + 1024] = dot_nt(
                mine, weights1[1024 * h : 1024 * h + 1024, 768:]
            ).astype(BF16)
        for t in total:
            if q == 0:
                t.start(2)
            if q == 1:
                t.start(0)
                t.chip_far()
            if q == 2:
                t.start(1, -1)
    for t in total:
        t.chip_near()
    gather_down.pass_on(1)
    total[0].pass_on()
    gather_up.start()
    total[1].pass_on()
    for line in line_cot:
        line.share()
    gather_down.pass_on(2)
    save_weights.wait()

    def norm2(at):
        values = tokens[at, :].astype(F32) + attended[at, :]
        attended[at, :] = values
        one, _ = norm_parts(values)
        own_rows[at, :] = (one * gain2[...] + bias2[...]).astype(BF16)

    def cot_rows(b):
        at = slice(256 * b, 256 * b + 256)
        gffn[at, :] = dot_nn(cots[at, :], down[...])

    for line in line_cot:
        line.finish()
    gather_down.finish()
    cot_rows(0)
    total[0].finish(attended)
    by_rows(64, norm2)
    line2[0].start()
    cot_rows(1)
    total[1].finish(attended)
    by_rows(64, norm2, 16, 64)
    gather_up.near()
    gather_up.pass_on(0)
    line2[0].forward()
    line2[1].start()
    cot_rows(2)
    gather_up.far()
    line2[0].share()
    cot_rows(3)
    gather_up.pass_on(-1)
    gather_up.pass_on(1)
    gather_up.pass_on(2)
    line2[0].finish()
    gather_up.finish()
    save_hat.wait()
    save_kept.wait()
    for t in total:
        t.part_sent()
        t.sent()
    for gather in (gather1, gather_down, gather_up):
        gather.pair_sent()

    sum_u = [SmallSum(net, own_u.at[k], slots_u.at[k], me, others) for k in range(2)]
    for k in range(2):
        if k == 1:
            line2[1].finish()
        for j in range(2):
            base = 512 * k + 256 * j
            act[base : base + 256, :] = dot_nn(rows[base : base + 256, :], up[...])

            def gelu(at, to):
                value = act[to, :]
                cdf = 0.5 * (1.0 + lax.erf(value * np.float32(0.5**0.5)))
                density = jnp.exp(-0.5 * value * value) * np.float32((2 * np.pi) ** -0.5)
                slope[to, :] = (cdf + value * density).astype(BF16)
                value = value * cdf
                act[to, :] = value
                partial[0, at, :] = lane_sums(value)
                partial[1, at, :] = lane_sums(value * value)
                grad = gffn[to, :]
                unit_sums[1] += fold8(grad)
                grad = grad * ffn_gain[...]
                partial[2, at, :] = lane_sums(grad)
                partial[3, at, :] = lane_sums(grad * value)

            block_rows(base, gelu)
            for i in range(4):
                own_u[k, i : i + 1, 256 * j : 256 * j + 256] = row_of(partial[i])
            if k == 0:
                (line2[1].share if j else line2[1].forward)()
        sum_u[k].start()

    total = line_sums(net, part, other, landing, True)
    ffn_b = kept
    for k in range(2):
        both = sum_u[k].total()
        center = both[0:1] * (1.0 / FF)
        inv_std = lax.rsqrt(both[1:2] * (1.0 / FF) - center * center + EPS)
        slant = (both[3:4] - center * both[2:3]) * inv_std * (1.0 / FF)
        its = slice(512 * k, 512 * k + 512)
        for i, row in enumerate((center, inv_std, both[2:3] * (1.0 / FF))):
            cols[i, its, :] = spread(row)

        def normed(at):
            hat = (act[at, :] - wide(cols[0, at, :], 1024)) * wide(cols[1, at, :], 1024)
            act[at, :] = hat
            ffn_b[at, :] = (hat * ffn_gain[...] + ffn_bias[...]).astype(BF16)
            unit_sums[0] += fold8(gffn[at, :] * hat)

        by_rows(512, normed, 16, 512 * k)
        cols[0, its, :] = spread(slant)
        if k == 1:
            total[0].chip_near()
        for j in range(2):
            base = pl.multiple_of(512 * k + 256 * ((net.x + j) % 2), 256)

            def back(at, to):
                grad = gffn[to, :] * ffn_gain[...] - wide(cols[2, to, :], 1024)
                grad = grad - act[to, :] * wide(cols[0, to, :], 1024)
                grad = grad * wide(cols[1, to, :], 1024)
                grad_up[to, :] = (grad * slope[to, :].astype(F32)).astype(BF16)

            block_rows(base, back)
            mine = grad_up[pl.ds(base, 256), :]
            for h in range(2):
                part[pl.ds(base, 256), 1024 * h : 1024 * h + 1024] = dot_nt(
                    mine, up[1024 * h : 1024 * h + 1024, :]
                ).astype(BF16)
            if j == 0:
                total[k].start(2, 0)
            else:
                total[k].start(1, -1)
                total[k].chip_far()
    total[0].pass_on()
    total[1].chip_near()

    weights_down = GridSum(net, weights1, landing_down, done.at[0], shard_down)
    weights_up = GridSum(net, up, landing_up, done.at[1], shard_up)
    lines = line_gathers(net, own_rows, part)

    def norm2_back(at):
        grad = grad_attended[at, :]
        one, inv = norm_parts(attended[at, :])
        sums[2] += fold8(grad * one)
        sums[3] += fold8(grad)
        value = cot[at, :].astype(F32) + norm_back(grad, gain2[...], one, inv)
        grad_attended[at, :] = value
        own_rows[at, :] = value.astype(BF16)

    def down_rows(dy):
        at = rows_along_y(net, dy)
        weights1[at, :] = dot_tn(cots[:, at], ffn_b[...]).astype(BF16)
        weights_down.start(dy)

    def out_rows(b):
        for h in range(2):
            cots[256 * b : 256 * b + 256, 1024 * h : 1024 * h + 1024] = dot_nt(
                ffn_b[256 * b : 256 * b + 256, :], down[1024 * h : 1024 * h + 1024, :]
            ).astype(BF16)

    def up_rows(dy):
        at = rows_along_y(net, dy)
        up[at, :] = dot_tn(rows[:, at], grad_up[...]).astype(BF16)
        weights_up.start(dy)

    load_hat = net.keep(hat_out, act.at[:, pl.ds(0, 256)])
    load_kept = net.keep(kept_out, slope)
    load_table = net.keep(table_in, gffn.at[:, pl.ds(0, 256)])
    for sender in line2 + line_cot + [gather1, gather_down, gather_up]:
        sender.sent()
    for t in total:
        t.part_sent()
    pl.semaphore_signal(credit.at[0], inc=1, device_id=net.along_x(0, 1), device_id_type=MESH)
    down_rows(2)
    total[1].pass_on()
    down_rows(1)
    down_rows(-1)
    pl.semaphore_wait(credit.at[0], 1)
    total[0].finish(grad_attended)
    total[0].sent()
    by_rows(64, norm2_back)
    lines[0].start()
    down_rows(0)
    total[1].finish(grad_attended)
    total[1].sent()
    by_rows(64, norm2_back, 16, 64)
    lines[1].start()
    weights_down.step()
    out_rows(0)
    out_rows(1)
    weights_down.step()
    lines[0].forward()
    out_rows(2)
    out_rows(3)
    load_weights = net.keep(weights1_out, down)
    weights_down.step(2)
    lines[1].forward()
    up_rows(2)
    up_rows(1)
    weights_down.step()
    lines[0].share()
    up_rows(-1)
    up_rows(0)
    load_rows = net.keep(rows1_out, rows)
    lines[1].share()
    weights_down.step(2)
    lines[0].finish()

    ctx_parts, grad_mixed, grads_qkv, gctx = kept.at[:, 256:512], kept.at[:, 0:256], grad_up, act
    sum_t = SmallSum(net, own_t, slots_t, me, others)
    load_hat.wait()
    load_kept.wait()
    load_table.wait()
    load_weights.wait()

    def context_grad(k):
        for j in range(2):
            base = 512 * k + 256 * j
            found = dot_nn(part[base : base + 256, :], down[:, 768:])
            for i in range(4):
                at = 128 * (4 * j + i) + 64 * k
                gctx[at : at + 64, 256:512] = found[64 * i : 64 * i + 64]
                ctx_parts[base + 64 * i : base + 64 * i + 64, :] = slope[at : at + 64, 768:]

    context_grad(0)
    lines[1].finish()
    total_out = line_sums(net, cots, other, landing, True)
    for t in total_out:
        t.start(2, 1, -1, 0)
    context_grad(1)
    for b in range(4):

        def scale(at, to):
            grad, one = gctx[to, 256:512], act[to, 0:256]
            inner_sums[0] += fold8(grad * one)
            inner_sums[1] += fold8(grad)
            grad = grad * my_gain[...]
            gctx[to, 256:512] = grad
            partial[0, at, :] = lane_sums(grad)
            partial[1, at, :] = lane_sums(grad * one)

        block_rows(256 * b, scale)
        for i in range(2):
            own_t[i : i + 1, 256 * b : 256 * b + 256] = row_of(partial[i])
    sum_t.start()
    for t in total_out:
        t.chip_far()
        t.chip_near()
    for line in lines:
        line.sent()
    both = sum_t.total() * (1.0 / D)
    for i, row in enumerate((inner_inv[...], both[0:1], both[1:2])):
        cols[i] = spread(row)

    def mixed_grad(at):
        inv, mean, slant = (wide(cols[i, at, :], 256) for i in range(3))
        grad = gctx[at, 256:512] - mean - act[at, 0:256] * slant
        grad_mixed[at, :] = (grad * inv).astype(BF16)

    by_rows(1024, mixed_grad, 64)
    total = line_sums(net, part, other, landing, False)
    weights_proj = GridSum(
        net, weights1.at[:, pl.ds(768, 256)], landing_proj, done.at[2, :, :, :, pl.ds(0, 256)], shard_proj,
    )
    weights_qkv = GridSum(
        net, weights1.at[:, pl.ds(0, 768)], landing_down.at[:, :, :, :, pl.ds(0, 768)],
        done.at[2, :, :, :, pl.ds(256, 768)], shard_qkv,
    )

    def output(at):
        layer_out[at, :] = (attended[at, :] + work[at, :]).astype(BF16)

    def proj_rows(dy):
        at = rows_along_y(net, dy)
        weights1[at, 768:] = dot_tn(part[:, at], ctx_parts[...]).astype(BF16)
        weights_proj.start(dy)

    for q in range(4):
        base = sequence_at(net, q)
        at = pl.ds(base, SLOTS)
        query, key, value = (slope[at, 256 * i : 256 * i + 256] for i in range(3))
        found = attend_back(query, key, value, grad_mixed[at, :], caps[base // SLOTS], table)
        for i in range(3):
            grads_qkv[at, 256 * i : 256 * i + 256] = found[i]
        if q == 0:
            weights_down.step(2)
        if q == 1:
            for t in total_out:
                t.pass_on()
            weights_down.step()
            weights_down.sent()
            weights_up.step(2)
        if q == 2:
            for dy in (2, 1, -1, 0):
                proj_rows(dy)
            weights_up.step(2)
    for q in range(4):
        at = pl.ds(sequence_at(net, q), SLOTS)
        mine = grads_qkv[at, :768]
        for h in range(2):
            part[at, 1024 * h : 1024 * h + 1024] = dot_nt(
                mine, down[1024 * h : 1024 * h + 1024, :768]
            ).astype(BF16)
        if q == 0:
            for t in total_out:
                t.finish(work)
                t.part_sent()
                t.sent()
            for to in (net.along_x(0, 1), net.along_x(1), net.along_x(-1)):
                pl.semaphore_signal(credit.at[1], inc=1, device_id=to, device_id_type=MESH)
            by_rows(128, output)
            io.put(layer_out)
            pl.semaphore_wait(credit.at[1], 3)
        for t in total:
            if q == 0:
                t.start(2)
            if q == 1:
                t.start(0)
                t.chip_far()
            if q == 2:
                t.start(1, -1)
    for t in total:
        t.chip_near()
    load_rows.wait()

    def qkv_rows(dy):
        at = rows_along_y(net, dy)
        weights1[at, :768] = dot_tn(rows[:, at], grads_qkv[:, :768]).astype(BF16)
        weights_qkv.start(dy)

    weights_proj.step()
    qkv_rows(2)
    total[0].pass_on()
    qkv_rows(1)
    total[1].pass_on()
    qkv_rows(-1)
    qkv_rows(0)
    weights_up.step(3)
    for k, (lane, n) in enumerate(((0, 256), (256, 256), (512, 1024), (1536, 1024))):
        terms = inner_sums[k] if k < 2 else unit_sums[k - 2]
        inner[0:1, lane : lane + n] = jnp.sum(terms, 0, keepdims=True)
    inner_grid = SmallSum(net, inner, inner_slots, me_grid, grid)
    inner_grid.start()

    for t in total:
        t.finish(work)

    def norm1_back(at):
        grad = work[at, :]
        one, inv = norm_parts(tokens[at, :].astype(F32))
        sums[0] += fold8(grad * one)
        sums[1] += fold8(grad)
        value = grad_attended[at, :] + norm_back(grad, gain1[...], one, inv)
        grad_input[at, :] = value.astype(BF16)

    by_rows(128, norm1_back)
    io.put(grad_input)
    for i in range(4):
        outer[i : i + 1, :] = jnp.sum(sums[i], 0, keepdims=True)
    outer_x = SmallSum(net, outer, line_slots, me, others)
    outer_x.start()
    weights_up.step(2)
    weights_proj.step(3)
    weights_qkv.step(2)
    outer_x.finish(half_sum)
    outer_grid = SmallSum(net, half_sum, grid_slots, me_grid, grid)
    outer_grid.start()
    weights_up.step(2)
    weights_proj.step(3)
    weights_qkv.step(2)
    inner_grid.finish(inner_whole)
    share_inner = PairShare(net, inner_whole, inner_out)
    share_inner.start()
    weights_proj.step()
    weights_qkv.step(4)
    weights_proj.step(3)
    outer_grid.finish(outer_out)
    share_inner.finish()
    io.put()
    weights_qkv.step(3)
    weights_down.step()
    for t in total:
        t.part_sent()
    for sender in [*total, weights_up, weights_proj, weights_qkv, sum_s, *sum_u, sum_t]:
        sender.sent()
    for sender in (share_caps, share_inner, inner_grid, outer_x, outer_grid):
        sender.sent()
    for weights in (weights_down, weights_up, weights_proj, weights_qkv):
        weights.pair_sent()
    net.close()


def layer_call(ins):
    big, half = VMEM((1024, D), BF16), VMEM((D, 1024), BF16)
    square, tall = VMEM((1024, 1024), F32), VMEM((1024, 1024), BF16)
    grid_land = VMEM((2, 5, 6, 32, 1024), BF16)
    unit, own, stats = VMEM((1, 1024), F32), VMEM((2, 1024), F32), VMEM((8, 2, 1024), F32)
    return comm_call(
        layer_kernel,
        "layer",
        1,
        ins,
        (VMEM, pltpu.SMEM) + (VMEM,) * 9 + (HBM,) * 7,
        (
            shape((1024, D), BF16),
            shape((D, 1024), BF16),
            shape((1024, 1024), BF16),
            shape((1024, 256), F32),
            shape((4, 32, 1024), BF16),
            shape((4, 32, 1024), BF16),
            shape((4, 32, 256), BF16),
            shape((4, 32, 768), BF16),
            shape((128, D), BF16),
            shape((128, D), BF16),
            shape((4, D), F32),
            shape((4, 1, 2560), F32),
        ),
        (HBM,) * 8 + (VMEM,) * 4,
        [
            VMEM((128, D), BF16),
            big,
            big,
            big,
            half,
            half,
            half,
            square,
            square,
            tall,
            tall,
            tall,
            VMEM((4, 256, 128), F32),
            VMEM((3, 1024, 128), F32),
            VMEM((8, 128), jnp.int32),
            VMEM((4, 8, 128), jnp.int32),
            unit,
            unit,
            VMEM((1, 256), F32),
            VMEM((128, D), F32),
            VMEM((128, D), F32),
            VMEM((128, D), F32),
            own,
            stats,
            VMEM((2, 4, 512), F32),
            VMEM((2, 8, 4, 512), F32),
            own,
            stats,
            VMEM((2, 4, 64, D), BF16),
            VMEM((2, 6, 32, D), BF16),
            grid_land,
            grid_land,
            VMEM((2, 5, 6, 32, 256), BF16),
            VMEM((3, 2, 2, 32, 1024), BF16),
            unit,
            VMEM((2, 8, 256), F32),
            VMEM((2, 8, 1024), F32),
            VMEM((4, 8, D), F32),
            VMEM((4, D), F32),
            VMEM((8, 4, D), F32),
            VMEM((16, 4, D), F32),
            VMEM((4, D), F32),
            VMEM((1, 2560), F32),
            VMEM((16, 1, 2560), F32),
            VMEM((1, 2560), F32),
        ],
        63,
        (46, 195, 36),
    )


def last_kernel(
    layer_in, input_in, shard_qkv, shard_proj, shard_up, shard_down, outer, inner,
    layer_out, grad_input, gain1, bias1, query, key, value, inner_gain, inner_bias, proj,
    gain2, bias2, up, ffn_gain, ffn_bias, down,
):
    layer_out[...] = layer_in[...]
    grad_input[...] = input_in[...]
    for i, ref in enumerate((gain1, bias1, gain2, bias2)):
        ref[...] = outer[i : i + 1, :]
    for d in range(4):
        for i, ref in enumerate((query, key, value)):
            ref[:, 256 * d : 256 * d + 256] = shard_qkv[d, :, 256 * i : 256 * i + 256].astype(F32)
        proj[:, 256 * d : 256 * d + 256] = shard_proj[d].astype(F32)
        up[:, 1024 * d : 1024 * d + 1024] = shard_up[d].astype(F32)
        down[:, 1024 * d : 1024 * d + 1024] = shard_down[d].astype(F32)
        for ref, lane, n in (
            (inner_gain, 0, 256), (inner_bias, 256, 256), (ffn_gain, 512, 1024), (ffn_bias, 1536, 1024),
        ):
            ref[:, n * d : n * d + n] = inner[d, :, lane : lane + n]


def whole(dims):
    return pl.BlockSpec(dims, lambda i: (0,) * len(dims))


def last_call(*ins):
    row, small, big = shape((1, D), F32), shape((32, 1024), F32), shape((32, 4096), F32)
    rows = shape((128, D), BF16)
    unit, wide = shape((1, 1024), F32), shape((1, 4096), F32)
    outs = (
        rows, rows, row, row, small, small, small, unit, unit, small, row, row, big, wide, wide, big,
    )
    return pl.pallas_call(
        last_kernel,
        out_shape=outs,
        grid=(1,),
        in_specs=[whole(v.shape) for v in ins],
        out_specs=[whole(v.shape) for v in outs],
        compiler_params=pltpu.CompilerParams(vmem_limit_bytes=63 << 20),
        name="results",
    )(*ins)


def per_device(
    tokens, caption_len, norm1_gain, norm1_bias, w_query, w_key, w_value, inner_gain, inner_bias,
    w_proj, norm2_gain, norm2_bias, w_up, ffn_norm_gain, ffn_norm_bias, w_down, cotangent,
):
    table = jnp.asarray(tables().reshape(1024, 256))
    line = lambda v: v.reshape(1, -1)
    *_, down, up, proj, qkv, layer_out, grad_input, outer, inner = layer_call((
        tokens, caption_len, line(norm1_gain), line(norm1_bias), line(inner_gain), line(inner_bias),
        line(norm2_gain), line(norm2_bias), line(ffn_norm_gain), line(ffn_norm_bias), cotangent,
        w_query, w_key, w_value, w_proj.T, w_up, w_down.T, table,
    ))
    (
        layer_out, grad_input, gain1, bias1, query, key, value, gain_i, bias_i, proj, gain2, bias2,
        up, gain_f, bias_f, down,
    ) = last_call(layer_out, grad_input, qkv, proj, up, down, outer, inner)
    flat = lambda v: v.reshape(-1)
    return (
        layer_out, grad_input, flat(gain1), flat(bias1), query, key, value, flat(gain_i),
        flat(bias_i), proj.T, flat(gain2), flat(bias2), up, flat(gain_f), flat(bias_f), down.T,
    )


def solution(mesh):
    rows = P(("seq", "ffn"), None)
    by_rows_, by_columns, half = P("seq", "ffn"), P("ffn", "seq"), P("ffn")
    return jax.shard_map(
        per_device,
        mesh=mesh,
        in_specs=(
            rows, P("seq"), P(), P(), by_rows_, by_rows_, by_rows_, half, half, by_columns,
            P(), P(), by_rows_, half, half, by_columns, rows,
        ),
        out_specs=(
            rows, rows, P(), P(), by_rows_, by_rows_, by_rows_, half, half, by_columns,
            P(), P(), by_rows_, half, half, by_columns,
        ),
        check_vma=False,
    )
```

```python
import functools

import jax
import jax.numpy as jnp
import numpy as np
from jax import lax
from jax.experimental import pallas as pl
from jax.experimental.pallas import tpu as pltpu
from jax.sharding import PartitionSpec as P

D = 2048
HEAD_DIM = 64
FF = 8192
SLOTS = 256
IMAGE = 64
EPS = 1e-05
F32 = jnp.float32
BF16 = jnp.bfloat16
MESH = pl.DeviceIdType.MESH
VMEM = pltpu.VMEM
HBM = pltpu.HBM


def device_at(y, x, z, c):
    return (((y * 2 + x % 2) * 4 + z) * 2 + c, x // 2)


def line_slot(x, c):
    return ((x % 2) * 2 + c) * 2 + x // 2


class Net:
    def __init__(self, send, recv, local):
        seq, ffn = lax.axis_index("seq"), lax.axis_index("ffn")
        self.y, self.z, self.c = seq // 16, (seq // 2) % 4, seq % 2
        self.x = ffn * 2 + (seq // 8) % 2
        self.send, self.recv, self.local = send, recv, local
        self.n_send, self.n_recv, self.n_local = 0, 0, 0

    def along_x(self, dx, dc=0):
        return device_at(self.y, (self.x + dx) % 4, self.z, (self.c + dc) % 2)

    def along_y(self, dy):
        return device_at((self.y + dy) % 4, self.x, self.z, self.c)

    def along_z(self, dz):
        return device_at(self.y, self.x, (self.z + dz) % 4, self.c)

    def pair(self, dx, dc):
        x = (self.x // 2) * 2 + (self.x + dx) % 2
        return device_at(self.y, x, self.z, (self.c + dc) % 2)

    def greet(self, partners):
        self.barrier, self.partners = pltpu.get_barrier_semaphore(), len(partners)
        for partner in partners:
            pl.semaphore_signal(self.barrier, inc=1, device_id=partner, device_id_type=MESH)

    def met(self):
        pl.semaphore_wait(self.barrier, self.partners)

    def out(self):
        self.n_send += 1
        return self.send.at[self.n_send - 1]

    def into(self):
        self.n_recv += 1
        return self.recv.at[self.n_recv - 1]

    def push(self, src, dst, device, out, into):
        pltpu.make_async_remote_copy(
            src_ref=src,
            dst_ref=dst,
            send_sem=out,
            recv_sem=into,
            device_id=device,
            device_id_type=MESH,
        ).start()

    def copies(self, semaphore, same_bytes):
        return pltpu.make_async_remote_copy(
            src_ref=same_bytes,
            dst_ref=same_bytes,
            send_sem=semaphore,
            recv_sem=semaphore,
            device_id=self.along_x(0, 1),
            device_id_type=MESH,
        )

    def arrived(self, into, same_bytes):
        self.copies(into, same_bytes).wait_recv()

    def left(self, out, same_bytes):
        self.copies(out, same_bytes).wait_send()

    def keep(self, src, dst):
        copy = pltpu.make_async_copy(src, dst, self.local.at[self.n_local])
        self.n_local += 1
        copy.start()
        return copy

    def close(self):
        found = self.n_send, self.n_recv, self.n_local
        assert found == tuple(s.shape[0] for s in (self.send, self.recv, self.local)), found


def add_into(dst, *terms):
    def step(i, carry):
        rows = pl.ds(pl.multiple_of(i * 16, 16), 16)
        total = terms[0][rows, :].astype(F32)
        for term in terms[1:]:
            total = total + term[rows, :].astype(F32)
        dst[rows, :] = total.astype(dst.dtype)
        return carry

    lax.fori_loop(0, dst.shape[0] // 16, step, 0)


def slot_row(slot, off, n, by_parts):
    return pl.multiple_of(off * 8 + slot * 64 if by_parts else slot * 128 + off, n)


class LineGather:
    def __init__(self, net, own, full, off=0, n=128, by_parts=False):
        self.net, self.full, self.off, self.n, self.by_parts = net, full, off, n, by_parts
        self.own = own.at[pl.ds(off, n)]
        self.own_half = [own.at[pl.ds(off + n // 2 * h, n // 2)] for h in range(2)]
        self.out = net.out()
        self.first, self.second, self.third, self.near, self.rest = (net.into() for _ in range(5))

    def block(self, dx, dc=0, half=None):
        net, n = self.net, self.n
        base = slot_row(line_slot((net.x + dx) % 4, (net.c + dc) % 2), self.off, n, self.by_parts)
        if half is None:
            return self.full.at[pl.ds(base, n)]
        return self.full.at[pl.ds(pl.multiple_of(base + n // 2 * half, n // 2), n // 2)]

    def push(self, src, dst, device, into):
        self.net.push(src, dst, device, self.out, into)

    def same(self, ref, device, into):
        self.net.push(ref, ref, device, self.out, into)

    def bytes_of(self, k):
        return self.full.at[pl.ds(0, k * self.n)]

    def start_first(self):
        net = self.net
        self.push(self.own_half[0], self.block(0, 0, 0), net.along_x(1), self.first)
        self.push(self.own_half[1], self.block(0, 0, 1), net.along_x(-1), self.first)

    def start_second(self):
        net = self.net
        self.push(self.own_half[1], self.block(0, 0, 1), net.along_x(1), self.second)
        self.push(self.own_half[0], self.block(0, 0, 0), net.along_x(-1), self.second)
        self.push(self.own, self.block(0), net.along_x(0, 1), self.rest)
        self.kept = net.keep(self.own, self.block(0))

    def start(self):
        self.start_first()
        self.start_second()

    def forward_first(self):
        net = self.net
        net.arrived(self.first, self.bytes_of(1))
        self.same(self.block(-1, 0, 0), net.along_x(1), self.third)
        self.same(self.block(1, 0, 1), net.along_x(-1), self.third)

    def forward_second(self):
        net = self.net
        net.arrived(self.second, self.bytes_of(1))
        self.same(self.block(-1), net.along_x(0, 1), self.near)
        self.same(self.block(1), net.along_x(0, 1), self.near)

    def forward(self):
        self.forward_first()
        self.forward_second()

    def share(self):
        net = self.net
        net.arrived(self.third, self.bytes_of(1))
        self.same(self.block(2, 0, 0), net.along_x(0, 1), self.rest)
        self.same(self.block(2, 0, 1), net.along_x(0, 1), self.rest)

    def finish_near(self):
        self.net.arrived(self.near, self.bytes_of(2))

    def finish(self):
        self.net.arrived(self.rest, self.bytes_of(2))
        self.kept.wait()

    def sent(self):
        self.net.left(self.out, self.bytes_of(7))


class RingSum:
    def __init__(self, net, mine, landing, ahead, behind, out):
        self.net, self.mine, self.landing = net, mine, landing
        self.ahead, self.behind, self.out = ahead, behind, out
        self.far, self.near = net.into(), net.into()

    def start_far(self):
        net, land = self.net, self.landing
        net.push(self.mine(2, 0), land.at[0], self.ahead, self.out, self.far)
        net.push(self.mine(2, 1), land.at[1], self.behind, self.out, self.far)

    def start_near(self, d):
        net, land = self.net, self.landing
        if d == 1:
            net.push(self.mine(1, 1), land.at[3], self.ahead, self.out, self.near)
        else:
            net.push(self.mine(-1, 0), land.at[4], self.behind, self.out, self.near)

    def pass_on(self):
        net, land = self.net, self.landing
        net.arrived(self.far, land.at[pl.ds(0, 2)])
        add_into(land.at[0], land.at[0], self.mine(1, 0))
        net.push(land.at[0], land.at[2], self.ahead, self.out, self.near)
        add_into(land.at[1], land.at[1], self.mine(-1, 1))
        net.push(land.at[1], land.at[5], self.behind, self.out, self.near)

    def finish(self, out=None, onto=False):
        net, land = self.net, self.landing
        net.arrived(self.near, land.at[pl.ds(2, 4)])
        for h in (0, 1):
            to = land.at[2 + h] if out is None else out(h)
            terms = self.mine(0, h), land.at[2 + h], land.at[4 + h]
            add_into(to, *terms, *([to] if onto else []))


class LineSum:
    def __init__(self, net, part, other, landing, off, by_parts):
        self.net, self.part, self.other, self.landing = net, part, other, landing
        self.off, self.by_parts = off, by_parts
        self.out, self.ring_out = net.out(), net.out()
        self.first, self.rest = net.into(), net.into()
        ends = net.along_x(1), net.along_x(-1)
        self.ring = RingSum(net, self.mine, landing, *ends, self.ring_out)

    def block(self, dx, dc):
        net = self.net
        slot = line_slot((net.x + dx) % 4, (net.c + dc) % 2)
        return self.part.at[pl.ds(slot_row(slot, self.off, 64, self.by_parts), 64)]

    def mine(self, d, half):
        return self.other.at[d % 4, pl.ds(32 * half, 32)]

    def start(self, *steps):
        for d in steps:
            into = self.first if d == 2 else self.rest
            place = self.other.at[d % 4]
            self.net.push(self.block(d, 1), place, self.net.along_x(0, 1), self.out, into)

    def add(self, d):
        add_into(self.other.at[d % 4], self.other.at[d % 4], self.block(d, 0))

    def chip_far(self):
        self.net.arrived(self.first, self.other.at[0])
        self.add(2)
        self.ring.start_far()

    def chip_near(self):
        self.net.arrived(self.rest, self.other.at[pl.ds(0, 3)])
        self.add(1)
        self.ring.start_near(1)
        self.add(-1)
        self.ring.start_near(-1)
        self.add(0)

    def part_sent(self):
        self.net.left(self.out, self.other)

    def pass_on(self):
        self.ring.pass_on()

    def finish(self, out, onto=False):
        self.ring.finish(lambda h: out.at[pl.ds(self.off + 32 * h, 32)], onto)

    def sent(self):
        self.net.left(self.ring_out, self.landing)


def line_sums(net, part, other, landing, by_parts):
    return [LineSum(net, part, other.at[k], landing.at[k], 64 * k, by_parts) for k in range(2)]


def line_gathers(net, own, full):
    return [LineGather(net, own, full, 64 * k, 64, True) for k in range(2)]


def shard_rows(ref, y, x_lo, z, c=None):
    if c is None:
        return ref.at[pl.ds(pl.multiple_of(((y * 2 + x_lo) * 4 + z) * 64, 64), 64)]
    return ref.at[pl.ds(pl.multiple_of((((y * 2 + x_lo) * 4 + z) * 2 + c) * 32, 32), 32)]


PAIR_STEPS = ((1, 0), (1, 1), (0, 1))


class GridGather:
    def __init__(self, net, pieces, full):
        self.net, self.pieces, self.full = net, pieces, full
        self.out, self.pair_out = net.out(), net.out()
        self.pair_into, self.last = net.into(), net.into()
        self.p, self.f = [net.into(), net.into()], [net.into(), net.into()]
        self.q = {(t, dp): net.into() for t in (0, 1) for dp in (0, -1, 1, 2)}

    def bytes_of(self, rows):
        return self.full.at[pl.ds(0, rows)]

    def exchange(self):
        net = self.net
        spot = shard_rows(self.full, net.y, net.x % 2, net.z, net.c)
        for dx, dc in PAIR_STEPS:
            to = ((net.x + dx) % 2) * 2 + (net.c + dc) % 2
            net.push(self.piece(to), spot, net.pair(dx, dc), self.pair_out, self.pair_into)
        self.kept = net.keep(self.piece((net.x % 2) * 2 + net.c), spot)

    def piece(self, d):
        return self.pieces.at[pl.ds(pl.multiple_of(32 * d, 32), 32)]

    def slab(self, t, dp, dq, half=None):
        net = self.net
        dy, dz = (dq, dp) if t == 0 else (dp, dq)
        return shard_rows(self.full, (net.y + dy) % 4, t, (net.z + dz) % 4, half)

    def to_p(self, t, d):
        return self.net.along_z(d) if t == 0 else self.net.along_y(d)

    def to_q(self, t, d):
        return self.net.along_y(d) if t == 0 else self.net.along_z(d)

    def same(self, ref, device, into):
        self.net.push(ref, ref, device, self.out, into)

    def second(self, t, dp):
        for d in (1, -1):
            self.same(self.slab(t, dp, 0), self.to_q(t, d), self.q[t, dp])

    def start(self):
        self.net.arrived(self.pair_into, self.bytes_of(96))
        self.kept.wait()
        for t in (0, 1):
            for d in (1, -1):
                self.same(self.slab(t, 0, 0), self.to_p(t, d), self.p[t])
        for t in (0, 1):
            self.second(t, 0)

    def near(self):
        for t in (0, 1):
            self.net.arrived(self.p[t], self.bytes_of(128))
            self.same(self.slab(t, -1, 0, 0), self.to_p(t, 1), self.f[t])
            self.same(self.slab(t, 1, 0, 1), self.to_p(t, -1), self.f[t])
        for t in (0, 1):
            self.second(t, -1)
            self.second(t, 1)

    def far(self):
        for t in (0, 1):
            self.net.arrived(self.f[t], self.bytes_of(64))
            self.second(t, 2)

    def pass_on(self, dp):
        for t in (0, 1):
            self.net.arrived(self.q[t, dp], self.bytes_of(128))
            self.same(self.slab(t, dp, -1, 0), self.to_q(t, 1), self.last)
            self.same(self.slab(t, dp, 1, 1), self.to_q(t, -1), self.last)

    def finish(self):
        self.net.arrived(self.last, self.bytes_of(512))

    def pair_sent(self):
        self.net.left(self.pair_out, self.bytes_of(96))

    def sent(self):
        self.net.left(self.out, self.bytes_of(1920))


class GridSum:
    def __init__(self, net, part, landing, done, shard):
        self.net, self.part, self.landing, self.done, self.shard = net, part, landing, done, shard
        self.out, self.pair_out, self.pair_into = net.out(), net.out(), net.into()
        self.rings = {}
        for t in (0, 1):
            for dp in (2, 1, -1, 0):
                self.rings[t, dp] = RingSum(
                    net,
                    functools.partial(self.term, t, dp),
                    landing.at[t, dp % 4],
                    self.to_q(t, 1),
                    self.to_q(t, -1),
                    self.out,
                )
            self.rings[t] = RingSum(
                net,
                functools.partial(self.column, t),
                landing.at[t, 4],
                self.to_p(t, 1),
                self.to_p(t, -1),
                self.out,
            )
        self.steps = [
            functools.partial(self.pass_on, 2),
            functools.partial(self.pass_on, 1),
            functools.partial(self.pass_on, -1),
            functools.partial(self.finish, 2),
            functools.partial(self.pass_on, 0),
            functools.partial(self.finish, 1),
            functools.partial(self.finish, -1),
            self.pass_on_last,
            functools.partial(self.finish, 0),
            self.finish_last,
            self.collect,
        ]

    def to_p(self, t, d):
        return self.net.along_z(d) if t == 0 else self.net.along_y(d)

    def to_q(self, t, d):
        return self.net.along_y(d) if t == 0 else self.net.along_z(d)

    def term(self, t, dp, dq, half):
        net = self.net
        dy, dz = (dq, dp) if t == 0 else (dp, dq)
        return shard_rows(self.part, (net.y + dy) % 4, t, (net.z + dz) % 4, half)

    def column(self, t, dp, half):
        return self.landing.at[t, dp % 4, 2 + half]

    def start(self, dy):
        for dp in (2, 1, -1, 0):
            if dy == 2:
                self.rings[0, dp].start_far()
            elif dy:
                self.rings[0, dp].start_near(dy)
        self.rings[1, dy].start_far()
        self.rings[1, dy].start_near(1)
        self.rings[1, dy].start_near(-1)

    def step(self, n=1):
        for _ in range(n):
            self.steps.pop(0)()

    def pass_on(self, dp):
        for t in (0, 1):
            self.rings[t, dp].pass_on()

    def finish(self, dp):
        for t in (0, 1):
            self.rings[t, dp].finish()
            if dp == 2:
                self.rings[t].start_far()
            elif dp:
                self.rings[t].start_near(dp)

    def pass_on_last(self):
        for t in (0, 1):
            self.rings[t].pass_on()

    def finish_last(self):
        net = self.net
        for t in (0, 1):
            self.rings[t].finish(lambda half: self.done.at[t, half])
        me = (net.x % 2) * 2 + net.c
        for dx, dc in PAIR_STEPS:
            src = self.done.at[(net.x + dx) % 2, (net.c + dc) % 2]
            net.push(src, self.shard.at[me], net.pair(dx, dc), self.pair_out, self.pair_into)
        self.kept = net.keep(self.done.at[net.x % 2, net.c], self.shard.at[me])

    def collect(self):
        self.net.arrived(self.pair_into, self.shard.at[pl.ds(0, 3)])
        self.kept.wait()

    def sent(self):
        self.net.left(self.out, self.part.at[pl.ds(0, 1920)])

    def pair_sent(self):
        self.net.left(self.pair_out, self.shard.at[pl.ds(0, 3)])


class SmallSum:
    def __init__(self, net, own, slots, me, partners):
        self.net, self.own, self.slots, self.me, self.partners = net, own, slots, me, partners
        self.out, self.into = net.out(), net.into()

    def start(self):
        for to, _ in self.partners:
            self.net.push(self.own, self.slots.at[self.me], to, self.out, self.into)
        self.slots[self.me] = self.own[...]

    def total(self):
        self.net.arrived(self.into, self.slots.at[pl.ds(0, len(self.partners))])
        total = self.slots[0]
        for i in range(1, self.slots.shape[0]):
            total = total + self.slots[i]
        return total

    def finish(self, out):
        out[...] = self.total()

    def sent(self):
        self.net.left(self.out, self.slots.at[pl.ds(0, len(self.partners))])


class PairShare:
    def __init__(self, net, own, slots):
        self.net, self.own, self.slots = net, own, slots
        self.out, self.into = net.out(), net.into()

    def start(self):
        net = self.net
        me = (net.x % 2) * 2 + net.c
        for dx, dc in PAIR_STEPS:
            net.push(self.own, self.slots.at[me], net.pair(dx, dc), self.out, self.into)
        self.slots[me] = self.own[...]

    def finish(self):
        self.net.arrived(self.into, self.slots.at[pl.ds(0, 3)])

    def sent(self):
        self.net.left(self.out, self.slots.at[pl.ds(0, 3)])


def line_partners(net):
    return [
        (net.along_x(dx, dc), ((net.x - dx) % 4) * 2 + (net.c + dc) % 2)
        for dx in range(4)
        for dc in range(2)
        if dx or dc
    ]


def grid_partners(net):
    return [
        (
            device_at((net.y + dy) % 4, net.x, (net.z + dz) % 4, net.c),
            ((net.y - dy) % 4) * 4 + (net.z - dz) % 4,
        )
        for dy in range(4)
        for dz in range(4)
        if dy or dz
    ]


def grid_neighbours(net):
    return [net.along_y(1), net.along_y(-1), net.along_z(1), net.along_z(-1)]


def spec(space):
    return pl.BlockSpec(memory_space=space)


def shape(dims, dtype):
    return jax.ShapeDtypeStruct(dims, dtype)


class Staged:
    def __init__(self, loads, stores):
        self.loads, self.stores, self.started = loads, stores, []
        for copy, _ in loads:
            copy.start()

    def wait(self, *refs):
        for copy, ref in list(self.loads):
            if not refs or any(ref is r for r in refs):
                copy.wait()
                self.loads = [pair for pair in self.loads if pair[1] is not ref]

    def put(self, *refs):
        for copy, ref in list(self.stores):
            if not refs or any(ref is r for r in refs):
                copy.start()
                self.started.append(copy)
                self.stores = [pair for pair in self.stores if pair[1] is not ref]

    def finish(self):
        self.wait()
        self.put()
        for copy in self.started:
            copy.wait()


def comm_call(body, name, collective_id, ins, in_spaces, outs, out_spaces, scratch, mib, sems):
    n_in, n_out = len(ins), len(outs)
    buffers = [space(v.shape, v.dtype) for v, space in zip(ins, in_spaces) if space is not HBM]
    buffers += [space(v.shape, v.dtype) for v, space in zip(outs, out_spaces) if space is not HBM]
    n = len(buffers)

    def kernel(*refs):
        sem = refs[-1]
        rest = list(refs[n_in + n_out : n_in + n_out + n])
        loads, stores, args = [], [], []
        for i, (ref, space) in enumerate(zip(refs, (*in_spaces, *out_spaces))):
            if space is HBM:
                args.append(ref)
                continue
            buffer = rest.pop(0)
            args.append(buffer)
            at = sem.at[len(loads) + len(stores)]
            if i < n_in:
                loads.append((pltpu.make_async_copy(ref, buffer, at), buffer))
            else:
                stores.append((pltpu.make_async_copy(buffer, ref, at), buffer))
        io = Staged(loads, stores)
        body(io, *args, *refs[n_in + n_out + n : -1])
        io.finish()

    return pl.pallas_call(
        kernel,
        out_shape=outs,
        in_specs=[spec(HBM)] * n_in,
        out_specs=[spec(HBM)] * n_out,
        scratch_shapes=buffers
        + scratch
        + [pltpu.SemaphoreType.REGULAR((3,))]
        + [pltpu.SemaphoreType.DMA((k,)) for k in (*sems, n)],
        compiler_params=pltpu.CompilerParams(
            collective_id=collective_id, has_side_effects=True, vmem_limit_bytes=mib << 20
        ),
        name=name,
    )(*ins)


def norm_parts(values):
    center = jnp.mean(values, -1, keepdims=True)
    spread = jnp.mean(values * values, -1, keepdims=True) - center * center
    inv_std = lax.rsqrt(spread + EPS)
    return (values - center) * inv_std, inv_std


def by_rows(rows, step, chunk=16, off=0):
    def body(i, carry):
        step(pl.ds(pl.multiple_of(off + i * chunk, chunk), chunk))
        return carry

    lax.fori_loop(0, rows // chunk, body, 0)


def norm_back(grad, gain, hat, inv_std):
    scaled = grad * gain
    return inv_std * (
        scaled
        - jnp.mean(scaled, -1, keepdims=True)
        - hat * jnp.mean(scaled * hat, -1, keepdims=True)
    )


def fold8(values):
    return values[:8] + values[8:]


def block_rows(base, step):
    def body(i, carry):
        step(
            pl.ds(pl.multiple_of(i * 16, 16), 16),
            pl.ds(pl.multiple_of(base + i * 16, 16), 16),
        )
        return carry

    lax.fori_loop(0, 16, body, 0)


def lane_sums(values):
    total = values[:, :128]
    for k in range(1, values.shape[1] // 128):
        total = total + values[:, 128 * k : 128 * k + 128]
    return total


def row_of(partial):
    return jnp.sum(partial.T, 0, keepdims=True)


def spread(row):
    return jnp.broadcast_to(row, (128, row.shape[1])).T


def wide(values, lanes):
    return jnp.concatenate([values] * (lanes // 128), 1)


def xpos_tables(direction):
    half = HEAD_DIM // 2
    pair = np.arange(half, dtype=np.float32)
    frequency = np.power(np.float32(10000.0), -pair / half).astype(np.float32)
    zeta = ((pair / half + 0.4) / 1.4).astype(np.float32)
    position = np.arange(SLOTS, dtype=np.float32)[:, None]
    angle = (position * frequency).astype(np.float32).astype(np.float64)
    decay = np.exp(direction * position / 512.0 * np.log(zeta.astype(np.float64)))
    cosine, sine = np.cos(angle) * decay, np.sin(angle) * decay
    cosine = np.concatenate([cosine] * 2, -1)
    sine = np.concatenate([-sine, sine], -1)
    return np.tile(cosine, (1, 4)).astype(np.float32), np.tile(sine, (1, 4)).astype(np.float32)


def tables():
    return np.stack([*xpos_tables(1.0), *xpos_tables(-1.0)])


def swapped(values):
    lane = lax.broadcasted_iota(jnp.int32, values.shape, 1)
    return jnp.where(lane % 64 < 32, pltpu.roll(values, 224, 1), pltpu.roll(values, 32, 1))


def dot_nn(a, b):
    return lax.dot_general(a, b, (((1,), (0,)), ((), ())), preferred_element_type=F32)


def dot_nt(a, b):
    return lax.dot_general(a, b, (((1,), (1,)), ((), ())), preferred_element_type=F32)


def dot_tn(a, b):
    return lax.dot_general(a, b, (((0,), (0,)), ((), ())), preferred_element_type=F32)


def head_of(values, head):
    lane = lax.broadcasted_iota(jnp.int32, values.shape, 1)
    return jnp.where(lane // 64 == head, values, jnp.zeros_like(values))


def head_probs(query, key, head, allowed):
    scores = dot_nt(head_of(query, head), key) * HEAD_DIM**-0.5
    scores = jnp.where(allowed, scores, -1e30)
    exps = jnp.exp(scores - jnp.max(scores, -1, keepdims=True))
    return exps / jnp.sum(exps, -1, keepdims=True)


def allowed_slots(cap):
    query = lax.broadcasted_iota(jnp.int32, (SLOTS, SLOTS), 0)
    key = lax.broadcasted_iota(jnp.int32, (SLOTS, SLOTS), 1)
    return (key <= query) & (key < IMAGE + cap[0:1, 0:1])


def attend(rows, weights, cap, table, at, kept, mixed):
    qkv = dot_nn(rows, weights[:, :768])
    query, key, value = qkv[:, :256], qkv[:, 256:512], qkv[:, 512:].astype(BF16)
    query = (query * table(0) + swapped(query) * table(1)).astype(BF16)
    key = (key * table(2) + swapped(key) * table(3)).astype(BF16)
    for i, part in enumerate((query, key, value)):
        kept[at, 256 * i : 256 * i + 256] = part
    allowed = allowed_slots(cap)
    total = jnp.zeros((SLOTS, 256), F32)
    for head in range(4):
        probs = head_probs(query, key, head, allowed).astype(BF16)
        total = total + dot_nn(probs, head_of(value, head))
    mixed[at, :256] = total


def attend_back(query, key, value, grad, cap, table):
    allowed = allowed_slots(cap)
    grad_query = jnp.zeros((SLOTS, 256), F32)
    grad_key = jnp.zeros((SLOTS, 256), F32)
    grad_value = jnp.zeros((SLOTS, 256), F32)
    for head in range(4):
        probs = head_probs(query, key, head, allowed)
        grad_head = head_of(grad, head)
        grad_probs = dot_nt(grad_head, value)
        grad_value = grad_value + dot_tn(probs.astype(BF16), grad_head)
        delta = jnp.sum(probs * grad_probs, -1, keepdims=True)
        grad_scores = (probs * (grad_probs - delta)).astype(BF16)
        grad_query = grad_query + dot_nn(grad_scores, head_of(key, head))
        grad_key = grad_key + dot_tn(grad_scores, head_of(query, head))
    grad_query = grad_query * HEAD_DIM**-0.5
    grad_key = grad_key * HEAD_DIM**-0.5
    return (
        (grad_query * table(0) + swapped(grad_query * table(1))).astype(BF16),
        (grad_key * table(2) + swapped(grad_key * table(3))).astype(BF16),
        grad_value.astype(BF16),
    )


def place_of(net):
    return (net.x % 2) * 2 + net.c


def my_lanes(ref, net, n):
    return ref[:, pl.ds(pl.multiple_of(place_of(net) * n, n), n)]


def sequence_at(net, q):
    seq_of = ((net.x + q // 2) % 2) * 2 + (net.c + 1 + q) % 2
    return pl.multiple_of(seq_of * SLOTS, SLOTS)


def rows_along_y(net, dy):
    return pl.ds(pl.multiple_of(((net.y + dy) % 4) * 512, 512), 512)


def layer_kernel(
    io, tokens, cap, gain1, bias1, inner_gain, inner_bias, gain2, bias2, ffn_gains, ffn_biases, cot,
    w_query, w_key, w_value, w_proj, w_up, w_down, table_in,
    rows1_out, weights1_out, kept_out, hat_out, shard_down, shard_up, shard_proj, shard_qkv,
    layer_out, grad_input, outer1_out, outer2_out, inner_out,
    own_rows, rows, cots, part, weights1, up, down, act, gffn, slope, kept, grad_up, partial, cols,
    caps_in, caps, ffn_gain, ffn_bias, my_gain, attended, grad_attended,
    proj_grads,     own_s, slots_s, own_u, slots_u, own_t, slots_t, other, landing, landing_down, landing_up,
    landing_proj, done, inner_inv, inner_sums, unit_sums, sums, outer, line_slots, grid_slots, line_whole,
    inner, inner_slots, inner_whole, credit, send, recv, local,
):
    net = Net(send, recv, local)
    others, grid = line_partners(net), grid_partners(net)
    net.greet([to for to, _ in others + grid])
    me, me_grid = net.x * 2 + net.c, net.y * 4 + net.z
    shards = [w_query, w_key, w_value, w_proj]
    load1 = [net.keep(w, act.at[pl.ds(32 * i, 32)]) for i, w in enumerate(shards)]
    load_table = net.keep(table_in, gffn.at[:, pl.ds(0, 256)])
    load2 = [
        net.keep(w.at[:, pl.ds(1024 * d, 1024)], act.at[pl.ds(128 + 128 * i + 32 * d, 32)])
        for i, w in enumerate((w_down, w_up))
        for d in range(4)
    ]
    gather1 = GridGather(
        net, slope.at[pl.ds(0, 128), pl.ds(0, 768)], weights1.at[:, pl.ds(0, 768)]
    )
    gather_proj = GridGather(
        net, slope.at[pl.ds(0, 128), pl.ds(768, 256)], weights1.at[:, pl.ds(768, 256)]
    )
    gather_down = GridGather(net, slope.at[pl.ds(128, 128)], down)
    gather_up = GridGather(net, slope.at[pl.ds(256, 128)], up)
    line1 = LineGather(net, own_rows, rows)
    line_cot = line_gathers(net, cot, cots)
    total = line_sums(net, part, other, landing, False)
    line2 = line_gathers(net, own_rows, rows)
    sum_s = SmallSum(net, own_s, slots_s, me, others)
    share_caps = PairShare(net, caps_in, caps)

    for i in range(4):
        load1[i].wait()
        for d in range(4):
            slope[32 * d : 32 * d + 32, 256 * i : 256 * i + 256] = act[
                32 * i : 32 * i + 32, 256 * d : 256 * d + 256
            ].astype(BF16)
    io.wait(tokens, cap, gain1, bias1)

    def norm1(at):
        one, _ = norm_parts(tokens[at, :].astype(F32))
        own_rows[at, :] = (one * gain1[...] + bias1[...]).astype(BF16)

    by_rows(128, norm1)
    caps_in[...] = jnp.full((8, 128), cap[0], jnp.int32)

    net.met()
    gather1.exchange()
    line1.start()
    gather_proj.exchange()
    share_caps.start()
    gather1.start()
    for copy in load2:
        copy.wait()
    slope[128:384, :] = act[128:384, :].astype(BF16)
    io.wait()
    for ref in (unit_sums, sums, inner_sums):
        ref[...] = jnp.zeros_like(ref)
    ffn_gain[...], ffn_bias[...] = my_lanes(ffn_gains, net, 1024), my_lanes(ffn_biases, net, 1024)
    my_gain[...] = my_lanes(inner_gain, net, 256)
    gather1.near()
    gather1.pass_on(0)
    gather1.far()
    line1.forward()
    gather_down.exchange()
    gather1.pass_on(-1)
    gather_proj.start()
    gather1.pass_on(1)
    gather1.pass_on(2)
    gather_up.exchange()
    for line in line_cot:
        line.start()
    gather_proj.near()
    gather_proj.pass_on(0)
    line1.finish_near()
    share_caps.finish()
    load_table.wait()
    gather1.finish()
    gather_proj.far()
    gather_down.start()

    table = lambda i: gffn[256 * i : 256 * i + 256, :256]
    for q in range(4):
        base = sequence_at(net, (q + 2) % 4)
        at = pl.ds(base, SLOTS)
        if q == 2:
            line1.finish()
            save_rows = net.keep(rows, rows1_out)
        attend(rows[at, :], weights1, caps.at[base // SLOTS], table, at, kept, act)
        both = act[at, :256]
        partial[0] = lane_sums(both)
        partial[1] = lane_sums(both * both)
        for i in range(2):
            own_s[i : i + 1, at] = row_of(partial[i])
        if q == 0:
            line1.share()
            gather_proj.pass_on(-1)
            gather_proj.pass_on(1)
        if q == 1:
            gather_proj.pass_on(2)
        if q == 2:
            gather_down.near()
            gather_down.pass_on(0)
            gather_up.start()
    sum_s.start()
    for line in line_cot:
        line.forward()
    gather_down.far()
    gather_proj.finish()
    save_weights = net.keep(weights1, weights1_out)
    both = sum_s.total()
    center = both[0:1] * (1.0 / D)
    inv_std = lax.rsqrt(both[1:2] * (1.0 / D) - center * center + EPS)
    inner_inv[...] = inv_std
    cols[0] = spread(center)
    cols[1] = spread(inv_std)
    my_bias = my_lanes(inner_bias, net, 256)

    def inner_norm(at):
        one = (act[at, :256] - wide(cols[0, at, :], 256)) * wide(cols[1, at, :], 256)
        act[at, 256:512] = one
        kept[at, 768:] = (one * my_gain[...] + my_bias).astype(BF16)

    by_rows(1024, inner_norm, 64)
    save_hat = net.keep(act.at[:, pl.ds(256, 256)], hat_out)
    save_kept = net.keep(kept, kept_out)
    save_rows.wait()
    line1.sent()
    for q in range(4):
        at = pl.ds(sequence_at(net, q), SLOTS)
        mine = kept[at, 768:]
        for h in range(2):
            part[at, 1024 * h : 1024 * h + 1024] = dot_nt(
                mine, weights1[1024 * h : 1024 * h + 1024, 768:]
            ).astype(BF16)
        for t in total:
            if q == 0:
                t.start(2)
            if q == 1:
                t.start(0)
                t.chip_far()
            if q == 2:
                t.start(1, -1)
    total[0].chip_near()
    total[0].pass_on()
    total[1].chip_near()
    gather_down.pass_on(-1)
    gather_down.pass_on(1)
    total[1].pass_on()
    for line in line_cot:
        line.share()
    gather_down.pass_on(2)
    gather_up.near()
    gather_up.pass_on(0)
    save_weights.wait()

    def norm2(at):
        values = tokens[at, :].astype(F32) + attended[at, :]
        attended[at, :] = values
        one, _ = norm_parts(values)
        own_rows[at, :] = (one * gain2[...] + bias2[...]).astype(BF16)

    def cot_rows(b):
        at = slice(256 * b, 256 * b + 256)
        gffn[at, :] = dot_nn(cots[at, :], down[...])

    total[0].finish(attended)
    by_rows(64, norm2)
    line2[0].start()
    gather_up.far()
    for line in line_cot:
        line.finish_near()
        line.finish()
    total[1].finish(attended)
    by_rows(64, norm2, 16, 64)
    line2[1].start_first()
    line2[0].forward_first()
    line2[1].start_second()
    gather_down.finish()
    gather_up.pass_on(-1)
    gather_up.pass_on(1)
    cot_rows(0)
    line2[0].forward_second()
    cot_rows(1)
    gather_up.pass_on(2)
    line2[1].forward_first()
    cot_rows(2)
    line2[0].share()
    cot_rows(3)
    line2[1].forward_second()
    gather_up.finish()
    for line in line2:
        line.finish_near()
    line2[0].finish()
    save_hat.wait()
    save_kept.wait()
    for t in total:
        t.part_sent()
        t.sent()
    for gather in (gather1, gather_proj, gather_down, gather_up):
        gather.pair_sent()

    sum_u = [SmallSum(net, own_u.at[k], slots_u.at[k], me, others) for k in range(2)]
    for k in range(2):
        if k == 1:
            line2[1].finish()
        for j in range(2):
            base = 512 * k + 256 * j
            act[base : base + 256, :] = dot_nn(rows[base : base + 256, :], up[...])

            def gelu(at, to):
                value = act[to, :]
                cdf = 0.5 * (1.0 + lax.erf(value * np.float32(0.5**0.5)))
                density = jnp.exp(-0.5 * value * value) * np.float32((2 * np.pi) ** -0.5)
                slope[to, :] = (cdf + value * density).astype(BF16)
                value = value * cdf
                act[to, :] = value
                partial[0, at, :] = lane_sums(value)
                partial[1, at, :] = lane_sums(value * value)
                grad = gffn[to, :]
                unit_sums[1] += fold8(grad)
                grad = grad * ffn_gain[...]
                partial[2, at, :] = lane_sums(grad)
                partial[3, at, :] = lane_sums(grad * value)

            block_rows(base, gelu)
            for i in range(4):
                own_u[k, i : i + 1, 256 * j : 256 * j + 256] = row_of(partial[i])
            if k == 0 and j == 0:
                line2[1].share()
        sum_u[k].start()

    total = line_sums(net, part, other, landing, True)
    ffn_b = kept
    for k in range(2):
        both = sum_u[k].total()
        center = both[0:1] * (1.0 / FF)
        inv_std = lax.rsqrt(both[1:2] * (1.0 / FF) - center * center + EPS)
        slant = (both[3:4] - center * both[2:3]) * inv_std * (1.0 / FF)
        its = slice(512 * k, 512 * k + 512)
        for i, row in enumerate((center, inv_std, both[2:3] * (1.0 / FF))):
            cols[i, its, :] = spread(row)

        def normed(at):
            hat = (act[at, :] - wide(cols[0, at, :], 1024)) * wide(cols[1, at, :], 1024)
            act[at, :] = hat
            ffn_b[at, :] = (hat * ffn_gain[...] + ffn_bias[...]).astype(BF16)
            unit_sums[0] += fold8(gffn[at, :] * hat)

        by_rows(512, normed, 16, 512 * k)
        cols[0, its, :] = spread(slant)
        if k == 1:
            total[0].chip_near()
        for j in range(2):
            base = pl.multiple_of(512 * k + 256 * ((net.x + j) % 2), 256)

            def back(at, to):
                grad = gffn[to, :] * ffn_gain[...] - wide(cols[2, to, :], 1024)
                grad = grad - act[to, :] * wide(cols[0, to, :], 1024)
                grad = grad * wide(cols[1, to, :], 1024)
                grad_up[to, :] = (grad * slope[to, :].astype(F32)).astype(BF16)

            block_rows(base, back)
            mine = grad_up[pl.ds(base, 256), :]
            for h in range(2):
                part[pl.ds(base, 256), 1024 * h : 1024 * h + 1024] = dot_nt(
                    mine, up[1024 * h : 1024 * h + 1024, :]
                ).astype(BF16)
            if j == 0:
                total[k].start(2, 0)
            else:
                total[k].start(1, -1)
                total[k].chip_far()
    total[0].pass_on()
    total[1].chip_near()

    weights_down = GridSum(net, weights1, landing_down, done.at[0], shard_down)
    weights_up = GridSum(net, up, landing_up, done.at[1], shard_up)
    lines = line_gathers(net, own_rows, part)

    def outer_sums(k):
        for i in range(2):
            outer[k, i : i + 1, :] = jnp.sum(sums[2 * k + i], 0, keepdims=True)
        return (
            SmallSum(net, outer.at[k], line_slots.at[k], me, others),
            SmallSum(net, line_whole.at[k], grid_slots.at[k], me_grid, grid),
        )

    def norm2_back(at):
        grad = grad_attended[at, :]
        one, inv = norm_parts(attended[at, :])
        sums[2] += fold8(grad * one)
        sums[3] += fold8(grad)
        value = cot[at, :].astype(F32) + norm_back(grad, gain2[...], one, inv)
        grad_attended[at, :] = value
        own_rows[at, :] = value.astype(BF16)

    def down_rows(dy):
        at = rows_along_y(net, dy)
        weights1[at, :] = dot_tn(cots[:, at], ffn_b[...]).astype(BF16)
        weights_down.start(dy)

    def out_rows(b):
        for h in range(2):
            cots[256 * b : 256 * b + 256, 1024 * h : 1024 * h + 1024] = dot_nt(
                ffn_b[256 * b : 256 * b + 256, :], down[1024 * h : 1024 * h + 1024, :]
            ).astype(BF16)

    def up_rows(dy):
        at = rows_along_y(net, dy)
        up[at, :] = dot_tn(rows[:, at], grad_up[...]).astype(BF16)
        weights_up.start(dy)

    load_hat = net.keep(hat_out, act.at[:, pl.ds(0, 256)])
    load_kept = net.keep(kept_out, slope)
    load_table = net.keep(table_in, gffn.at[:, pl.ds(0, 256)])
    for sender in line2 + line_cot + [gather1, gather_proj, gather_down, gather_up]:
        sender.sent()
    for t in total:
        t.part_sent()
    pl.semaphore_signal(credit.at[0], inc=1, device_id=net.along_x(0, 1), device_id_type=MESH)
    down_rows(2)
    down_rows(1)
    total[1].pass_on()
    down_rows(-1)
    pl.semaphore_wait(credit.at[0], 1)
    total[0].finish(grad_attended)
    total[0].sent()
    by_rows(64, norm2_back)
    lines[0].start()
    down_rows(0)
    out_rows(0)
    out_rows(1)
    total[1].finish(grad_attended)
    total[1].sent()
    by_rows(64, norm2_back, 16, 64)
    lines[1].start()
    outer2_x, outer2_grid = outer_sums(1)
    outer2_x.start()
    weights_down.step()
    lines[0].forward_first()
    out_rows(2)
    weights_down.step()
    lines[0].forward_second()
    out_rows(3)
    load_weights = net.keep(weights1_out, down)
    weights_down.step()
    lines[1].forward_first()
    up_rows(2)
    weights_down.step()
    lines[1].forward_second()
    up_rows(1)
    lines[0].share()
    up_rows(-1)
    weights_down.step()
    lines[1].share()
    up_rows(0)
    load_rows = net.keep(rows1_out, rows)
    weights_down.step(2)
    lines[0].finish_near()
    lines[0].finish()
    outer2_x.finish(line_whole.at[1])
    outer2_grid.start()

    ctx_parts, grad_mixed, grads_qkv, gctx = kept.at[:, 256:512], kept.at[:, 0:256], grad_up, act
    sum_t = SmallSum(net, own_t, slots_t, me, others)
    load_hat.wait()
    load_kept.wait()
    load_table.wait()
    load_weights.wait()

    def context_grad(k):
        for j in range(2):
            base = 512 * k + 256 * j
            found = dot_nn(part[base : base + 256, :], down[:, 768:])
            for i in range(4):
                at = 128 * (4 * j + i) + 64 * k
                gctx[at : at + 64, 256:512] = found[64 * i : 64 * i + 64]
                ctx_parts[base + 64 * i : base + 64 * i + 64, :] = slope[at : at + 64, 768:]

    context_grad(0)
    lines[1].finish_near()
    lines[1].finish()
    total_out = line_sums(net, cots, other, landing, True)
    for t in total_out:
        t.start(2, 1, -1, 0)
    context_grad(1)
    for b in range(4):

        def scale(at, to):
            grad, one = gctx[to, 256:512], act[to, 0:256]
            inner_sums[0] += fold8(grad * one)
            inner_sums[1] += fold8(grad)
            grad = grad * my_gain[...]
            gctx[to, 256:512] = grad
            partial[0, at, :] = lane_sums(grad)
            partial[1, at, :] = lane_sums(grad * one)

        block_rows(256 * b, scale)
        for i in range(2):
            own_t[i : i + 1, 256 * b : 256 * b + 256] = row_of(partial[i])
    sum_t.start()
    for t in total_out:
        t.chip_far()
    for t in total_out:
        t.chip_near()
    weights_proj = GridSum(net, proj_grads, landing_proj, done.at[2, :, :, :, pl.ds(0, 256)], shard_proj)
    for dy in (2, 1, -1, 0):
        at = rows_along_y(net, dy)
        proj_grads[at, :] = dot_tn(ctx_parts[...], part[:, at]).T.astype(BF16)
        weights_proj.start(dy)
    for line in lines:
        line.sent()
    both = sum_t.total() * (1.0 / D)
    for i, row in enumerate((inner_inv[...], both[0:1], both[1:2])):
        cols[i] = spread(row)

    def mixed_grad(at):
        inv, mean, slant = (wide(cols[i, at, :], 256) for i in range(3))
        grad = gctx[at, 256:512] - mean - act[at, 0:256] * slant
        grad_mixed[at, :] = (grad * inv).astype(BF16)

    by_rows(1024, mixed_grad, 64)
    total = line_sums(net, part, other, landing, False)
    weights_qkv = GridSum(
        net, weights1.at[:, pl.ds(0, 768)], landing_down.at[:, :, :, :, pl.ds(0, 768)],
        done.at[2, :, :, :, pl.ds(256, 768)], shard_qkv,
    )

    def output(at):
        layer_out[at, :] = attended[at, :].astype(BF16)

    def qkv_rows(dy):
        at = rows_along_y(net, dy)
        weights1[at, :768] = dot_tn(rows[:, at], grads_qkv[:, :768]).astype(BF16)
        weights_qkv.start(dy)

    def first_rows(q):
        at = pl.ds(sequence_at(net, q), SLOTS)
        mine = grads_qkv[at, :768]
        for h in range(2):
            part[at, 1024 * h : 1024 * h + 1024] = dot_nt(
                mine, down[1024 * h : 1024 * h + 1024, :768]
            ).astype(BF16)

    for q in range(4):
        base = sequence_at(net, q)
        at = pl.ds(base, SLOTS)
        query, key, value = (slope[at, 256 * i : 256 * i + 256] for i in range(3))
        found = attend_back(query, key, value, grad_mixed[at, :], caps[base // SLOTS], table)
        for i in range(3):
            grads_qkv[at, 256 * i : 256 * i + 256] = found[i]
        if q == 0:
            weights_down.step(2)
            weights_up.step(2)
        if q == 1:
            weights_down.step()
            weights_down.sent()
            for to in grid_neighbours(net):
                pl.semaphore_signal(credit.at[2], inc=1, device_id=to, device_id_type=MESH)
            for t in total_out:
                t.pass_on()
            weights_up.step()
        if q == 2:
            weights_up.step(2)
            weights_proj.step(3)
        if q == 3:
            weights_up.step(2)
    for t in total_out:
        t.finish(attended, True)
        t.part_sent()
        t.sent()
    for to in (net.along_x(0, 1), net.along_x(1), net.along_x(-1)):
        pl.semaphore_signal(credit.at[1], inc=1, device_id=to, device_id_type=MESH)
    first_rows(0)
    pl.semaphore_wait(credit.at[1], 3)
    for t in total:
        t.start(2)
    first_rows(1)
    for t in total:
        t.start(0)
        t.chip_far()
    load_rows.wait()
    pl.semaphore_wait(credit.at[2], 4)
    qkv_rows(2)
    qkv_rows(1)
    first_rows(2)
    for t in total:
        t.start(1, -1)
    first_rows(3)
    for t in total:
        t.chip_near()
    qkv_rows(-1)
    qkv_rows(0)
    for t in total:
        t.pass_on()
    weights_up.step(2)
    weights_qkv.step(3)
    weights_proj.step(3)
    by_rows(128, output)
    io.put(layer_out)
    weights_qkv.step(2)
    for k, (lane, n) in enumerate(((0, 256), (256, 256), (512, 1024), (1536, 1024))):
        terms = inner_sums[k] if k < 2 else unit_sums[k - 2]
        inner[0:1, lane : lane + n] = jnp.sum(terms, 0, keepdims=True)
    inner_grid = SmallSum(net, inner, inner_slots, me_grid, grid)
    inner_grid.start()

    def norm1_back(at):
        grad = attended[at, :]
        one, inv = norm_parts(tokens[at, :].astype(F32))
        sums[0] += fold8(grad * one)
        sums[1] += fold8(grad)
        value = grad_attended[at, :] + norm_back(grad, gain1[...], one, inv)
        grad_input[at, :] = value.astype(BF16)

    total[0].finish(attended)
    by_rows(64, norm1_back)
    weights_up.step()
    weights_proj.step(3)
    weights_qkv.step(2)
    total[1].finish(attended)
    by_rows(64, norm1_back, 16, 64)
    io.put(grad_input)
    outer1_x, outer1_grid = outer_sums(0)
    outer1_x.start()
    weights_qkv.step(2)
    outer1_x.finish(line_whole.at[0])
    outer1_grid.start()
    weights_qkv.step()
    weights_proj.step()
    inner_grid.finish(inner_whole)
    share_inner = PairShare(net, inner_whole, inner_out)
    share_inner.start()
    for weights in (weights_down, weights_up, weights_proj):
        weights.step()
    outer2_grid.finish(outer2_out)
    outer1_grid.finish(outer1_out)
    share_inner.finish()
    io.put()
    weights_qkv.step()
    for t in total:
        t.part_sent()
    for sender in [*total, weights_up, weights_proj, weights_qkv, sum_s, *sum_u, sum_t]:
        sender.sent()
    for sender in (share_caps, share_inner, inner_grid, outer1_x, outer1_grid, outer2_x, outer2_grid):
        sender.sent()
    for weights in (weights_down, weights_up, weights_proj, weights_qkv):
        weights.pair_sent()
    net.close()


def layer_call(ins):
    big, half = VMEM((1024, D), BF16), VMEM((D, 1024), BF16)
    square, tall = VMEM((1024, 1024), F32), VMEM((1024, 1024), BF16)
    grid_land = VMEM((2, 5, 6, 32, 1024), BF16)
    unit, own, stats = VMEM((1, 1024), F32), VMEM((2, 1024), F32), VMEM((8, 2, 1024), F32)
    return comm_call(
        layer_kernel,
        "layer",
        1,
        ins,
        (VMEM, pltpu.SMEM) + (VMEM,) * 9 + (HBM,) * 7,
        (
            shape((1024, D), BF16),
            shape((D, 1024), BF16),
            shape((1024, 1024), BF16),
            shape((1024, 256), F32),
            shape((4, 32, 1024), BF16),
            shape((4, 32, 1024), BF16),
            shape((4, 32, 256), BF16),
            shape((4, 32, 768), BF16),
            shape((128, D), BF16),
            shape((128, D), BF16),
            shape((2, D), F32),
            shape((2, D), F32),
            shape((4, 1, 2560), F32),
        ),
        (HBM,) * 8 + (VMEM,) * 5,
        [
            VMEM((128, D), BF16),
            big,
            big,
            big,
            half,
            half,
            half,
            square,
            square,
            tall,
            tall,
            tall,
            VMEM((4, 256, 128), F32),
            VMEM((3, 1024, 128), F32),
            VMEM((8, 128), jnp.int32),
            VMEM((4, 8, 128), jnp.int32),
            unit,
            unit,
            VMEM((1, 256), F32),
            VMEM((128, D), F32),
            VMEM((128, D), F32),
            VMEM((D, 256), BF16),
            own,
            stats,
            VMEM((2, 4, 512), F32),
            VMEM((2, 8, 4, 512), F32),
            own,
            stats,
            VMEM((2, 4, 64, D), BF16),
            VMEM((2, 6, 32, D), BF16),
            grid_land,
            grid_land,
            VMEM((2, 5, 6, 32, 256), BF16),
            VMEM((3, 2, 2, 32, 1024), BF16),
            unit,
            VMEM((2, 8, 256), F32),
            VMEM((2, 8, 1024), F32),
            VMEM((4, 8, D), F32),
            VMEM((2, 2, D), F32),
            VMEM((2, 8, 2, D), F32),
            VMEM((2, 16, 2, D), F32),
            VMEM((2, 2, D), F32),
            VMEM((1, 2560), F32),
            VMEM((16, 1, 2560), F32),
            VMEM((1, 2560), F32),
        ],
        63,
        (50, 218, 37),
    )


def last_kernel(
    layer_in, input_in, shard_qkv, shard_proj, shard_up, shard_down, outer1, outer2, inner,
    layer_out, grad_input, gain1, bias1, query, key, value, inner_gain, inner_bias, proj,
    gain2, bias2, up, ffn_gain, ffn_bias, down,
):
    layer_out[...] = layer_in[...]
    grad_input[...] = input_in[...]
    for i, refs in enumerate(((gain1, gain2), (bias1, bias2))):
        refs[0][...] = outer1[i : i + 1, :]
        refs[1][...] = outer2[i : i + 1, :]
    for d in range(4):
        for i, ref in enumerate((query, key, value)):
            ref[:, 256 * d : 256 * d + 256] = shard_qkv[d, :, 256 * i : 256 * i + 256].astype(F32)
        proj[:, 256 * d : 256 * d + 256] = shard_proj[d].astype(F32)
        up[:, 1024 * d : 1024 * d + 1024] = shard_up[d].astype(F32)
        down[:, 1024 * d : 1024 * d + 1024] = shard_down[d].astype(F32)
        for ref, lane, n in (
            (inner_gain, 0, 256), (inner_bias, 256, 256), (ffn_gain, 512, 1024), (ffn_bias, 1536, 1024),
        ):
            ref[:, n * d : n * d + n] = inner[d, :, lane : lane + n]


def whole(dims):
    return pl.BlockSpec(dims, lambda i: (0,) * len(dims))


def last_call(*ins):
    row, small, big = shape((1, D), F32), shape((32, 1024), F32), shape((32, 4096), F32)
    rows = shape((128, D), BF16)
    unit, wide = shape((1, 1024), F32), shape((1, 4096), F32)
    outs = (
        rows, rows, row, row, small, small, small, unit, unit, small, row, row, big, wide, wide, big,
    )
    return pl.pallas_call(
        last_kernel,
        out_shape=outs,
        grid=(1,),
        in_specs=[whole(v.shape) for v in ins],
        out_specs=[whole(v.shape) for v in outs],
        compiler_params=pltpu.CompilerParams(vmem_limit_bytes=63 << 20),
        name="results",
    )(*ins)


def per_device(
    tokens, caption_len, norm1_gain, norm1_bias, w_query, w_key, w_value, inner_gain, inner_bias,
    w_proj, norm2_gain, norm2_bias, w_up, ffn_norm_gain, ffn_norm_bias, w_down, cotangent,
):
    table = jnp.asarray(tables().reshape(1024, 256))
    line = lambda v: v.reshape(1, -1)
    *_, down, up, proj, qkv, layer_out, grad_input, outer1, outer2, inner = layer_call((
        tokens, caption_len, line(norm1_gain), line(norm1_bias), line(inner_gain), line(inner_bias),
        line(norm2_gain), line(norm2_bias), line(ffn_norm_gain), line(ffn_norm_bias), cotangent,
        w_query, w_key, w_value, w_proj.T, w_up, w_down.T, table,
    ))
    (
        layer_out, grad_input, gain1, bias1, query, key, value, gain_i, bias_i, proj, gain2, bias2,
        up, gain_f, bias_f, down,
    ) = last_call(layer_out, grad_input, qkv, proj, up, down, outer1, outer2, inner)
    flat = lambda v: v.reshape(-1)
    return (
        layer_out, grad_input, flat(gain1), flat(bias1), query, key, value, flat(gain_i),
        flat(bias_i), proj.T, flat(gain2), flat(bias2), up, flat(gain_f), flat(bias_f), down.T,
    )


def solution(mesh):
    rows = P(("seq", "ffn"), None)
    by_rows_, by_columns, half = P("seq", "ffn"), P("ffn", "seq"), P("ffn")
    return jax.shard_map(
        per_device,
        mesh=mesh,
        in_specs=(
            rows, P("seq"), P(), P(), by_rows_, by_rows_, by_rows_, half, half, by_columns,
            P(), P(), by_rows_, half, half, by_columns, rows,
        ),
        out_specs=(
            rows, rows, P(), P(), by_rows_, by_rows_, by_rows_, half, half, by_columns,
            P(), P(), by_rows_, half, half, by_columns,
        ),
        check_vma=False,
    )
```

```python
import functools

import jax
import jax.numpy as jnp
import numpy as np
from jax import lax
from jax.experimental import pallas as pl
from jax.experimental.pallas import tpu as pltpu
from jax.sharding import PartitionSpec as P

D = 2048
HEAD_DIM = 64
FF = 8192
SLOTS = 256
IMAGE = 64
EPS = 1e-05
F32 = jnp.float32
BF16 = jnp.bfloat16
MESH = pl.DeviceIdType.MESH
VMEM = pltpu.VMEM
HBM = pltpu.HBM


def device_at(y, x, z, c):
    return (((y * 2 + x % 2) * 4 + z) * 2 + c, x // 2)


def line_slot(x, c):
    return ((x % 2) * 2 + c) * 2 + x // 2


class Net:
    def __init__(self, send, recv, local):
        seq, ffn = lax.axis_index("seq"), lax.axis_index("ffn")
        self.y, self.z, self.c = seq // 16, (seq // 2) % 4, seq % 2
        self.x = ffn * 2 + (seq // 8) % 2
        self.send, self.recv, self.local = send, recv, local
        self.n_send, self.n_recv, self.n_local = 0, 0, 0

    def along_x(self, dx, dc=0):
        return device_at(self.y, (self.x + dx) % 4, self.z, (self.c + dc) % 2)

    def along_y(self, dy):
        return device_at((self.y + dy) % 4, self.x, self.z, self.c)

    def along_z(self, dz):
        return device_at(self.y, self.x, (self.z + dz) % 4, self.c)

    def pair(self, dx, dc):
        x = (self.x // 2) * 2 + (self.x + dx) % 2
        return device_at(self.y, x, self.z, (self.c + dc) % 2)

    def greet(self, partners):
        self.barrier, self.partners = pltpu.get_barrier_semaphore(), len(partners)
        for partner in partners:
            pl.semaphore_signal(self.barrier, inc=1, device_id=partner, device_id_type=MESH)

    def met(self):
        pl.semaphore_wait(self.barrier, self.partners)

    def out(self):
        self.n_send += 1
        return self.send.at[self.n_send - 1]

    def into(self):
        self.n_recv += 1
        return self.recv.at[self.n_recv - 1]

    def push(self, src, dst, device, out, into):
        pltpu.make_async_remote_copy(
            src_ref=src,
            dst_ref=dst,
            send_sem=out,
            recv_sem=into,
            device_id=device,
            device_id_type=MESH,
        ).start()

    def copies(self, semaphore, same_bytes):
        return pltpu.make_async_remote_copy(
            src_ref=same_bytes,
            dst_ref=same_bytes,
            send_sem=semaphore,
            recv_sem=semaphore,
            device_id=self.along_x(0, 1),
            device_id_type=MESH,
        )

    def arrived(self, into, same_bytes):
        self.copies(into, same_bytes).wait_recv()

    def left(self, out, same_bytes):
        self.copies(out, same_bytes).wait_send()

    def keep(self, src, dst):
        copy = pltpu.make_async_copy(src, dst, self.local.at[self.n_local])
        self.n_local += 1
        copy.start()
        return copy

    def close(self):
        found = self.n_send, self.n_recv, self.n_local
        assert found == tuple(s.shape[0] for s in (self.send, self.recv, self.local)), found


def add_into(dst, *terms):
    def step(i, carry):
        rows = pl.ds(pl.multiple_of(i * 16, 16), 16)
        total = terms[0][rows, :].astype(F32)
        for term in terms[1:]:
            total = total + term[rows, :].astype(F32)
        dst[rows, :] = total.astype(dst.dtype)
        return carry

    lax.fori_loop(0, dst.shape[0] // 16, step, 0)


def slot_row(slot, off, n, by_parts):
    return pl.multiple_of(off * 8 + slot * 64 if by_parts else slot * 128 + off, n)


class LineGather:
    def __init__(self, net, own, full, off=0, n=128, by_parts=False):
        self.net, self.full, self.off, self.n, self.by_parts = net, full, off, n, by_parts
        self.own = own.at[pl.ds(off, n)]
        self.own_half = [own.at[pl.ds(off + n // 2 * h, n // 2)] for h in range(2)]
        self.out = net.out()
        self.first, self.second, self.third, self.near, self.rest = (net.into() for _ in range(5))

    def block(self, dx, dc=0, half=None):
        net, n = self.net, self.n
        base = slot_row(line_slot((net.x + dx) % 4, (net.c + dc) % 2), self.off, n, self.by_parts)
        if half is None:
            return self.full.at[pl.ds(base, n)]
        return self.full.at[pl.ds(pl.multiple_of(base + n // 2 * half, n // 2), n // 2)]

    def push(self, src, dst, device, into):
        self.net.push(src, dst, device, self.out, into)

    def same(self, ref, device, into):
        self.net.push(ref, ref, device, self.out, into)

    def bytes_of(self, k):
        return self.full.at[pl.ds(0, k * self.n)]

    def start_first(self):
        net = self.net
        self.push(self.own_half[0], self.block(0, 0, 0), net.along_x(1), self.first)
        self.push(self.own_half[1], self.block(0, 0, 1), net.along_x(-1), self.first)

    def start_second(self):
        net = self.net
        self.push(self.own_half[1], self.block(0, 0, 1), net.along_x(1), self.second)
        self.push(self.own_half[0], self.block(0, 0, 0), net.along_x(-1), self.second)
        self.push(self.own, self.block(0), net.along_x(0, 1), self.rest)
        self.kept = net.keep(self.own, self.block(0))

    def start(self):
        self.start_first()
        self.start_second()

    def forward_first(self):
        net = self.net
        net.arrived(self.first, self.bytes_of(1))
        self.same(self.block(-1, 0, 0), net.along_x(1), self.third)
        self.same(self.block(1, 0, 1), net.along_x(-1), self.third)

    def forward_second(self):
        net = self.net
        net.arrived(self.second, self.bytes_of(1))
        self.same(self.block(-1), net.along_x(0, 1), self.near)
        self.same(self.block(1), net.along_x(0, 1), self.near)

    def forward(self):
        self.forward_first()
        self.forward_second()

    def share(self):
        net = self.net
        net.arrived(self.third, self.bytes_of(1))
        self.same(self.block(2, 0, 0), net.along_x(0, 1), self.rest)
        self.same(self.block(2, 0, 1), net.along_x(0, 1), self.rest)

    def finish_near(self):
        self.net.arrived(self.near, self.bytes_of(2))

    def finish(self):
        self.net.arrived(self.rest, self.bytes_of(2))
        self.kept.wait()

    def sent(self):
        self.net.left(self.out, self.bytes_of(7))


class RingSum:
    def __init__(self, net, mine, landing, ahead, behind, out, far, near):
        self.net, self.mine, self.landing = net, mine, landing
        self.ahead, self.behind, self.out = ahead, behind, out
        self.far, self.near = far, near

    def start_far(self):
        net, land = self.net, self.landing
        net.push(self.mine(2, 0), land.at[0], self.ahead, self.out, self.far)
        net.push(self.mine(2, 1), land.at[1], self.behind, self.out, self.far)

    def start_near(self, d):
        net, land = self.net, self.landing
        if d == 1:
            net.push(self.mine(1, 1), land.at[3], self.ahead, self.out, self.near)
        else:
            net.push(self.mine(-1, 0), land.at[4], self.behind, self.out, self.near)

    def pass_on(self):
        net, land = self.net, self.landing
        add_into(land.at[0], land.at[0], self.mine(1, 0))
        net.push(land.at[0], land.at[2], self.ahead, self.out, self.near)
        add_into(land.at[1], land.at[1], self.mine(-1, 1))
        net.push(land.at[1], land.at[5], self.behind, self.out, self.near)

    def finish(self, out=None, onto=False):
        land = self.landing
        for h in (0, 1):
            to = land.at[2 + h] if out is None else out(h)
            terms = self.mine(0, h), land.at[2 + h], land.at[4 + h]
            add_into(to, *terms, *([to] if onto else []))


class LineSum:
    def __init__(self, net, part, other, landing, off, by_parts):
        self.net, self.part, self.other, self.landing = net, part, other, landing
        self.off, self.by_parts = off, by_parts
        self.out, self.ring_out = net.out(), net.out()
        self.first, self.rest = net.into(), net.into()
        ends = net.along_x(1), net.along_x(-1)
        self.far, self.near = net.into(), net.into()
        self.ring = RingSum(net, self.mine, landing, *ends, self.ring_out, self.far, self.near)

    def block(self, dx, dc):
        net = self.net
        slot = line_slot((net.x + dx) % 4, (net.c + dc) % 2)
        return self.part.at[pl.ds(slot_row(slot, self.off, 64, self.by_parts), 64)]

    def mine(self, d, half):
        return self.other.at[d % 4, pl.ds(32 * half, 32)]

    def start(self, *steps):
        for d in steps:
            into = self.first if d == 2 else self.rest
            place = self.other.at[d % 4]
            self.net.push(self.block(d, 1), place, self.net.along_x(0, 1), self.out, into)

    def add(self, d):
        add_into(self.other.at[d % 4], self.other.at[d % 4], self.block(d, 0))

    def chip_far(self):
        self.net.arrived(self.first, self.other.at[0])
        self.add(2)
        self.ring.start_far()

    def chip_near(self):
        self.net.arrived(self.rest, self.other.at[pl.ds(0, 3)])
        self.add(1)
        self.ring.start_near(1)
        self.add(-1)
        self.ring.start_near(-1)
        self.add(0)

    def part_sent(self):
        self.net.left(self.out, self.other)

    def pass_on(self):
        self.net.arrived(self.far, self.landing.at[pl.ds(0, 2)])
        self.ring.pass_on()

    def finish(self, out, onto=False):
        self.net.arrived(self.near, self.landing.at[pl.ds(2, 4)])
        self.ring.finish(lambda h: out.at[pl.ds(self.off + 32 * h, 32)], onto)

    def sent(self):
        self.net.left(self.ring_out, self.landing)


def line_sums(net, part, other, landing, by_parts):
    return [LineSum(net, part, other.at[k], landing.at[k], 64 * k, by_parts) for k in range(2)]


def line_gathers(net, own, full):
    return [LineGather(net, own, full, 64 * k, 64, True) for k in range(2)]


def shard_rows(ref, y, x_lo, z, c=None):
    if c is None:
        return ref.at[pl.ds(pl.multiple_of(((y * 2 + x_lo) * 4 + z) * 64, 64), 64)]
    return ref.at[pl.ds(pl.multiple_of((((y * 2 + x_lo) * 4 + z) * 2 + c) * 32, 32), 32)]


PAIR_STEPS = ((1, 0), (1, 1), (0, 1))


class GridGather:
    def __init__(self, net, pieces, full):
        self.net, self.pieces, self.full = net, pieces, full
        self.out, self.pair_out = net.out(), net.out()
        self.pair_into, self.last = net.into(), net.into()
        self.p, self.f = net.into(), net.into()
        self.q = {dp: net.into() for dp in (0, -1, 1, 2)}

    def bytes_of(self, rows):
        return self.full.at[pl.ds(0, rows)]

    def exchange(self):
        net = self.net
        spot = shard_rows(self.full, net.y, net.x % 2, net.z, net.c)
        for dx, dc in PAIR_STEPS:
            to = ((net.x + dx) % 2) * 2 + (net.c + dc) % 2
            net.push(self.piece(to), spot, net.pair(dx, dc), self.pair_out, self.pair_into)
        self.kept = net.keep(self.piece((net.x % 2) * 2 + net.c), spot)

    def piece(self, d):
        return self.pieces.at[pl.ds(pl.multiple_of(32 * d, 32), 32)]

    def slab(self, t, dp, dq, half=None):
        net = self.net
        dy, dz = (dq, dp) if t == 0 else (dp, dq)
        return shard_rows(self.full, (net.y + dy) % 4, t, (net.z + dz) % 4, half)

    def to_p(self, t, d):
        return self.net.along_z(d) if t == 0 else self.net.along_y(d)

    def to_q(self, t, d):
        return self.net.along_y(d) if t == 0 else self.net.along_z(d)

    def same(self, ref, device, into):
        self.net.push(ref, ref, device, self.out, into)

    def second(self, t, dp):
        for d in (1, -1):
            self.same(self.slab(t, dp, 0), self.to_q(t, d), self.q[dp])

    def start(self):
        self.net.arrived(self.pair_into, self.bytes_of(96))
        self.kept.wait()
        for t in (0, 1):
            for d in (1, -1):
                self.same(self.slab(t, 0, 0), self.to_p(t, d), self.p)
        for t in (0, 1):
            self.second(t, 0)

    def near(self):
        self.net.arrived(self.p, self.bytes_of(256))
        for t in (0, 1):
            self.same(self.slab(t, -1, 0, 0), self.to_p(t, 1), self.f)
            self.same(self.slab(t, 1, 0, 1), self.to_p(t, -1), self.f)
        for t in (0, 1):
            self.second(t, -1)
            self.second(t, 1)

    def far(self):
        self.net.arrived(self.f, self.bytes_of(128))
        for t in (0, 1):
            self.second(t, 2)

    def pass_on(self, dp):
        self.net.arrived(self.q[dp], self.bytes_of(256))
        for t in (0, 1):
            self.same(self.slab(t, dp, -1, 0), self.to_q(t, 1), self.last)
            self.same(self.slab(t, dp, 1, 1), self.to_q(t, -1), self.last)

    def finish(self):
        self.net.arrived(self.last, self.bytes_of(512))

    def pair_sent(self):
        self.net.left(self.pair_out, self.bytes_of(96))

    def sent(self):
        self.net.left(self.out, self.bytes_of(1920))


class GridSum:
    def __init__(self, net, part, landing, done, shard):
        self.net, self.part, self.landing, self.done, self.shard = net, part, landing, done, shard
        self.out, self.pair_out, self.pair_into = net.out(), net.out(), net.into()
        self.rings = {}
        self.far = {dp: net.into() for dp in (2, 1, -1, 0, None)}
        self.near = {dp: net.into() for dp in (2, 1, -1, 0, None)}
        for t in (0, 1):
            for dp in (2, 1, -1, 0):
                self.rings[t, dp] = RingSum(
                    net,
                    functools.partial(self.term, t, dp),
                    landing.at[t, dp % 4],
                    self.to_q(t, 1),
                    self.to_q(t, -1),
                    self.out,
                    self.far[dp],
                    self.near[dp],
                )
            self.rings[t] = RingSum(
                net,
                functools.partial(self.column, t),
                landing.at[t, 4],
                self.to_p(t, 1),
                self.to_p(t, -1),
                self.out,
                self.far[None],
                self.near[None],
            )
        self.steps = [
            functools.partial(self.pass_on, 2),
            functools.partial(self.pass_on, 1),
            functools.partial(self.pass_on, -1),
            functools.partial(self.finish, 2),
            functools.partial(self.pass_on, 0),
            functools.partial(self.finish, 1),
            functools.partial(self.finish, -1),
            self.pass_on_last,
            functools.partial(self.finish, 0),
            self.finish_last,
            self.collect,
        ]

    def to_p(self, t, d):
        return self.net.along_z(d) if t == 0 else self.net.along_y(d)

    def to_q(self, t, d):
        return self.net.along_y(d) if t == 0 else self.net.along_z(d)

    def term(self, t, dp, dq, half):
        net = self.net
        dy, dz = (dq, dp) if t == 0 else (dp, dq)
        return shard_rows(self.part, (net.y + dy) % 4, t, (net.z + dz) % 4, half)

    def column(self, t, dp, half):
        return self.landing.at[t, dp % 4, 2 + half]

    def start(self, dy):
        for dp in (2, 1, -1, 0):
            if dy == 2:
                self.rings[0, dp].start_far()
            elif dy:
                self.rings[0, dp].start_near(dy)
        self.rings[1, dy].start_far()
        self.rings[1, dy].start_near(1)
        self.rings[1, dy].start_near(-1)

    def step(self, n=1):
        for _ in range(n):
            self.steps.pop(0)()

    def bytes_of(self, rows):
        return self.part.at[pl.ds(0, rows)]

    def pass_on(self, dp):
        self.net.arrived(self.far[dp], self.bytes_of(128))
        for t in (0, 1):
            self.rings[t, dp].pass_on()

    def finish(self, dp):
        self.net.arrived(self.near[dp], self.bytes_of(256))
        for t in (0, 1):
            self.rings[t, dp].finish()
            if dp == 2:
                self.rings[t].start_far()
            elif dp:
                self.rings[t].start_near(dp)

    def pass_on_last(self):
        self.net.arrived(self.far[None], self.bytes_of(128))
        for t in (0, 1):
            self.rings[t].pass_on()

    def finish_last(self):
        net = self.net
        net.arrived(self.near[None], self.bytes_of(256))
        for t in (0, 1):
            self.rings[t].finish(lambda half: self.done.at[t, half])
        me = (net.x % 2) * 2 + net.c
        for dx, dc in PAIR_STEPS:
            src = self.done.at[(net.x + dx) % 2, (net.c + dc) % 2]
            net.push(src, self.shard.at[me], net.pair(dx, dc), self.pair_out, self.pair_into)
        self.kept = net.keep(self.done.at[net.x % 2, net.c], self.shard.at[me])

    def collect(self):
        self.net.arrived(self.pair_into, self.shard.at[pl.ds(0, 3)])
        self.kept.wait()

    def sent(self):
        self.net.left(self.out, self.part.at[pl.ds(0, 1920)])

    def pair_sent(self):
        self.net.left(self.pair_out, self.shard.at[pl.ds(0, 3)])


class SmallSum:
    def __init__(self, net, own, slots, me, partners):
        self.net, self.own, self.slots, self.me, self.partners = net, own, slots, me, partners
        self.out, self.into = net.out(), net.into()

    def start(self):
        for to, _ in self.partners:
            self.net.push(self.own, self.slots.at[self.me], to, self.out, self.into)
        self.slots[self.me] = self.own[...]

    def total(self):
        self.net.arrived(self.into, self.slots.at[pl.ds(0, len(self.partners))])
        total = self.slots[0]
        for i in range(1, self.slots.shape[0]):
            total = total + self.slots[i]
        return total

    def finish(self, out):
        out[...] = self.total()

    def sent(self):
        self.net.left(self.out, self.slots.at[pl.ds(0, len(self.partners))])


class PairShare:
    def __init__(self, net, own, slots):
        self.net, self.own, self.slots = net, own, slots
        self.out, self.into = net.out(), net.into()

    def start(self):
        net = self.net
        me = (net.x % 2) * 2 + net.c
        for dx, dc in PAIR_STEPS:
            net.push(self.own, self.slots.at[me], net.pair(dx, dc), self.out, self.into)
        self.slots[me] = self.own[...]

    def finish(self):
        self.net.arrived(self.into, self.slots.at[pl.ds(0, 3)])

    def sent(self):
        self.net.left(self.out, self.slots.at[pl.ds(0, 3)])


def line_partners(net):
    return [
        (net.along_x(dx, dc), ((net.x - dx) % 4) * 2 + (net.c + dc) % 2)
        for dx in range(4)
        for dc in range(2)
        if dx or dc
    ]


def grid_partners(net):
    return [
        (
            device_at((net.y + dy) % 4, net.x, (net.z + dz) % 4, net.c),
            ((net.y - dy) % 4) * 4 + (net.z - dz) % 4,
        )
        for dy in range(4)
        for dz in range(4)
        if dy or dz
    ]


def grid_neighbours(net):
    return [net.along_y(1), net.along_y(-1), net.along_z(1), net.along_z(-1)]


def spec(space):
    return pl.BlockSpec(memory_space=space)


def shape(dims, dtype):
    return jax.ShapeDtypeStruct(dims, dtype)


class Staged:
    def __init__(self, loads, stores):
        self.loads, self.stores, self.started = loads, stores, []
        for copy, _ in loads:
            copy.start()

    def wait(self, *refs):
        for copy, ref in list(self.loads):
            if not refs or any(ref is r for r in refs):
                copy.wait()
                self.loads = [pair for pair in self.loads if pair[1] is not ref]

    def put(self, *refs):
        for copy, ref in list(self.stores):
            if not refs or any(ref is r for r in refs):
                copy.start()
                self.started.append(copy)
                self.stores = [pair for pair in self.stores if pair[1] is not ref]

    def finish(self):
        self.wait()
        self.put()
        for copy in self.started:
            copy.wait()


def comm_call(body, name, collective_id, ins, in_spaces, outs, out_spaces, scratch, mib, sems):
    n_in, n_out = len(ins), len(outs)
    buffers = [space(v.shape, v.dtype) for v, space in zip(ins, in_spaces) if space is not HBM]
    buffers += [space(v.shape, v.dtype) for v, space in zip(outs, out_spaces) if space is not HBM]
    n = len(buffers)

    def kernel(*refs):
        sem = refs[-1]
        rest = list(refs[n_in + n_out : n_in + n_out + n])
        loads, stores, args = [], [], []
        for i, (ref, space) in enumerate(zip(refs, (*in_spaces, *out_spaces))):
            if space is HBM:
                args.append(ref)
                continue
            buffer = rest.pop(0)
            args.append(buffer)
            at = sem.at[len(loads) + len(stores)]
            if i < n_in:
                loads.append((pltpu.make_async_copy(ref, buffer, at), buffer))
            else:
                stores.append((pltpu.make_async_copy(buffer, ref, at), buffer))
        io = Staged(loads, stores)
        body(io, *args, *refs[n_in + n_out + n : -1])
        io.finish()

    return pl.pallas_call(
        kernel,
        out_shape=outs,
        in_specs=[spec(HBM)] * n_in,
        out_specs=[spec(HBM)] * n_out,
        scratch_shapes=buffers
        + scratch
        + [pltpu.SemaphoreType.REGULAR((3,))]
        + [pltpu.SemaphoreType.DMA((k,)) for k in (*sems, n)],
        compiler_params=pltpu.CompilerParams(
            collective_id=collective_id, has_side_effects=True, vmem_limit_bytes=mib << 20
        ),
        name=name,
    )(*ins)


def norm_parts(values):
    center = jnp.mean(values, -1, keepdims=True)
    spread = jnp.mean(values * values, -1, keepdims=True) - center * center
    inv_std = lax.rsqrt(spread + EPS)
    return (values - center) * inv_std, inv_std


def by_rows(rows, step, chunk=16, off=0):
    def body(i, carry):
        step(pl.ds(pl.multiple_of(off + i * chunk, chunk), chunk))
        return carry

    lax.fori_loop(0, rows // chunk, body, 0)


def norm_back(grad, gain, hat, inv_std):
    scaled = grad * gain
    return inv_std * (
        scaled
        - jnp.mean(scaled, -1, keepdims=True)
        - hat * jnp.mean(scaled * hat, -1, keepdims=True)
    )


def fold8(values):
    return values[:8] + values[8:]


def block_rows(base, step):
    def body(i, carry):
        step(
            pl.ds(pl.multiple_of(i * 16, 16), 16),
            pl.ds(pl.multiple_of(base + i * 16, 16), 16),
        )
        return carry

    lax.fori_loop(0, 16, body, 0)


def lane_sums(values):
    total = values[:, :128]
    for k in range(1, values.shape[1] // 128):
        total = total + values[:, 128 * k : 128 * k + 128]
    return total


def row_of(partial):
    return jnp.sum(partial.T, 0, keepdims=True)


def spread(row):
    return jnp.broadcast_to(row, (128, row.shape[1])).T


def wide(values, lanes):
    return jnp.concatenate([values] * (lanes // 128), 1)


def xpos_tables(direction):
    half = HEAD_DIM // 2
    pair = np.arange(half, dtype=np.float32)
    frequency = np.power(np.float32(10000.0), -pair / half).astype(np.float32)
    zeta = ((pair / half + 0.4) / 1.4).astype(np.float32)
    position = np.arange(SLOTS, dtype=np.float32)[:, None]
    angle = (position * frequency).astype(np.float32).astype(np.float64)
    decay = np.exp(direction * position / 512.0 * np.log(zeta.astype(np.float64)))
    cosine, sine = np.cos(angle) * decay, np.sin(angle) * decay
    cosine = np.concatenate([cosine] * 2, -1)
    sine = np.concatenate([-sine, sine], -1)
    return np.tile(cosine, (1, 4)).astype(np.float32), np.tile(sine, (1, 4)).astype(np.float32)


def tables():
    return np.stack([*xpos_tables(1.0), *xpos_tables(-1.0)])


def swapped(values):
    lane = lax.broadcasted_iota(jnp.int32, values.shape, 1)
    return jnp.where(lane % 64 < 32, pltpu.roll(values, 224, 1), pltpu.roll(values, 32, 1))


def dot_nn(a, b):
    return lax.dot_general(a, b, (((1,), (0,)), ((), ())), preferred_element_type=F32)


def dot_nt(a, b):
    return lax.dot_general(a, b, (((1,), (1,)), ((), ())), preferred_element_type=F32)


def dot_tn(a, b):
    return lax.dot_general(a, b, (((0,), (0,)), ((), ())), preferred_element_type=F32)


def head_of(values, head):
    lane = lax.broadcasted_iota(jnp.int32, values.shape, 1)
    return jnp.where(lane // 64 == head, values, jnp.zeros_like(values))


def head_probs(query, key, head, allowed):
    scores = dot_nt(head_of(query, head), key) * HEAD_DIM**-0.5
    scores = jnp.where(allowed, scores, -1e30)
    exps = jnp.exp(scores - jnp.max(scores, -1, keepdims=True))
    return exps / jnp.sum(exps, -1, keepdims=True)


def allowed_slots(cap):
    query = lax.broadcasted_iota(jnp.int32, (SLOTS, SLOTS), 0)
    key = lax.broadcasted_iota(jnp.int32, (SLOTS, SLOTS), 1)
    return (key <= query) & (key < IMAGE + cap[0:1, 0:1])


def attend(rows, weights, cap, table, at, kept, mixed):
    qkv = dot_nn(rows, weights[:, :768])
    query, key, value = qkv[:, :256], qkv[:, 256:512], qkv[:, 512:].astype(BF16)
    query = (query * table(0) + swapped(query) * table(1)).astype(BF16)
    key = (key * table(2) + swapped(key) * table(3)).astype(BF16)
    for i, part in enumerate((query, key, value)):
        kept[at, 256 * i : 256 * i + 256] = part
    allowed = allowed_slots(cap)
    total = jnp.zeros((SLOTS, 256), F32)
    for head in range(4):
        probs = head_probs(query, key, head, allowed).astype(BF16)
        total = total + dot_nn(probs, head_of(value, head))
    mixed[at, :256] = total


def attend_back(query, key, value, grad, cap, table):
    allowed = allowed_slots(cap)
    grad_query = jnp.zeros((SLOTS, 256), F32)
    grad_key = jnp.zeros((SLOTS, 256), F32)
    grad_value = jnp.zeros((SLOTS, 256), F32)
    for head in range(4):
        probs = head_probs(query, key, head, allowed)
        grad_head = head_of(grad, head)
        grad_probs = dot_nt(grad_head, value)
        grad_value = grad_value + dot_tn(probs.astype(BF16), grad_head)
        delta = jnp.sum(probs * grad_probs, -1, keepdims=True)
        grad_scores = (probs * (grad_probs - delta)).astype(BF16)
        grad_query = grad_query + dot_nn(grad_scores, head_of(key, head))
        grad_key = grad_key + dot_tn(grad_scores, head_of(query, head))
    grad_query = grad_query * HEAD_DIM**-0.5
    grad_key = grad_key * HEAD_DIM**-0.5
    return (
        (grad_query * table(0) + swapped(grad_query * table(1))).astype(BF16),
        (grad_key * table(2) + swapped(grad_key * table(3))).astype(BF16),
        grad_value.astype(BF16),
    )


def place_of(net):
    return (net.x % 2) * 2 + net.c


def my_lanes(ref, net, n):
    return ref[:, pl.ds(pl.multiple_of(place_of(net) * n, n), n)]


def sequence_at(net, q):
    seq_of = ((net.x + q // 2) % 2) * 2 + (net.c + 1 + q) % 2
    return pl.multiple_of(seq_of * SLOTS, SLOTS)


def rows_along_y(net, dy):
    return pl.ds(pl.multiple_of(((net.y + dy) % 4) * 512, 512), 512)


def layer_kernel(
    io, tokens, cap, gain1, bias1, inner_gain, inner_bias, gain2, bias2, ffn_gains, ffn_biases, cot,
    w_query, w_key, w_value, w_proj, w_up, w_down, table_in,
    rows1_out, weights1_out, kept_out, hat_out, shard_down, shard_up, shard_proj, shard_qkv,
    layer_out, grad_input, outer1_out, outer2_out, inner_out,
    own_rows, rows, cots, part, weights1, up, down, act, gffn, slope, kept, grad_up, partial, cols,
    caps_in, caps, ffn_gain, ffn_bias, my_gain, attended, grad_attended,
    proj_grads,     own_s, slots_s, own_u, slots_u, own_t, slots_t, other, landing, landing_down, landing_up,
    landing_proj, done, inner_inv, inner_sums, unit_sums, sums, outer, line_slots, grid_slots, line_whole,
    inner, inner_slots, inner_whole, credit, send, recv, local,
):
    net = Net(send, recv, local)
    others, grid = line_partners(net), grid_partners(net)
    net.greet([to for to, _ in others + grid])
    me, me_grid = net.x * 2 + net.c, net.y * 4 + net.z
    shards = [w_query, w_key, w_value, w_proj]
    load1 = [net.keep(w, act.at[pl.ds(32 * i, 32)]) for i, w in enumerate(shards)]
    load_table = net.keep(table_in, gffn.at[:, pl.ds(0, 256)])
    load2 = [
        net.keep(w.at[:, pl.ds(1024 * d, 1024)], act.at[pl.ds(128 + 128 * i + 32 * d, 32)])
        for i, w in enumerate((w_down, w_up))
        for d in range(4)
    ]
    gather1 = GridGather(
        net, slope.at[pl.ds(0, 128), pl.ds(0, 768)], weights1.at[:, pl.ds(0, 768)]
    )
    gather_proj = GridGather(
        net, slope.at[pl.ds(0, 128), pl.ds(768, 256)], weights1.at[:, pl.ds(768, 256)]
    )
    gather_down = GridGather(net, slope.at[pl.ds(128, 128)], down)
    gather_up = GridGather(net, slope.at[pl.ds(256, 128)], up)
    line1 = LineGather(net, own_rows, rows)
    line_cot = line_gathers(net, cot, cots)
    total = line_sums(net, part, other, landing, False)
    line2 = line_gathers(net, own_rows, rows)
    sum_s = SmallSum(net, own_s, slots_s, me, others)
    share_caps = PairShare(net, caps_in, caps)

    for i in range(4):
        load1[i].wait()
        for d in range(4):
            slope[32 * d : 32 * d + 32, 256 * i : 256 * i + 256] = act[
                32 * i : 32 * i + 32, 256 * d : 256 * d + 256
            ].astype(BF16)
    io.wait(tokens, cap, gain1, bias1)

    def norm1(at):
        one, _ = norm_parts(tokens[at, :].astype(F32))
        own_rows[at, :] = (one * gain1[...] + bias1[...]).astype(BF16)

    by_rows(128, norm1)
    caps_in[...] = jnp.full((8, 128), cap[0], jnp.int32)

    net.met()
    gather1.exchange()
    line1.start()
    gather_proj.exchange()
    share_caps.start()
    gather1.start()
    for copy in load2:
        copy.wait()
    slope[128:384, :] = act[128:384, :].astype(BF16)
    io.wait()
    for ref in (unit_sums, sums, inner_sums):
        ref[...] = jnp.zeros_like(ref)
    ffn_gain[...], ffn_bias[...] = my_lanes(ffn_gains, net, 1024), my_lanes(ffn_biases, net, 1024)
    my_gain[...] = my_lanes(inner_gain, net, 256)
    gather1.near()
    gather1.pass_on(0)
    gather1.far()
    line1.forward()
    gather_down.exchange()
    gather1.pass_on(-1)
    gather1.pass_on(1)
    gather1.pass_on(2)
    gather_proj.start()
    gather_up.exchange()
    for line in line_cot:
        line.start()
    line1.finish_near()
    share_caps.finish()
    load_table.wait()
    gather1.finish()

    table = lambda i: gffn[256 * i : 256 * i + 256, :256]
    for q in range(4):
        base = sequence_at(net, (q + 2) % 4)
        at = pl.ds(base, SLOTS)
        if q == 2:
            line1.finish()
            save_rows = net.keep(rows, rows1_out)
        attend(rows[at, :], weights1, caps.at[base // SLOTS], table, at, kept, act)
        both = act[at, :256]
        partial[0] = lane_sums(both)
        partial[1] = lane_sums(both * both)
        for i in range(2):
            own_s[i : i + 1, at] = row_of(partial[i])
        if q == 0:
            line1.share()
            gather_proj.near()
            gather_proj.pass_on(0)
        if q == 1:
            gather_proj.far()
            gather_proj.pass_on(-1)
            gather_proj.pass_on(1)
            gather_down.start()
        if q == 2:
            gather_proj.pass_on(2)
    sum_s.start()
    for line in line_cot:
        line.forward()
    gather_down.near()
    gather_up.start()
    gather_proj.finish()
    save_weights = net.keep(weights1, weights1_out)
    both = sum_s.total()
    center = both[0:1] * (1.0 / D)
    inv_std = lax.rsqrt(both[1:2] * (1.0 / D) - center * center + EPS)
    inner_inv[...] = inv_std
    cols[0] = spread(center)
    cols[1] = spread(inv_std)
    my_bias = my_lanes(inner_bias, net, 256)

    def inner_norm(at):
        one = (act[at, :256] - wide(cols[0, at, :], 256)) * wide(cols[1, at, :], 256)
        act[at, 256:512] = one
        kept[at, 768:] = (one * my_gain[...] + my_bias).astype(BF16)

    by_rows(1024, inner_norm, 64)
    gather_down.pass_on(0)
    gather_down.far()
    save_hat = net.keep(act.at[:, pl.ds(256, 256)], hat_out)
    save_kept = net.keep(kept, kept_out)
    save_rows.wait()
    line1.sent()
    for q in range(4):
        at = pl.ds(sequence_at(net, q), SLOTS)
        mine = kept[at, 768:]
        for h in range(2):
            part[at, 1024 * h : 1024 * h + 1024] = dot_nt(
                mine, weights1[1024 * h : 1024 * h + 1024, 768:]
            ).astype(BF16)
        for t in total:
            if q == 0:
                t.start(2)
            if q == 1:
                t.start(0)
                t.chip_far()
            if q == 2:
                t.start(1, -1)
    total[0].chip_near()
    total[0].pass_on()
    total[1].chip_near()
    gather_down.pass_on(-1)
    gather_down.pass_on(1)
    total[1].pass_on()
    for line in line_cot:
        line.share()
    gather_up.near()
    gather_up.pass_on(0)
    save_weights.wait()

    def norm2(at):
        values = tokens[at, :].astype(F32) + attended[at, :]
        attended[at, :] = values
        one, _ = norm_parts(values)
        own_rows[at, :] = (one * gain2[...] + bias2[...]).astype(BF16)

    def cot_rows(b):
        at = slice(256 * b, 256 * b + 256)
        gffn[at, :] = dot_nn(cots[at, :], down[...])

    total[0].finish(attended)
    by_rows(64, norm2)
    line2[0].start()
    gather_down.pass_on(2)
    for line in line_cot:
        line.finish_near()
        line.finish()
    total[1].finish(attended)
    by_rows(64, norm2, 16, 64)
    line2[1].start_first()
    line2[0].forward_first()
    line2[1].start_second()
    gather_up.far()
    gather_down.finish()
    cot_rows(0)
    gather_up.pass_on(-1)
    gather_up.pass_on(1)
    line2[0].forward_second()
    cot_rows(1)
    gather_up.pass_on(2)
    line2[1].forward_first()
    cot_rows(2)
    line2[0].share()
    cot_rows(3)
    line2[1].forward_second()
    gather_up.finish()
    line2[0].finish_near()
    line2[0].finish()
    save_hat.wait()
    save_kept.wait()
    for t in total:
        t.part_sent()
        t.sent()
    for gather in (gather1, gather_proj, gather_down, gather_up):
        gather.pair_sent()

    sum_u = [SmallSum(net, own_u.at[k], slots_u.at[k], me, others) for k in range(2)]
    for k in range(2):
        if k == 1:
            line2[1].finish_near()
            line2[1].finish()
        for j in range(2):
            base = 512 * k + 256 * j
            act[base : base + 256, :] = dot_nn(rows[base : base + 256, :], up[...])

            def gelu(at, to):
                value = act[to, :]
                cdf = 0.5 * (1.0 + lax.erf(value * np.float32(0.5**0.5)))
                density = jnp.exp(-0.5 * value * value) * np.float32((2 * np.pi) ** -0.5)
                slope[to, :] = (cdf + value * density).astype(BF16)
                value = value * cdf
                act[to, :] = value
                partial[0, at, :] = lane_sums(value)
                partial[1, at, :] = lane_sums(value * value)
                grad = gffn[to, :]
                unit_sums[1] += fold8(grad)
                grad = grad * ffn_gain[...]
                partial[2, at, :] = lane_sums(grad)
                partial[3, at, :] = lane_sums(grad * value)

            block_rows(base, gelu)
            for i in range(4):
                own_u[k, i : i + 1, 256 * j : 256 * j + 256] = row_of(partial[i])
            if k == 0 and j == 0:
                line2[1].share()
        sum_u[k].start()

    total = line_sums(net, part, other, landing, True)
    ffn_b = kept
    for k in range(2):
        both = sum_u[k].total()
        center = both[0:1] * (1.0 / FF)
        inv_std = lax.rsqrt(both[1:2] * (1.0 / FF) - center * center + EPS)
        slant = (both[3:4] - center * both[2:3]) * inv_std * (1.0 / FF)
        its = slice(512 * k, 512 * k + 512)
        for i, row in enumerate((center, inv_std, both[2:3] * (1.0 / FF))):
            cols[i, its, :] = spread(row)

        def normed(at):
            hat = (act[at, :] - wide(cols[0, at, :], 1024)) * wide(cols[1, at, :], 1024)
            act[at, :] = hat
            ffn_b[at, :] = (hat * ffn_gain[...] + ffn_bias[...]).astype(BF16)
            unit_sums[0] += fold8(gffn[at, :] * hat)

        by_rows(512, normed, 16, 512 * k)
        cols[0, its, :] = spread(slant)
        if k == 1:
            total[0].chip_near()
        for j in range(2):
            base = pl.multiple_of(512 * k + 256 * ((net.x + j) % 2), 256)

            def back(at, to):
                grad = gffn[to, :] * ffn_gain[...] - wide(cols[2, to, :], 1024)
                grad = grad - act[to, :] * wide(cols[0, to, :], 1024)
                grad = grad * wide(cols[1, to, :], 1024)
                grad_up[to, :] = (grad * slope[to, :].astype(F32)).astype(BF16)

            block_rows(base, back)
            mine = grad_up[pl.ds(base, 256), :]
            for h in range(2):
                part[pl.ds(base, 256), 1024 * h : 1024 * h + 1024] = dot_nt(
                    mine, up[1024 * h : 1024 * h + 1024, :]
                ).astype(BF16)
            if j == 0:
                total[k].start(2, 0)
            else:
                total[k].start(1, -1)
                total[k].chip_far()
    total[0].pass_on()
    total[1].chip_near()

    weights_down = GridSum(net, weights1, landing_down, done.at[0], shard_down)
    weights_up = GridSum(net, up, landing_up, done.at[1], shard_up)
    lines = line_gathers(net, own_rows, part)

    def outer_sums(k):
        for i in range(2):
            outer[k, i : i + 1, :] = jnp.sum(sums[2 * k + i], 0, keepdims=True)
        return (
            SmallSum(net, outer.at[k], line_slots.at[k], me, others),
            SmallSum(net, line_whole.at[k], grid_slots.at[k], me_grid, grid),
        )

    def norm2_back(at):
        grad = grad_attended[at, :]
        one, inv = norm_parts(attended[at, :])
        sums[2] += fold8(grad * one)
        sums[3] += fold8(grad)
        value = cot[at, :].astype(F32) + norm_back(grad, gain2[...], one, inv)
        grad_attended[at, :] = value
        own_rows[at, :] = value.astype(BF16)

    def down_rows(dy):
        at = rows_along_y(net, dy)
        weights1[at, :] = dot_tn(cots[:, at], ffn_b[...]).astype(BF16)
        weights_down.start(dy)

    def out_rows(b):
        for h in range(2):
            cots[256 * b : 256 * b + 256, 1024 * h : 1024 * h + 1024] = dot_nt(
                ffn_b[256 * b : 256 * b + 256, :], down[1024 * h : 1024 * h + 1024, :]
            ).astype(BF16)

    def up_rows(dy):
        at = rows_along_y(net, dy)
        up[at, :] = dot_tn(rows[:, at], grad_up[...]).astype(BF16)
        weights_up.start(dy)

    load_hat = net.keep(hat_out, act.at[:, pl.ds(0, 256)])
    load_kept = net.keep(kept_out, slope)
    load_table = net.keep(table_in, gffn.at[:, pl.ds(0, 256)])
    for sender in line2 + line_cot + [gather1, gather_proj, gather_down, gather_up]:
        sender.sent()
    for t in total:
        t.part_sent()
    pl.semaphore_signal(credit.at[0], inc=1, device_id=net.along_x(0, 1), device_id_type=MESH)
    down_rows(2)
    down_rows(1)
    down_rows(-1)
    total[1].pass_on()
    down_rows(0)
    pl.semaphore_wait(credit.at[0], 1)
    total[0].finish(grad_attended)
    total[0].sent()
    by_rows(64, norm2_back)
    lines[0].start()
    out_rows(0)
    out_rows(1)
    up_rows(2)
    total[1].finish(grad_attended)
    total[1].sent()
    by_rows(64, norm2_back, 16, 64)
    lines[1].start()
    outer2_x, outer2_grid = outer_sums(1)
    outer2_x.start()
    weights_down.step()
    lines[0].forward_first()
    out_rows(2)
    weights_down.step()
    lines[0].forward_second()
    out_rows(3)
    load_weights = net.keep(weights1_out, down)
    weights_down.step()
    up_rows(1)
    lines[1].forward_first()
    weights_down.step()
    lines[1].forward_second()
    up_rows(-1)
    lines[0].share()
    weights_down.step()
    up_rows(0)
    lines[1].share()
    load_rows = net.keep(rows1_out, rows)
    weights_down.step(2)
    lines[0].finish_near()
    lines[0].finish()
    outer2_x.finish(line_whole.at[1])
    outer2_grid.start()

    ctx_parts, grad_mixed, grads_qkv, gctx = kept.at[:, 256:512], kept.at[:, 0:256], grad_up, act
    sum_t = SmallSum(net, own_t, slots_t, me, others)
    load_hat.wait()
    load_kept.wait()
    load_table.wait()
    load_weights.wait()

    def context_grad(k):
        for j in range(2):
            base = 512 * k + 256 * j
            found = dot_nn(part[base : base + 256, :], down[:, 768:])
            for i in range(4):
                at = 128 * (4 * j + i) + 64 * k
                gctx[at : at + 64, 256:512] = found[64 * i : 64 * i + 64]
                ctx_parts[base + 64 * i : base + 64 * i + 64, :] = slope[at : at + 64, 768:]

    context_grad(0)
    lines[1].finish_near()
    lines[1].finish()
    total_out = line_sums(net, cots, other, landing, True)
    for t in total_out:
        t.start(2, 1, -1, 0)
    context_grad(1)
    for b in range(4):

        def scale(at, to):
            grad, one = gctx[to, 256:512], act[to, 0:256]
            inner_sums[0] += fold8(grad * one)
            inner_sums[1] += fold8(grad)
            grad = grad * my_gain[...]
            gctx[to, 256:512] = grad
            partial[0, at, :] = lane_sums(grad)
            partial[1, at, :] = lane_sums(grad * one)

        block_rows(256 * b, scale)
        for i in range(2):
            own_t[i : i + 1, 256 * b : 256 * b + 256] = row_of(partial[i])
    sum_t.start()
    for t in total_out:
        t.chip_far()
    for t in total_out:
        t.chip_near()
    weights_proj = GridSum(net, proj_grads, landing_proj, done.at[2, :, :, :, pl.ds(0, 256)], shard_proj)
    for dy in (2, 1, -1, 0):
        at = rows_along_y(net, dy)
        proj_grads[at, :] = dot_tn(ctx_parts[...], part[:, at]).T.astype(BF16)
        weights_proj.start(dy)
    for line in lines:
        line.sent()
    both = sum_t.total() * (1.0 / D)
    for i, row in enumerate((inner_inv[...], both[0:1], both[1:2])):
        cols[i] = spread(row)

    def mixed_grad(at):
        inv, mean, slant = (wide(cols[i, at, :], 256) for i in range(3))
        grad = gctx[at, 256:512] - mean - act[at, 0:256] * slant
        grad_mixed[at, :] = (grad * inv).astype(BF16)

    by_rows(1024, mixed_grad, 64)
    total = line_sums(net, part, other, landing, False)
    weights_qkv = GridSum(
        net, weights1.at[:, pl.ds(0, 768)], landing_down.at[:, :, :, :, pl.ds(0, 768)],
        done.at[2, :, :, :, pl.ds(256, 768)], shard_qkv,
    )

    def output(at):
        layer_out[at, :] = attended[at, :].astype(BF16)

    def qkv_rows(dy):
        at = rows_along_y(net, dy)
        weights1[at, :768] = dot_tn(rows[:, at], grads_qkv[:, :768]).astype(BF16)
        weights_qkv.start(dy)

    def first_rows(q):
        at = pl.ds(sequence_at(net, q), SLOTS)
        mine = grads_qkv[at, :768]
        for h in range(2):
            part[at, 1024 * h : 1024 * h + 1024] = dot_nt(
                mine, down[1024 * h : 1024 * h + 1024, :768]
            ).astype(BF16)

    for q in range(4):
        base = sequence_at(net, q)
        at = pl.ds(base, SLOTS)
        query, key, value = (slope[at, 256 * i : 256 * i + 256] for i in range(3))
        found = attend_back(query, key, value, grad_mixed[at, :], caps[base // SLOTS], table)
        for i in range(3):
            grads_qkv[at, 256 * i : 256 * i + 256] = found[i]
        if q == 0:
            weights_down.step(2)
            weights_up.step(2)
        if q == 1:
            weights_down.step()
            weights_down.sent()
            for to in grid_neighbours(net):
                pl.semaphore_signal(credit.at[2], inc=1, device_id=to, device_id_type=MESH)
            for t in total_out:
                t.pass_on()
            weights_up.step()
        if q == 2:
            weights_up.step(2)
            weights_proj.step(3)
        if q == 3:
            weights_up.step(2)
    load_rows.wait()
    pl.semaphore_wait(credit.at[2], 4)
    qkv_rows(2)
    qkv_rows(1)
    for t in total_out:
        t.finish(attended, True)
        t.part_sent()
        t.sent()
    for to in (net.along_x(0, 1), net.along_x(1), net.along_x(-1)):
        pl.semaphore_signal(credit.at[1], inc=1, device_id=to, device_id_type=MESH)
    first_rows(0)
    pl.semaphore_wait(credit.at[1], 3)
    for t in total:
        t.start(2)
    first_rows(1)
    for t in total:
        t.start(0)
        t.chip_far()
    qkv_rows(-1)
    first_rows(2)
    for t in total:
        t.start(1, -1)
    first_rows(3)
    for t in total:
        t.chip_near()
    qkv_rows(0)
    for t in total:
        t.pass_on()
    weights_up.step(2)
    weights_qkv.step(3)
    weights_proj.step(3)
    by_rows(128, output)
    io.put(layer_out)
    for k, (lane, n) in enumerate(((0, 256), (256, 256), (512, 1024), (1536, 1024))):
        terms = inner_sums[k] if k < 2 else unit_sums[k - 2]
        inner[0:1, lane : lane + n] = jnp.sum(terms, 0, keepdims=True)
    inner_grid = SmallSum(net, inner, inner_slots, me_grid, grid)
    inner_grid.start()

    def norm1_back(at):
        grad = attended[at, :]
        one, inv = norm_parts(tokens[at, :].astype(F32))
        sums[0] += fold8(grad * one)
        sums[1] += fold8(grad)
        value = grad_attended[at, :] + norm_back(grad, gain1[...], one, inv)
        grad_input[at, :] = value.astype(BF16)

    total[0].finish(attended)
    by_rows(64, norm1_back)
    weights_qkv.step(2)
    weights_up.step()
    weights_proj.step(3)
    weights_qkv.step(2)
    total[1].finish(attended)
    by_rows(64, norm1_back, 16, 64)
    io.put(grad_input)
    outer1_x, outer1_grid = outer_sums(0)
    outer1_x.start()
    weights_qkv.step(2)
    outer1_x.finish(line_whole.at[0])
    outer1_grid.start()
    weights_qkv.step()
    weights_proj.step()
    inner_grid.finish(inner_whole)
    share_inner = PairShare(net, inner_whole, inner_out)
    share_inner.start()
    for weights in (weights_down, weights_up, weights_proj):
        weights.step()
    outer2_grid.finish(outer2_out)
    outer1_grid.finish(outer1_out)
    share_inner.finish()
    io.put()
    weights_qkv.step()
    for t in total:
        t.part_sent()
    for sender in [*total, weights_up, weights_proj, weights_qkv, sum_s, *sum_u, sum_t]:
        sender.sent()
    for sender in (share_caps, share_inner, inner_grid, outer1_x, outer1_grid, outer2_x, outer2_grid):
        sender.sent()
    for weights in (weights_down, weights_up, weights_proj, weights_qkv):
        weights.pair_sent()
    net.close()


def layer_call(ins):
    big, half = VMEM((1024, D), BF16), VMEM((D, 1024), BF16)
    square, tall = VMEM((1024, 1024), F32), VMEM((1024, 1024), BF16)
    grid_land = VMEM((2, 5, 6, 32, 1024), BF16)
    unit, own, stats = VMEM((1, 1024), F32), VMEM((2, 1024), F32), VMEM((8, 2, 1024), F32)
    return comm_call(
        layer_kernel,
        "layer",
        1,
        ins,
        (VMEM, pltpu.SMEM) + (VMEM,) * 9 + (HBM,) * 7,
        (
            shape((1024, D), BF16),
            shape((D, 1024), BF16),
            shape((1024, 1024), BF16),
            shape((1024, 256), F32),
            shape((4, 32, 1024), BF16),
            shape((4, 32, 1024), BF16),
            shape((4, 32, 256), BF16),
            shape((4, 32, 768), BF16),
            shape((128, D), BF16),
            shape((128, D), BF16),
            shape((2, D), F32),
            shape((2, D), F32),
            shape((4, 1, 2560), F32),
        ),
        (HBM,) * 8 + (VMEM,) * 5,
        [
            VMEM((128, D), BF16),
            big,
            big,
            big,
            half,
            half,
            half,
            square,
            square,
            tall,
            tall,
            tall,
            VMEM((4, 256, 128), F32),
            VMEM((3, 1024, 128), F32),
            VMEM((8, 128), jnp.int32),
            VMEM((4, 8, 128), jnp.int32),
            unit,
            unit,
            VMEM((1, 256), F32),
            VMEM((128, D), F32),
            VMEM((128, D), F32),
            VMEM((D, 256), BF16),
            own,
            stats,
            VMEM((2, 4, 512), F32),
            VMEM((2, 8, 4, 512), F32),
            own,
            stats,
            VMEM((2, 4, 64, D), BF16),
            VMEM((2, 6, 32, D), BF16),
            grid_land,
            grid_land,
            VMEM((2, 5, 6, 32, 256), BF16),
            VMEM((3, 2, 2, 32, 1024), BF16),
            unit,
            VMEM((2, 8, 256), F32),
            VMEM((2, 8, 1024), F32),
            VMEM((4, 8, D), F32),
            VMEM((2, 2, D), F32),
            VMEM((2, 8, 2, D), F32),
            VMEM((2, 16, 2, D), F32),
            VMEM((2, 2, D), F32),
            VMEM((1, 2560), F32),
            VMEM((16, 1, 2560), F32),
            VMEM((1, 2560), F32),
        ],
        63,
        (50, 154, 37),
    )


def last_kernel(
    layer_in, input_in, shard_qkv, shard_proj, shard_up, shard_down, outer1, outer2, inner,
    layer_out, grad_input, gain1, bias1, query, key, value, inner_gain, inner_bias, proj,
    gain2, bias2, up, ffn_gain, ffn_bias, down,
):
    layer_out[...] = layer_in[...]
    grad_input[...] = input_in[...]
    for i, refs in enumerate(((gain1, gain2), (bias1, bias2))):
        refs[0][...] = outer1[i : i + 1, :]
        refs[1][...] = outer2[i : i + 1, :]
    for d in range(4):
        for i, ref in enumerate((query, key, value)):
            ref[:, 256 * d : 256 * d + 256] = shard_qkv[d, :, 256 * i : 256 * i + 256].astype(F32)
        proj[:, 256 * d : 256 * d + 256] = shard_proj[d].astype(F32)
        up[:, 1024 * d : 1024 * d + 1024] = shard_up[d].astype(F32)
        down[:, 1024 * d : 1024 * d + 1024] = shard_down[d].astype(F32)
        for ref, lane, n in (
            (inner_gain, 0, 256), (inner_bias, 256, 256), (ffn_gain, 512, 1024), (ffn_bias, 1536, 1024),
        ):
            ref[:, n * d : n * d + n] = inner[d, :, lane : lane + n]


def whole(dims):
    return pl.BlockSpec(dims, lambda i: (0,) * len(dims))


def last_call(*ins):
    row, small, big = shape((1, D), F32), shape((32, 1024), F32), shape((32, 4096), F32)
    rows = shape((128, D), BF16)
    unit, wide = shape((1, 1024), F32), shape((1, 4096), F32)
    outs = (
        rows, rows, row, row, small, small, small, unit, unit, small, row, row, big, wide, wide, big,
    )
    return pl.pallas_call(
        last_kernel,
        out_shape=outs,
        grid=(1,),
        in_specs=[whole(v.shape) for v in ins],
        out_specs=[whole(v.shape) for v in outs],
        compiler_params=pltpu.CompilerParams(vmem_limit_bytes=63 << 20),
        name="results",
    )(*ins)


def per_device(
    tokens, caption_len, norm1_gain, norm1_bias, w_query, w_key, w_value, inner_gain, inner_bias,
    w_proj, norm2_gain, norm2_bias, w_up, ffn_norm_gain, ffn_norm_bias, w_down, cotangent,
):
    table = jnp.asarray(tables().reshape(1024, 256))
    line = lambda v: v.reshape(1, -1)
    *_, down, up, proj, qkv, layer_out, grad_input, outer1, outer2, inner = layer_call((
        tokens, caption_len, line(norm1_gain), line(norm1_bias), line(inner_gain), line(inner_bias),
        line(norm2_gain), line(norm2_bias), line(ffn_norm_gain), line(ffn_norm_bias), cotangent,
        w_query, w_key, w_value, w_proj.T, w_up, w_down.T, table,
    ))
    (
        layer_out, grad_input, gain1, bias1, query, key, value, gain_i, bias_i, proj, gain2, bias2,
        up, gain_f, bias_f, down,
    ) = last_call(layer_out, grad_input, qkv, proj, up, down, outer1, outer2, inner)
    flat = lambda v: v.reshape(-1)
    return (
        layer_out, grad_input, flat(gain1), flat(bias1), query, key, value, flat(gain_i),
        flat(bias_i), proj.T, flat(gain2), flat(bias2), up, flat(gain_f), flat(bias_f), down.T,
    )


def solution(mesh):
    rows = P(("seq", "ffn"), None)
    by_rows_, by_columns, half = P("seq", "ffn"), P("ffn", "seq"), P("ffn")
    return jax.shard_map(
        per_device,
        mesh=mesh,
        in_specs=(
            rows, P("seq"), P(), P(), by_rows_, by_rows_, by_rows_, half, half, by_columns,
            P(), P(), by_rows_, half, half, by_columns, rows,
        ),
        out_specs=(
            rows, rows, P(), P(), by_rows_, by_rows_, by_rows_, half, half, by_columns,
            P(), P(), by_rows_, half, half, by_columns,
        ),
        check_vma=False,
    )
```

```python
import functools

import jax
import jax.numpy as jnp
import numpy as np
from jax import lax
from jax.experimental import pallas as pl
from jax.experimental.pallas import tpu as pltpu
from jax.sharding import PartitionSpec as P

D = 2048
HEAD_DIM = 64
FF = 8192
SLOTS = 256
IMAGE = 64
EPS = 1e-05
F32 = jnp.float32
BF16 = jnp.bfloat16
MESH = pl.DeviceIdType.MESH
VMEM = pltpu.VMEM
HBM = pltpu.HBM


def device_at(y, x, z, c):
    return (((y * 2 + x % 2) * 4 + z) * 2 + c, x // 2)


def line_slot(x, c):
    return ((x % 2) * 2 + c) * 2 + x // 2


class Net:
    def __init__(self, send, recv, local):
        seq, ffn = lax.axis_index("seq"), lax.axis_index("ffn")
        self.y, self.z, self.c = seq // 16, (seq // 2) % 4, seq % 2
        self.x = ffn * 2 + (seq // 8) % 2
        self.send, self.recv, self.local = send, recv, local
        self.n_send, self.n_recv, self.n_local = 0, 0, 0

    def along_x(self, dx, dc=0):
        return device_at(self.y, (self.x + dx) % 4, self.z, (self.c + dc) % 2)

    def along_y(self, dy):
        return device_at((self.y + dy) % 4, self.x, self.z, self.c)

    def along_z(self, dz):
        return device_at(self.y, self.x, (self.z + dz) % 4, self.c)

    def pair(self, dx, dc):
        x = (self.x // 2) * 2 + (self.x + dx) % 2
        return device_at(self.y, x, self.z, (self.c + dc) % 2)

    def greet(self, partners):
        self.barrier, self.partners = pltpu.get_barrier_semaphore(), len(partners)
        for partner in partners:
            pl.semaphore_signal(self.barrier, inc=1, device_id=partner, device_id_type=MESH)

    def met(self):
        pl.semaphore_wait(self.barrier, self.partners)

    def out(self):
        self.n_send += 1
        return self.send.at[self.n_send - 1]

    def into(self):
        self.n_recv += 1
        return self.recv.at[self.n_recv - 1]

    def push(self, src, dst, device, out, into):
        pltpu.make_async_remote_copy(
            src_ref=src,
            dst_ref=dst,
            send_sem=out,
            recv_sem=into,
            device_id=device,
            device_id_type=MESH,
        ).start()

    def copies(self, semaphore, same_bytes):
        return pltpu.make_async_remote_copy(
            src_ref=same_bytes,
            dst_ref=same_bytes,
            send_sem=semaphore,
            recv_sem=semaphore,
            device_id=self.along_x(0, 1),
            device_id_type=MESH,
        )

    def arrived(self, into, same_bytes):
        self.copies(into, same_bytes).wait_recv()

    def left(self, out, same_bytes):
        self.copies(out, same_bytes).wait_send()

    def keep(self, src, dst):
        copy = pltpu.make_async_copy(src, dst, self.local.at[self.n_local])
        self.n_local += 1
        copy.start()
        return copy

    def close(self):
        found = self.n_send, self.n_recv, self.n_local
        assert found == tuple(s.shape[0] for s in (self.send, self.recv, self.local)), found


def add_into(dst, *terms):
    def step(i, carry):
        rows = pl.ds(pl.multiple_of(i * 16, 16), 16)
        total = terms[0][rows, :].astype(F32)
        for term in terms[1:]:
            total = total + term[rows, :].astype(F32)
        dst[rows, :] = total.astype(dst.dtype)
        return carry

    lax.fori_loop(0, dst.shape[0] // 16, step, 0)


def slot_row(slot, off, n, by_parts):
    return pl.multiple_of(off * 8 + slot * 64 if by_parts else slot * 128 + off, n)


class LineGather:
    def __init__(self, net, own, full, off=0, n=128, by_parts=False):
        self.net, self.full, self.off, self.n, self.by_parts = net, full, off, n, by_parts
        self.own = own.at[pl.ds(off, n)]
        self.own_half = [own.at[pl.ds(off + n // 2 * h, n // 2)] for h in range(2)]
        self.out = net.out()
        self.first, self.second, self.third, self.near, self.rest = (net.into() for _ in range(5))

    def block(self, dx, dc=0, half=None):
        net, n = self.net, self.n
        base = slot_row(line_slot((net.x + dx) % 4, (net.c + dc) % 2), self.off, n, self.by_parts)
        if half is None:
            return self.full.at[pl.ds(base, n)]
        return self.full.at[pl.ds(pl.multiple_of(base + n // 2 * half, n // 2), n // 2)]

    def push(self, src, dst, device, into):
        self.net.push(src, dst, device, self.out, into)

    def same(self, ref, device, into):
        self.net.push(ref, ref, device, self.out, into)

    def bytes_of(self, k):
        return self.full.at[pl.ds(0, k * self.n)]

    def start_first(self):
        net = self.net
        self.push(self.own_half[0], self.block(0, 0, 0), net.along_x(1), self.first)
        self.push(self.own_half[1], self.block(0, 0, 1), net.along_x(-1), self.first)

    def start_second(self):
        net = self.net
        self.push(self.own_half[1], self.block(0, 0, 1), net.along_x(1), self.second)
        self.push(self.own_half[0], self.block(0, 0, 0), net.along_x(-1), self.second)
        self.push(self.own, self.block(0), net.along_x(0, 1), self.rest)
        self.kept = net.keep(self.own, self.block(0))

    def start(self):
        self.start_first()
        self.start_second()

    def forward_first(self):
        net = self.net
        net.arrived(self.first, self.bytes_of(1))
        self.same(self.block(-1, 0, 0), net.along_x(1), self.third)
        self.same(self.block(1, 0, 1), net.along_x(-1), self.third)

    def forward_second(self):
        net = self.net
        net.arrived(self.second, self.bytes_of(1))
        self.same(self.block(-1), net.along_x(0, 1), self.near)
        self.same(self.block(1), net.along_x(0, 1), self.near)

    def forward(self):
        self.forward_first()
        self.forward_second()

    def share(self):
        net = self.net
        net.arrived(self.third, self.bytes_of(1))
        self.same(self.block(2, 0, 0), net.along_x(0, 1), self.rest)
        self.same(self.block(2, 0, 1), net.along_x(0, 1), self.rest)

    def finish_near(self):
        self.net.arrived(self.near, self.bytes_of(2))

    def finish(self):
        self.net.arrived(self.rest, self.bytes_of(2))
        self.kept.wait()

    def sent(self):
        self.net.left(self.out, self.bytes_of(7))


class RingSum:
    def __init__(self, net, mine, landing, ahead, behind, out, far, near):
        self.net, self.mine, self.landing = net, mine, landing
        self.ahead, self.behind, self.out = ahead, behind, out
        self.far, self.near = far, near

    def start_far(self):
        net, land = self.net, self.landing
        net.push(self.mine(2, 0), land.at[0], self.ahead, self.out, self.far)
        net.push(self.mine(2, 1), land.at[1], self.behind, self.out, self.far)

    def start_near(self, d):
        net, land = self.net, self.landing
        if d == 1:
            net.push(self.mine(1, 1), land.at[3], self.ahead, self.out, self.near)
        else:
            net.push(self.mine(-1, 0), land.at[4], self.behind, self.out, self.near)

    def pass_on(self):
        net, land = self.net, self.landing
        add_into(land.at[0], land.at[0], self.mine(1, 0))
        net.push(land.at[0], land.at[2], self.ahead, self.out, self.near)
        add_into(land.at[1], land.at[1], self.mine(-1, 1))
        net.push(land.at[1], land.at[5], self.behind, self.out, self.near)

    def finish(self, out=None, onto=False):
        land = self.landing
        for h in (0, 1):
            to = land.at[2 + h] if out is None else out(h)
            terms = self.mine(0, h), land.at[2 + h], land.at[4 + h]
            add_into(to, *terms, *([to] if onto else []))


class LineSum:
    def __init__(self, net, part, other, landing, off, by_parts):
        self.net, self.part, self.other, self.landing = net, part, other, landing
        self.off, self.by_parts = off, by_parts
        self.out, self.ring_out = net.out(), net.out()
        self.first, self.rest = net.into(), net.into()
        ends = net.along_x(1), net.along_x(-1)
        self.far, self.near = net.into(), net.into()
        self.ring = RingSum(net, self.mine, landing, *ends, self.ring_out, self.far, self.near)

    def block(self, dx, dc):
        net = self.net
        slot = line_slot((net.x + dx) % 4, (net.c + dc) % 2)
        return self.part.at[pl.ds(slot_row(slot, self.off, 64, self.by_parts), 64)]

    def mine(self, d, half):
        return self.other.at[d % 4, pl.ds(32 * half, 32)]

    def start(self, *steps):
        for d in steps:
            into = self.first if d == 2 else self.rest
            place = self.other.at[d % 4]
            self.net.push(self.block(d, 1), place, self.net.along_x(0, 1), self.out, into)

    def add(self, d):
        add_into(self.other.at[d % 4], self.other.at[d % 4], self.block(d, 0))

    def chip_far(self):
        self.net.arrived(self.first, self.other.at[0])
        self.add(2)
        self.ring.start_far()

    def chip_near(self):
        self.net.arrived(self.rest, self.other.at[pl.ds(0, 3)])
        self.add(1)
        self.ring.start_near(1)
        self.add(-1)
        self.ring.start_near(-1)
        self.add(0)

    def part_sent(self):
        self.net.left(self.out, self.other)

    def pass_on(self):
        self.net.arrived(self.far, self.landing.at[pl.ds(0, 2)])
        self.ring.pass_on()

    def finish(self, out, onto=False):
        self.net.arrived(self.near, self.landing.at[pl.ds(2, 4)])
        self.ring.finish(lambda h: out.at[pl.ds(self.off + 32 * h, 32)], onto)

    def sent(self):
        self.net.left(self.ring_out, self.landing)


def line_sums(net, part, other, landing, by_parts):
    return [LineSum(net, part, other.at[k], landing.at[k], 64 * k, by_parts) for k in range(2)]


def line_gathers(net, own, full):
    return [LineGather(net, own, full, 64 * k, 64, True) for k in range(2)]


def shard_rows(ref, y, x_lo, z, c=None):
    if c is None:
        return ref.at[pl.ds(pl.multiple_of(((y * 2 + x_lo) * 4 + z) * 64, 64), 64)]
    return ref.at[pl.ds(pl.multiple_of((((y * 2 + x_lo) * 4 + z) * 2 + c) * 32, 32), 32)]


PAIR_STEPS = ((1, 0), (1, 1), (0, 1))


class GridGather:
    def __init__(self, net, pieces, full):
        self.net, self.pieces, self.full = net, pieces, full
        self.out, self.pair_out = net.out(), net.out()
        self.pair_into, self.last = net.into(), net.into()
        self.p, self.f = net.into(), net.into()
        self.q = {dp: net.into() for dp in (0, -1, 1, 2)}

    def bytes_of(self, rows):
        return self.full.at[pl.ds(0, rows)]

    def exchange(self):
        net = self.net
        spot = shard_rows(self.full, net.y, net.x % 2, net.z, net.c)
        for dx, dc in PAIR_STEPS:
            to = ((net.x + dx) % 2) * 2 + (net.c + dc) % 2
            net.push(self.piece(to), spot, net.pair(dx, dc), self.pair_out, self.pair_into)
        self.kept = net.keep(self.piece((net.x % 2) * 2 + net.c), spot)

    def piece(self, d):
        return self.pieces.at[pl.ds(pl.multiple_of(32 * d, 32), 32)]

    def slab(self, t, dp, dq, half=None):
        net = self.net
        dy, dz = (dq, dp) if t == 0 else (dp, dq)
        return shard_rows(self.full, (net.y + dy) % 4, t, (net.z + dz) % 4, half)

    def to_p(self, t, d):
        return self.net.along_z(d) if t == 0 else self.net.along_y(d)

    def to_q(self, t, d):
        return self.net.along_y(d) if t == 0 else self.net.along_z(d)

    def same(self, ref, device, into):
        self.net.push(ref, ref, device, self.out, into)

    def second(self, t, dp):
        for d in (1, -1):
            self.same(self.slab(t, dp, 0), self.to_q(t, d), self.q[dp])

    def start(self):
        self.net.arrived(self.pair_into, self.bytes_of(96))
        self.kept.wait()
        for t in (0, 1):
            for d in (1, -1):
                self.same(self.slab(t, 0, 0), self.to_p(t, d), self.p)
        for t in (0, 1):
            self.second(t, 0)

    def near(self):
        self.net.arrived(self.p, self.bytes_of(256))
        for t in (0, 1):
            self.same(self.slab(t, -1, 0, 0), self.to_p(t, 1), self.f)
            self.same(self.slab(t, 1, 0, 1), self.to_p(t, -1), self.f)
        for t in (0, 1):
            self.second(t, -1)
            self.second(t, 1)

    def far(self):
        self.net.arrived(self.f, self.bytes_of(128))
        for t in (0, 1):
            self.second(t, 2)

    def pass_on(self, dp):
        self.net.arrived(self.q[dp], self.bytes_of(256))
        for t in (0, 1):
            self.same(self.slab(t, dp, -1, 0), self.to_q(t, 1), self.last)
            self.same(self.slab(t, dp, 1, 1), self.to_q(t, -1), self.last)

    def finish(self):
        self.net.arrived(self.last, self.bytes_of(512))

    def pair_sent(self):
        self.net.left(self.pair_out, self.bytes_of(96))

    def sent(self):
        self.net.left(self.out, self.bytes_of(1920))


class GridSum:
    def __init__(self, net, part, landing, done, shard):
        self.net, self.part, self.landing, self.done, self.shard = net, part, landing, done, shard
        self.out, self.pair_out, self.pair_into = net.out(), net.out(), net.into()
        self.rings = {}
        self.far = {dp: net.into() for dp in (2, 1, -1, 0, None)}
        self.near = {dp: net.into() for dp in (2, 1, -1, 0, None)}
        for t in (0, 1):
            for dp in (2, 1, -1, 0):
                self.rings[t, dp] = RingSum(
                    net,
                    functools.partial(self.term, t, dp),
                    landing.at[t, dp % 4],
                    self.to_q(t, 1),
                    self.to_q(t, -1),
                    self.out,
                    self.far[dp],
                    self.near[dp],
                )
            self.rings[t] = RingSum(
                net,
                functools.partial(self.column, t),
                landing.at[t, 4],
                self.to_p(t, 1),
                self.to_p(t, -1),
                self.out,
                self.far[None],
                self.near[None],
            )
        self.steps = [
            functools.partial(self.pass_on, 2),
            functools.partial(self.pass_on, 1),
            functools.partial(self.pass_on, -1),
            functools.partial(self.finish, 2),
            functools.partial(self.pass_on, 0),
            functools.partial(self.finish, 1),
            functools.partial(self.finish, -1),
            self.pass_on_last,
            functools.partial(self.finish, 0),
            self.finish_last,
            self.collect,
        ]

    def to_p(self, t, d):
        return self.net.along_z(d) if t == 0 else self.net.along_y(d)

    def to_q(self, t, d):
        return self.net.along_y(d) if t == 0 else self.net.along_z(d)

    def term(self, t, dp, dq, half):
        net = self.net
        dy, dz = (dq, dp) if t == 0 else (dp, dq)
        return shard_rows(self.part, (net.y + dy) % 4, t, (net.z + dz) % 4, half)

    def column(self, t, dp, half):
        return self.landing.at[t, dp % 4, 2 + half]

    def start(self, dy):
        for dp in (2, 1, -1, 0):
            if dy == 2:
                self.rings[0, dp].start_far()
            elif dy:
                self.rings[0, dp].start_near(dy)
        self.rings[1, dy].start_far()
        self.rings[1, dy].start_near(1)
        self.rings[1, dy].start_near(-1)

    def step(self, n=1):
        for _ in range(n):
            self.steps.pop(0)()

    def bytes_of(self, rows):
        return self.part.at[pl.ds(0, rows)]

    def pass_on(self, dp):
        self.net.arrived(self.far[dp], self.bytes_of(128))
        for t in (0, 1):
            self.rings[t, dp].pass_on()

    def finish(self, dp):
        self.net.arrived(self.near[dp], self.bytes_of(256))
        for t in (0, 1):
            self.rings[t, dp].finish()
            if dp == 2:
                self.rings[t].start_far()
            elif dp:
                self.rings[t].start_near(dp)

    def pass_on_last(self):
        self.net.arrived(self.far[None], self.bytes_of(128))
        for t in (0, 1):
            self.rings[t].pass_on()

    def finish_last(self):
        net = self.net
        net.arrived(self.near[None], self.bytes_of(256))
        for t in (0, 1):
            self.rings[t].finish(lambda half: self.done.at[t, half])
        me = (net.x % 2) * 2 + net.c
        for dx, dc in PAIR_STEPS:
            src = self.done.at[(net.x + dx) % 2, (net.c + dc) % 2]
            net.push(src, self.shard.at[me], net.pair(dx, dc), self.pair_out, self.pair_into)
        self.kept = net.keep(self.done.at[net.x % 2, net.c], self.shard.at[me])

    def collect(self):
        self.net.arrived(self.pair_into, self.shard.at[pl.ds(0, 3)])
        self.kept.wait()

    def sent(self):
        self.net.left(self.out, self.part.at[pl.ds(0, 1920)])

    def pair_sent(self):
        self.net.left(self.pair_out, self.shard.at[pl.ds(0, 3)])


class SmallSum:
    def __init__(self, net, own, slots, me, partners):
        self.net, self.own, self.slots, self.me, self.partners = net, own, slots, me, partners
        self.out, self.into = net.out(), net.into()

    def start(self):
        for to, _ in self.partners:
            self.net.push(self.own, self.slots.at[self.me], to, self.out, self.into)
        self.slots[self.me] = self.own[...]

    def total(self):
        self.net.arrived(self.into, self.slots.at[pl.ds(0, len(self.partners))])
        total = self.slots[0]
        for i in range(1, self.slots.shape[0]):
            total = total + self.slots[i]
        return total

    def finish(self, out):
        out[...] = self.total()

    def sent(self):
        self.net.left(self.out, self.slots.at[pl.ds(0, len(self.partners))])


class PairShare:
    def __init__(self, net, own, slots):
        self.net, self.own, self.slots = net, own, slots
        self.out, self.into = net.out(), net.into()

    def start(self):
        net = self.net
        me = (net.x % 2) * 2 + net.c
        for dx, dc in PAIR_STEPS:
            net.push(self.own, self.slots.at[me], net.pair(dx, dc), self.out, self.into)
        self.slots[me] = self.own[...]

    def finish(self):
        self.net.arrived(self.into, self.slots.at[pl.ds(0, 3)])

    def sent(self):
        self.net.left(self.out, self.slots.at[pl.ds(0, 3)])


def line_partners(net):
    return [
        (net.along_x(dx, dc), ((net.x - dx) % 4) * 2 + (net.c + dc) % 2)
        for dx in range(4)
        for dc in range(2)
        if dx or dc
    ]


def grid_partners(net):
    return [
        (
            device_at((net.y + dy) % 4, net.x, (net.z + dz) % 4, net.c),
            ((net.y - dy) % 4) * 4 + (net.z - dz) % 4,
        )
        for dy in range(4)
        for dz in range(4)
        if dy or dz
    ]


def grid_neighbours(net):
    return [net.along_y(1), net.along_y(-1), net.along_z(1), net.along_z(-1)]


def spec(space):
    return pl.BlockSpec(memory_space=space)


def shape(dims, dtype):
    return jax.ShapeDtypeStruct(dims, dtype)


class Staged:
    def __init__(self, loads, stores):
        self.loads, self.stores, self.started = loads, stores, []
        for copy, _ in loads:
            copy.start()

    def wait(self, *refs):
        for copy, ref in list(self.loads):
            if not refs or any(ref is r for r in refs):
                copy.wait()
                self.loads = [pair for pair in self.loads if pair[1] is not ref]

    def put(self, *refs):
        for copy, ref in list(self.stores):
            if not refs or any(ref is r for r in refs):
                copy.start()
                self.started.append(copy)
                self.stores = [pair for pair in self.stores if pair[1] is not ref]

    def finish(self):
        self.wait()
        self.put()
        for copy in self.started:
            copy.wait()


def comm_call(body, name, collective_id, ins, in_spaces, outs, out_spaces, scratch, mib, sems):
    n_in, n_out = len(ins), len(outs)
    buffers = [space(v.shape, v.dtype) for v, space in zip(ins, in_spaces) if space is not HBM]
    buffers += [space(v.shape, v.dtype) for v, space in zip(outs, out_spaces) if space is not HBM]
    n = len(buffers)

    def kernel(*refs):
        sem = refs[-1]
        rest = list(refs[n_in + n_out : n_in + n_out + n])
        loads, stores, args = [], [], []
        for i, (ref, space) in enumerate(zip(refs, (*in_spaces, *out_spaces))):
            if space is HBM:
                args.append(ref)
                continue
            buffer = rest.pop(0)
            args.append(buffer)
            at = sem.at[len(loads) + len(stores)]
            if i < n_in:
                loads.append((pltpu.make_async_copy(ref, buffer, at), buffer))
            else:
                stores.append((pltpu.make_async_copy(buffer, ref, at), buffer))
        io = Staged(loads, stores)
        body(io, *args, *refs[n_in + n_out + n : -1])
        io.finish()

    return pl.pallas_call(
        kernel,
        out_shape=outs,
        in_specs=[spec(HBM)] * n_in,
        out_specs=[spec(HBM)] * n_out,
        scratch_shapes=buffers
        + scratch
        + [pltpu.SemaphoreType.REGULAR((3,))]
        + [pltpu.SemaphoreType.DMA((k,)) for k in (*sems, n)],
        compiler_params=pltpu.CompilerParams(
            collective_id=collective_id, has_side_effects=True, vmem_limit_bytes=mib << 20
        ),
        name=name,
    )(*ins)


def norm_parts(values):
    center = jnp.mean(values, -1, keepdims=True)
    spread = jnp.mean(values * values, -1, keepdims=True) - center * center
    inv_std = lax.rsqrt(spread + EPS)
    return (values - center) * inv_std, inv_std


def by_rows(rows, step, chunk=16, off=0):
    def body(i, carry):
        step(pl.ds(pl.multiple_of(off + i * chunk, chunk), chunk))
        return carry

    lax.fori_loop(0, rows // chunk, body, 0)


def norm_back(grad, gain, hat, inv_std):
    scaled = grad * gain
    return inv_std * (
        scaled
        - jnp.mean(scaled, -1, keepdims=True)
        - hat * jnp.mean(scaled * hat, -1, keepdims=True)
    )


def fold8(values):
    return values[:8] + values[8:]


def block_rows(base, step):
    def body(i, carry):
        step(
            pl.ds(pl.multiple_of(i * 16, 16), 16),
            pl.ds(pl.multiple_of(base + i * 16, 16), 16),
        )
        return carry

    lax.fori_loop(0, 16, body, 0)


def lane_sums(values):
    total = values[:, :128]
    for k in range(1, values.shape[1] // 128):
        total = total + values[:, 128 * k : 128 * k + 128]
    return total


def row_of(partial):
    return jnp.sum(partial.T, 0, keepdims=True)


def spread(row):
    return jnp.broadcast_to(row, (128, row.shape[1])).T


def wide(values, lanes):
    return jnp.concatenate([values] * (lanes // 128), 1)


def xpos_tables(direction):
    half = HEAD_DIM // 2
    pair = np.arange(half, dtype=np.float32)
    frequency = np.power(np.float32(10000.0), -pair / half).astype(np.float32)
    zeta = ((pair / half + 0.4) / 1.4).astype(np.float32)
    position = np.arange(SLOTS, dtype=np.float32)[:, None]
    angle = (position * frequency).astype(np.float32).astype(np.float64)
    decay = np.exp(direction * position / 512.0 * np.log(zeta.astype(np.float64)))
    cosine, sine = np.cos(angle) * decay, np.sin(angle) * decay
    cosine = np.concatenate([cosine] * 2, -1)
    sine = np.concatenate([-sine, sine], -1)
    return np.tile(cosine, (1, 4)).astype(np.float32), np.tile(sine, (1, 4)).astype(np.float32)


def tables():
    return np.stack([*xpos_tables(1.0), *xpos_tables(-1.0)])


def swapped(values):
    lane = lax.broadcasted_iota(jnp.int32, values.shape, 1)
    return jnp.where(lane % 64 < 32, pltpu.roll(values, 224, 1), pltpu.roll(values, 32, 1))


def dot_nn(a, b):
    return lax.dot_general(a, b, (((1,), (0,)), ((), ())), preferred_element_type=F32)


def dot_nt(a, b):
    return lax.dot_general(a, b, (((1,), (1,)), ((), ())), preferred_element_type=F32)


def dot_tn(a, b):
    return lax.dot_general(a, b, (((0,), (0,)), ((), ())), preferred_element_type=F32)


def head_of(values, head):
    lane = lax.broadcasted_iota(jnp.int32, values.shape, 1)
    return jnp.where(lane // 64 == head, values, jnp.zeros_like(values))


def head_probs(query, key, head, allowed):
    scores = dot_nt(head_of(query, head), key) * HEAD_DIM**-0.5
    scores = jnp.where(allowed, scores, -1e30)
    exps = jnp.exp(scores - jnp.max(scores, -1, keepdims=True))
    return exps / jnp.sum(exps, -1, keepdims=True)


def allowed_slots(cap):
    query = lax.broadcasted_iota(jnp.int32, (SLOTS, SLOTS), 0)
    key = lax.broadcasted_iota(jnp.int32, (SLOTS, SLOTS), 1)
    return (key <= query) & (key < IMAGE + cap[0:1, 0:1])


def attend(rows, weights, cap, table, at, kept, mixed):
    qkv = dot_nn(rows, weights[:, :768])
    query, key, value = qkv[:, :256], qkv[:, 256:512], qkv[:, 512:].astype(BF16)
    query = (query * table(0) + swapped(query) * table(1)).astype(BF16)
    key = (key * table(2) + swapped(key) * table(3)).astype(BF16)
    for i, part in enumerate((query, key, value)):
        kept[at, 256 * i : 256 * i + 256] = part
    allowed = allowed_slots(cap)
    total = jnp.zeros((SLOTS, 256), F32)
    for head in range(4):
        probs = head_probs(query, key, head, allowed).astype(BF16)
        total = total + dot_nn(probs, head_of(value, head))
    mixed[at, :256] = total


def attend_back(query, key, value, grad, cap, table):
    allowed = allowed_slots(cap)
    grad_query = jnp.zeros((SLOTS, 256), F32)
    grad_key = jnp.zeros((SLOTS, 256), F32)
    grad_value = jnp.zeros((SLOTS, 256), F32)
    for head in range(4):
        probs = head_probs(query, key, head, allowed)
        grad_head = head_of(grad, head)
        grad_probs = dot_nt(grad_head, value)
        grad_value = grad_value + dot_tn(probs.astype(BF16), grad_head)
        delta = jnp.sum(probs * grad_probs, -1, keepdims=True)
        grad_scores = (probs * (grad_probs - delta)).astype(BF16)
        grad_query = grad_query + dot_nn(grad_scores, head_of(key, head))
        grad_key = grad_key + dot_tn(grad_scores, head_of(query, head))
    grad_query = grad_query * HEAD_DIM**-0.5
    grad_key = grad_key * HEAD_DIM**-0.5
    return (
        (grad_query * table(0) + swapped(grad_query * table(1))).astype(BF16),
        (grad_key * table(2) + swapped(grad_key * table(3))).astype(BF16),
        grad_value.astype(BF16),
    )


def place_of(net):
    return (net.x % 2) * 2 + net.c


def my_lanes(ref, net, n):
    return ref[:, pl.ds(pl.multiple_of(place_of(net) * n, n), n)]


def sequence_at(net, q):
    seq_of = ((net.x + q // 2) % 2) * 2 + (net.c + 1 + q) % 2
    return pl.multiple_of(seq_of * SLOTS, SLOTS)


def rows_along_y(net, dy):
    return pl.ds(pl.multiple_of(((net.y + dy) % 4) * 512, 512), 512)


def layer_kernel(
    io, tokens, cap, gain1, bias1, inner_gain, inner_bias, gain2, bias2, ffn_gains, ffn_biases, cot,
    w_query, w_key, w_value, w_proj, w_up, w_down, table_in,
    rows1_out, weights1_out, kept_out, hat_out, shard_down, shard_up, shard_proj, shard_qkv,
    layer_out, grad_input, outer1_out, outer2_out, inner_out,
    own_rows, rows, cots, part, weights1, up, down, act, gffn, slope, kept, grad_up, partial, cols,
    caps_in, caps, ffn_gain, ffn_bias, my_gain, attended, grad_attended,
    proj_grads,     own_s, slots_s, own_u, slots_u, own_t, slots_t, other, landing, landing_down, landing_up,
    landing_proj, done, inner_inv, inner_sums, unit_sums, sums, outer, line_slots, grid_slots, line_whole,
    inner, inner_slots, inner_whole, credit, send, recv, local,
):
    net = Net(send, recv, local)
    others, grid = line_partners(net), grid_partners(net)
    net.greet([to for to, _ in others + grid])
    me, me_grid = net.x * 2 + net.c, net.y * 4 + net.z
    shards = [w_query, w_key, w_value, w_proj]
    load1 = [net.keep(w, act.at[pl.ds(32 * i, 32)]) for i, w in enumerate(shards)]
    load_table = net.keep(table_in, gffn.at[:, pl.ds(0, 256)])
    load2 = [
        net.keep(w.at[:, pl.ds(1024 * d, 1024)], act.at[pl.ds(128 + 128 * i + 32 * d, 32)])
        for i, w in enumerate((w_down, w_up))
        for d in range(4)
    ]
    gather1 = GridGather(
        net, slope.at[pl.ds(0, 128), pl.ds(0, 768)], weights1.at[:, pl.ds(0, 768)]
    )
    gather_proj = GridGather(
        net, slope.at[pl.ds(0, 128), pl.ds(768, 256)], weights1.at[:, pl.ds(768, 256)]
    )
    gather_down = GridGather(net, slope.at[pl.ds(128, 128)], down)
    gather_up = GridGather(net, slope.at[pl.ds(256, 128)], up)
    line1 = LineGather(net, own_rows, rows)
    line_cot = line_gathers(net, cot, cots)
    total = line_sums(net, part, other, landing, False)
    line2 = line_gathers(net, own_rows, rows)
    sum_s = SmallSum(net, own_s, slots_s, me, others)
    share_caps = PairShare(net, caps_in, caps)

    for i in range(4):
        load1[i].wait()
        for d in range(4):
            slope[32 * d : 32 * d + 32, 256 * i : 256 * i + 256] = act[
                32 * i : 32 * i + 32, 256 * d : 256 * d + 256
            ].astype(BF16)
    io.wait(tokens, cap, gain1, bias1)

    def norm1(at):
        one, _ = norm_parts(tokens[at, :].astype(F32))
        own_rows[at, :] = (one * gain1[...] + bias1[...]).astype(BF16)

    by_rows(128, norm1)
    caps_in[...] = jnp.full((8, 128), cap[0], jnp.int32)

    net.met()
    gather1.exchange()
    line1.start()
    gather_proj.exchange()
    share_caps.start()
    gather1.start()
    for copy in load2:
        copy.wait()
    slope[128:384, :] = act[128:384, :].astype(BF16)
    io.wait()
    for ref in (unit_sums, sums, inner_sums):
        ref[...] = jnp.zeros_like(ref)
    ffn_gain[...], ffn_bias[...] = my_lanes(ffn_gains, net, 1024), my_lanes(ffn_biases, net, 1024)
    my_gain[...] = my_lanes(inner_gain, net, 256)
    gather1.near()
    gather1.pass_on(0)
    gather1.far()
    line1.forward()
    gather_down.exchange()
    gather1.pass_on(-1)
    gather1.pass_on(1)
    gather1.pass_on(2)
    gather_proj.start()
    gather_up.exchange()
    for line in line_cot:
        line.start()
    line1.finish_near()
    share_caps.finish()
    load_table.wait()
    gather1.finish()

    table = lambda i: gffn[256 * i : 256 * i + 256, :256]
    for q in range(4):
        base = sequence_at(net, (q + 2) % 4)
        at = pl.ds(base, SLOTS)
        if q == 2:
            line1.finish()
            save_rows = net.keep(rows, rows1_out)
        attend(rows[at, :], weights1, caps.at[base // SLOTS], table, at, kept, act)
        both = act[at, :256]
        partial[0] = lane_sums(both)
        partial[1] = lane_sums(both * both)
        for i in range(2):
            own_s[i : i + 1, at] = row_of(partial[i])
        if q == 0:
            line1.share()
            gather_proj.near()
            gather_proj.pass_on(0)
        if q == 1:
            gather_proj.far()
            gather_proj.pass_on(-1)
            gather_proj.pass_on(1)
            gather_down.start()
        if q == 2:
            gather_proj.pass_on(2)
    sum_s.start()
    for line in line_cot:
        line.forward()
    gather_down.near()
    gather_up.start()
    gather_proj.finish()
    save_weights = net.keep(weights1, weights1_out)
    both = sum_s.total()
    center = both[0:1] * (1.0 / D)
    inv_std = lax.rsqrt(both[1:2] * (1.0 / D) - center * center + EPS)
    inner_inv[...] = inv_std
    cols[0] = spread(center)
    cols[1] = spread(inv_std)
    my_bias = my_lanes(inner_bias, net, 256)

    def inner_norm(at):
        one = (act[at, :256] - wide(cols[0, at, :], 256)) * wide(cols[1, at, :], 256)
        act[at, 256:512] = one
        kept[at, 768:] = (one * my_gain[...] + my_bias).astype(BF16)

    by_rows(1024, inner_norm, 64)
    gather_down.pass_on(0)
    gather_down.far()
    save_hat = net.keep(act.at[:, pl.ds(256, 256)], hat_out)
    save_kept = net.keep(kept, kept_out)
    save_rows.wait()
    line1.sent()
    for q in range(4):
        at = pl.ds(sequence_at(net, q), SLOTS)
        mine = kept[at, 768:]
        for h in range(2):
            part[at, 1024 * h : 1024 * h + 1024] = dot_nt(
                mine, weights1[1024 * h : 1024 * h + 1024, 768:]
            ).astype(BF16)
        for t in total:
            if q == 0:
                t.start(2)
            if q == 1:
                t.start(0)
                t.chip_far()
            if q == 2:
                t.start(1, -1)
    total[0].chip_near()
    total[0].pass_on()
    total[1].chip_near()
    gather_down.pass_on(-1)
    gather_down.pass_on(1)
    total[1].pass_on()
    for line in line_cot:
        line.share()
    gather_up.near()
    gather_up.pass_on(0)
    save_weights.wait()

    def norm2(at):
        values = tokens[at, :].astype(F32) + attended[at, :]
        attended[at, :] = values
        one, _ = norm_parts(values)
        own_rows[at, :] = (one * gain2[...] + bias2[...]).astype(BF16)

    def cot_rows(b):
        at = slice(256 * b, 256 * b + 256)
        gffn[at, :] = dot_nn(cots[at, :], down[...])

    total[0].finish(attended)
    by_rows(64, norm2)
    line2[0].start()
    gather_down.pass_on(2)
    for line in line_cot:
        line.finish_near()
        line.finish()
    total[1].finish(attended)
    by_rows(64, norm2, 16, 64)
    line2[1].start_first()
    line2[0].forward_first()
    line2[1].start_second()
    gather_up.far()
    gather_down.finish()
    cot_rows(0)
    gather_up.pass_on(-1)
    gather_up.pass_on(1)
    line2[0].forward_second()
    cot_rows(1)
    gather_up.pass_on(2)
    line2[1].forward_first()
    cot_rows(2)
    line2[0].share()
    cot_rows(3)
    line2[1].forward_second()
    gather_up.finish()
    line2[0].finish_near()
    line2[0].finish()
    save_hat.wait()
    save_kept.wait()
    for t in total:
        t.part_sent()
        t.sent()
    for gather in (gather1, gather_proj, gather_down, gather_up):
        gather.pair_sent()

    sum_u = [SmallSum(net, own_u.at[k], slots_u.at[k], me, others) for k in range(2)]
    for k in range(2):
        if k == 1:
            line2[1].finish_near()
            line2[1].finish()
        for j in range(2):
            base = 512 * k + 256 * j
            act[base : base + 256, :] = dot_nn(rows[base : base + 256, :], up[...])

            def gelu(at, to):
                value = act[to, :]
                cdf = 0.5 * (1.0 + lax.erf(value * np.float32(0.5**0.5)))
                density = jnp.exp(-0.5 * value * value) * np.float32((2 * np.pi) ** -0.5)
                slope[to, :] = (cdf + value * density).astype(BF16)
                value = value * cdf
                act[to, :] = value
                partial[0, at, :] = lane_sums(value)
                partial[1, at, :] = lane_sums(value * value)
                grad = gffn[to, :]
                unit_sums[1] += fold8(grad)
                grad = grad * ffn_gain[...]
                partial[2, at, :] = lane_sums(grad)
                partial[3, at, :] = lane_sums(grad * value)

            block_rows(base, gelu)
            for i in range(4):
                own_u[k, i : i + 1, 256 * j : 256 * j + 256] = row_of(partial[i])
            if k == 0 and j == 0:
                line2[1].share()
        sum_u[k].start()

    total = line_sums(net, part, other, landing, True)
    ffn_b = kept
    for k in range(2):
        both = sum_u[k].total()
        center = both[0:1] * (1.0 / FF)
        inv_std = lax.rsqrt(both[1:2] * (1.0 / FF) - center * center + EPS)
        slant = (both[3:4] - center * both[2:3]) * inv_std * (1.0 / FF)
        its = slice(512 * k, 512 * k + 512)
        for i, row in enumerate((center, inv_std, both[2:3] * (1.0 / FF))):
            cols[i, its, :] = spread(row)

        def normed(at):
            hat = (act[at, :] - wide(cols[0, at, :], 1024)) * wide(cols[1, at, :], 1024)
            act[at, :] = hat
            ffn_b[at, :] = (hat * ffn_gain[...] + ffn_bias[...]).astype(BF16)
            unit_sums[0] += fold8(gffn[at, :] * hat)

        by_rows(512, normed, 16, 512 * k)
        cols[0, its, :] = spread(slant)
        if k == 1:
            total[0].chip_near()
        for j in range(2):
            base = pl.multiple_of(512 * k + 256 * ((net.x + j) % 2), 256)

            def back(at, to):
                grad = gffn[to, :] * ffn_gain[...] - wide(cols[2, to, :], 1024)
                grad = grad - act[to, :] * wide(cols[0, to, :], 1024)
                grad = grad * wide(cols[1, to, :], 1024)
                grad_up[to, :] = (grad * slope[to, :].astype(F32)).astype(BF16)

            block_rows(base, back)
            mine = grad_up[pl.ds(base, 256), :]
            for h in range(2):
                part[pl.ds(base, 256), 1024 * h : 1024 * h + 1024] = dot_nt(
                    mine, up[1024 * h : 1024 * h + 1024, :]
                ).astype(BF16)
            if j == 0:
                total[k].start(2, 0)
            else:
                total[k].start(1, -1)
                total[k].chip_far()
    total[0].pass_on()
    total[1].chip_near()

    weights_down = GridSum(net, weights1, landing_down, done.at[0], shard_down)
    weights_up = GridSum(net, up, landing_up, done.at[1], shard_up)
    lines = line_gathers(net, own_rows, part)

    def outer_sums(k):
        for i in range(2):
            outer[k, i : i + 1, :] = jnp.sum(sums[2 * k + i], 0, keepdims=True)
        return (
            SmallSum(net, outer.at[k], line_slots.at[k], me, others),
            SmallSum(net, line_whole.at[k], grid_slots.at[k], me_grid, grid),
        )

    def norm2_back(at):
        grad = grad_attended[at, :]
        one, inv = norm_parts(attended[at, :])
        sums[2] += fold8(grad * one)
        sums[3] += fold8(grad)
        value = cot[at, :].astype(F32) + norm_back(grad, gain2[...], one, inv)
        grad_attended[at, :] = value
        own_rows[at, :] = value.astype(BF16)

    def down_rows(dy):
        at = rows_along_y(net, dy)
        weights1[at, :] = dot_tn(cots[:, at], ffn_b[...]).astype(BF16)
        weights_down.start(dy)

    def out_rows(b):
        for h in range(2):
            cots[256 * b : 256 * b + 256, 1024 * h : 1024 * h + 1024] = dot_nt(
                ffn_b[256 * b : 256 * b + 256, :], down[1024 * h : 1024 * h + 1024, :]
            ).astype(BF16)

    def up_rows(dy):
        at = rows_along_y(net, dy)
        up[at, :] = dot_tn(rows[:, at], grad_up[...]).astype(BF16)
        weights_up.start(dy)

    load_hat = net.keep(hat_out, act.at[:, pl.ds(0, 256)])
    load_kept = net.keep(kept_out, slope)
    load_table = net.keep(table_in, gffn.at[:, pl.ds(0, 256)])
    for sender in line2 + line_cot + [gather1, gather_proj, gather_down, gather_up]:
        sender.sent()
    for t in total:
        t.part_sent()
    pl.semaphore_signal(credit.at[0], inc=1, device_id=net.along_x(0, 1), device_id_type=MESH)
    down_rows(2)
    down_rows(1)
    down_rows(-1)
    total[1].pass_on()
    down_rows(0)
    pl.semaphore_wait(credit.at[0], 1)
    total[0].finish(grad_attended)
    total[0].sent()
    by_rows(64, norm2_back)
    lines[0].start()
    out_rows(0)
    out_rows(1)
    up_rows(2)
    total[1].finish(grad_attended)
    total[1].sent()
    by_rows(64, norm2_back, 16, 64)
    lines[1].start()
    outer2_x, outer2_grid = outer_sums(1)
    outer2_x.start()
    weights_down.step()
    lines[0].forward_first()
    out_rows(2)
    weights_down.step()
    lines[0].forward_second()
    out_rows(3)
    load_weights = net.keep(weights1_out, down)
    weights_down.step()
    up_rows(1)
    lines[1].forward_first()
    weights_down.step()
    lines[1].forward_second()
    up_rows(-1)
    lines[0].share()
    weights_down.step()
    up_rows(0)
    lines[1].share()
    load_rows = net.keep(rows1_out, rows)
    weights_down.step(2)
    lines[0].finish_near()
    lines[0].finish()
    outer2_x.finish(line_whole.at[1])
    outer2_grid.start()

    ctx_parts, grad_mixed, grads_qkv, gctx = kept.at[:, 256:512], kept.at[:, 0:256], grad_up, act
    sum_t = SmallSum(net, own_t, slots_t, me, others)
    load_hat.wait()
    load_kept.wait()
    load_table.wait()
    load_weights.wait()

    def context_grad(k):
        for j in range(2):
            base = 512 * k + 256 * j
            found = dot_nn(part[base : base + 256, :], down[:, 768:])
            for i in range(4):
                at = 128 * (4 * j + i) + 64 * k
                gctx[at : at + 64, 256:512] = found[64 * i : 64 * i + 64]
                ctx_parts[base + 64 * i : base + 64 * i + 64, :] = slope[at : at + 64, 768:]

    context_grad(0)
    lines[1].finish_near()
    lines[1].finish()
    total_out = line_sums(net, cots, other, landing, True)
    for t in total_out:
        t.start(2, 1, -1, 0)
    context_grad(1)
    for b in range(4):

        def scale(at, to):
            grad, one = gctx[to, 256:512], act[to, 0:256]
            inner_sums[0] += fold8(grad * one)
            inner_sums[1] += fold8(grad)
            grad = grad * my_gain[...]
            gctx[to, 256:512] = grad
            partial[0, at, :] = lane_sums(grad)
            partial[1, at, :] = lane_sums(grad * one)

        block_rows(256 * b, scale)
        for i in range(2):
            own_t[i : i + 1, 256 * b : 256 * b + 256] = row_of(partial[i])
    sum_t.start()
    for t in total_out:
        t.chip_far()
    for t in total_out:
        t.chip_near()
    weights_proj = GridSum(net, proj_grads, landing_proj, done.at[2, :, :, :, pl.ds(0, 256)], shard_proj)
    for dy in (2, 1, -1, 0):
        at = rows_along_y(net, dy)
        proj_grads[at, :] = dot_tn(ctx_parts[...], part[:, at]).T.astype(BF16)
        weights_proj.start(dy)
    for line in lines:
        line.sent()
    both = sum_t.total() * (1.0 / D)
    for i, row in enumerate((inner_inv[...], both[0:1], both[1:2])):
        cols[i] = spread(row)

    def mixed_grad(at):
        inv, mean, slant = (wide(cols[i, at, :], 256) for i in range(3))
        grad = gctx[at, 256:512] - mean - act[at, 0:256] * slant
        grad_mixed[at, :] = (grad * inv).astype(BF16)

    by_rows(1024, mixed_grad, 64)
    total = line_sums(net, part, other, landing, False)
    weights_qkv = GridSum(
        net, weights1.at[:, pl.ds(0, 768)], landing_down.at[:, :, :, :, pl.ds(0, 768)],
        done.at[2, :, :, :, pl.ds(256, 768)], shard_qkv,
    )

    def output(at):
        layer_out[at, :] = attended[at, :].astype(BF16)

    def qkv_rows(dy):
        at = rows_along_y(net, dy)
        weights1[at, :768] = dot_tn(rows[:, at], grads_qkv[:, :768]).astype(BF16)
        weights_qkv.start(dy)

    def first_rows(q):
        at = pl.ds(sequence_at(net, q), SLOTS)
        mine = grads_qkv[at, :768]
        for h in range(2):
            part[at, 1024 * h : 1024 * h + 1024] = dot_nt(
                mine, down[1024 * h : 1024 * h + 1024, :768]
            ).astype(BF16)

    for q in range(4):
        base = sequence_at(net, q)
        at = pl.ds(base, SLOTS)
        query, key, value = (slope[at, 256 * i : 256 * i + 256] for i in range(3))
        found = attend_back(query, key, value, grad_mixed[at, :], caps[base // SLOTS], table)
        for i in range(3):
            grads_qkv[at, 256 * i : 256 * i + 256] = found[i]
        if q == 0:
            weights_down.step(2)
            weights_up.step(2)
        if q == 1:
            weights_down.step()
            weights_down.sent()
            for to in grid_neighbours(net):
                pl.semaphore_signal(credit.at[2], inc=1, device_id=to, device_id_type=MESH)
            for t in total_out:
                t.pass_on()
            weights_up.step()
        if q == 2:
            weights_up.step(2)
            weights_proj.step(3)
        if q == 3:
            weights_up.step(2)
    load_rows.wait()
    pl.semaphore_wait(credit.at[2], 4)
    qkv_rows(2)
    qkv_rows(1)
    for t in total_out:
        t.finish(attended, True)
        t.part_sent()
        t.sent()
    for to in (net.along_x(0, 1), net.along_x(1), net.along_x(-1)):
        pl.semaphore_signal(credit.at[1], inc=1, device_id=to, device_id_type=MESH)
    first_rows(0)
    pl.semaphore_wait(credit.at[1], 3)
    for t in total:
        t.start(2)
    first_rows(1)
    for t in total:
        t.start(0)
        t.chip_far()
    first_rows(2)
    for t in total:
        t.start(1, -1)
    first_rows(3)
    for t in total:
        t.chip_near()
    qkv_rows(-1)
    qkv_rows(0)
    for t in total:
        t.pass_on()
    weights_up.step(2)
    weights_qkv.step(3)
    weights_proj.step(3)
    by_rows(128, output)
    io.put(layer_out)
    for k, (lane, n) in enumerate(((0, 256), (256, 256), (512, 1024), (1536, 1024))):
        terms = inner_sums[k] if k < 2 else unit_sums[k - 2]
        inner[0:1, lane : lane + n] = jnp.sum(terms, 0, keepdims=True)
    inner_grid = SmallSum(net, inner, inner_slots, me_grid, grid)
    inner_grid.start()

    def norm1_back(at):
        grad = attended[at, :]
        one, inv = norm_parts(tokens[at, :].astype(F32))
        sums[0] += fold8(grad * one)
        sums[1] += fold8(grad)
        value = grad_attended[at, :] + norm_back(grad, gain1[...], one, inv)
        grad_input[at, :] = value.astype(BF16)

    weights_qkv.step(2)
    total[0].finish(attended)
    by_rows(64, norm1_back)
    weights_up.step()
    weights_proj.step(3)
    weights_qkv.step(2)
    total[1].finish(attended)
    by_rows(64, norm1_back, 16, 64)
    io.put(grad_input)
    outer1_x, outer1_grid = outer_sums(0)
    outer1_x.start()
    weights_qkv.step(2)
    outer1_x.finish(line_whole.at[0])
    outer1_grid.start()
    weights_qkv.step()
    weights_proj.step()
    inner_grid.finish(inner_whole)
    share_inner = PairShare(net, inner_whole, inner_out)
    share_inner.start()
    for weights in (weights_down, weights_up, weights_proj):
        weights.step()
    outer2_grid.finish(outer2_out)
    outer1_grid.finish(outer1_out)
    share_inner.finish()
    io.put()
    weights_qkv.step()
    for t in total:
        t.part_sent()
    for sender in [*total, weights_up, weights_proj, weights_qkv, sum_s, *sum_u, sum_t]:
        sender.sent()
    for sender in (share_caps, share_inner, inner_grid, outer1_x, outer1_grid, outer2_x, outer2_grid):
        sender.sent()
    for weights in (weights_down, weights_up, weights_proj, weights_qkv):
        weights.pair_sent()
    net.close()


def layer_call(ins):
    big, half = VMEM((1024, D), BF16), VMEM((D, 1024), BF16)
    square, tall = VMEM((1024, 1024), F32), VMEM((1024, 1024), BF16)
    grid_land = VMEM((2, 5, 6, 32, 1024), BF16)
    unit, own, stats = VMEM((1, 1024), F32), VMEM((2, 1024), F32), VMEM((8, 2, 1024), F32)
    return comm_call(
        layer_kernel,
        "layer",
        1,
        ins,
        (VMEM, pltpu.SMEM) + (VMEM,) * 9 + (HBM,) * 7,
        (
            shape((1024, D), BF16),
            shape((D, 1024), BF16),
            shape((1024, 1024), BF16),
            shape((1024, 256), F32),
            shape((4, 32, 1024), BF16),
            shape((4, 32, 1024), BF16),
            shape((4, 32, 256), BF16),
            shape((4, 32, 768), BF16),
            shape((128, D), BF16),
            shape((128, D), BF16),
            shape((2, D), F32),
            shape((2, D), F32),
            shape((4, 1, 2560), F32),
        ),
        (HBM,) * 8 + (VMEM,) * 5,
        [
            VMEM((128, D), BF16),
            big,
            big,
            big,
            half,
            half,
            half,
            square,
            square,
            tall,
            tall,
            tall,
            VMEM((4, 256, 128), F32),
            VMEM((3, 1024, 128), F32),
            VMEM((8, 128), jnp.int32),
            VMEM((4, 8, 128), jnp.int32),
            unit,
            unit,
            VMEM((1, 256), F32),
            VMEM((128, D), F32),
            VMEM((128, D), F32),
            VMEM((D, 256), BF16),
            own,
            stats,
            VMEM((2, 4, 512), F32),
            VMEM((2, 8, 4, 512), F32),
            own,
            stats,
            VMEM((2, 4, 64, D), BF16),
            VMEM((2, 6, 32, D), BF16),
            grid_land,
            grid_land,
            VMEM((2, 5, 6, 32, 256), BF16),
            VMEM((3, 2, 2, 32, 1024), BF16),
            unit,
            VMEM((2, 8, 256), F32),
            VMEM((2, 8, 1024), F32),
            VMEM((4, 8, D), F32),
            VMEM((2, 2, D), F32),
            VMEM((2, 8, 2, D), F32),
            VMEM((2, 16, 2, D), F32),
            VMEM((2, 2, D), F32),
            VMEM((1, 2560), F32),
            VMEM((16, 1, 2560), F32),
            VMEM((1, 2560), F32),
        ],
        63,
        (50, 154, 37),
    )


def last_kernel(
    layer_in, input_in, shard_qkv, shard_proj, shard_up, shard_down, outer1, outer2, inner,
    layer_out, grad_input, gain1, bias1, query, key, value, inner_gain, inner_bias, proj,
    gain2, bias2, up, ffn_gain, ffn_bias, down,
):
    layer_out[...] = layer_in[...]
    grad_input[...] = input_in[...]
    for i, refs in enumerate(((gain1, gain2), (bias1, bias2))):
        refs[0][...] = outer1[i : i + 1, :]
        refs[1][...] = outer2[i : i + 1, :]
    for d in range(4):
        for i, ref in enumerate((query, key, value)):
            ref[:, 256 * d : 256 * d + 256] = shard_qkv[d, :, 256 * i : 256 * i + 256].astype(F32)
        proj[:, 256 * d : 256 * d + 256] = shard_proj[d].astype(F32)
        up[:, 1024 * d : 1024 * d + 1024] = shard_up[d].astype(F32)
        down[:, 1024 * d : 1024 * d + 1024] = shard_down[d].astype(F32)
        for ref, lane, n in (
            (inner_gain, 0, 256), (inner_bias, 256, 256), (ffn_gain, 512, 1024), (ffn_bias, 1536, 1024),
        ):
            ref[:, n * d : n * d + n] = inner[d, :, lane : lane + n]


def whole(dims):
    return pl.BlockSpec(dims, lambda i: (0,) * len(dims))


def last_call(*ins):
    row, small, big = shape((1, D), F32), shape((32, 1024), F32), shape((32, 4096), F32)
    rows = shape((128, D), BF16)
    unit, wide = shape((1, 1024), F32), shape((1, 4096), F32)
    outs = (
        rows, rows, row, row, small, small, small, unit, unit, small, row, row, big, wide, wide, big,
    )
    return pl.pallas_call(
        last_kernel,
        out_shape=outs,
        grid=(1,),
        in_specs=[whole(v.shape) for v in ins],
        out_specs=[whole(v.shape) for v in outs],
        compiler_params=pltpu.CompilerParams(vmem_limit_bytes=63 << 20),
        name="results",
    )(*ins)


def per_device(
    tokens, caption_len, norm1_gain, norm1_bias, w_query, w_key, w_value, inner_gain, inner_bias,
    w_proj, norm2_gain, norm2_bias, w_up, ffn_norm_gain, ffn_norm_bias, w_down, cotangent,
):
    table = jnp.asarray(tables().reshape(1024, 256))
    line = lambda v: v.reshape(1, -1)
    *_, down, up, proj, qkv, layer_out, grad_input, outer1, outer2, inner = layer_call((
        tokens, caption_len, line(norm1_gain), line(norm1_bias), line(inner_gain), line(inner_bias),
        line(norm2_gain), line(norm2_bias), line(ffn_norm_gain), line(ffn_norm_bias), cotangent,
        w_query, w_key, w_value, w_proj.T, w_up, w_down.T, table,
    ))
    (
        layer_out, grad_input, gain1, bias1, query, key, value, gain_i, bias_i, proj, gain2, bias2,
        up, gain_f, bias_f, down,
    ) = last_call(layer_out, grad_input, qkv, proj, up, down, outer1, outer2, inner)
    flat = lambda v: v.reshape(-1)
    return (
        layer_out, grad_input, flat(gain1), flat(bias1), query, key, value, flat(gain_i),
        flat(bias_i), proj.T, flat(gain2), flat(bias2), up, flat(gain_f), flat(bias_f), down.T,
    )


def solution(mesh):
    rows = P(("seq", "ffn"), None)
    by_rows_, by_columns, half = P("seq", "ffn"), P("ffn", "seq"), P("ffn")
    return jax.shard_map(
        per_device,
        mesh=mesh,
        in_specs=(
            rows, P("seq"), P(), P(), by_rows_, by_rows_, by_rows_, half, half, by_columns,
            P(), P(), by_rows_, half, half, by_columns, rows,
        ),
        out_specs=(
            rows, rows, P(), P(), by_rows_, by_rows_, by_rows_, half, half, by_columns,
            P(), P(), by_rows_, half, half, by_columns,
        ),
        check_vma=False,
    )
```
